32 devices in a mesh: batch: 16 (over z, y, x), branch: 2 (over core).
Axes of the slice: x: 2, y: 2, z: 4, core: 2. Of those that a mesh axis runs over, the one named last changes fastest.
Arguments:
- inputs: bfloat16 [8192, 2048], P('batch', 'branch'), may hold values from -6 to 6
- cotangent: bfloat16 [8192, 2048], P('batch', 'branch'), may hold values from -7.2 to 7.2
- segment_ids: int32 [16, 512], P('batch'), may hold values from 0 to 2, never falling along the last dimension, each value on 1 to 256 neighbouring positions
- w_qkv: float32 [2048, 3, 2048], P('batch', None, 'branch'), may hold values from -0.125 to 0.125
- w_out: float32 [2048, 2048], P('branch', 'batch'), may hold values from -0.75 to 0.75
- w_fc1: float32 [2048, 8192], P('batch', 'branch'), may hold values from -0.125 to 0.125
- w_fc2: float32 [8192, 2048], P('branch', 'batch'), may hold values from -0.0625 to 0.0625
- norm_params: float32 [4, 2048], replicated, may hold values from -1.2 to 3.5, as said below
- proj_bias: float32 [5, 2048], P(None, 'branch'), may hold values from -4 to 4
- fc1_bias: float32 [8192], P('branch'), may hold values from -4 to 4
- qkv_rows: float32 [2048], P('batch'), may hold values from 2348810.2 to 9563013
- qkv_cols: float32 [3, 2048], P(None, 'branch'), may hold values from 838860.8 to 3187671
- out_rows: float32 [2048], P('branch'), may hold values from 72142.03 to 285212.7
- out_cols: float32 [2048], P('batch'), may hold values from 72142.03 to 285212.7
- fc1_rows: float32 [2048], P('batch'), may hold values from 1677721.6 to 6710886.5
- fc1_cols: float32 [8192], P('branch'), may hold values from 419430.4 to 1677721.6
- fc2_rows: float32 [8192], P('branch'), may hold values from 1140850.8 to 4529848.5
- fc2_cols: float32 [2048], P('batch'), may hold values from 4563403 to 18119394
- norm_second: float32 [4, 2048], replicated, may hold values from 1556.48 to 6225.92
- bias_second: float32 [5, 2048], P(None, 'branch'), may hold values from 1556.48 to 6225.92
- fc1b_second: float32 [8192], P('branch'), may hold values from 163.84 to 655.36
Outputs:
- output: bfloat16 [8192, 2048], P('batch', 'branch')
- input_grad: bfloat16 [8192, 2048], P('batch', 'branch')
- qkv_grad: float32 [2048, 3, 2048], P('batch', None, 'branch')
- qkv_weight: float32 [2048, 3, 2048], P('batch', None, 'branch')
- qkv_row_stat: float32 [2048], P('batch')
- qkv_col_stat: float32 [3, 2048], P(None, 'branch')
- qkv_copy: bfloat16 [2048, 3, 2048], P('batch', None, 'branch')
- out_grad: float32 [2048, 2048], P('branch', 'batch')
- out_weight: float32 [2048, 2048], P('branch', 'batch')
- out_row_stat: float32 [2048], P('branch')
- out_col_stat: float32 [2048], P('batch')
- out_copy: bfloat16 [2048, 2048], P('branch', 'batch')
- fc1_grad: float32 [2048, 8192], P('batch', 'branch')
- fc1_weight: float32 [2048, 8192], P('batch', 'branch')
- fc1_row_stat: float32 [2048], P('batch')
- fc1_col_stat: float32 [8192], P('branch')
- fc1_copy: bfloat16 [2048, 8192], P('batch', 'branch')
- fc2_grad: float32 [8192, 2048], P('branch', 'batch')
- fc2_weight: float32 [8192, 2048], P('branch', 'batch')
- fc2_row_stat: float32 [8192], P('branch')
- fc2_col_stat: float32 [2048], P('batch')
- fc2_copy: bfloat16 [8192, 2048], P('branch', 'batch')
- norm_grad: float32 [4, 2048], replicated
- norm_moment: float32 [4, 2048], replicated
- norm_new: float32 [4, 2048], replicated
- bias_grad: float32 [5, 2048], P(None, 'branch')
- bias_moment: float32 [5, 2048], P(None, 'branch')
- bias_new: float32 [5, 2048], P(None, 'branch')
- fc1b_grad: float32 [8192], P('branch')
- fc1b_moment: float32 [8192], P('branch')
- fc1b_new: float32 [8192], P('branch')
The draws below stay inside these ranges and needn't reach their ends.
Inputs may be any that keep to these rules, and one draw needn't show every extreme that they name: `segment_ids`: within each pack the ids never fall, each of the 3 ids is present, and one id holds exactly 256 positions, none more. `norm_params`: rows 0 and 2 are positive.
All inputs are finite; a program needn't handle non-finite values.
Results may differ from the reference program's by a relative error of at most 0.0065.
The reference program's roundings to bfloat16 on the way count: a program that leaves them out, or rounds other values in their place, can miss the bound.
Values may be sent and summed in bfloat16 or wider, within the bound.
A program may use at most 320 MiB of HBM per device.

```python
import math
import jax
import jax.numpy as jnp
import numpy as np
from jax import lax

D = 2048
HEADS = 16
HD = 128
ROT = 32
FF = 8192
TOK_DEV = 512
SEGS = 3
STEP = 10
PACKS = 16
TOKENS = 8192


def rising(extent, growth):
    return growth ** (jnp.arange(extent, dtype=jnp.float32) / (extent - 1))


def draw_cotangent(key, part):
    key = jax.random.fold_in(key, 11)
    values = jax.random.truncated_normal(key, -4.0, 4.0, (TOKENS, D), jnp.float32)
    return (values * 0.6 * rising(D, 3.0)[None, :]).astype(jnp.bfloat16)


def draw_norm_params(key, part):
    key = jax.random.fold_in(key, 23)
    gain_key, shift_key = jax.random.split(key)
    gain_rows = 0.6 * rising(D, 3.0)[None, :] * jax.random.uniform(gain_key, (2, D), jnp.float32, 0.75, 1.25)
    shift_rows = 0.3 * jax.random.truncated_normal(shift_key, -4.0, 4.0, (2, D), jnp.float32)
    return jnp.stack([gain_rows[0], shift_rows[0], gain_rows[1], shift_rows[1]]).astype(jnp.float32)


def level_of(key, shape, pieces, low, top_value):
    gain, own = 1.0, jax.random.fold_in(key, 6)
    for dim, parts in pieces:
        draws = jnp.exp(jax.random.uniform(jax.random.fold_in(own, dim), (parts,), jnp.float32, low / len(pieces), top_value / len(pieces)))
        gain = gain * jnp.repeat(draws, shape[dim] // parts).reshape([-1 if axis == dim else 1 for axis in range(len(shape))])
    return gain


def length_profile(count, total, bound, slope):
    weights = [(1 << 20) // math.isqrt(standing ** slope) + 1 for standing in range(2, count + 1)]
    rest, counts = total - bound - (count - 1), [1] * (count - 1)
    while rest > 0:
        candidates = [i for i in range(count - 1) if counts[i] < bound]
        mass, left = sum([weights[i] for i in candidates]), rest
        for i in candidates:
            extra = min(bound - counts[i], max(1, left * weights[i] // mass), rest)
            counts[i] = counts[i] + extra
            rest = rest - extra
    return np.array([bound] + counts)


def ragged(stream_key, count, total, limit, skew):
    if count == 2:
        one = jax.random.randint(stream_key, (), max(1, total - limit), min(limit, total - 1) + 1)
        return jnp.stack([one, total - one])
    tallies = jnp.asarray(length_profile(count, total, limit, skew), jnp.int32)
    couples = (count - 1) // 2
    source_of, receiver = tallies[1:1 + 2 * couples:2], tallies[2:2 + 2 * couples:2]
    margin = jnp.minimum(source_of - 1, limit - receiver)
    passed = jax.random.randint(jax.random.fold_in(stream_key, 1), (couples,), 0, 1 << 20) % (margin + 1)
    tallies = tallies.at[1:1 + 2 * couples:2].set(source_of - passed).at[2:2 + 2 * couples:2].set(receiver + passed)
    return tallies[jax.random.permutation(jax.random.fold_in(stream_key, 2), count)]


def centred(stream_key, shape, deviation, bound, cuts=(), held_as=jnp.bfloat16):
    gain = level_of(stream_key, shape, cuts, -0.22, 0.18) if cuts else 1.0
    values = jax.random.normal(stream_key, shape, jnp.float32) * deviation * gain
    return jnp.minimum(jnp.maximum(values, -bound), bound).astype(held_as)


def setup_inputs(seed: int = 0) -> dict:
    arg_keys = jax.random.split(jax.random.key(seed), 22)
    inputs = centred(arg_keys[0], (TOKENS, D), 1.0, 6.0, ((0, 16), (1, 2)))
    cotangent = draw_cotangent(jax.random.fold_in(arg_keys[21], 71), 0)
    segment_ids = jax.vmap(lambda own: jnp.searchsorted(jnp.cumsum(ragged(own, SEGS, TOK_DEV, TOK_DEV // 2, 2)), jnp.arange(TOK_DEV), side="right"))(jax.random.split(arg_keys[2], PACKS)).reshape((PACKS, TOK_DEV)).astype(jnp.int32)
    w_qkv = centred(arg_keys[3], (D, 3, D), D ** -0.5, 0.125, ((0, 16), (2, 2)), jnp.float32)
    w_out = centred(arg_keys[4], (D, D), (D // 32) ** -0.5, 0.75, ((0, 2), (1, 16)), jnp.float32)
    w_fc1 = centred(arg_keys[5], (D, FF), D ** -0.5, 0.125, ((0, 16), (1, 2)), jnp.float32)
    w_fc2 = centred(arg_keys[6], (FF, D), FF ** -0.5, 0.0625, ((0, 2), (1, 16)), jnp.float32)
    norm_params = draw_norm_params(jax.random.fold_in(arg_keys[21], 71), 0)
    proj_bias = centred(arg_keys[8], (5, D), 0.3, 4.0, ((1, 2),), jnp.float32)
    fc1_bias = centred(arg_keys[9], (FF,), 0.3, 4.0, ((0, 2),), jnp.float32)
    qkv_rows = jnp.clip(jnp.exp(math.log(9563013) - 1.403994 * jax.random.uniform(arg_keys[10], (D,), jnp.float32) ** level_of(arg_keys[10], (D,), ((0, 16),), -0.2, 0.2)), 2348810.2, 9563013)
    qkv_cols = jnp.clip(jnp.exp(math.log(3187671) - 1.335001 * jax.random.uniform(arg_keys[11], (3, D), jnp.float32) ** level_of(arg_keys[11], (3, D), ((1, 2),), -0.2, 0.2)), 838860.8, 3187671)
    out_rows = jnp.clip(jnp.exp(math.log(285212.7) - 1.37459834 * jax.random.uniform(arg_keys[12], (D,), jnp.float32) ** level_of(arg_keys[12], (D,), ((0, 2),), -0.2, 0.2)), 72142.03, 285212.7)
    out_cols = jnp.clip(jnp.exp(math.log(285212.7) - 1.37459834 * jax.random.uniform(arg_keys[13], (D,), jnp.float32) ** level_of(arg_keys[13], (D,), ((0, 16),), -0.2, 0.2)), 72142.03, 285212.7)
    fc1_rows = jnp.clip(jnp.exp(math.log(6710886.5) - 1.3862944 * jax.random.uniform(arg_keys[14], (D,), jnp.float32) ** level_of(arg_keys[14], (D,), ((0, 16),), -0.2, 0.2)), 1677721.6, 6710886.5)
    fc1_cols = jnp.clip(jnp.exp(math.log(1677721.6) - 1.3862944 * jax.random.uniform(arg_keys[15], (FF,), jnp.float32) ** level_of(arg_keys[15], (FF,), ((0, 2),), -0.2, 0.2)), 419430.4, 1677721.6)
    fc2_rows = jnp.clip(jnp.exp(math.log(4529848.5) - 1.3789142 * jax.random.uniform(arg_keys[16], (FF,), jnp.float32) ** level_of(arg_keys[16], (FF,), ((0, 2),), -0.2, 0.2)), 1140850.8, 4529848.5)
    fc2_cols = jnp.clip(jnp.exp(math.log(18119394) - 1.3789142 * jax.random.uniform(arg_keys[17], (D,), jnp.float32) ** level_of(arg_keys[17], (D,), ((0, 16),), -0.2, 0.2)), 4563403, 18119394)
    norm_second = jnp.clip(jnp.exp(jax.random.uniform(arg_keys[18], (4, D), jnp.float32, math.log(1556.48), math.log(6225.92))), 1556.48, 6225.92)
    bias_second = jnp.clip(jnp.exp(math.log(6225.92) - 1.3862944 * jax.random.uniform(arg_keys[19], (5, D), jnp.float32) ** level_of(arg_keys[19], (5, D), ((1, 2),), -0.2, 0.2)), 1556.48, 6225.92)
    fc1b_second = jnp.clip(jnp.exp(math.log(655.36) - 1.3862944 * jax.random.uniform(arg_keys[20], (FF,), jnp.float32) ** level_of(arg_keys[20], (FF,), ((0, 2),), -0.2, 0.2)), 163.84, 655.36)
    return {"inputs": inputs, "cotangent": cotangent, "segment_ids": segment_ids, "w_qkv": w_qkv, "w_out": w_out, "w_fc1": w_fc1, "w_fc2": w_fc2, "norm_params": norm_params, "proj_bias": proj_bias, "fc1_bias": fc1_bias, "qkv_rows": qkv_rows, "qkv_cols": qkv_cols, "out_rows": out_rows, "out_cols": out_cols, "fc1_rows": fc1_rows, "fc1_cols": fc1_cols, "fc2_rows": fc2_rows, "fc2_cols": fc2_cols, "norm_second": norm_second, "bias_second": bias_second, "fc1b_second": fc1b_second}


@jax.custom_vjp
def low(v):
    return lax.optimization_barrier(v.astype(jnp.bfloat16)).astype(jnp.float32)

@jax.custom_vjp
def low_back(v):
    return v

def low_keep(v):
    return (low(v), None)

def low_pass(kept, grad):
    return (grad,)

def back_keep(v):
    return (v, None)

def back_low(kept, grad):
    return (low(grad),)
low.defvjp(low_keep, low_pass)
low_back.defvjp(back_keep, back_low)
EPS_NORM = 1e-05
EPS_SQUARE = 1e-30
RATE = 0.3
FLOOR_RATE = 0.001
HIGH = lax.Precision.HIGHEST

def layer_norm(values, gain_row, shift_row):
    row_mean = lax.optimization_barrier(jnp.mean(values, axis=-1, keepdims=True))
    centered = values - row_mean
    variance = lax.optimization_barrier(jnp.mean(centered * centered, axis=-1, keepdims=True))
    return centered * lax.rsqrt(variance + EPS_NORM) * gain_row + shift_row

def rotate(tensor, cos_rows, sin_rows):
    halfway = ROT // 2
    first_part = tensor[..., :halfway]
    second_part = tensor[..., halfway:ROT]
    cos_part = cos_rows[:, None, :]
    sin_part = sin_rows[:, None, :]
    return jnp.concatenate([first_part * cos_part - second_part * sin_part, second_part * cos_part + first_part * sin_part, tensor[..., ROT:]], axis=-1)

def forward(values_in, segment, w_qkv, w_out, w_fc1, w_fc2, norm_params, proj_bias, fc1_bias):
    pack_length = values_in.shape[0]
    hidden_one = low(layer_norm(values_in, norm_params[0], norm_params[1]))
    hidden_two = low(layer_norm(values_in, norm_params[2], norm_params[3]))
    projected = jnp.dot(hidden_one, low(w_qkv).reshape(D, 3 * D), precision=HIGH).reshape(pack_length, 3, D)
    projected = low_back(projected + proj_bias[0:3][None])
    positions_idx = jnp.arange(pack_length)
    earlier = lax.optimization_barrier(jnp.sum((segment[None, :] < segment[:, None]).astype(jnp.int32), axis=1))
    places = (positions_idx - earlier).astype(jnp.float32)
    frequency = 10000.0 ** (-2.0 * jnp.arange(ROT // 2, dtype=jnp.float32) / ROT)
    angles = places[:, None] * frequency[None, :]
    cos_rows = jnp.cos(angles)
    sin_rows = jnp.sin(angles)
    queries = low_back(low(rotate(projected[:, 0].reshape(pack_length, HEADS, HD), cos_rows, sin_rows)))
    keys_rot = low_back(low(rotate(projected[:, 1].reshape(pack_length, HEADS, HD), cos_rows, sin_rows)))
    values_low = low(projected[:, 2].reshape(pack_length, HEADS, HD))
    allowed = (segment[None, :] == segment[:, None]) & (positions_idx[None, :] <= positions_idx[:, None])
    scores = low_back(jnp.einsum('qhd,khd->hqk', queries, keys_rot, precision=HIGH) * HD ** (-0.5))
    scores = jnp.where(allowed[None], scores, -1e+30)
    largest = lax.optimization_barrier(jnp.max(scores, axis=-1, keepdims=True))
    exponent = jnp.exp(scores - largest)
    probabilities = exponent / lax.optimization_barrier(jnp.sum(exponent, axis=-1, keepdims=True))
    context = jnp.einsum('hqk,khd->qhd', low(probabilities), values_low, precision=HIGH).reshape(pack_length, D)
    context = low_back(low(context))
    attention = jnp.dot(context, low(w_out), precision=HIGH)
    pre_act = low_back(jnp.dot(hidden_two, low(w_fc1), precision=HIGH) + fc1_bias)
    activated = low(jax.nn.gelu(pre_act, approximate=False))
    feed_out = jnp.dot(activated, low(w_fc2), precision=HIGH)
    return values_in + attention + feed_out + proj_bias[3] + proj_bias[4]

def decay_rate():
    return 1.0 - STEP ** (-0.8)

def factored(weight, gradient, rows_old, cols_old):
    decay = decay_rate()
    square = gradient * gradient + EPS_SQUARE
    rows_new = decay * rows_old + (1.0 - decay) * lax.optimization_barrier(jnp.sum(square, axis=1))
    cols_new = decay * cols_old + (1.0 - decay) * lax.optimization_barrier(jnp.sum(square, axis=0))
    update = gradient * jnp.sqrt(jnp.sum(rows_new)) * lax.rsqrt(rows_new)[:, None] * lax.rsqrt(cols_new)[None, :]
    clip_factor = jnp.maximum(1.0, jnp.sqrt(jnp.mean(update * update)))
    step_rate = RATE * jnp.maximum(FLOOR_RATE, jnp.sqrt(jnp.mean(weight * weight)))
    return (weight - step_rate * update / clip_factor, rows_new, cols_new)

def unfactored(vector, gradient, second):
    decay = decay_rate()
    second_new = decay * second + (1.0 - decay) * (gradient * gradient + EPS_SQUARE)
    update = gradient * lax.rsqrt(second_new)
    clip_factor = jnp.maximum(1.0, jnp.sqrt(lax.optimization_barrier(jnp.mean(update * update, axis=-1, keepdims=True))))
    step_rate = RATE * jnp.maximum(FLOOR_RATE, jnp.sqrt(lax.optimization_barrier(jnp.mean(vector * vector, axis=-1, keepdims=True))))
    return (second_new, vector - step_rate * update / clip_factor)

def reference(inputs, cotangent, segment_ids, w_qkv, w_out, w_fc1, w_fc2, norm_params, proj_bias, fc1_bias, qkv_rows, qkv_cols, out_rows, out_cols, fc1_rows, fc1_cols, fc2_rows, fc2_cols, norm_second, bias_second, fc1b_second):
    params = (w_qkv, w_out, w_fc1, w_fc2, norm_params, proj_bias, fc1_bias)
    packed_in = inputs.astype(jnp.float32).reshape(PACKS, TOK_DEV, D)
    packed_back = cotangent.astype(jnp.float32).reshape(PACKS, TOK_DEV, D)

    def one_pack(running, pack_item):
        pack_in, pack_back, segment = pack_item

        def apply_pack(values_in, *weights):
            return forward(values_in, segment, *weights)
        result, pull_back = jax.vjp(apply_pack, pack_in, *params)
        gradients = pull_back(pack_back)
        running = tuple((left + right for left, right in zip(running, gradients[1:])))
        return (running, (result.astype(jnp.bfloat16), gradients[0].astype(jnp.bfloat16)))
    zero_grads = tuple((jnp.zeros_like(weight) for weight in params))
    running, (outputs, input_grads) = lax.scan(one_pack, zero_grads, (packed_in, packed_back, segment_ids))
    qkv_grad, out_grad, fc1_grad, fc2_grad, norm_grad, bias_grad, fc1b_grad = running
    qkv_next, qkv_rows_new, qkv_cols_new = factored(w_qkv.reshape(D, 3 * D), qkv_grad.reshape(D, 3 * D), qkv_rows, qkv_cols.reshape(3 * D))
    out_next, out_rows_new, out_cols_new = factored(w_out, out_grad, out_rows, out_cols)
    fc1_next, fc1_rows_new, fc1_cols_new = factored(w_fc1, fc1_grad, fc1_rows, fc1_cols)
    fc2_next, fc2_rows_new, fc2_cols_new = factored(w_fc2, fc2_grad, fc2_rows, fc2_cols)
    norm_moment, norm_new = unfactored(norm_params, norm_grad, norm_second)
    bias_moment, bias_new = unfactored(proj_bias, bias_grad, bias_second)
    fc1b_moment, fc1b_new = unfactored(fc1_bias[None], fc1b_grad[None], fc1b_second[None])
    qkv_next = qkv_next.reshape(D, 3, D)
    return (outputs.reshape(TOKENS, D), input_grads.reshape(TOKENS, D), qkv_grad, qkv_next, qkv_rows_new, qkv_cols_new.reshape(3, D), qkv_next.astype(jnp.bfloat16), out_grad, out_next, out_rows_new, out_cols_new, out_next.astype(jnp.bfloat16), fc1_grad, fc1_next, fc1_rows_new, fc1_cols_new, fc1_next.astype(jnp.bfloat16), fc2_grad, fc2_next, fc2_rows_new, fc2_cols_new, fc2_next.astype(jnp.bfloat16), norm_grad, norm_moment, norm_new, bias_grad, bias_moment, bias_new, fc1b_grad, fc1b_moment[0], fc1b_new[0])
```

```python
import jax
import jax.numpy as jnp
from jax import lax
from jax.sharding import PartitionSpec as P

D = 2048
HD = 128
ROT = 32
FF = 8192
STEP = 10


EPS_NORM = 1e-05
EPS_SQUARE = 1e-30
RATE = 0.3
FLOOR_RATE = 0.001


def norm_parts(values, gain_row, shift_row):
    row_mean = jnp.mean(values, axis=-1, keepdims=True)
    centered = values - row_mean
    inverse = lax.rsqrt(jnp.mean(centered * centered, axis=-1, keepdims=True) + EPS_NORM)
    normed = centered * inverse
    return (normed, inverse, normed * gain_row + shift_row)


def rotate(tensor, cos_rows, sin_rows, direction):
    halfway = ROT // 2
    first_part = tensor[..., :halfway]
    second_part = tensor[..., halfway:ROT]
    cos_part = cos_rows[:, None, :]
    sin_part = sin_rows[:, None, :] * direction
    return jnp.concatenate(
        [
            first_part * cos_part - second_part * sin_part,
            second_part * cos_part + first_part * sin_part,
            tensor[..., ROT:].astype(jnp.float32),
        ],
        axis=-1,
    )


def decay_rate():
    return 1.0 - STEP ** (-0.8)


def squares(gradient):
    return gradient * gradient + EPS_SQUARE


def renew_stat(old_stat, new_sum):
    decay = decay_rate()
    return decay * old_stat + (1.0 - decay) * new_sum


def ratio_sum(gradient, rows_new, cols_new):
    return jnp.sum(gradient * gradient * (1.0 / rows_new)[:, None] * (1.0 / cols_new)[None, :])


def finish(weight, gradient, rows_new, cols_new, row_total, inverse_sum, old_square, entries):
    update = (
        gradient * jnp.sqrt(row_total) * lax.rsqrt(rows_new)[:, None] * lax.rsqrt(cols_new)[None, :]
    )
    clip_factor = jnp.maximum(1.0, jnp.sqrt(row_total * inverse_sum / entries))
    step_rate = RATE * jnp.maximum(FLOOR_RATE, jnp.sqrt(old_square / entries))
    return weight - step_rate * update / clip_factor


def second_step(gradient, second):
    second_new = renew_stat(second, squares(gradient))
    return (second_new, gradient * lax.rsqrt(second_new))


def vector_finish(vector, update, update_square, old_square, entries):
    clip_factor = jnp.maximum(1.0, jnp.sqrt(update_square / entries))[..., None]
    step_rate = RATE * jnp.maximum(FLOOR_RATE, jnp.sqrt(old_square / entries))[..., None]
    return vector - step_rate * update / clip_factor


INNER = 4
FF_CUTS = 4


def swap_pairs(count, step):
    return [(i, i ^ step) for i in range(count)]


def share_inner(value, count):
    return [value] + [lax.ppermute(value, "batch", swap_pairs(count, d)) for d in range(1, INNER)]


def block_of(array, index, size, axis=0):
    return lax.dynamic_slice_in_dim(array, index * size, size, axis)


def gather_rows(local, count, q, o):
    outer = count // INNER
    rows, width = local.shape[1:]
    plane = jnp.zeros((INNER, rows, width), local.dtype)
    for d in range(INNER):
        piece = lax.dynamic_index_in_dim(local, q ^ d, 0, keepdims=False)
        if d:
            piece = lax.ppermute(piece, "batch", swap_pairs(count, d))
        plane = lax.dynamic_update_index_in_dim(plane, piece, q ^ d, 0)
    plane = plane.reshape(INNER * rows, width)
    right, left = [plane], [plane]
    for s in range(1, outer):
        ahead = [
            (i * INNER + j, (i + 1) * INNER + j) for i in range(s - 1, outer - 1) for j in range(INNER)
        ]
        behind = [
            (i * INNER + j, (i - 1) * INNER + j) for i in range(1, outer - s + 1) for j in range(INNER)
        ]
        right.append(lax.ppermute(right[-1], "batch", ahead))
        left.append(lax.ppermute(left[-1], "batch", behind))
    whole = jnp.zeros((outer, INNER * rows, width), local.dtype)
    whole = lax.dynamic_update_index_in_dim(whole, plane, o, 0)
    for s in range(1, outer):
        piece = jnp.where(o >= s, right[s], left[outer - s])
        whole = lax.dynamic_update_index_in_dim(whole, piece, lax.rem(o - s + outer, outer), 0)
    return whole.reshape(count * rows, width)


def scatter_rows(partial, count, q, o):
    outer = count // INNER
    size = partial.shape[0] // outer
    from_left, from_right = None, None
    for t in range(1, outer):
        ahead = [(i * INNER + j, (i + 1) * INNER + j) for i in range(0, t) for j in range(INNER)]
        behind = [
            (i * INNER + j, (i - 1) * INNER + j) for i in range(outer - t, outer) for j in range(INNER)
        ]
        up = block_of(partial, jnp.minimum(o + outer - t, outer - 1), size)
        down = block_of(partial, jnp.maximum(o - outer + t, 0), size)
        if t > 1:
            up = up + from_left.astype(jnp.float32)
            down = down + from_right.astype(jnp.float32)
        from_left = lax.ppermute(up.astype(jnp.bfloat16), "batch", ahead)
        from_right = lax.ppermute(down.astype(jnp.bfloat16), "batch", behind)
    final = block_of(partial, o, size)
    final = final + from_left.astype(jnp.float32) + from_right.astype(jnp.float32)
    small = size // INNER
    blocks = [block_of(final, q, small)]
    for d in range(1, INNER):
        piece = block_of(final, q ^ d, small).astype(jnp.bfloat16)
        piece = lax.ppermute(piece, "batch", swap_pairs(count, d))
        blocks.append(piece.astype(jnp.float32))
    return blocks


def swap_core(value):
    return lax.ppermute(value, "branch", [(0, 1), (1, 0)])


def join_core(own, other, c, axis):
    return jnp.where(
        c == 0, jnp.concatenate([own, other], axis), jnp.concatenate([other, own], axis)
    )


def reduce_group(left, right_terms, count, c):
    half = right_terms[0].shape[0] // 2

    def product(part):
        return sum(
            lax.dot_general(
                one, block_of(two, part, half), (((1,), (1,)), ((), ())),
                preferred_element_type=jnp.float32,
            )
            for one, two in zip(left, right_terms)
        )

    theirs = swap_core(product(1 - c).astype(jnp.bfloat16))
    total = product(c) + theirs.astype(jnp.float32)
    slots = total.reshape(INNER, -1, half)
    result = slots[0]
    for d in range(1, INNER):
        piece = lax.ppermute(slots[d].astype(jnp.bfloat16), "batch", swap_pairs(count, d))
        result = result + piece.astype(jnp.float32)
    return result


def attend(projected, context_grad, allowed, cos_rows, sin_rows):
    def turn(tensor, direction):
        return rotate_slots(tensor, cos_rows, sin_rows, direction)

    queries = turn(projected[:, :, 0], 1.0).astype(jnp.bfloat16)
    keys_rot = turn(projected[:, :, 1], 1.0).astype(jnp.bfloat16)
    values_in = projected[:, :, 2].astype(jnp.bfloat16)
    score_scale = HD ** (-0.5)
    raw_scores = (
        jnp.einsum("gqd,gkd->gqk", queries, keys_rot, preferred_element_type=jnp.float32)
        * score_scale
    )
    scores = jnp.where(allowed, raw_scores, -1e30)
    largest = jnp.max(scores, axis=-1, keepdims=True)
    exponent = jnp.exp(scores - largest)
    probabilities = exponent / jnp.sum(exponent, axis=-1, keepdims=True)
    weights_soft = probabilities.astype(jnp.bfloat16)
    context = jnp.einsum(
        "gqk,gkd->gqd", weights_soft, values_in, preferred_element_type=jnp.float32
    ).astype(jnp.bfloat16)
    grad_values = jnp.einsum(
        "gqk,gqd->gkd", weights_soft, context_grad, preferred_element_type=jnp.float32
    )
    grad_probs = jnp.einsum(
        "gqd,gkd->gqk", context_grad, values_in, preferred_element_type=jnp.float32
    )
    inner_sum = jnp.sum(probabilities * grad_probs, axis=-1, keepdims=True)
    grad_scores = (probabilities * (grad_probs - inner_sum)).astype(jnp.bfloat16)
    grad_queries = (
        jnp.einsum("gqk,gkd->gqd", grad_scores, keys_rot, preferred_element_type=jnp.float32)
        * score_scale
    ).astype(jnp.bfloat16)
    grad_keys = (
        jnp.einsum("gqk,gqd->gkd", grad_scores, queries, preferred_element_type=jnp.float32)
        * score_scale
    ).astype(jnp.bfloat16)
    grad_projected = jnp.concatenate(
        [turn(grad_queries, -1.0), turn(grad_keys, -1.0), grad_values], axis=-1
    ).astype(jnp.bfloat16)
    return context, grad_projected


def rotate_slots(tensor, cos_rows, sin_rows, direction):
    halfway = ROT // 2
    first_part = tensor[..., :halfway]
    second_part = tensor[..., halfway:ROT]
    sin_part = sin_rows * direction
    return jnp.concatenate(
        [
            first_part * cos_rows - second_part * sin_part,
            second_part * cos_rows + first_part * sin_part,
            tensor[..., ROT:].astype(jnp.float32),
        ],
        axis=-1,
    )


def weight_grad(left, right):
    return lax.dot_general(
        left, right, (((0,), (0,)), ((), ())), preferred_element_type=jnp.float32
    )


def on_device(
    inputs,
    cotangent,
    segment_ids,
    w_qkv,
    w_out,
    w_fc1,
    w_fc2,
    norm_params,
    proj_bias,
    fc1_bias,
    qkv_rows,
    qkv_cols,
    out_rows,
    out_cols,
    fc1_rows,
    fc1_cols,
    fc2_rows,
    fc2_cols,
    norm_second,
    bias_second,
    fc1b_second,
):
    tokens = inputs.shape[0]
    local_width = inputs.shape[1]
    local_hidden = fc1_bias.shape[0]
    rows = w_qkv.shape[0]
    count = lax.axis_size("batch")
    c = lax.axis_index("branch")
    b = lax.axis_index("batch")
    q = lax.rem(b, INNER)
    o = b // INNER
    group = INNER * tokens
    width_q = local_width // INNER
    heads_q = width_q // HD
    hidden_q = local_hidden // INNER
    cut = hidden_q // FF_CUTS
    own_start = c * local_width
    hidden_start = c * local_hidden
    batch_first = (b == 0).astype(jnp.float32)
    branch_first = (c == 0).astype(jnp.float32)
    old_norms = lax.psum(
        (
            jnp.sum(w_qkv * w_qkv),
            jnp.sum(w_out * w_out),
            jnp.sum(w_fc1 * w_fc1),
            jnp.sum(w_fc2 * w_fc2),
            jnp.sum(proj_bias * proj_bias, axis=1) * batch_first,
            jnp.sum(fc1_bias * fc1_bias) * batch_first,
        ),
        ("batch", "branch"),
    )

    def slots_of(array):
        mine = jnp.stack(share_inner(array, count))
        return join_core(mine, swap_core(mine), c, 2).reshape(group, 2 * local_width)

    qkv_low = w_qkv.astype(jnp.bfloat16).reshape(rows, 3, INNER, heads_q, HD)
    out_low = w_out.astype(jnp.bfloat16).reshape(INNER, heads_q, HD, rows)
    fc1_low = w_fc1.astype(jnp.bfloat16).reshape(rows, INNER, FF_CUTS, cut)
    fc2_low = w_fc2.astype(jnp.bfloat16).reshape(INNER, FF_CUTS, cut, rows)

    full_in = slots_of(inputs)
    heads_whole = []
    for h in range(heads_q):
        one = qkv_low[:, :, :, h].transpose(2, 0, 1, 3).reshape(INNER, rows, 3 * HD)
        two = out_low[:, h].transpose(0, 2, 1)
        heads_whole.append(gather_rows(jnp.concatenate([one, two], axis=2), count, q, o))
    full_back = slots_of(cotangent)
    cuts_whole = []
    for k in range(FF_CUTS):
        one = fc1_low[:, :, k].transpose(1, 0, 2)
        two = fc2_low[:, k].transpose(0, 2, 1)
        cuts_whole.append(gather_rows(jnp.concatenate([one, two], axis=2), count, q, o))

    in_float = full_in.astype(jnp.float32)
    row_mean = jnp.mean(in_float, axis=-1, keepdims=True)
    centered = in_float - row_mean
    inverse = lax.rsqrt(jnp.mean(centered * centered, axis=-1, keepdims=True) + EPS_NORM)
    normed = centered * inverse
    hidden_one = (normed * norm_params[0] + norm_params[1]).astype(jnp.bfloat16)
    hidden_two = (normed * norm_params[2] + norm_params[3]).astype(jnp.bfloat16)

    segment = jnp.concatenate(share_inner(segment_ids, count), axis=0)
    positions_idx = jnp.arange(tokens)
    earlier = jnp.sum((segment[:, None, :] < segment[:, :, None]).astype(jnp.int32), axis=2)
    places = (positions_idx[None] - earlier).astype(jnp.float32)
    frequency = 10000.0 ** (-2.0 * jnp.arange(ROT // 2, dtype=jnp.float32) / ROT)
    angles = places[:, :, None] * frequency[None, None, :]
    cos_rows = jnp.cos(angles)
    sin_rows = jnp.sin(angles)
    allowed = (segment[:, None, :] == segment[:, :, None]) & (
        positions_idx[None, :] <= positions_idx[:, None]
    )

    contexts, grads_flat, grad_heads = [], [], []
    for h in range(heads_q):
        whole = heads_whole[h]
        bias = block_of(proj_bias[0:3], q * heads_q + h, HD, 1).reshape(3 * HD)
        projected = (
            jnp.dot(hidden_one, whole[:, : 3 * HD], preferred_element_type=jnp.float32) + bias
        ).reshape(INNER, tokens, 3, HD)
        grad_context = (
            jnp.dot(full_back, whole[:, 3 * HD :], preferred_element_type=jnp.float32)
            .astype(jnp.bfloat16)
            .reshape(INNER, tokens, HD)
        )
        context, grad_projected = attend(projected, grad_context, allowed, cos_rows, sin_rows)
        context = context.reshape(group, HD)
        grad_projected = grad_projected.reshape(group, 3 * HD)
        contexts.append(context)
        grads_flat.append(grad_projected)
        partial = jnp.concatenate(
            [weight_grad(hidden_one, grad_projected), weight_grad(full_back, context)], axis=1
        )
        grad_heads.append(scatter_rows(partial, count, q, o))
    context = jnp.concatenate(contexts, axis=1)
    grad_flat = jnp.concatenate(grads_flat, axis=1)
    own_one = reduce_group([grad_flat], [jnp.concatenate([w[:, : 3 * HD] for w in heads_whole], axis=1)], count, c)

    activations, grads_pre, grad_cuts = [], [], []
    for k in range(FF_CUTS):
        whole = cuts_whole[k]
        bias = block_of(fc1_bias, q * FF_CUTS + k, cut)
        pre_act = jnp.dot(hidden_two, whole[:, :cut], preferred_element_type=jnp.float32) + bias
        activated, gelu_pull = jax.vjp(
            lambda preact_in: jax.nn.gelu(preact_in, approximate=False), pre_act
        )
        activated = activated.astype(jnp.bfloat16)
        grad_act = jnp.dot(full_back, whole[:, cut:], preferred_element_type=jnp.float32)
        grad_pre = gelu_pull(grad_act)[0].astype(jnp.bfloat16)
        activations.append(activated)
        grads_pre.append(grad_pre)
        partial = jnp.concatenate(
            [weight_grad(hidden_two, grad_pre), weight_grad(full_back, activated)], axis=1
        )
        grad_cuts.append(scatter_rows(partial, count, q, o))
    grad_pre = jnp.concatenate(grads_pre, axis=1)
    own_two = reduce_group(
        [grad_pre], [jnp.concatenate([w[:, :cut] for w in cuts_whole], axis=1)], count, c
    )
    branch_sum = reduce_group(
        [context, jnp.concatenate(activations, axis=1)],
        [
            jnp.concatenate([w[:, 3 * HD :] for w in heads_whole], axis=1),
            jnp.concatenate([w[:, cut:] for w in cuts_whole], axis=1),
        ],
        count,
        c,
    )
    output = (inputs.astype(jnp.float32) + branch_sum + proj_bias[3] + proj_bias[4]).astype(
        jnp.bfloat16
    )

    back_float = cotangent.astype(jnp.float32)
    inverse_own = inverse[:tokens]
    normed_own = block_of(normed[:tokens], c, local_width, 1)
    gain_a = block_of(norm_params[0], c, local_width)
    gain_b = block_of(norm_params[2], c, local_width)
    scaled_a = own_one * gain_a
    scaled_b = own_two * gain_b
    row_terms = lax.psum(
        (
            jnp.sum(scaled_a + scaled_b, axis=-1),
            jnp.sum((scaled_a + scaled_b) * normed_own, axis=-1),
        ),
        "branch",
    )
    input_grad = (
        inverse_own
        * (
            scaled_a
            + scaled_b
            - row_terms[0][:, None] / D
            - normed_own * (row_terms[1][:, None] / D)
        )
        + back_float
    ).astype(jnp.bfloat16)
    norm_local = jnp.stack(
        [
            jnp.sum(own_one * normed_own, axis=0),
            jnp.sum(own_one, axis=0),
            jnp.sum(own_two * normed_own, axis=0),
            jnp.sum(own_two, axis=0),
        ]
    )
    norm_part = lax.dynamic_update_slice_in_dim(
        jnp.zeros((4, D), jnp.float32), norm_local, own_start, 1
    )
    back_sum = jnp.sum(back_float, axis=0)
    qkv_bias = jnp.sum(
        grad_flat.astype(jnp.float32).reshape(group, heads_q, 3, HD), axis=0
    ).transpose(1, 0, 2).reshape(3, width_q)
    bias_part = lax.dynamic_update_slice(
        jnp.zeros((5, local_width), jnp.float32),
        jnp.stack([back_sum, back_sum]),
        (3, 0),
    )
    bias_part = lax.dynamic_update_slice(bias_part, qkv_bias, (0, q * width_q))
    fc1b_part = lax.dynamic_update_slice_in_dim(
        jnp.zeros((local_hidden,), jnp.float32),
        jnp.sum(grad_pre.astype(jnp.float32), axis=0),
        q * hidden_q,
        0,
    )
    norm_grad = lax.psum(norm_part, ("batch", "branch"))
    bias_grad, fc1b_grad = lax.psum((bias_part, fc1b_part), "batch")

    def place(blocks, axis):
        whole = jnp.stack(blocks, axis)
        out = jnp.zeros_like(whole)
        for d in range(INNER):
            out = lax.dynamic_update_index_in_dim(out, blocks[d], q ^ d, axis)
        return out

    qkv_grad = jnp.stack(
        [
            place([grad_heads[h][d][:, : 3 * HD].reshape(rows, 3, HD) for d in range(INNER)], 2)
            for h in range(heads_q)
        ],
        3,
    ).reshape(rows, 3 * local_width)
    out_grad = jnp.stack(
        [
            place([grad_heads[h][d][:, 3 * HD :].T for d in range(INNER)], 0)
            for h in range(heads_q)
        ],
        1,
    ).reshape(local_width, rows)
    fc1_grad = jnp.stack(
        [place([grad_cuts[k][d][:, :cut] for d in range(INNER)], 1) for k in range(FF_CUTS)], 2
    ).reshape(rows, local_hidden)
    fc2_grad = jnp.stack(
        [place([grad_cuts[k][d][:, cut:].T for d in range(INNER)], 0) for k in range(FF_CUTS)], 1
    ).reshape(local_hidden, rows)
    qkv_flat = w_qkv.reshape(qkv_grad.shape)
    qkv_cols_flat = qkv_cols.reshape(-1)
    qkv_square = squares(qkv_grad)
    fc1_square = squares(fc1_grad)
    out_square = squares(out_grad)
    fc2_square = squares(fc2_grad)
    pair_sums = lax.psum(
        (
            jnp.sum(qkv_square, axis=1),
            jnp.sum(fc1_square, axis=1),
            jnp.sum(out_square, axis=0),
            jnp.sum(fc2_square, axis=0),
        ),
        "branch",
    )
    qkv_rows_new = renew_stat(qkv_rows, pair_sums[0])
    fc1_rows_new = renew_stat(fc1_rows, pair_sums[1])
    out_cols_new = renew_stat(out_cols, pair_sums[2])
    fc2_cols_new = renew_stat(fc2_cols, pair_sums[3])
    bias_moment, bias_update = second_step(bias_grad, bias_second)
    fc1b_moment, fc1b_update = second_step(fc1b_grad, fc1b_second)
    cross_sums = lax.psum(
        (
            jnp.sum(qkv_square, axis=0),
            jnp.sum(fc1_square, axis=0),
            jnp.sum(out_square, axis=1),
            jnp.sum(fc2_square, axis=1),
        ),
        "batch",
    )
    qkv_cols_new = renew_stat(qkv_cols_flat, cross_sums[0])
    fc1_cols_new = renew_stat(fc1_cols, cross_sums[1])
    out_rows_new = renew_stat(out_rows, cross_sums[2])
    fc2_rows_new = renew_stat(fc2_rows, cross_sums[3])
    overall = lax.psum(
        (
            jnp.sum(qkv_rows_new) * branch_first,
            ratio_sum(qkv_grad, qkv_rows_new, qkv_cols_new),
            jnp.sum(fc1_rows_new) * branch_first,
            ratio_sum(fc1_grad, fc1_rows_new, fc1_cols_new),
            jnp.sum(out_rows_new) * batch_first,
            ratio_sum(out_grad, out_rows_new, out_cols_new),
            jnp.sum(fc2_rows_new) * batch_first,
            ratio_sum(fc2_grad, fc2_rows_new, fc2_cols_new),
            jnp.sum(bias_update * bias_update, axis=1) * batch_first,
            jnp.sum(fc1b_update * fc1b_update) * batch_first,
        ),
        ("batch", "branch"),
    )
    (
        qkv_total,
        qkv_inverse,
        fc1_total,
        fc1_inverse,
        out_total,
        out_inverse,
        fc2_total,
        fc2_inverse,
        bias_usq,
        fc1b_usq,
    ) = overall
    qkv_next = finish(
        qkv_flat,
        qkv_grad,
        qkv_rows_new,
        qkv_cols_new,
        qkv_total,
        qkv_inverse,
        old_norms[0],
        3 * D * D,
    )
    out_next = finish(
        w_out, out_grad, out_rows_new, out_cols_new, out_total, out_inverse, old_norms[1], D * D
    )
    fc1_next = finish(
        w_fc1, fc1_grad, fc1_rows_new, fc1_cols_new, fc1_total, fc1_inverse, old_norms[2], D * FF
    )
    fc2_next = finish(
        w_fc2, fc2_grad, fc2_rows_new, fc2_cols_new, fc2_total, fc2_inverse, old_norms[3], FF * D
    )
    bias_new = vector_finish(proj_bias, bias_update, bias_usq, old_norms[4], D)
    fc1b_new = vector_finish(fc1_bias, fc1b_update, fc1b_usq, old_norms[5], FF)
    norm_moment, norm_update = second_step(norm_grad, norm_second)
    norm_new = vector_finish(
        norm_params,
        norm_update,
        jnp.sum(norm_update * norm_update, axis=1),
        jnp.sum(norm_params * norm_params, axis=1),
        D,
    )
    qkv_shape = w_qkv.shape
    qkv_next = qkv_next.reshape(qkv_shape)
    return (
        output,
        input_grad,
        qkv_grad.reshape(qkv_shape),
        qkv_next,
        qkv_rows_new,
        qkv_cols_new.reshape(qkv_cols.shape),
        qkv_next.astype(jnp.bfloat16),
        out_grad,
        out_next,
        out_rows_new,
        out_cols_new,
        out_next.astype(jnp.bfloat16),
        fc1_grad,
        fc1_next,
        fc1_rows_new,
        fc1_cols_new,
        fc1_next.astype(jnp.bfloat16),
        fc2_grad,
        fc2_next,
        fc2_rows_new,
        fc2_cols_new,
        fc2_next.astype(jnp.bfloat16),
        norm_grad,
        norm_moment,
        norm_new,
        bias_grad,
        bias_moment,
        bias_new,
        fc1b_grad,
        fc1b_moment,
        fc1b_new,
    )


def solution(mesh):
    in_specs = (
        P("batch", "branch"),
        P("batch", "branch"),
        P("batch", None),
        P("batch", None, "branch"),
        P("branch", "batch"),
        P("batch", "branch"),
        P("branch", "batch"),
        P(),
        P(None, "branch"),
        P("branch"),
        P("batch"),
        P(None, "branch"),
        P("branch"),
        P("batch"),
        P("batch"),
        P("branch"),
        P("branch"),
        P("batch"),
        P(),
        P(None, "branch"),
        P("branch"),
    )
    out_specs = (
        P("batch", "branch"),
        P("batch", "branch"),
        P("batch", None, "branch"),
        P("batch", None, "branch"),
        P("batch"),
        P(None, "branch"),
        P("batch", None, "branch"),
        P("branch", "batch"),
        P("branch", "batch"),
        P("branch"),
        P("batch"),
        P("branch", "batch"),
        P("batch", "branch"),
        P("batch", "branch"),
        P("batch"),
        P("branch"),
        P("batch", "branch"),
        P("branch", "batch"),
        P("branch", "batch"),
        P("branch"),
        P("batch"),
        P("branch", "batch"),
        P(),
        P(),
        P(),
        P(None, "branch"),
        P(None, "branch"),
        P(None, "branch"),
        P("branch"),
        P("branch"),
        P("branch"),
    )
    return jax.shard_map(
        on_device, mesh=mesh, in_specs=in_specs, out_specs=out_specs, check_vma=False
    )
```

```python
import functools

import jax
import jax.numpy as jnp
from jax import lax
from jax.experimental import pallas as pl
from jax.experimental.pallas import tpu as pltpu
from jax.sharding import PartitionSpec as P

D = 2048
HD = 128
ROT = 32
FF = 8192
STEP = 10


EPS_NORM = 1e-05
EPS_SQUARE = 1e-30
RATE = 0.3
FLOOR_RATE = 0.001


def decay_rate():
    return 1.0 - STEP ** (-0.8)


def squares(gradient):
    return gradient * gradient + EPS_SQUARE


def renew_stat(old_stat, new_sum):
    decay = decay_rate()
    return decay * old_stat + (1.0 - decay) * new_sum


def ratio_sum(gradient, rows_new, cols_new):
    return jnp.sum(gradient * gradient * (1.0 / rows_new)[:, None] * (1.0 / cols_new)[None, :])


def finish(weight, gradient, rows_new, cols_new, row_total, inverse_sum, old_square, entries):
    update = (
        gradient * jnp.sqrt(row_total) * lax.rsqrt(rows_new)[:, None] * lax.rsqrt(cols_new)[None, :]
    )
    clip_factor = jnp.maximum(1.0, jnp.sqrt(row_total * inverse_sum / entries))
    step_rate = RATE * jnp.maximum(FLOOR_RATE, jnp.sqrt(old_square / entries))
    return weight - step_rate * update / clip_factor


def second_step(gradient, second):
    second_new = renew_stat(second, squares(gradient))
    return (second_new, gradient * lax.rsqrt(second_new))


def vector_finish(vector, update, update_square, old_square, entries):
    clip_factor = jnp.maximum(1.0, jnp.sqrt(update_square / entries))[..., None]
    step_rate = RATE * jnp.maximum(FLOOR_RATE, jnp.sqrt(old_square / entries))[..., None]
    return vector - step_rate * update / clip_factor


INNER = 4
HEADS_DEV = 2
CUTS = 4
CHUNKS = HEADS_DEV + CUTS
CUT = 256
WIDE = 512
MESH = pl.DeviceIdType.MESH


def flip(index, step):
    return index + step * (1 - 2 * lax.rem(index // step, 2))


def nn(left, right):
    return jnp.dot(left, right, preferred_element_type=jnp.float32)


def nt(left, right):
    return lax.dot_general(
        left, right, (((1,), (1,)), ((), ())), preferred_element_type=jnp.float32
    )


def tn(left, right):
    return lax.dot_general(
        left, right, (((0,), (0,)), ((), ())), preferred_element_type=jnp.float32
    )


def block_kernel(
    count,
    wst,
    xin,
    yin,
    cos_ref,
    sin_ref,
    norm_ref,
    bias_h,
    bias_f,
    gr,
    rsb,
    sibb,
    xr,
    xo,
    qb,
    fb,
    H1,
    H2,
    DY,
    W,
    OC,
    DQ,
    TT,
    G,
    sbuf,
    fbuf,
    land,
    sib_send,
    sib_land,
    psend,
    own,
    a2a_s,
    a2a_r,
    loc_s,
    ag_s,
    ag_r,
    x_s,
    x_r,
    sx_s,
    sx_r,
    rs_s,
    rs_r,
    gr_s,
    gr_r,
    sib_s,
    sib_r,
    p_s,
    p_r,
    tmp_s,
):
    outer = count // INNER
    S = outer - 1
    T, half = xin.shape
    R = wst.shape[2]
    block = INNER * R
    QT = T // 2
    b = lax.axis_index("batch")
    c = lax.axis_index("branch")
    q = lax.rem(b, INNER)
    o = b // INNER
    bx, by = flip(b, 1), flip(b, 2)
    bxy = flip(bx, 2)
    near = (bx, by, bxy)
    da = 1 + c
    db = 2 - c
    b_first = bx * (1 - c) + by * c
    b_second = by * (1 - c) + bx * c

    def remote(src, dst, ssem, rsem, to_b, to_c):
        return pltpu.make_async_remote_copy(
            src_ref=src,
            dst_ref=dst,
            send_sem=ssem,
            recv_sem=rsem,
            device_id=(to_b, to_c),
            device_id_type=MESH,
        )

    barrier = pltpu.get_barrier_semaphore()
    for who in near:
        pl.semaphore_signal(barrier, inc=1, device_id=(who, c), device_id_type=MESH)
    pl.semaphore_signal(barrier, inc=1, device_id=(b, 1 - c), device_id_type=MESH)

    @pl.when(o > 0)
    def _():
        pl.semaphore_signal(barrier, inc=1, device_id=(b - INNER, c), device_id_type=MESH)

    @pl.when(o < outer - 1)
    def _():
        pl.semaphore_signal(barrier, inc=1, device_id=(b + INNER, c), device_id_type=MESH)

    pl.semaphore_wait(barrier, 4 + jnp.minimum(o, 1) + jnp.minimum(outer - 1 - o, 1))

    def a2a_copy(k, d, received=False):
        to = near[d - 1]
        row = (to if received else b) * R
        return remote(
            wst.at[k, lax.rem(to, INNER)],
            W.at[k, pl.ds(pl.multiple_of(row, 16), R)],
            a2a_s.at[k, d - 1],
            a2a_r.at[k, d - 1],
            to,
            c,
        )

    def a2a_local(k):
        return pltpu.make_async_copy(
            wst.at[k, q], W.at[k, pl.ds(pl.multiple_of(b * R, 16), R)], loc_s.at[k]
        )

    def a2a_start(k):
        for d in range(1, INNER):
            a2a_copy(k, d).start()
        a2a_local(k).start()

    def a2a_wait(k):
        for d in range(1, INNER):
            a2a_copy(k, d, True).wait_recv()
        a2a_local(k).wait()

    def ag_copy(k, way, s, part):
        rows = pl.ds(pl.multiple_of(part * block, 16), block)
        to = b + INNER if way == 0 else b - INNER
        return remote(
            W.at[k, rows], W.at[k, rows], ag_s.at[k, way, s - 1], ag_r.at[k, way, s - 1], to, c
        )

    def ag_sends(k, s, what):
        @pl.when((o >= s - 1) & (o <= outer - 2))
        def _():
            what(ag_copy(k, 0, s, o - s + 1))

        @pl.when((o >= 1) & (o <= outer - s))
        def _():
            what(ag_copy(k, 1, s, o + s - 1))

    def ag_wait(k, s):
        @pl.when(o >= s)
        def _():
            ag_copy(k, 0, s, o - s).wait_recv()

        @pl.when(o <= outer - 1 - s)
        def _():
            ag_copy(k, 1, s, o + s).wait_recv()

    def ag_range(low, high):
        def step(n, carry):
            k = n // S
            s = lax.rem(n, S) + 1

            @pl.when(s == 1)
            def _():
                a2a_wait(k)

            @pl.when(s > 1)
            def _():
                ag_wait(k, s - 1)

            ag_sends(k, s, lambda copy: copy.start())
            return carry

        lax.fori_loop(low, high, step, 0)

    def ag(low, high):
        ag_range(low * S // 3, high * S // 3)

    def spot(buf, slot):
        return buf.at[
            pl.ds(pl.multiple_of(slot * T, 16), T), pl.ds(pl.multiple_of(c * half, 128), half)
        ]

    def other_spot(buf, slot):
        return buf.at[
            pl.ds(pl.multiple_of(slot * T, 16), T), pl.ds(pl.multiple_of((1 - c) * half, 128), half)
        ]

    def sx_copy(i, buf, slot, src=None):
        place = spot(buf, slot)
        return remote(place if src is None else src, place, sx_s.at[i, slot], sx_r.at[i, slot], b, 1 - c)

    def sx_wait(i, buf, slot):
        remote(
            other_spot(buf, slot), other_spot(buf, slot), sx_s.at[i, slot], sx_r.at[i, slot], b, 1 - c
        ).wait_recv()

    def x_first(i, src, buf):
        return remote(src, spot(buf, da), x_s.at[i, da - 1], x_r.at[i, da - 1], b_first, c)

    def x_second(i, src, buf):
        return remote(src, spot(buf, db), x_s.at[i, db - 1], x_r.at[i, db - 1], b_second, c)

    def x_forward(i, buf):
        return remote(spot(buf, da), spot(buf, 3), x_s.at[i, 2], x_r.at[i, 2], b_second, c)

    def x_diag(i, buf):
        return remote(spot(buf, 3), spot(buf, 3), x_s.at[i, 2], x_r.at[i, 2], b_second, c)

    def x_local(i, src, buf):
        return pltpu.make_async_copy(src, spot(buf, 0), tmp_s.at[i])

    def gather_one(i, src, buf):
        x_first(i, src, buf).start()
        x_local(i, src, buf).start()
        sx_copy(i, buf, 0, src).start()

    def gather_two(i, src, buf):
        x_first(i, src, buf).wait_recv()
        x_second(i, src, buf).start()
        x_forward(i, buf).start()
        sx_copy(i, buf, da).start()

    def gather_three(i, src, buf):
        x_second(i, src, buf).wait_recv()
        sx_copy(i, buf, db).start()
        x_diag(i, buf).wait_recv()
        sx_copy(i, buf, 3).start()

    def gather_sent(i, src, buf):
        x_first(i, src, buf).wait_send()
        x_second(i, src, buf).wait_send()
        x_forward(i, buf).wait_send()
        sx_copy(i, buf, 0, src).wait_send()
        for slot in range(1, INNER):
            sx_copy(i, buf, slot).wait_send()

    def norm_rows(slot):
        def step(i, carry):
            rows = pl.ds(pl.multiple_of(slot * T + i * 128, 128), 128)
            values = H1[rows, :].astype(jnp.float32)
            mean = jnp.mean(values, axis=-1, keepdims=True)
            centered = values - mean
            inverse = lax.rsqrt(jnp.mean(centered * centered, axis=-1, keepdims=True) + EPS_NORM)
            normed = centered * inverse
            H1[rows, :] = (normed * norm_ref[0:1, :] + norm_ref[1:2, :]).astype(jnp.bfloat16)
            H2[rows, :] = (normed * norm_ref[2:3, :] + norm_ref[3:4, :]).astype(jnp.bfloat16)
            return carry

        lax.fori_loop(0, T // 128, step, 0)

    lane = lax.broadcasted_iota(jnp.int32, (T, HD), 1)
    scale = HD ** (-0.5)

    def partner(tensor):
        return jnp.where(
            lane < ROT // 2,
            pltpu.roll(tensor, HD - ROT // 2, 1),
            jnp.where(lane < ROT, pltpu.roll(tensor, ROT // 2, 1), 0.0),
        )

    def head_piece(h, slot):
        rows = pl.ds(pl.multiple_of(slot * T, 128), T)
        cos_rows, sin_rows = cos_ref[rows, :], sin_ref[rows, :]
        projected = nn(H1[rows, :], W[h, :, : 3 * HD]) + bias_h[h]
        first = projected[:, :HD]
        queries = (first * cos_rows + partner(first) * sin_rows).astype(jnp.bfloat16)
        second = projected[:, HD : 2 * HD]
        keys = (second * cos_rows + partner(second) * sin_rows).astype(jnp.bfloat16)
        values = projected[:, 2 * HD :].astype(jnp.bfloat16)
        back = nn(DY[rows, :], W[h, :, 3 * HD :]).astype(jnp.bfloat16)
        starts = sin_rows[:, ROT : ROT + 1]
        contexts, grad_q = [], []
        grad_k, grad_v = [None, None], [None, None]
        for i in range(2):
            seen = QT * (i + 1)
            part = slice(QT * i, QT * (i + 1))
            raw = nt(queries[part], keys[:seen]) * scale
            query_at = lax.broadcasted_iota(jnp.int32, (QT, seen), 0) + QT * i
            key_at = lax.broadcasted_iota(jnp.int32, (QT, seen), 1)
            allowed = (key_at <= query_at) & (key_at.astype(jnp.float32) >= starts[part])
            scores = jnp.where(allowed, raw, -1e30)
            exponent = jnp.exp(scores - jnp.max(scores, axis=-1, keepdims=True))
            probs = exponent / jnp.sum(exponent, axis=-1, keepdims=True)
            soft = probs.astype(jnp.bfloat16)
            contexts.append(nn(soft, values[:seen]).astype(jnp.bfloat16))
            grad_probs = nt(back[part], values[:seen])
            inner = jnp.sum(probs * grad_probs, axis=-1, keepdims=True)
            grad_scores = (probs * (grad_probs - inner)).astype(jnp.bfloat16)
            grad_q.append((nn(grad_scores, keys[:seen]) * scale).astype(jnp.bfloat16))
            for j in range(i + 1):
                cut = slice(QT * j, QT * (j + 1))
                term_v = tn(soft[:, cut], back[part])
                term_k = tn(grad_scores[:, cut], queries[part])
                grad_v[j] = term_v if grad_v[j] is None else grad_v[j] + term_v
                grad_k[j] = term_k if grad_k[j] is None else grad_k[j] + term_k
        context = jnp.concatenate(contexts, axis=0)
        dq = jnp.concatenate(grad_q, axis=0).astype(jnp.float32)
        dk = (jnp.concatenate(grad_k, axis=0) * scale).astype(jnp.bfloat16).astype(jnp.float32)
        dv = jnp.concatenate(grad_v, axis=0)
        turned = jnp.concatenate(
            [
                dq * cos_rows - partner(dq) * sin_rows,
                dk * cos_rows - partner(dk) * sin_rows,
                dv,
            ],
            axis=1,
        ).astype(jnp.bfloat16)
        OC[h, rows, :] = context
        DQ[h, rows, :] = turned
        TT[: 3 * HD, rows] = turned.T
        TT[3 * HD :, rows] = context.T
        total = jnp.sum(turned.astype(jnp.float32), axis=0, keepdims=True)
        qb[h] = jnp.where(slot == 0, total, qb[h] + total)

    def cut_piece(f, slot):
        def step(i, total):
            rows = pl.ds(pl.multiple_of(slot * T + i * QT, 128), QT)
            k = HEADS_DEV + f
            pre = nn(H2[rows, :], W[k, :, :CUT]) + bias_f[f]
            grad = nn(DY[rows, :], W[k, :, CUT:])
            normal = 0.5 * (1.0 + lax.erf(pre * (0.5**0.5)))
            slope = normal + pre * (jnp.exp(-0.5 * pre * pre) * (0.5 * 0.7978845608028654))
            active = (pre * normal).astype(jnp.bfloat16)
            pulled = (grad * slope).astype(jnp.bfloat16)
            H1[rows, pl.ds(pl.multiple_of(f * CUT, CUT), CUT)] = active
            H1[rows, pl.ds(pl.multiple_of(CUTS * CUT + f * CUT, CUT), CUT)] = pulled
            TT[:CUT, rows] = pulled.T
            TT[CUT:, rows] = active.T
            return total + jnp.sum(pulled.astype(jnp.float32), axis=0, keepdims=True)

        total = lax.fori_loop(0, 2, step, jnp.zeros((1, CUT), jnp.float32))
        fb[f] = jnp.where(slot == 0, total, fb[f] + total)

    def grads(k, left, edge):
        def step(j, carry):
            cols = pl.ds(pl.multiple_of(j * block, 128), block)
            G[lax.rem(k, 2), j, :edge, :] = nn(TT[:edge, :], left[:, cols])
            G[lax.rem(k, 2), j, edge:, :] = nn(TT[edge:, :], DY[:, cols])
            return carry

        lax.fori_loop(0, outer, step, 0)

    def rs_copy(k, way, t):
        n = k * S + t - 1
        to = b + INNER if way == 0 else b - INNER
        return remote(
            sbuf.at[way, lax.rem(n, 2)],
            rsb.at[k, way, t - 1],
            rs_s.at[k, way, t - 1],
            rs_r.at[k, way, t - 1],
            to,
            c,
        )

    def rs_sends(way, t):
        if way == 0:
            return (o <= t - 1) & (o <= outer - 2)
        return (o >= outer - t) & (o >= 1)

    def rs_receives(way, t):
        if way == 0:
            return (o >= 1) & (o <= t)
        return (o <= outer - 2) & (o >= outer - 1 - t)

    def rs_fetch(k, way, t):
        rs_copy(k, way, t).wait_recv()
        load = pltpu.make_async_copy(rsb.at[k, way, t - 1], land.at[way], tmp_s.at[2 + way])
        load.start()
        load.wait()

    def rs_range(low, high):
        def step(n, carry):
            k = n // S
            t = lax.rem(n, S) + 1
            for way in range(2):
                owner = o + outer - t if way == 0 else o - outer + t

                before = jnp.maximum(n - 2, 0)
                k_before = before // S
                t_before = lax.rem(before, S) + 1

                @pl.when((n >= 2) & rs_sends(way, t_before))
                def _():
                    rs_copy(k_before, way, t_before).wait_send()

                @pl.when(rs_sends(way, t))
                def _():
                    @pl.when(rs_receives(way, t - 1) & (t > 1))
                    def _():
                        rs_fetch(k, way, t - 1)
                        sbuf[way, lax.rem(n, 2)] = (
                            G[lax.rem(k, 2), owner] + land[way].astype(jnp.float32)
                        ).astype(jnp.bfloat16)

                    @pl.when(jnp.logical_not(rs_receives(way, t - 1) & (t > 1)))
                    def _():
                        sbuf[way, lax.rem(n, 2)] = G[lax.rem(k, 2), owner].astype(jnp.bfloat16)

                    rs_copy(k, way, t).start()

            return carry

        lax.fori_loop(low, high, step, 0)

    def rs(low, high):
        rs_range(low * S // 3, high * S // 3)

    def gr_copy(k, d, received=False):
        to = near[d - 1]
        slot = lax.rem(to, INNER)
        return remote(
            fbuf.at[lax.rem(k, 2), pl.ds(pl.multiple_of(slot * R, 16), R)],
            gr.at[k, slot if received else q],
            gr_s.at[k, d - 1],
            gr_r.at[k, d - 1],
            to,
            c,
        )

    def gr_local(k):
        return pltpu.make_async_copy(
            fbuf.at[lax.rem(k, 2), pl.ds(pl.multiple_of(q * R, 16), R)],
            gr.at[k, q],
            gr_s.at[k, 3],
        )

    def gr_sent(k):
        for d in range(1, INNER):
            gr_copy(k, d).wait_send()
        gr_local(k).wait()

    def rs_final(k):
        for way in range(2):

            @pl.when(rs_receives(way, S))
            def _():
                rs_fetch(k, way, S)
                G[lax.rem(k, 2), o] = G[lax.rem(k, 2), o] + land[way].astype(jnp.float32)

        @pl.when(k >= 2)
        def _():
            gr_sent(k - 2)

        fbuf[lax.rem(k, 2)] = G[lax.rem(k, 2), o].T.astype(jnp.bfloat16)
        for d in range(1, INNER):
            gr_copy(k, d).start()
        gr_local(k).start()

    TILE = T // 2
    TILES = 2 * INNER

    def tile_slot(i):
        return INNER - 1 - i // 2

    def product(which, i, side):
        row = pl.multiple_of(tile_slot(i) * T + lax.rem(i, 2) * TILE, 128)
        rows = pl.ds(row, TILE)
        features = pl.ds(pl.multiple_of(side * half, 128), half)
        terms = []
        if which == 0:
            for h in range(HEADS_DEV):
                terms.append(nt(DQ[h, rows, :], W[h, features, : 3 * HD]))
        elif which == 1:
            for f in range(CUTS):
                low = (CUTS + f) * CUT
                terms.append(nt(H1[rows, low : low + CUT], W[HEADS_DEV + f, features, :CUT]))
        else:
            for h in range(HEADS_DEV):
                terms.append(nt(OC[h, rows, :], W[h, features, 3 * HD :]))
            for f in range(CUTS):
                low = f * CUT
                terms.append(nt(H1[rows, low : low + CUT], W[HEADS_DEV + f, features, CUT:]))
        return functools.reduce(lambda one, two: one + two, terms)

    def sib_copy(which, i):
        return remote(
            sib_send.at[lax.rem(i, 2)],
            sibb.at[which, i],
            sib_s.at[which, i],
            sib_r.at[which, i],
            b,
            1 - c,
        )

    def plane_copy(which, i):
        slot = tile_slot(i)
        low, high = lax.rem(slot, 2), slot // 2
        to = b + low * (1 - 2 * lax.rem(b, 2)) + high * 2 * (1 - 2 * lax.rem(b // 2, 2))
        return remote(
            psend.at[lax.rem(i, 2)],
            xr.at[which, slot - 1, pl.ds(pl.multiple_of(lax.rem(i, 2) * TILE, 16), TILE)],
            p_s.at[which, i],
            p_r.at[which, i],
            to,
            c,
        )

    def tile_a(which, i):
        @pl.when(i >= 2)
        def _():
            sib_copy(which, i - 2).wait_send()

        sib_send[lax.rem(i, 2)] = product(which, i, 1 - c).astype(jnp.bfloat16)
        sib_copy(which, i).start()

    def tile_b(which, i):
        own[...] = product(which, i, c)
        sib_copy(which, i).wait_recv()
        load = pltpu.make_async_copy(sibb.at[which, i], sib_land, tmp_s.at[4])
        load.start()
        load.wait()
        own[...] = own[...] + sib_land[...].astype(jnp.float32)

        @pl.when(i < TILES - 2)
        def _():
            @pl.when(i >= 2)
            def _():
                plane_copy(which, i - 2).wait_send()

            psend[lax.rem(i, 2)] = own[...].astype(jnp.bfloat16)
            plane_copy(which, i).start()

        @pl.when(i >= TILES - 2)
        def _():
            keep = pltpu.make_async_copy(
                own,
                xo.at[which, pl.ds(pl.multiple_of(lax.rem(i, 2) * TILE, 8), TILE)],
                tmp_s.at[5],
            )
            keep.start()
            keep.wait()

    def sum_tiles(which, beside):
        tile_a(which, 0)

        def step(i, carry):
            @pl.when(i < TILES - 1)
            def _():
                tile_a(which, i + 1)

            tile_b(which, i)
            beside(i)
            return carry

        lax.fori_loop(0, TILES, step, 0)

    def sum_sent(which):
        for i in range(TILES - 2, TILES):
            sib_copy(which, i).wait_send()
        for i in range(TILES - 4, TILES - 2):
            plane_copy(which, i).wait_send()

    def share(low, high, i, pieces, run):
        first, last = low * S // 3, high * S // 3
        run(first + (last - first) * i // pieces, first + (last - first) * (i + 1) // pieces)

    a2a_start(0)
    a2a_start(1)
    gather_one(0, xin, H1)
    ag(0, 1)
    gather_two(0, xin, H1)
    a2a_start(2)
    gather_one(1, yin, DY)
    ag(1, 2)
    x_local(0, xin, H1).wait()
    sx_wait(0, H1, 0)
    norm_rows(0)
    ag(2, 3)
    gather_three(0, xin, H1)
    gather_two(1, yin, DY)
    for k in range(3, CHUNKS):
        a2a_start(k)
    gather_sent(0, xin, H1)
    for slot in range(1, INNER):
        sx_wait(0, H1, slot)
        norm_rows(slot)
        ag(2 + slot, 3 + slot)
    ag(6, 7)
    gather_three(1, yin, DY)
    x_local(1, yin, DY).wait()
    for slot in range(INNER):
        sx_wait(1, DY, slot)
    gather_sent(1, yin, DY)

    def head_step(h, carry):
        ag_wait(h, S)

        def slot_step(slot, inner_carry):
            head_piece(h, slot)
            share(7 + 2 * h, 9 + 2 * h, slot, INNER, ag_range)
            share(0, 3 * h, slot, INNER, rs_range)
            return inner_carry

        lax.fori_loop(0, INNER, slot_step, 0)

        @pl.when(h == 1)
        def _():
            rs_final(0)

        grads(h, H1, 3 * HD)
        return carry

    lax.fori_loop(0, HEADS_DEV, head_step, 0)

    def beside_one(i):
        share(11, 12, i, TILES, ag_range)
        share(3, 6, i, TILES, rs_range)

    sum_tiles(0, beside_one)
    rs_final(1)

    def cut_step(f, carry):
        ag_wait(HEADS_DEV + f, S)

        def slot_step(slot, inner_carry):
            cut_piece(f, slot)
            share(12 + 2 * f, jnp.minimum(14 + 2 * f, 18), slot, INNER, ag_range)
            share(jnp.maximum(6, 3 + 3 * f), 6 + 3 * f, slot, INNER, rs_range)
            return inner_carry

        lax.fori_loop(0, INNER, slot_step, 0)

        @pl.when(f >= 1)
        def _():
            rs_final(1 + f)

        grads(HEADS_DEV + f, H2, CUT)
        return carry

    lax.fori_loop(0, CUTS, cut_step, 0)
    sum_sent(0)
    sum_tiles(1, lambda i: share(15, 17, i, TILES, rs_range))
    sum_sent(1)
    sum_tiles(2, lambda i: share(17, 18, i, TILES, rs_range))
    sum_sent(2)
    rs_final(CHUNKS - 1)

    gr_sent(CHUNKS - 2)
    gr_sent(CHUNKS - 1)

    def drain_chunk(k, carry):
        for d in range(1, INNER):
            a2a_copy(k, d).wait_send()
            gr_copy(k, d, True).wait_recv()

        def drain_step(s, inner_carry):
            ag_sends(k, s, lambda copy: copy.wait_send())
            return inner_carry

        lax.fori_loop(1, S + 1, drain_step, 0)
        return carry

    lax.fori_loop(0, CHUNKS, drain_chunk, 0)
    for n in range(CHUNKS * S - 2, CHUNKS * S):
        for way in range(2):

            @pl.when(rs_sends(way, n % S + 1))
            def _():
                rs_copy(n // S, way, n % S + 1).wait_send()

    for which in range(3):

        def drain_tile(i, carry):
            plane_copy(which, i).wait_recv()
            return carry

        lax.fori_loop(0, TILES - 2, drain_tile, 0)


def block_call(count, wst, xin, yin, cos_rows, sin_rows, norm_params, bias_h, bias_f):
    outer = count // INNER
    S = outer - 1
    tokens, half = xin.shape
    group = INNER * tokens
    rows = wst.shape[2]
    tile = tokens // 2
    low, high = jnp.bfloat16, jnp.float32
    any_spec = pl.BlockSpec(memory_space=pl.ANY)
    vmem_spec = pl.BlockSpec(memory_space=pltpu.VMEM)
    dma = pltpu.SemaphoreType.DMA
    return pl.pallas_call(
        functools.partial(block_kernel, count),
        out_shape=[
            jax.ShapeDtypeStruct((CHUNKS, INNER, rows, WIDE), low),
            jax.ShapeDtypeStruct((CHUNKS, 2, S, WIDE, INNER * rows), low),
            jax.ShapeDtypeStruct((3, 2 * INNER, tile, half), low),
            jax.ShapeDtypeStruct((3, INNER - 1, tokens, half), low),
            jax.ShapeDtypeStruct((3, tokens, half), high),
            jax.ShapeDtypeStruct((HEADS_DEV, 1, 3 * HD), high),
            jax.ShapeDtypeStruct((CUTS, 1, CUT), high),
        ],
        in_specs=[any_spec] * 3 + [vmem_spec] * 5,
        out_specs=[any_spec] * 5 + [vmem_spec] * 2,
        scratch_shapes=[
            pltpu.VMEM((group, D), low),
            pltpu.VMEM((group, D), low),
            pltpu.VMEM((group, D), low),
            pltpu.VMEM((CHUNKS, D, WIDE), low),
            pltpu.VMEM((HEADS_DEV, group, HD), low),
            pltpu.VMEM((HEADS_DEV, group, 3 * HD), low),
            pltpu.VMEM((WIDE, group), low),
            pltpu.VMEM((2, outer, WIDE, INNER * rows), high),
            pltpu.VMEM((2, 2, WIDE, INNER * rows), low),
            pltpu.VMEM((2, INNER * rows, WIDE), low),
            pltpu.VMEM((2, WIDE, INNER * rows), low),
            pltpu.VMEM((2, tile, half), low),
            pltpu.VMEM((tile, half), low),
            pltpu.VMEM((2, tile, half), low),
            pltpu.VMEM((tile, half), high),
            dma((CHUNKS, INNER - 1)),
            dma((CHUNKS, INNER - 1)),
            dma((CHUNKS,)),
            dma((CHUNKS, 2, S)),
            dma((CHUNKS, 2, S)),
            dma((2, INNER - 1)),
            dma((2, INNER - 1)),
            dma((2, INNER)),
            dma((2, INNER)),
            dma((CHUNKS, 2, S)),
            dma((CHUNKS, 2, S)),
            dma((CHUNKS, INNER)),
            dma((CHUNKS, INNER - 1)),
            dma((3, 2 * INNER)),
            dma((3, 2 * INNER)),
            dma((3, 2 * INNER)),
            dma((3, 2 * INNER)),
            dma((6,)),
        ],
        compiler_params=pltpu.CompilerParams(
            collective_id=0, has_side_effects=True, vmem_limit_bytes=64 * 1024 * 1024
        ),
        cost_estimate=pl.CostEstimate(
            flops=80_000_000_000, bytes_accessed=60_000_000, transcendentals=10_000_000
        ),
    )(wst, xin, yin, cos_rows, sin_rows, norm_params, bias_h, bias_f)


def swap_pairs(count, step):
    return [(i, i ^ step) for i in range(count)]


def block_of(array, index, size, axis=0):
    return lax.dynamic_slice_in_dim(array, index * size, size, axis)


def on_device(
    inputs,
    cotangent,
    segment_ids,
    w_qkv,
    w_out,
    w_fc1,
    w_fc2,
    norm_params,
    proj_bias,
    fc1_bias,
    qkv_rows,
    qkv_cols,
    out_rows,
    out_cols,
    fc1_rows,
    fc1_cols,
    fc2_rows,
    fc2_cols,
    norm_second,
    bias_second,
    fc1b_second,
):
    tokens = inputs.shape[0]
    local_width = inputs.shape[1]
    local_hidden = fc1_bias.shape[0]
    rows = w_qkv.shape[0]
    count = lax.axis_size("batch")
    c = lax.axis_index("branch")
    b = lax.axis_index("batch")
    q = lax.rem(b, INNER)
    group = INNER * tokens
    width_q = local_width // INNER
    hidden_q = local_hidden // INNER
    own_start = c * local_width
    batch_first = (b == 0).astype(jnp.float32)
    branch_first = (c == 0).astype(jnp.float32)
    old_norms = lax.psum(
        (
            jnp.sum(w_qkv * w_qkv),
            jnp.sum(w_out * w_out),
            jnp.sum(w_fc1 * w_fc1),
            jnp.sum(w_fc2 * w_fc2),
            jnp.sum(proj_bias * proj_bias, axis=1) * batch_first,
            jnp.sum(fc1_bias * fc1_bias) * batch_first,
        ),
        ("batch", "branch"),
    )
    qkv_low = w_qkv.astype(jnp.bfloat16).reshape(rows, 3, INNER, HEADS_DEV, HD)
    out_low = w_out.astype(jnp.bfloat16).reshape(INNER, HEADS_DEV, HD, rows)
    fc1_low = w_fc1.astype(jnp.bfloat16).reshape(rows, INNER, CUTS, CUT)
    fc2_low = w_fc2.astype(jnp.bfloat16).reshape(INNER, CUTS, CUT, rows)
    heads_low = jnp.concatenate(
        [
            qkv_low.transpose(3, 2, 0, 1, 4).reshape(HEADS_DEV, INNER, rows, 3 * HD),
            out_low.transpose(1, 0, 3, 2),
        ],
        axis=3,
    )
    cuts_low = jnp.concatenate(
        [fc1_low.transpose(2, 1, 0, 3), fc2_low.transpose(1, 0, 3, 2)], axis=3
    )
    wst = jnp.concatenate([heads_low, cuts_low], axis=0)

    segment = jnp.concatenate(
        [segment_ids]
        + [lax.ppermute(segment_ids, "batch", swap_pairs(count, d)) for d in range(1, INNER)],
        axis=0,
    )
    positions_idx = jnp.arange(tokens)
    earlier = jnp.sum((segment[:, None, :] < segment[:, :, None]).astype(jnp.int32), axis=2)
    starts = earlier.astype(jnp.float32).reshape(group, 1)
    places = (positions_idx[None] - earlier).astype(jnp.float32).reshape(group, 1)
    frequency = 10000.0 ** (-2.0 * jnp.arange(ROT // 2, dtype=jnp.float32) / ROT)
    angles = places * frequency[None, :]
    cos_part = jnp.cos(angles)
    sin_part = jnp.sin(angles)
    rest = (group, HD - ROT)
    cos_rows = jnp.concatenate([cos_part, cos_part, jnp.ones(rest, jnp.float32)], axis=1)
    sin_rows = jnp.concatenate([-sin_part, sin_part, jnp.broadcast_to(starts, rest)], axis=1)
    bias_h = (
        block_of(proj_bias[0:3], q, width_q, 1)
        .reshape(3, HEADS_DEV, HD)
        .transpose(1, 0, 2)
        .reshape(HEADS_DEV, 1, 3 * HD)
    )
    bias_f = block_of(fc1_bias, q, hidden_q).reshape(CUTS, 1, CUT)
    received, _, _, plane_parts, plane_own, head_bias, cut_bias = block_call(
        count, wst, inputs, cotangent, cos_rows, sin_rows, norm_params, bias_h, bias_f
    )
    own_one, own_two, branch_sum = (
        plane_own[i] + jnp.sum(plane_parts[i].astype(jnp.float32), axis=0) for i in range(3)
    )
    output = (inputs.astype(jnp.float32) + branch_sum + proj_bias[3] + proj_bias[4]).astype(
        jnp.bfloat16
    )

    back_float = cotangent.astype(jnp.float32)
    in_float = inputs.astype(jnp.float32)
    row_sums = lax.psum(jnp.sum(in_float, axis=-1, keepdims=True), "branch")
    centered = in_float - row_sums / D
    variance = lax.psum(jnp.sum(centered * centered, axis=-1, keepdims=True), "branch") / D
    inverse_own = lax.rsqrt(variance + EPS_NORM)
    normed_own = centered * inverse_own
    gain_a = block_of(norm_params[0], c, local_width)
    gain_b = block_of(norm_params[2], c, local_width)
    scaled = own_one * gain_a + own_two * gain_b
    row_terms = lax.psum(
        (jnp.sum(scaled, axis=-1), jnp.sum(scaled * normed_own, axis=-1)),
        "branch",
    )
    input_grad = (
        inverse_own
        * (scaled - row_terms[0][:, None] / D - normed_own * (row_terms[1][:, None] / D))
        + back_float
    ).astype(jnp.bfloat16)
    norm_local = jnp.stack(
        [
            jnp.sum(own_one * normed_own, axis=0),
            jnp.sum(own_one, axis=0),
            jnp.sum(own_two * normed_own, axis=0),
            jnp.sum(own_two, axis=0),
        ]
    )
    norm_part = lax.dynamic_update_slice_in_dim(
        jnp.zeros((4, D), jnp.float32), norm_local, own_start, 1
    )
    back_sum = jnp.sum(back_float, axis=0)
    qkv_bias = head_bias.reshape(HEADS_DEV, 3, HD).transpose(1, 0, 2).reshape(3, width_q)
    bias_part = lax.dynamic_update_slice(
        jnp.zeros((5, local_width), jnp.float32), jnp.stack([back_sum, back_sum]), (3, 0)
    )
    bias_part = lax.dynamic_update_slice(bias_part, qkv_bias, (0, q * width_q))
    fc1b_part = lax.dynamic_update_slice_in_dim(
        jnp.zeros((local_hidden,), jnp.float32), cut_bias.reshape(hidden_q), q * hidden_q, 0
    )
    norm_grad = lax.psum(norm_part, ("batch", "branch"))
    bias_grad, fc1b_grad = lax.psum((bias_part, fc1b_part), "batch")

    received = received.astype(jnp.float32)
    heads_back, cuts_back = received[:HEADS_DEV], received[HEADS_DEV:]
    qkv_grad = (
        heads_back[..., : 3 * HD]
        .reshape(HEADS_DEV, INNER, rows, 3, HD)
        .transpose(2, 3, 1, 0, 4)
        .reshape(rows, 3 * local_width)
    )
    out_grad = heads_back[..., 3 * HD :].transpose(1, 0, 3, 2).reshape(local_width, rows)
    fc1_grad = cuts_back[..., :CUT].transpose(2, 1, 0, 3).reshape(rows, local_hidden)
    fc2_grad = cuts_back[..., CUT:].transpose(1, 0, 3, 2).reshape(local_hidden, rows)
    qkv_flat = w_qkv.reshape(qkv_grad.shape)
    qkv_cols_flat = qkv_cols.reshape(-1)
    qkv_square = squares(qkv_grad)
    fc1_square = squares(fc1_grad)
    out_square = squares(out_grad)
    fc2_square = squares(fc2_grad)
    pair_sums = lax.psum(
        (
            jnp.sum(qkv_square, axis=1),
            jnp.sum(fc1_square, axis=1),
            jnp.sum(out_square, axis=0),
            jnp.sum(fc2_square, axis=0),
        ),
        "branch",
    )
    qkv_rows_new = renew_stat(qkv_rows, pair_sums[0])
    fc1_rows_new = renew_stat(fc1_rows, pair_sums[1])
    out_cols_new = renew_stat(out_cols, pair_sums[2])
    fc2_cols_new = renew_stat(fc2_cols, pair_sums[3])
    bias_moment, bias_update = second_step(bias_grad, bias_second)
    fc1b_moment, fc1b_update = second_step(fc1b_grad, fc1b_second)
    cross_sums = lax.psum(
        (
            jnp.sum(qkv_square, axis=0),
            jnp.sum(fc1_square, axis=0),
            jnp.sum(out_square, axis=1),
            jnp.sum(fc2_square, axis=1),
        ),
        "batch",
    )
    qkv_cols_new = renew_stat(qkv_cols_flat, cross_sums[0])
    fc1_cols_new = renew_stat(fc1_cols, cross_sums[1])
    out_rows_new = renew_stat(out_rows, cross_sums[2])
    fc2_rows_new = renew_stat(fc2_rows, cross_sums[3])
    overall = lax.psum(
        (
            jnp.sum(qkv_rows_new) * branch_first,
            ratio_sum(qkv_grad, qkv_rows_new, qkv_cols_new),
            jnp.sum(fc1_rows_new) * branch_first,
            ratio_sum(fc1_grad, fc1_rows_new, fc1_cols_new),
            jnp.sum(out_rows_new) * batch_first,
            ratio_sum(out_grad, out_rows_new, out_cols_new),
            jnp.sum(fc2_rows_new) * batch_first,
            ratio_sum(fc2_grad, fc2_rows_new, fc2_cols_new),
            jnp.sum(bias_update * bias_update, axis=1) * batch_first,
            jnp.sum(fc1b_update * fc1b_update) * batch_first,
        ),
        ("batch", "branch"),
    )
    (
        qkv_total,
        qkv_inverse,
        fc1_total,
        fc1_inverse,
        out_total,
        out_inverse,
        fc2_total,
        fc2_inverse,
        bias_usq,
        fc1b_usq,
    ) = overall
    qkv_next = finish(
        qkv_flat,
        qkv_grad,
        qkv_rows_new,
        qkv_cols_new,
        qkv_total,
        qkv_inverse,
        old_norms[0],
        3 * D * D,
    )
    out_next = finish(
        w_out, out_grad, out_rows_new, out_cols_new, out_total, out_inverse, old_norms[1], D * D
    )
    fc1_next = finish(
        w_fc1, fc1_grad, fc1_rows_new, fc1_cols_new, fc1_total, fc1_inverse, old_norms[2], D * FF
    )
    fc2_next = finish(
        w_fc2, fc2_grad, fc2_rows_new, fc2_cols_new, fc2_total, fc2_inverse, old_norms[3], FF * D
    )
    bias_new = vector_finish(proj_bias, bias_update, bias_usq, old_norms[4], D)
    fc1b_new = vector_finish(fc1_bias, fc1b_update, fc1b_usq, old_norms[5], FF)
    norm_moment, norm_update = second_step(norm_grad, norm_second)
    norm_new = vector_finish(
        norm_params,
        norm_update,
        jnp.sum(norm_update * norm_update, axis=1),
        jnp.sum(norm_params * norm_params, axis=1),
        D,
    )
    qkv_shape = w_qkv.shape
    qkv_next = qkv_next.reshape(qkv_shape)
    return (
        output,
        input_grad,
        qkv_grad.reshape(qkv_shape),
        qkv_next,
        qkv_rows_new,
        qkv_cols_new.reshape(qkv_cols.shape),
        qkv_next.astype(jnp.bfloat16),
        out_grad,
        out_next,
        out_rows_new,
        out_cols_new,
        out_next.astype(jnp.bfloat16),
        fc1_grad,
        fc1_next,
        fc1_rows_new,
        fc1_cols_new,
        fc1_next.astype(jnp.bfloat16),
        fc2_grad,
        fc2_next,
        fc2_rows_new,
        fc2_cols_new,
        fc2_next.astype(jnp.bfloat16),
        norm_grad,
        norm_moment,
        norm_new,
        bias_grad,
        bias_moment,
        bias_new,
        fc1b_grad,
        fc1b_moment,
        fc1b_new,
    )


def solution(mesh):
    in_specs = (
        P("batch", "branch"),
        P("batch", "branch"),
        P("batch", None),
        P("batch", None, "branch"),
        P("branch", "batch"),
        P("batch", "branch"),
        P("branch", "batch"),
        P(),
        P(None, "branch"),
        P("branch"),
        P("batch"),
        P(None, "branch"),
        P("branch"),
        P("batch"),
        P("batch"),
        P("branch"),
        P("branch"),
        P("batch"),
        P(),
        P(None, "branch"),
        P("branch"),
    )
    out_specs = (
        P("batch", "branch"),
        P("batch", "branch"),
        P("batch", None, "branch"),
        P("batch", None, "branch"),
        P("batch"),
        P(None, "branch"),
        P("batch", None, "branch"),
        P("branch", "batch"),
        P("branch", "batch"),
        P("branch"),
        P("batch"),
        P("branch", "batch"),
        P("batch", "branch"),
        P("batch", "branch"),
        P("batch"),
        P("branch"),
        P("batch", "branch"),
        P("branch", "batch"),
        P("branch", "batch"),
        P("branch"),
        P("batch"),
        P("branch", "batch"),
        P(),
        P(),
        P(),
        P(None, "branch"),
        P(None, "branch"),
        P(None, "branch"),
        P("branch"),
        P("branch"),
        P("branch"),
    )
    return jax.shard_map(
        on_device, mesh=mesh, in_specs=in_specs, out_specs=out_specs, check_vma=False
    )
```

```python
import functools

import jax
import jax.numpy as jnp
from jax import lax
from jax.experimental import pallas as pl
from jax.experimental.pallas import tpu as pltpu
from jax.sharding import PartitionSpec as P

D = 2048
HD = 128
ROT = 32
FF = 8192
STEP = 10


EPS_NORM = 1e-05
EPS_SQUARE = 1e-30
RATE = 0.3
FLOOR_RATE = 0.001


def decay_rate():
    return 1.0 - STEP ** (-0.8)


def squares(gradient):
    return gradient * gradient + EPS_SQUARE


def renew_stat(old_stat, new_sum):
    decay = decay_rate()
    return decay * old_stat + (1.0 - decay) * new_sum


def ratio_sum(gradient, rows_new, cols_new):
    return jnp.sum(gradient * gradient * (1.0 / rows_new)[:, None] * (1.0 / cols_new)[None, :])


def finish(weight, gradient, rows_new, cols_new, row_total, inverse_sum, old_square, entries):
    update = (
        gradient * jnp.sqrt(row_total) * lax.rsqrt(rows_new)[:, None] * lax.rsqrt(cols_new)[None, :]
    )
    clip_factor = jnp.maximum(1.0, jnp.sqrt(row_total * inverse_sum / entries))
    step_rate = RATE * jnp.maximum(FLOOR_RATE, jnp.sqrt(old_square / entries))
    return weight - step_rate * update / clip_factor


def second_step(gradient, second):
    second_new = renew_stat(second, squares(gradient))
    return (second_new, gradient * lax.rsqrt(second_new))


def vector_finish(vector, update, update_square, old_square, entries):
    clip_factor = jnp.maximum(1.0, jnp.sqrt(update_square / entries))[..., None]
    step_rate = RATE * jnp.maximum(FLOOR_RATE, jnp.sqrt(old_square / entries))[..., None]
    return vector - step_rate * update / clip_factor


INNER = 4
HEADS_DEV = 2
CUTS = 4
CHUNKS = HEADS_DEV + CUTS
CUT = 256
WIDE = 512
MESH = pl.DeviceIdType.MESH


def flip(index, step):
    return index + step * (1 - 2 * lax.rem(index // step, 2))


def nn(left, right):
    return jnp.dot(left, right, preferred_element_type=jnp.float32)


def nt(left, right):
    return lax.dot_general(
        left, right, (((1,), (1,)), ((), ())), preferred_element_type=jnp.float32
    )


def tn(left, right):
    return lax.dot_general(
        left, right, (((0,), (0,)), ((), ())), preferred_element_type=jnp.float32
    )


def block_kernel(
    count,
    wst,
    xin,
    yin,
    turn_ref,
    norm_ref,
    bias_h,
    bias_f,
    gr,
    xr,
    xo,
    qb,
    fb,
    H1,
    H2,
    DY,
    W,
    TA,
    G,
    sbuf,
    fbuf,
    rsb,
    sib_send,
    sib_land,
    psend,
    own,
    a2a_s,
    a2a_r,
    loc_s,
    ag_s,
    ag_r,
    x_s,
    x_r,
    sx_s,
    sx_r,
    rs_s,
    rs_r,
    gr_s,
    gr_r,
    sib_s,
    sib_r,
    p_s,
    p_r,
    tmp_s,
    free_s,
):
    outer = count // INNER
    S = outer - 1
    T, half = xin.shape
    R = wst.shape[2]
    block = INNER * R
    QT = T // 2
    b = lax.axis_index("batch")
    c = lax.axis_index("branch")
    q = lax.rem(b, INNER)
    o = b // INNER
    bx, by = flip(b, 1), flip(b, 2)
    bxy = flip(bx, 2)
    near = (bx, by, bxy)
    da = 1 + c
    db = 2 - c
    b_first = bx * (1 - c) + by * c
    b_second = by * (1 - c) + bx * c

    def remote(src, dst, ssem, rsem, to_b, to_c):
        return pltpu.make_async_remote_copy(
            src_ref=src,
            dst_ref=dst,
            send_sem=ssem,
            recv_sem=rsem,
            device_id=(to_b, to_c),
            device_id_type=MESH,
        )

    barrier = pltpu.get_barrier_semaphore()
    for who in near:
        pl.semaphore_signal(barrier, inc=1, device_id=(who, c), device_id_type=MESH)
    pl.semaphore_signal(barrier, inc=1, device_id=(b, 1 - c), device_id_type=MESH)

    @pl.when(o > 0)
    def _():
        pl.semaphore_signal(barrier, inc=1, device_id=(b - INNER, c), device_id_type=MESH)

    @pl.when(o < outer - 1)
    def _():
        pl.semaphore_signal(barrier, inc=1, device_id=(b + INNER, c), device_id_type=MESH)

    pl.semaphore_wait(barrier, 4 + jnp.minimum(o, 1) + jnp.minimum(outer - 1 - o, 1))

    def a2a_copy(k, d, received=False):
        to = near[d - 1]
        row = (to if received else b) * R
        return remote(
            wst.at[k, lax.rem(to, INNER)],
            W.at[k, pl.ds(pl.multiple_of(row, 16), R)],
            a2a_s.at[k, d - 1],
            a2a_r.at[k, d - 1],
            to,
            c,
        )

    def a2a_local(k):
        return pltpu.make_async_copy(
            wst.at[k, q], W.at[k, pl.ds(pl.multiple_of(b * R, 16), R)], loc_s.at[k]
        )

    def a2a_start(k):
        for d in range(1, INNER):
            a2a_copy(k, d).start()
        a2a_local(k).start()

    def a2a_wait(k):
        for d in range(1, INNER):
            a2a_copy(k, d, True).wait_recv()
        a2a_local(k).wait()

    def ag_copy(k, way, s, part):
        rows = pl.ds(pl.multiple_of(part * block, 16), block)
        to = b + INNER if way == 0 else b - INNER
        return remote(
            W.at[k, rows], W.at[k, rows], ag_s.at[k, way, s - 1], ag_r.at[k, way, s - 1], to, c
        )

    def ag_sends(k, s, what):
        @pl.when((o >= s - 1) & (o <= outer - 2))
        def _():
            what(ag_copy(k, 0, s, o - s + 1))

        @pl.when((o >= 1) & (o <= outer - s))
        def _():
            what(ag_copy(k, 1, s, o + s - 1))

    def ag_wait(k, s):
        @pl.when(o >= s)
        def _():
            ag_copy(k, 0, s, o - s).wait_recv()

        @pl.when(o <= outer - 1 - s)
        def _():
            ag_copy(k, 1, s, o + s).wait_recv()

    def ag_range(low, high):
        def step(n, carry):
            k = n // S
            s = lax.rem(n, S) + 1

            @pl.when(s == 1)
            def _():
                a2a_wait(k)

            @pl.when(s > 1)
            def _():
                ag_wait(k, s - 1)

            ag_sends(k, s, lambda copy: copy.start())
            return carry

        lax.fori_loop(low, high, step, 0)

    def ag(low, high):
        ag_range(low * S // 3, high * S // 3)

    def spot(buf, slot):
        return buf.at[
            pl.ds(pl.multiple_of(slot * T, 16), T), pl.ds(pl.multiple_of(c * half, 128), half)
        ]

    def other_spot(buf, slot):
        return buf.at[
            pl.ds(pl.multiple_of(slot * T, 16), T), pl.ds(pl.multiple_of((1 - c) * half, 128), half)
        ]

    def sx_copy(i, buf, slot, src=None):
        place = spot(buf, slot)
        return remote(place if src is None else src, place, sx_s.at[i, slot], sx_r.at[i, slot], b, 1 - c)

    def sx_wait(i, buf, slot):
        remote(
            other_spot(buf, slot), other_spot(buf, slot), sx_s.at[i, slot], sx_r.at[i, slot], b, 1 - c
        ).wait_recv()

    def x_first(i, src, buf):
        return remote(src, spot(buf, da), x_s.at[i, da - 1], x_r.at[i, da - 1], b_first, c)

    def x_second(i, src, buf):
        return remote(src, spot(buf, db), x_s.at[i, db - 1], x_r.at[i, db - 1], b_second, c)

    def x_forward(i, buf):
        return remote(spot(buf, da), spot(buf, 3), x_s.at[i, 2], x_r.at[i, 2], b_second, c)

    def x_diag(i, buf):
        return remote(spot(buf, 3), spot(buf, 3), x_s.at[i, 2], x_r.at[i, 2], b_second, c)

    def x_local(i, src, buf):
        return pltpu.make_async_copy(src, spot(buf, 0), tmp_s.at[i])

    def gather_one(i, src, buf):
        x_first(i, src, buf).start()
        x_local(i, src, buf).start()
        sx_copy(i, buf, 0, src).start()

    def gather_two(i, src, buf):
        x_first(i, src, buf).wait_recv()
        x_second(i, src, buf).start()
        x_forward(i, buf).start()
        sx_copy(i, buf, da).start()

    def gather_three(i, src, buf):
        x_second(i, src, buf).wait_recv()
        sx_copy(i, buf, db).start()
        x_diag(i, buf).wait_recv()
        sx_copy(i, buf, 3).start()

    def gather_sent(i, src, buf):
        x_first(i, src, buf).wait_send()
        x_second(i, src, buf).wait_send()
        x_forward(i, buf).wait_send()
        sx_copy(i, buf, 0, src).wait_send()
        for slot in range(1, INNER):
            sx_copy(i, buf, slot).wait_send()

    def norm_rows(slot):
        def step(i, carry):
            rows = pl.ds(pl.multiple_of(slot * T + i * 64, 64), 64)
            values = H1[rows, :].astype(jnp.float32)
            mean = jnp.mean(values, axis=-1, keepdims=True)
            centered = values - mean
            inverse = lax.rsqrt(jnp.mean(centered * centered, axis=-1, keepdims=True) + EPS_NORM)
            normed = centered * inverse
            H1[rows, :] = (normed * norm_ref[0:1, :] + norm_ref[1:2, :]).astype(jnp.bfloat16)
            H2[rows, :] = (normed * norm_ref[2:3, :] + norm_ref[3:4, :]).astype(jnp.bfloat16)
            return carry

        lax.fori_loop(0, T // 64, step, 0)

    lane = lax.broadcasted_iota(jnp.int32, (T, HD), 1)
    scale = HD ** (-0.5)

    def partner(tensor):
        return jnp.where(
            lane < ROT // 2,
            pltpu.roll(tensor, HD - ROT // 2, 1),
            jnp.where(lane < ROT, pltpu.roll(tensor, ROT // 2, 1), 0.0),
        )

    def head_piece(h, slot):
        rows = pl.ds(pl.multiple_of(slot * T, 128), T)
        table = turn_ref[rows, :]
        cos_rows = jnp.where(lane < ROT, table, 1.0)
        sin_rows = pltpu.roll(table, HD - ROT, 1)
        projected = nn(H1[rows, :], W[h, :, : 3 * HD]) + bias_h[h]
        first = projected[:, :HD]
        queries = (first * cos_rows + partner(first) * sin_rows).astype(jnp.bfloat16)
        second = projected[:, HD : 2 * HD]
        keys = (second * cos_rows + partner(second) * sin_rows).astype(jnp.bfloat16)
        values = projected[:, 2 * HD :].astype(jnp.bfloat16)
        back = nn(DY[rows, :], W[h, :, 3 * HD :]).astype(jnp.bfloat16)
        starts = table[:, 2 * ROT : 2 * ROT + 1]
        contexts, grad_q = [], []
        grad_k, grad_v = [None, None], [None, None]
        for i in range(2):
            seen = QT * (i + 1)
            part = slice(QT * i, QT * (i + 1))
            raw = nt(queries[part], keys[:seen]) * scale
            query_at = lax.broadcasted_iota(jnp.int32, (QT, seen), 0) + QT * i
            key_at = lax.broadcasted_iota(jnp.int32, (QT, seen), 1)
            allowed = (key_at <= query_at) & (key_at.astype(jnp.float32) >= starts[part])
            scores = jnp.where(allowed, raw, -1e30)
            exponent = jnp.exp(scores - jnp.max(scores, axis=-1, keepdims=True))
            probs = exponent * (1.0 / jnp.sum(exponent, axis=-1, keepdims=True))
            soft = probs.astype(jnp.bfloat16)
            contexts.append(nn(soft, values[:seen]).astype(jnp.bfloat16))
            grad_probs = nt(back[part], values[:seen])
            inner = jnp.sum(probs * grad_probs, axis=-1, keepdims=True)
            grad_scores = (probs * (grad_probs - inner)).astype(jnp.bfloat16)
            grad_q.append((nn(grad_scores, keys[:seen]) * scale).astype(jnp.bfloat16))
            for j in range(i + 1):
                cut = slice(QT * j, QT * (j + 1))
                term_v = tn(soft[:, cut], back[part])
                term_k = tn(grad_scores[:, cut], queries[part])
                grad_v[j] = term_v if grad_v[j] is None else grad_v[j] + term_v
                grad_k[j] = term_k if grad_k[j] is None else grad_k[j] + term_k
        context = jnp.concatenate(contexts, axis=0)
        dq = jnp.concatenate(grad_q, axis=0).astype(jnp.float32)
        dk = (jnp.concatenate(grad_k, axis=0) * scale).astype(jnp.bfloat16).astype(jnp.float32)
        dv = jnp.concatenate(grad_v, axis=0)
        turned = jnp.concatenate(
            [
                dq * cos_rows - partner(dq) * sin_rows,
                dk * cos_rows - partner(dk) * sin_rows,
                dv,
            ],
            axis=1,
        ).astype(jnp.bfloat16)
        TA[h, : 3 * HD, rows] = turned.T
        TA[h, 3 * HD :, rows] = context.T
        total = jnp.sum(turned.astype(jnp.float32), axis=0, keepdims=True)
        qb[h] = jnp.where(slot == 0, total, qb[h] + total)

    def cut_piece(f, slot):
        rows = pl.ds(pl.multiple_of(slot * T, 128), T)
        k = HEADS_DEV + f
        pre = nn(H2[rows, :], W[k, :, :CUT]) + bias_f[f]
        grad = nn(DY[rows, :], W[k, :, CUT:])
        normal = 0.5 * (1.0 + lax.erf(pre * (0.5**0.5)))
        slope = normal + pre * (jnp.exp(-0.5 * pre * pre) * (0.5 * 0.7978845608028654))
        active = (pre * normal).astype(jnp.bfloat16)
        pulled = (grad * slope).astype(jnp.bfloat16)
        low = pl.multiple_of(f * WIDE, WIDE)
        H1[pl.ds(low, CUT), rows] = pulled.T
        H1[pl.ds(low + CUT, CUT), rows] = active.T
        total = jnp.sum(pulled.astype(jnp.float32), axis=0, keepdims=True)
        fb[f] = jnp.where(slot == 0, total, fb[f] + total)

    def grads(k, turned, left, edge):
        def step(j, carry):
            cols = pl.ds(pl.multiple_of(j * block, 128), block)
            G[lax.rem(k, 2), j, :edge, :] = nn(turned(0, edge), left[:, cols])
            G[lax.rem(k, 2), j, edge:, :] = nn(turned(edge, WIDE - edge), DY[:, cols])
            return carry

        lax.fori_loop(0, outer, step, 0)

    def head_turned(h):
        return lambda low, size: TA[h, pl.ds(low, size), :]

    def cut_turned(f):
        return lambda low, size: H1[pl.ds(pl.multiple_of(f * WIDE + low, 128), size), :]

    def rs_copy(k, way, t):
        to = b + INNER if way == 0 else b - INNER
        return remote(
            sbuf.at[way],
            rsb.at[way, t - 1],
            rs_s.at[k, way, t - 1],
            rs_r.at[k, way, t - 1],
            to,
            c,
        )

    def rs_sends(way, t):
        if way == 0:
            return (o <= t - 1) & (o <= outer - 2)
        return (o >= outer - t) & (o >= 1)

    def rs_receives(way, t):
        if way == 0:
            return (o >= 1) & (o <= t)
        return (o <= outer - 2) & (o >= outer - 1 - t)

    def rs_fetch(k, way, t):
        rs_copy(k, way, t).wait_recv()
        return rsb[way, t - 1].astype(jnp.float32)

    def rs_range(low, high):
        def step(n, carry):
            k = n // S
            t = lax.rem(n, S) + 1

            @pl.when((t == 1) & (k >= 1) & (o < outer - 1))
            def _():
                pl.semaphore_wait(free_s.at[0], 1)

            @pl.when((t == 1) & (k >= 1) & (o > 0))
            def _():
                pl.semaphore_wait(free_s.at[1], 1)

            for way in range(2):
                owner = o + outer - t if way == 0 else o - outer + t

                before = jnp.maximum(n - 1, 0)
                k_before = before // S
                t_before = lax.rem(before, S) + 1

                @pl.when((n >= 1) & rs_sends(way, t_before))
                def _():
                    rs_copy(k_before, way, t_before).wait_send()

                @pl.when(rs_sends(way, t))
                def _():
                    @pl.when(rs_receives(way, t - 1) & (t > 1))
                    def _():
                        sbuf[way] = (
                            G[lax.rem(k, 2), owner] + rs_fetch(k, way, t - 1)
                        ).astype(jnp.bfloat16)

                    @pl.when(jnp.logical_not(rs_receives(way, t - 1) & (t > 1)))
                    def _():
                        sbuf[way] = G[lax.rem(k, 2), owner].astype(jnp.bfloat16)

                    rs_copy(k, way, t).start()

            return carry

        lax.fori_loop(low, high, step, 0)

    def rs(low, high):
        rs_range(low * S // 3, high * S // 3)

    def gr_copy(k, d, received=False):
        to = near[d - 1]
        slot = lax.rem(to, INNER)
        return remote(
            fbuf.at[pl.ds(pl.multiple_of(slot * R, 16), R)],
            gr.at[k, slot if received else q],
            gr_s.at[k, d - 1],
            gr_r.at[k, d - 1],
            to,
            c,
        )

    def gr_local(k):
        return pltpu.make_async_copy(
            fbuf.at[pl.ds(pl.multiple_of(q * R, 16), R)],
            gr.at[k, q],
            gr_s.at[k, 3],
        )

    def gr_sent(k):
        for d in range(1, INNER):
            gr_copy(k, d).wait_send()
        gr_local(k).wait()

    def rs_final(k):
        for way in range(2):

            @pl.when(rs_receives(way, S))
            def _():
                G[lax.rem(k, 2), o] = G[lax.rem(k, 2), o] + rs_fetch(k, way, S)

        @pl.when((k < CHUNKS - 1) & (o > 0))
        def _():
            pl.semaphore_signal(
                free_s.at[0], inc=1, device_id=(b - INNER, c), device_id_type=MESH
            )

        @pl.when((k < CHUNKS - 1) & (o < outer - 1))
        def _():
            pl.semaphore_signal(
                free_s.at[1], inc=1, device_id=(b + INNER, c), device_id_type=MESH
            )

        @pl.when(k >= 1)
        def _():
            gr_sent(k - 1)

        fbuf[...] = G[lax.rem(k, 2), o].T.astype(jnp.bfloat16)
        for d in range(1, INNER):
            gr_copy(k, d).start()
        gr_local(k).start()

    TILE = T // 2
    TILES = 2 * INNER

    def tile_slot(i):
        return INNER - 1 - i // 2

    def product(which, i, side):
        at = pl.multiple_of(tile_slot(i) * T + lax.rem(i, 2) * TILE, 128)
        toks = pl.ds(at, TILE)
        features = pl.ds(pl.multiple_of(side * half, 128), half)
        terms = []
        if which == 0:
            for h in range(HEADS_DEV):
                terms.append((h, slice(0, 3 * HD), lambda h=h: TA[h, : 3 * HD, toks]))
        elif which == 1:
            for f in range(CUTS):
                low = f * WIDE
                terms.append(
                    (HEADS_DEV + f, slice(0, CUT), lambda low=low: H1[low : low + CUT, toks])
                )
        else:
            for h in range(HEADS_DEV):
                terms.append((h, slice(3 * HD, WIDE), lambda h=h: TA[h, 3 * HD :, toks]))
            for f in range(CUTS):
                low = f * WIDE + CUT
                terms.append(
                    (HEADS_DEV + f, slice(CUT, WIDE), lambda low=low: H1[low : low + CUT, toks])
                )
        for place, (k, cols, right) in enumerate(terms):
            term = nn(W[k, features, cols], right())
            own[...] = term if place == 0 else own[...] + term

    def sib_copy(which, i):
        return remote(
            sib_send.at[lax.rem(i, 2)],
            sib_land.at[lax.rem(i, 4)],
            sib_s.at[which, i],
            sib_r.at[which, i],
            b,
            1 - c,
        )

    def plane_copy(which, i):
        slot = tile_slot(i)
        low, high = lax.rem(slot, 2), slot // 2
        to = b + low * (1 - 2 * lax.rem(b, 2)) + high * 2 * (1 - 2 * lax.rem(b // 2, 2))
        return remote(
            psend.at[lax.rem(i, 2)],
            xr.at[which, slot - 1, lax.rem(i, 2)],
            p_s.at[which, i],
            p_r.at[which, i],
            to,
            c,
        )

    def tile_a(which, i):
        @pl.when(i >= 2)
        def _():
            sib_copy(which, i - 2).wait_send()

        product(which, i, 1 - c)
        sib_send[lax.rem(i, 2)] = own[...].astype(jnp.bfloat16)
        sib_copy(which, i).start()

    def tile_b(which, i):
        product(which, i, c)
        sib_copy(which, i).wait_recv()

        @pl.when(i < TILES - 2)
        def _():
            @pl.when(i >= 2)
            def _():
                plane_copy(which, i - 2).wait_send()

            psend[lax.rem(i, 2)] = (
                own[...] + sib_land[lax.rem(i, 4)].astype(jnp.float32)
            ).astype(jnp.bfloat16)
            plane_copy(which, i).start()

        @pl.when(i >= TILES - 2)
        def _():
            own[...] = own[...] + sib_land[lax.rem(i, 4)].astype(jnp.float32)
            keep = pltpu.make_async_copy(own, xo.at[which, lax.rem(i, 2)], tmp_s.at[2])
            keep.start()
            keep.wait()

    def sum_tiles(which, beside):
        tile_a(which, 0)

        def step(i, carry):
            @pl.when(i < TILES - 1)
            def _():
                tile_a(which, i + 1)

            tile_b(which, i)
            beside(i)
            return carry

        lax.fori_loop(0, TILES, step, 0)

    def sum_sent(which):
        for i in range(TILES - 2, TILES):
            sib_copy(which, i).wait_send()
        for i in range(TILES - 4, TILES - 2):
            plane_copy(which, i).wait_send()

    def share(low, high, i, pieces, run):
        first, last = low * S // 3, high * S // 3
        run(first + (last - first) * i // pieces, first + (last - first) * (i + 1) // pieces)

    a2a_start(0)
    a2a_start(1)
    gather_one(0, xin, H1)
    ag(0, 1)
    gather_two(0, xin, H1)
    a2a_start(2)
    gather_one(1, yin, DY)
    ag(1, 2)
    x_local(0, xin, H1).wait()
    sx_wait(0, H1, 0)
    norm_rows(0)
    ag(2, 3)
    gather_three(0, xin, H1)
    gather_two(1, yin, DY)
    for k in range(3, CHUNKS):
        a2a_start(k)
    gather_sent(0, xin, H1)
    for slot in range(1, INNER):
        sx_wait(0, H1, slot)
        norm_rows(slot)
        ag(2 + slot, 3 + slot)
    ag(6, 7)
    gather_three(1, yin, DY)
    x_local(1, yin, DY).wait()
    for slot in range(INNER):
        sx_wait(1, DY, slot)
    gather_sent(1, yin, DY)

    def head_step(h, carry):
        ag_wait(h, S)

        def slot_step(slot, inner_carry):
            head_piece(h, slot)
            share(7 + 2 * h, 9 + 2 * h, slot, INNER, ag_range)
            share(0, 3 * h, slot, INNER, rs_range)
            return inner_carry

        lax.fori_loop(0, INNER, slot_step, 0)

        @pl.when(h == 1)
        def _():
            rs_final(0)

        grads(h, head_turned(h), H1, 3 * HD)
        return carry

    lax.fori_loop(0, HEADS_DEV, head_step, 0)

    def beside_one(i):
        share(11, 12, i, TILES, ag_range)
        share(3, 6, i, TILES, rs_range)

    sum_tiles(0, beside_one)
    rs_final(1)

    def cut_step(f, carry):
        ag_wait(HEADS_DEV + f, S)

        def slot_step(slot, inner_carry):
            cut_piece(f, slot)
            share(12 + 2 * f, jnp.minimum(14 + 2 * f, 18), slot, INNER, ag_range)
            share(jnp.maximum(6, 3 + 3 * f), 6 + 3 * f, slot, INNER, rs_range)
            return inner_carry

        lax.fori_loop(0, INNER, slot_step, 0)

        @pl.when(f >= 1)
        def _():
            rs_final(1 + f)

        grads(HEADS_DEV + f, cut_turned(f), H2, CUT)
        return carry

    lax.fori_loop(0, CUTS, cut_step, 0)
    sum_sent(0)
    sum_tiles(1, lambda i: share(15, 17, i, TILES, rs_range))
    sum_sent(1)
    sum_tiles(2, lambda i: share(17, 18, i, TILES, rs_range))
    sum_sent(2)
    rs_final(CHUNKS - 1)

    gr_sent(CHUNKS - 1)

    def drain_chunk(k, carry):
        for d in range(1, INNER):
            a2a_copy(k, d).wait_send()
            gr_copy(k, d, True).wait_recv()

        def drain_step(s, inner_carry):
            ag_sends(k, s, lambda copy: copy.wait_send())
            return inner_carry

        lax.fori_loop(1, S + 1, drain_step, 0)
        return carry

    lax.fori_loop(0, CHUNKS, drain_chunk, 0)
    for way in range(2):

        @pl.when(rs_sends(way, S))
        def _():
            rs_copy(CHUNKS - 1, way, S).wait_send()

    for which in range(3):

        def drain_tile(i, carry):
            plane_copy(which, i).wait_recv()
            return carry

        lax.fori_loop(0, TILES - 2, drain_tile, 0)


def block_call(count, wst, xin, yin, turns, norm_params, bias_h, bias_f):
    outer = count // INNER
    S = outer - 1
    tokens, half = xin.shape
    group = INNER * tokens
    rows = wst.shape[2]
    tile = tokens // 2
    low, high = jnp.bfloat16, jnp.float32
    any_spec = pl.BlockSpec(memory_space=pl.ANY)
    vmem_spec = pl.BlockSpec(memory_space=pltpu.VMEM)
    dma = pltpu.SemaphoreType.DMA
    return pl.pallas_call(
        functools.partial(block_kernel, count),
        out_shape=[
            jax.ShapeDtypeStruct((CHUNKS, INNER, rows, WIDE), low),
            jax.ShapeDtypeStruct((3, INNER - 1, 2, half, tile), low),
            jax.ShapeDtypeStruct((3, 2, half, tile), high),
            jax.ShapeDtypeStruct((HEADS_DEV, 1, 3 * HD), high),
            jax.ShapeDtypeStruct((CUTS, 1, CUT), high),
        ],
        in_specs=[any_spec] * 3 + [vmem_spec] * 4,
        out_specs=[any_spec] * 3 + [vmem_spec] * 2,
        scratch_shapes=[
            pltpu.VMEM((group, D), low),
            pltpu.VMEM((group, D), low),
            pltpu.VMEM((group, D), low),
            pltpu.VMEM((CHUNKS, D, WIDE), low),
            pltpu.VMEM((HEADS_DEV, WIDE, group), low),
            pltpu.VMEM((2, outer, WIDE, INNER * rows), high),
            pltpu.VMEM((2, WIDE, INNER * rows), low),
            pltpu.VMEM((INNER * rows, WIDE), low),
            pltpu.VMEM((2, S, WIDE, INNER * rows), low),
            pltpu.VMEM((2, half, tile), low),
            pltpu.VMEM((4, half, tile), low),
            pltpu.VMEM((2, half, tile), low),
            pltpu.VMEM((half, tile), high),
            dma((CHUNKS, INNER - 1)),
            dma((CHUNKS, INNER - 1)),
            dma((CHUNKS,)),
            dma((CHUNKS, 2, S)),
            dma((CHUNKS, 2, S)),
            dma((2, INNER - 1)),
            dma((2, INNER - 1)),
            dma((2, INNER)),
            dma((2, INNER)),
            dma((CHUNKS, 2, S)),
            dma((CHUNKS, 2, S)),
            dma((CHUNKS, INNER)),
            dma((CHUNKS, INNER - 1)),
            dma((3, 2 * INNER)),
            dma((3, 2 * INNER)),
            dma((3, 2 * INNER)),
            dma((3, 2 * INNER)),
            dma((3,)),
            pltpu.SemaphoreType.REGULAR((2,)),
        ],
        compiler_params=pltpu.CompilerParams(
            collective_id=0, has_side_effects=True, vmem_limit_bytes=64 * 1024 * 1024
        ),
        cost_estimate=pl.CostEstimate(
            flops=80_000_000_000, bytes_accessed=60_000_000, transcendentals=10_000_000
        ),
    )(wst, xin, yin, turns, norm_params, bias_h, bias_f)


def swap_pairs(count, step):
    return [(i, i ^ step) for i in range(count)]


def block_of(array, index, size, axis=0):
    return lax.dynamic_slice_in_dim(array, index * size, size, axis)


def on_device(
    inputs,
    cotangent,
    segment_ids,
    w_qkv,
    w_out,
    w_fc1,
    w_fc2,
    norm_params,
    proj_bias,
    fc1_bias,
    qkv_rows,
    qkv_cols,
    out_rows,
    out_cols,
    fc1_rows,
    fc1_cols,
    fc2_rows,
    fc2_cols,
    norm_second,
    bias_second,
    fc1b_second,
):
    tokens = inputs.shape[0]
    local_width = inputs.shape[1]
    local_hidden = fc1_bias.shape[0]
    rows = w_qkv.shape[0]
    count = lax.axis_size("batch")
    c = lax.axis_index("branch")
    b = lax.axis_index("batch")
    q = lax.rem(b, INNER)
    group = INNER * tokens
    width_q = local_width // INNER
    hidden_q = local_hidden // INNER
    own_start = c * local_width
    batch_first = (b == 0).astype(jnp.float32)
    branch_first = (c == 0).astype(jnp.float32)
    old_norms = lax.psum(
        (
            jnp.sum(w_qkv * w_qkv),
            jnp.sum(w_out * w_out),
            jnp.sum(w_fc1 * w_fc1),
            jnp.sum(w_fc2 * w_fc2),
            jnp.sum(proj_bias * proj_bias, axis=1) * batch_first,
            jnp.sum(fc1_bias * fc1_bias) * batch_first,
        ),
        ("batch", "branch"),
    )
    qkv_low = w_qkv.astype(jnp.bfloat16).reshape(rows, 3, INNER, HEADS_DEV, HD)
    out_low = w_out.astype(jnp.bfloat16).reshape(INNER, HEADS_DEV, HD, rows)
    fc1_low = w_fc1.astype(jnp.bfloat16).reshape(rows, INNER, CUTS, CUT)
    fc2_low = w_fc2.astype(jnp.bfloat16).reshape(INNER, CUTS, CUT, rows)
    heads_low = jnp.concatenate(
        [
            qkv_low.transpose(3, 2, 0, 1, 4).reshape(HEADS_DEV, INNER, rows, 3 * HD),
            out_low.transpose(1, 0, 3, 2),
        ],
        axis=3,
    )
    cuts_low = jnp.concatenate(
        [fc1_low.transpose(2, 1, 0, 3), fc2_low.transpose(1, 0, 3, 2)], axis=3
    )
    wst = jnp.concatenate([heads_low, cuts_low], axis=0)

    segment = jnp.concatenate(
        [segment_ids]
        + [lax.ppermute(segment_ids, "batch", swap_pairs(count, d)) for d in range(1, INNER)],
        axis=0,
    )
    positions_idx = jnp.arange(tokens)
    earlier = jnp.sum((segment[:, None, :] < segment[:, :, None]).astype(jnp.int32), axis=2)
    starts = earlier.astype(jnp.float32).reshape(group, 1)
    places = (positions_idx[None] - earlier).astype(jnp.float32).reshape(group, 1)
    frequency = 10000.0 ** (-2.0 * jnp.arange(ROT // 2, dtype=jnp.float32) / ROT)
    angles = places * frequency[None, :]
    cos_part = jnp.cos(angles)
    sin_part = jnp.sin(angles)
    rest = (group, HD - 2 * ROT)
    turns = jnp.concatenate(
        [cos_part, cos_part, -sin_part, sin_part, jnp.broadcast_to(starts, rest)], axis=1
    )
    bias_h = (
        block_of(proj_bias[0:3], q, width_q, 1)
        .reshape(3, HEADS_DEV, HD)
        .transpose(1, 0, 2)
        .reshape(HEADS_DEV, 1, 3 * HD)
    )
    bias_f = block_of(fc1_bias, q, hidden_q).reshape(CUTS, 1, CUT)
    received, plane_parts, plane_own, head_bias, cut_bias = block_call(
        count, wst, inputs, cotangent, turns, norm_params, bias_h, bias_f
    )
    own_one, own_two, branch_sum = (
        (plane_own[i] + jnp.sum(plane_parts[i].astype(jnp.float32), axis=0))
        .transpose(0, 2, 1)
        .reshape(tokens, local_width)
        for i in range(3)
    )
    output = (inputs.astype(jnp.float32) + branch_sum + proj_bias[3] + proj_bias[4]).astype(
        jnp.bfloat16
    )

    back_float = cotangent.astype(jnp.float32)
    in_float = inputs.astype(jnp.float32)
    row_sums = lax.psum(jnp.sum(in_float, axis=-1, keepdims=True), "branch")
    centered = in_float - row_sums / D
    variance = lax.psum(jnp.sum(centered * centered, axis=-1, keepdims=True), "branch") / D
    inverse_own = lax.rsqrt(variance + EPS_NORM)
    normed_own = centered * inverse_own
    gain_a = block_of(norm_params[0], c, local_width)
    gain_b = block_of(norm_params[2], c, local_width)
    scaled = own_one * gain_a + own_two * gain_b
    row_terms = lax.psum(
        (jnp.sum(scaled, axis=-1), jnp.sum(scaled * normed_own, axis=-1)),
        "branch",
    )
    input_grad = (
        inverse_own
        * (scaled - row_terms[0][:, None] / D - normed_own * (row_terms[1][:, None] / D))
        + back_float
    ).astype(jnp.bfloat16)
    norm_local = jnp.stack(
        [
            jnp.sum(own_one * normed_own, axis=0),
            jnp.sum(own_one, axis=0),
            jnp.sum(own_two * normed_own, axis=0),
            jnp.sum(own_two, axis=0),
        ]
    )
    norm_part = lax.dynamic_update_slice_in_dim(
        jnp.zeros((4, D), jnp.float32), norm_local, own_start, 1
    )
    back_sum = jnp.sum(back_float, axis=0)
    qkv_bias = head_bias.reshape(HEADS_DEV, 3, HD).transpose(1, 0, 2).reshape(3, width_q)
    bias_part = lax.dynamic_update_slice(
        jnp.zeros((5, local_width), jnp.float32), jnp.stack([back_sum, back_sum]), (3, 0)
    )
    bias_part = lax.dynamic_update_slice(bias_part, qkv_bias, (0, q * width_q))
    fc1b_part = lax.dynamic_update_slice_in_dim(
        jnp.zeros((local_hidden,), jnp.float32), cut_bias.reshape(hidden_q), q * hidden_q, 0
    )
    norm_grad = lax.psum(norm_part, ("batch", "branch"))
    bias_grad, fc1b_grad = lax.psum((bias_part, fc1b_part), "batch")

    received = received.astype(jnp.float32)
    heads_back, cuts_back = received[:HEADS_DEV], received[HEADS_DEV:]
    qkv_grad = (
        heads_back[..., : 3 * HD]
        .reshape(HEADS_DEV, INNER, rows, 3, HD)
        .transpose(2, 3, 1, 0, 4)
        .reshape(rows, 3 * local_width)
    )
    out_grad = heads_back[..., 3 * HD :].transpose(1, 0, 3, 2).reshape(local_width, rows)
    fc1_grad = cuts_back[..., :CUT].transpose(2, 1, 0, 3).reshape(rows, local_hidden)
    fc2_grad = cuts_back[..., CUT:].transpose(1, 0, 3, 2).reshape(local_hidden, rows)
    qkv_flat = w_qkv.reshape(qkv_grad.shape)
    qkv_cols_flat = qkv_cols.reshape(-1)
    qkv_square = squares(qkv_grad)
    fc1_square = squares(fc1_grad)
    out_square = squares(out_grad)
    fc2_square = squares(fc2_grad)
    pair_sums = lax.psum(
        (
            jnp.sum(qkv_square, axis=1),
            jnp.sum(fc1_square, axis=1),
            jnp.sum(out_square, axis=0),
            jnp.sum(fc2_square, axis=0),
        ),
        "branch",
    )
    qkv_rows_new = renew_stat(qkv_rows, pair_sums[0])
    fc1_rows_new = renew_stat(fc1_rows, pair_sums[1])
    out_cols_new = renew_stat(out_cols, pair_sums[2])
    fc2_cols_new = renew_stat(fc2_cols, pair_sums[3])
    bias_moment, bias_update = second_step(bias_grad, bias_second)
    fc1b_moment, fc1b_update = second_step(fc1b_grad, fc1b_second)
    cross_sums = lax.psum(
        (
            jnp.sum(qkv_square, axis=0),
            jnp.sum(fc1_square, axis=0),
            jnp.sum(out_square, axis=1),
            jnp.sum(fc2_square, axis=1),
        ),
        "batch",
    )
    qkv_cols_new = renew_stat(qkv_cols_flat, cross_sums[0])
    fc1_cols_new = renew_stat(fc1_cols, cross_sums[1])
    out_rows_new = renew_stat(out_rows, cross_sums[2])
    fc2_rows_new = renew_stat(fc2_rows, cross_sums[3])
    overall = lax.psum(
        (
            jnp.sum(qkv_rows_new) * branch_first,
            ratio_sum(qkv_grad, qkv_rows_new, qkv_cols_new),
            jnp.sum(fc1_rows_new) * branch_first,
            ratio_sum(fc1_grad, fc1_rows_new, fc1_cols_new),
            jnp.sum(out_rows_new) * batch_first,
            ratio_sum(out_grad, out_rows_new, out_cols_new),
            jnp.sum(fc2_rows_new) * batch_first,
            ratio_sum(fc2_grad, fc2_rows_new, fc2_cols_new),
            jnp.sum(bias_update * bias_update, axis=1) * batch_first,
            jnp.sum(fc1b_update * fc1b_update) * batch_first,
        ),
        ("batch", "branch"),
    )
    (
        qkv_total,
        qkv_inverse,
        fc1_total,
        fc1_inverse,
        out_total,
        out_inverse,
        fc2_total,
        fc2_inverse,
        bias_usq,
        fc1b_usq,
    ) = overall
    qkv_next = finish(
        qkv_flat,
        qkv_grad,
        qkv_rows_new,
        qkv_cols_new,
        qkv_total,
        qkv_inverse,
        old_norms[0],
        3 * D * D,
    )
    out_next = finish(
        w_out, out_grad, out_rows_new, out_cols_new, out_total, out_inverse, old_norms[1], D * D
    )
    fc1_next = finish(
        w_fc1, fc1_grad, fc1_rows_new, fc1_cols_new, fc1_total, fc1_inverse, old_norms[2], D * FF
    )
    fc2_next = finish(
        w_fc2, fc2_grad, fc2_rows_new, fc2_cols_new, fc2_total, fc2_inverse, old_norms[3], FF * D
    )
    bias_new = vector_finish(proj_bias, bias_update, bias_usq, old_norms[4], D)
    fc1b_new = vector_finish(fc1_bias, fc1b_update, fc1b_usq, old_norms[5], FF)
    norm_moment, norm_update = second_step(norm_grad, norm_second)
    norm_new = vector_finish(
        norm_params,
        norm_update,
        jnp.sum(norm_update * norm_update, axis=1),
        jnp.sum(norm_params * norm_params, axis=1),
        D,
    )
    qkv_shape = w_qkv.shape
    qkv_next = qkv_next.reshape(qkv_shape)
    return (
        output,
        input_grad,
        qkv_grad.reshape(qkv_shape),
        qkv_next,
        qkv_rows_new,
        qkv_cols_new.reshape(qkv_cols.shape),
        qkv_next.astype(jnp.bfloat16),
        out_grad,
        out_next,
        out_rows_new,
        out_cols_new,
        out_next.astype(jnp.bfloat16),
        fc1_grad,
        fc1_next,
        fc1_rows_new,
        fc1_cols_new,
        fc1_next.astype(jnp.bfloat16),
        fc2_grad,
        fc2_next,
        fc2_rows_new,
        fc2_cols_new,
        fc2_next.astype(jnp.bfloat16),
        norm_grad,
        norm_moment,
        norm_new,
        bias_grad,
        bias_moment,
        bias_new,
        fc1b_grad,
        fc1b_moment,
        fc1b_new,
    )


def solution(mesh):
    in_specs = (
        P("batch", "branch"),
        P("batch", "branch"),
        P("batch", None),
        P("batch", None, "branch"),
        P("branch", "batch"),
        P("batch", "branch"),
        P("branch", "batch"),
        P(),
        P(None, "branch"),
        P("branch"),
        P("batch"),
        P(None, "branch"),
        P("branch"),
        P("batch"),
        P("batch"),
        P("branch"),
        P("branch"),
        P("batch"),
        P(),
        P(None, "branch"),
        P("branch"),
    )
    out_specs = (
        P("batch", "branch"),
        P("batch", "branch"),
        P("batch", None, "branch"),
        P("batch", None, "branch"),
        P("batch"),
        P(None, "branch"),
        P("batch", None, "branch"),
        P("branch", "batch"),
        P("branch", "batch"),
        P("branch"),
        P("batch"),
        P("branch", "batch"),
        P("batch", "branch"),
        P("batch", "branch"),
        P("batch"),
        P("branch"),
        P("batch", "branch"),
        P("branch", "batch"),
        P("branch", "batch"),
        P("branch"),
        P("batch"),
        P("branch", "batch"),
        P(),
        P(),
        P(),
        P(None, "branch"),
        P(None, "branch"),
        P(None, "branch"),
        P("branch"),
        P("branch"),
        P("branch"),
    )
    return jax.shard_map(
        on_device, mesh=mesh, in_specs=in_specs, out_specs=out_specs, check_vma=False
    )
```

```python
import functools

import jax
import jax.numpy as jnp
from jax import lax
from jax.experimental import pallas as pl
from jax.experimental.pallas import tpu as pltpu
from jax.sharding import PartitionSpec as P

D = 2048
HD = 128
ROT = 32
FF = 8192
STEP = 10


EPS_NORM = 1e-05
EPS_SQUARE = 1e-30
RATE = 0.3
FLOOR_RATE = 0.001


def decay_rate():
    return 1.0 - STEP ** (-0.8)


def squares(gradient):
    return gradient * gradient + EPS_SQUARE


def renew_stat(old_stat, new_sum):
    decay = decay_rate()
    return decay * old_stat + (1.0 - decay) * new_sum


def second_step(gradient, second):
    second_new = renew_stat(second, squares(gradient))
    return (second_new, gradient * lax.rsqrt(second_new))


INNER = 4
HEADS_DEV = 2
CUTS = 4
CHUNKS = HEADS_DEV + CUTS
CUT = 256
WIDE = 512
MESH = pl.DeviceIdType.MESH


def flip(index, step):
    return index + step * (1 - 2 * lax.rem(index // step, 2))


def nn(left, right):
    return jnp.dot(left, right, preferred_element_type=jnp.float32)


def nt(left, right):
    return lax.dot_general(
        left, right, (((1,), (1,)), ((), ())), preferred_element_type=jnp.float32
    )


def tn(left, right):
    return lax.dot_general(
        left, right, (((0,), (0,)), ((), ())), preferred_element_type=jnp.float32
    )


def block_kernel(
    count,
    wst,
    xin,
    yin,
    turn_ref,
    norm_ref,
    bias_h,
    bias_f,
    gr,
    xr,
    xo,
    qb,
    fb,
    cs,
    st,
    H1,
    H2,
    DY,
    W,
    TA,
    G,
    sbuf,
    fbuf,
    rsb,
    sib_send,
    sib_land,
    psend,
    own,
    a2a_s,
    a2a_r,
    loc_s,
    ag_s,
    ag_r,
    x_s,
    x_r,
    sx_s,
    sx_r,
    rs_s,
    rs_r,
    gr_s,
    gr_r,
    sib_s,
    sib_r,
    p_s,
    p_r,
    tmp_s,
    free_s,
):
    outer = count // INNER
    S = outer - 1
    T, half = xin.shape
    R = wst.shape[2]
    block = INNER * R
    QT = T // 2
    b = lax.axis_index("batch")
    c = lax.axis_index("branch")
    q = lax.rem(b, INNER)
    o = b // INNER
    bx, by = flip(b, 1), flip(b, 2)
    bxy = flip(bx, 2)
    near = (bx, by, bxy)
    da = 1 + c
    db = 2 - c
    b_first = bx * (1 - c) + by * c
    b_second = by * (1 - c) + bx * c

    def remote(src, dst, ssem, rsem, to_b, to_c):
        return pltpu.make_async_remote_copy(
            src_ref=src,
            dst_ref=dst,
            send_sem=ssem,
            recv_sem=rsem,
            device_id=(to_b, to_c),
            device_id_type=MESH,
        )

    barrier = pltpu.get_barrier_semaphore()
    for who in near:
        pl.semaphore_signal(barrier, inc=1, device_id=(who, c), device_id_type=MESH)
    pl.semaphore_signal(barrier, inc=1, device_id=(b, 1 - c), device_id_type=MESH)

    @pl.when(o > 0)
    def _():
        pl.semaphore_signal(barrier, inc=1, device_id=(b - INNER, c), device_id_type=MESH)

    @pl.when(o < outer - 1)
    def _():
        pl.semaphore_signal(barrier, inc=1, device_id=(b + INNER, c), device_id_type=MESH)

    pl.semaphore_wait(barrier, 4 + jnp.minimum(o, 1) + jnp.minimum(outer - 1 - o, 1))

    def a2a_copy(k, d, received=False):
        to = near[d - 1]
        row = (to if received else b) * R
        return remote(
            wst.at[k, lax.rem(to, INNER)],
            W.at[k, pl.ds(pl.multiple_of(row, 16), R)],
            a2a_s.at[k, d - 1],
            a2a_r.at[k, d - 1],
            to,
            c,
        )

    def a2a_local(k):
        return pltpu.make_async_copy(
            wst.at[k, q], W.at[k, pl.ds(pl.multiple_of(b * R, 16), R)], loc_s.at[k]
        )

    def a2a_start(k):
        for d in range(1, INNER):
            a2a_copy(k, d).start()
        a2a_local(k).start()

    def a2a_wait(k):
        for d in range(1, INNER):
            a2a_copy(k, d, True).wait_recv()
        a2a_local(k).wait()

    def ag_copy(k, way, s, part):
        rows = pl.ds(pl.multiple_of(part * block, 16), block)
        to = b + INNER if way == 0 else b - INNER
        return remote(
            W.at[k, rows], W.at[k, rows], ag_s.at[k, way, s - 1], ag_r.at[k, way, s - 1], to, c
        )

    def ag_sends(k, s, what):
        @pl.when((o >= s - 1) & (o <= outer - 2))
        def _():
            what(ag_copy(k, 0, s, o - s + 1))

        @pl.when((o >= 1) & (o <= outer - s))
        def _():
            what(ag_copy(k, 1, s, o + s - 1))

    def ag_wait(k, s):
        @pl.when(o >= s)
        def _():
            ag_copy(k, 0, s, o - s).wait_recv()

        @pl.when(o <= outer - 1 - s)
        def _():
            ag_copy(k, 1, s, o + s).wait_recv()

    def ag_range(low, high):
        def step(n, carry):
            k = n // S
            s = lax.rem(n, S) + 1

            @pl.when(s == 1)
            def _():
                a2a_wait(k)

            @pl.when(s > 1)
            def _():
                ag_wait(k, s - 1)

            ag_sends(k, s, lambda copy: copy.start())
            return carry

        lax.fori_loop(low, high, step, 0)

    def ag(low, high):
        ag_range(low * S // 3, high * S // 3)

    def spot(buf, slot):
        return buf.at[
            pl.ds(pl.multiple_of(slot * T, 16), T), pl.ds(pl.multiple_of(c * half, 128), half)
        ]

    def other_spot(buf, slot):
        return buf.at[
            pl.ds(pl.multiple_of(slot * T, 16), T), pl.ds(pl.multiple_of((1 - c) * half, 128), half)
        ]

    def sx_copy(i, buf, slot, src=None):
        place = spot(buf, slot)
        return remote(place if src is None else src, place, sx_s.at[i, slot], sx_r.at[i, slot], b, 1 - c)

    def sx_wait(i, buf, slot):
        remote(
            other_spot(buf, slot), other_spot(buf, slot), sx_s.at[i, slot], sx_r.at[i, slot], b, 1 - c
        ).wait_recv()

    def x_first(i, src, buf):
        return remote(src, spot(buf, da), x_s.at[i, da - 1], x_r.at[i, da - 1], b_first, c)

    def x_second(i, src, buf):
        return remote(src, spot(buf, db), x_s.at[i, db - 1], x_r.at[i, db - 1], b_second, c)

    def x_forward(i, buf):
        return remote(spot(buf, da), spot(buf, 3), x_s.at[i, 2], x_r.at[i, 2], b_second, c)

    def x_diag(i, buf):
        return remote(spot(buf, 3), spot(buf, 3), x_s.at[i, 2], x_r.at[i, 2], b_second, c)

    def x_local(i, src, buf):
        return pltpu.make_async_copy(src, spot(buf, 0), tmp_s.at[i])

    def gather_one(i, src, buf):
        x_first(i, src, buf).start()
        x_local(i, src, buf).start()
        sx_copy(i, buf, 0, src).start()

    def gather_two(i, src, buf):
        x_first(i, src, buf).wait_recv()
        x_second(i, src, buf).start()
        x_forward(i, buf).start()
        sx_copy(i, buf, da).start()

    def gather_three(i, src, buf):
        x_second(i, src, buf).wait_recv()
        sx_copy(i, buf, db).start()
        x_diag(i, buf).wait_recv()
        sx_copy(i, buf, 3).start()

    def gather_sent(i, src, buf):
        x_first(i, src, buf).wait_send()
        x_second(i, src, buf).wait_send()
        x_forward(i, buf).wait_send()
        sx_copy(i, buf, 0, src).wait_send()
        for slot in range(1, INNER):
            sx_copy(i, buf, slot).wait_send()

    lane_n = lax.broadcasted_iota(jnp.int32, (64, 128), 1)

    def norm_rows(slot):
        def step(i, carry):
            rows = pl.ds(pl.multiple_of(slot * T + i * 64, 64), 64)
            values = H1[rows, :].astype(jnp.float32)
            mean = jnp.mean(values, axis=-1, keepdims=True)
            centered = values - mean
            inverse = lax.rsqrt(jnp.mean(centered * centered, axis=-1, keepdims=True) + EPS_NORM)
            normed = centered * inverse
            if slot == 0:
                st[pl.ds(pl.multiple_of(i * 64, 64), 64), :] = jnp.where(lane_n == 0, mean, inverse)
            H1[rows, :] = (normed * norm_ref[0:1, :] + norm_ref[1:2, :]).astype(jnp.bfloat16)
            H2[rows, :] = (normed * norm_ref[2:3, :] + norm_ref[3:4, :]).astype(jnp.bfloat16)
            return carry

        lax.fori_loop(0, T // 64, step, 0)

    lane = lax.broadcasted_iota(jnp.int32, (T, HD), 1)
    scale = HD ** (-0.5)

    def partner(tensor):
        return jnp.where(
            lane < ROT // 2,
            pltpu.roll(tensor, HD - ROT // 2, 1),
            jnp.where(lane < ROT, pltpu.roll(tensor, ROT // 2, 1), 0.0),
        )

    def turns_of(rows):
        table = turn_ref[rows, :]
        cos_rows = jnp.where(lane < ROT, table, 1.0)
        sin_rows = pltpu.roll(table, HD - ROT, 1)
        return cos_rows, sin_rows, table[:, 2 * ROT : 2 * ROT + 1]

    def project_piece(h, slot):
        rows = pl.ds(pl.multiple_of(slot * T, 128), T)
        cos_rows, sin_rows, _ = turns_of(rows)
        projected = nn(H1[rows, :], W[h, :, : 3 * HD]) + bias_h[h]
        first = projected[:, :HD]
        queries = (first * cos_rows + partner(first) * sin_rows).astype(jnp.bfloat16)
        second = projected[:, HD : 2 * HD]
        keys = (second * cos_rows + partner(second) * sin_rows).astype(jnp.bfloat16)
        values = projected[:, 2 * HD :].astype(jnp.bfloat16)
        start = pl.multiple_of(slot * T, 128)
        TA[h, :, pl.ds(start, HD)] = queries
        TA[h, :, pl.ds(start + HD, HD)] = keys
        TA[h, :, pl.ds(start + 2 * HD, HD)] = values

    def head_piece(h, slot):
        start = pl.multiple_of(slot * T, 128)
        rows = pl.ds(start, T)
        cos_rows, sin_rows, starts = turns_of(rows)
        queries = TA[h, :, pl.ds(start, HD)]
        keys = TA[h, :, pl.ds(start + HD, HD)]
        values = TA[h, :, pl.ds(start + 2 * HD, HD)]
        back = nn(DY[rows, :], W[h, :, 3 * HD :]).astype(jnp.bfloat16)
        contexts, grad_q = [], []
        grad_k, grad_v = [None, None], [None, None]
        for i in range(2):
            seen = QT * (i + 1)
            part = slice(QT * i, QT * (i + 1))
            raw = nt(queries[part], keys[:seen]) * scale
            query_at = lax.broadcasted_iota(jnp.int32, (QT, seen), 0) + QT * i
            key_at = lax.broadcasted_iota(jnp.int32, (QT, seen), 1)
            allowed = (key_at <= query_at) & (key_at.astype(jnp.float32) >= starts[part])
            scores = jnp.where(allowed, raw, -1e30)
            exponent = jnp.exp(scores - jnp.max(scores, axis=-1, keepdims=True))
            probs = exponent * (1.0 / jnp.sum(exponent, axis=-1, keepdims=True))
            soft = probs.astype(jnp.bfloat16)
            contexts.append(nn(soft, values[:seen]).astype(jnp.bfloat16))
            grad_probs = nt(back[part], values[:seen])
            inner = jnp.sum(probs * grad_probs, axis=-1, keepdims=True)
            grad_scores = (probs * (grad_probs - inner)).astype(jnp.bfloat16)
            grad_q.append((nn(grad_scores, keys[:seen]) * scale).astype(jnp.bfloat16))
            for j in range(i + 1):
                cut = slice(QT * j, QT * (j + 1))
                term_v = tn(soft[:, cut], back[part])
                term_k = tn(grad_scores[:, cut], queries[part])
                grad_v[j] = term_v if grad_v[j] is None else grad_v[j] + term_v
                grad_k[j] = term_k if grad_k[j] is None else grad_k[j] + term_k
        context = jnp.concatenate(contexts, axis=0)
        dq = jnp.concatenate(grad_q, axis=0).astype(jnp.float32)
        dk = (jnp.concatenate(grad_k, axis=0) * scale).astype(jnp.bfloat16).astype(jnp.float32)
        dv = jnp.concatenate(grad_v, axis=0)
        turned = jnp.concatenate(
            [
                dq * cos_rows - partner(dq) * sin_rows,
                dk * cos_rows - partner(dk) * sin_rows,
                dv,
            ],
            axis=1,
        ).astype(jnp.bfloat16)
        TA[h, : 3 * HD, rows] = turned.T
        TA[h, 3 * HD :, rows] = context.T
        total = jnp.sum(turned.astype(jnp.float32), axis=0, keepdims=True)
        qb[h] = jnp.where(slot == 0, total, qb[h] + total)

    def cut_piece(f, slot):
        rows = pl.ds(pl.multiple_of(slot * T, 128), T)
        k = HEADS_DEV + f
        pre = nn(H2[rows, :], W[k, :, :CUT]) + bias_f[f]
        grad = nn(DY[rows, :], W[k, :, CUT:])
        normal = 0.5 * (1.0 + lax.erf(pre * (0.5**0.5)))
        slope = normal + pre * (jnp.exp(-0.5 * pre * pre) * (0.5 * 0.7978845608028654))
        active = (pre * normal).astype(jnp.bfloat16)
        pulled = (grad * slope).astype(jnp.bfloat16)
        low = pl.multiple_of(f * WIDE, WIDE)
        H1[pl.ds(low, CUT), rows] = pulled.T
        H1[pl.ds(low + CUT, CUT), rows] = active.T
        total = jnp.sum(pulled.astype(jnp.float32), axis=0, keepdims=True)
        fb[f] = jnp.where(slot == 0, total, fb[f] + total)

    def grads(k, turned, left, edge):
        def step(j, carry):
            cols = pl.ds(pl.multiple_of(j * block, 128), block)
            G[lax.rem(k, 2), j, :edge, :] = nn(turned(0, edge), left[:, cols])
            G[lax.rem(k, 2), j, edge:, :] = nn(turned(edge, WIDE - edge), DY[:, cols])
            return carry

        lax.fori_loop(0, outer, step, 0)

    def head_turned(h):
        return lambda low, size: TA[h, pl.ds(low, size), :]

    def cut_turned(f):
        return lambda low, size: H1[pl.ds(pl.multiple_of(f * WIDE + low, 128), size), :]

    def rs_copy(k, way, t):
        to = b + INNER if way == 0 else b - INNER
        return remote(
            sbuf.at[way],
            rsb.at[way, t - 1],
            rs_s.at[k, way, t - 1],
            rs_r.at[k, way, t - 1],
            to,
            c,
        )

    def rs_sends(way, t):
        if way == 0:
            return (o <= t - 1) & (o <= outer - 2)
        return (o >= outer - t) & (o >= 1)

    def rs_receives(way, t):
        if way == 0:
            return (o >= 1) & (o <= t)
        return (o <= outer - 2) & (o >= outer - 1 - t)

    def rs_fetch(k, way, t):
        rs_copy(k, way, t).wait_recv()
        return rsb[way, t - 1].astype(jnp.float32)

    def rs_range(low, high):
        def step(n, carry):
            k = n // S
            t = lax.rem(n, S) + 1

            @pl.when((t == 1) & (k >= 1) & (o < outer - 1))
            def _():
                pl.semaphore_wait(free_s.at[0], 1)

            @pl.when((t == 1) & (k >= 1) & (o > 0))
            def _():
                pl.semaphore_wait(free_s.at[1], 1)

            for way in range(2):
                owner = o + outer - t if way == 0 else o - outer + t

                before = jnp.maximum(n - 1, 0)
                k_before = before // S
                t_before = lax.rem(before, S) + 1

                @pl.when((n >= 1) & rs_sends(way, t_before))
                def _():
                    rs_copy(k_before, way, t_before).wait_send()

                @pl.when(rs_sends(way, t))
                def _():
                    @pl.when(rs_receives(way, t - 1) & (t > 1))
                    def _():
                        sbuf[way] = (
                            G[lax.rem(k, 2), owner] + rs_fetch(k, way, t - 1)
                        ).astype(jnp.bfloat16)

                    @pl.when(jnp.logical_not(rs_receives(way, t - 1) & (t > 1)))
                    def _():
                        sbuf[way] = G[lax.rem(k, 2), owner].astype(jnp.bfloat16)

                    rs_copy(k, way, t).start()

            return carry

        lax.fori_loop(low, high, step, 0)

    def rs(low, high):
        rs_range(low * S // 3, high * S // 3)

    def gr_copy(k, d, received=False):
        to = near[d - 1]
        slot = lax.rem(to, INNER)
        return remote(
            fbuf.at[pl.ds(pl.multiple_of(slot * R, 16), R)],
            gr.at[k, slot if received else q],
            gr_s.at[k, d - 1],
            gr_r.at[k, d - 1],
            to,
            c,
        )

    def gr_local(k):
        return pltpu.make_async_copy(
            fbuf.at[pl.ds(pl.multiple_of(q * R, 16), R)],
            gr.at[k, q],
            gr_s.at[k, 3],
        )

    def gr_sent(k):
        for d in range(1, INNER):
            gr_copy(k, d).wait_send()
        gr_local(k).wait()

    def rs_final(k):
        for way in range(2):

            @pl.when(rs_receives(way, S))
            def _():
                G[lax.rem(k, 2), o] = G[lax.rem(k, 2), o] + rs_fetch(k, way, S)

        @pl.when((k < CHUNKS - 1) & (o > 0))
        def _():
            pl.semaphore_signal(
                free_s.at[0], inc=1, device_id=(b - INNER, c), device_id_type=MESH
            )

        @pl.when((k < CHUNKS - 1) & (o < outer - 1))
        def _():
            pl.semaphore_signal(
                free_s.at[1], inc=1, device_id=(b + INNER, c), device_id_type=MESH
            )

        @pl.when(k >= 1)
        def _():
            gr_sent(k - 1)

        final = G[lax.rem(k, 2), o].T
        cs[k] = jnp.sum(squares(final), axis=0, keepdims=True)
        fbuf[...] = final.astype(jnp.bfloat16)
        for d in range(1, INNER):
            gr_copy(k, d).start()
        gr_local(k).start()

    TILE = T // 2
    TILES = 2 * INNER
    PER_ROW = D // TILE

    def tile_slot(i):
        return INNER - 1 - i // 2

    def product(which, i, side):
        at = pl.multiple_of(tile_slot(i) * T + lax.rem(i, 2) * TILE, 128)
        toks = pl.ds(at, TILE)
        features = pl.ds(pl.multiple_of(side * half, 128), half)
        terms = []
        if which == 0:
            for h in range(HEADS_DEV):
                terms.append((h, slice(0, 3 * HD), lambda h=h: TA[h, : 3 * HD, toks]))
        elif which == 1:
            for f in range(CUTS):
                low = f * WIDE
                terms.append(
                    (HEADS_DEV + f, slice(0, CUT), lambda low=low: H1[low : low + CUT, toks])
                )
        else:
            for h in range(HEADS_DEV):
                terms.append((h, slice(3 * HD, WIDE), lambda h=h: TA[h, 3 * HD :, toks]))
            for f in range(CUTS):
                low = f * WIDE + CUT
                terms.append(
                    (HEADS_DEV + f, slice(CUT, WIDE), lambda low=low: H1[low : low + CUT, toks])
                )
        for place, (k, cols, right) in enumerate(terms):
            term = nn(W[k, features, cols], right())
            own[...] = term if place == 0 else own[...] + term

    def sib_copy(which, i):
        return remote(
            sib_send.at[lax.rem(i, 2)],
            sib_land.at[lax.rem(i, 4)],
            sib_s.at[which, i],
            sib_r.at[which, i],
            b,
            1 - c,
        )

    def plane_copy(which, i):
        slot = tile_slot(i)
        low, high = lax.rem(slot, 2), slot // 2
        to = b + low * (1 - 2 * lax.rem(b, 2)) + high * 2 * (1 - 2 * lax.rem(b // 2, 2))
        if which == 0:
            src = psend.at[lax.rem(i, 2)]
        else:
            t = (which - 1) * (TILES - 2) + i
            src = H2.at[
                pl.ds(pl.multiple_of(t // PER_ROW * half, 128), half),
                pl.ds(pl.multiple_of(lax.rem(t, PER_ROW) * TILE, 128), TILE),
            ]
        return remote(
            src,
            xr.at[which, slot - 1, lax.rem(i, 2)],
            p_s.at[which, i],
            p_r.at[which, i],
            to,
            c,
        )

    def tile_a(which, i):
        @pl.when(i >= 2)
        def _():
            sib_copy(which, i - 2).wait_send()

        product(which, i, 1 - c)
        sib_send[lax.rem(i, 2)] = own[...].astype(jnp.bfloat16)
        sib_copy(which, i).start()

    def tile_b(which, i):
        product(which, i, c)
        sib_copy(which, i).wait_recv()

        @pl.when(i < TILES - 2)
        def _():
            total = (own[...] + sib_land[lax.rem(i, 4)].astype(jnp.float32)).astype(jnp.bfloat16)
            if which == 0:

                @pl.when(i >= 2)
                def _():
                    plane_copy(which, i - 2).wait_send()

                psend[lax.rem(i, 2)] = total
            else:
                t = (which - 1) * (TILES - 2) + i
                H2[
                    pl.ds(pl.multiple_of(t // PER_ROW * half, 128), half),
                    pl.ds(pl.multiple_of(lax.rem(t, PER_ROW) * TILE, 128), TILE),
                ] = total
            plane_copy(which, i).start()

        @pl.when(i >= TILES - 2)
        def _():
            own[...] = own[...] + sib_land[lax.rem(i, 4)].astype(jnp.float32)
            keep = pltpu.make_async_copy(own, xo.at[which, lax.rem(i, 2)], tmp_s.at[2])
            keep.start()
            keep.wait()

    def sum_tiles(which, beside):
        tile_a(which, 0)

        def step(i, carry):
            @pl.when(i < TILES - 1)
            def _():
                tile_a(which, i + 1)

            tile_b(which, i)
            beside(i)
            return carry

        lax.fori_loop(0, TILES, step, 0)

    def sum_sent(which):
        for i in range(TILES - 2, TILES):
            sib_copy(which, i).wait_send()
        for i in range(TILES - 4, TILES - 2):
            plane_copy(which, i).wait_send()

    def share(low, high, i, pieces, run):
        first, last = low * S // 3, high * S // 3
        steps = last - first
        run(
            first + (steps * i + pieces - 1) // pieces,
            first + (steps * (i + 1) + pieces - 1) // pieces,
        )

    a2a_start(0)
    gather_one(0, xin, H1)
    a2a_start(1)
    ag(0, 1)
    gather_two(0, xin, H1)
    gather_one(1, yin, DY)
    a2a_start(2)
    ag(1, 2)
    x_local(0, xin, H1).wait()
    sx_wait(0, H1, 0)
    norm_rows(0)
    ag(2, 3)
    gather_three(0, xin, H1)
    gather_two(1, yin, DY)
    for k in range(3, CHUNKS):
        a2a_start(k)
    gather_sent(0, xin, H1)
    for slot in range(1, INNER):
        sx_wait(0, H1, slot)
        norm_rows(slot)
        ag(2 + slot, 3 + slot)

    def project_step(h, carry):
        ag_wait(h, S)

        def slot_step(slot, inner_carry):
            project_piece(h, slot)
            return inner_carry

        lax.fori_loop(0, INNER, slot_step, 0)
        ag(6 + h, 7 + h)
        return carry

    project_step(0, 0)
    gather_three(1, yin, DY)
    project_step(1, 0)
    x_local(1, yin, DY).wait()
    for slot in range(INNER):
        sx_wait(1, DY, slot)
    gather_sent(1, yin, DY)

    def head_step(h, carry):
        def slot_step(slot, inner_carry):
            head_piece(h, slot)
            share(8 + 2 * h, 10 + 2 * h, slot, INNER, ag_range)
            share(0, 3 * h, slot, INNER, rs_range)
            return inner_carry

        lax.fori_loop(0, INNER, slot_step, 0)
        grads(h, head_turned(h), H1, 3 * HD)

        @pl.when(h == 1)
        def _():
            rs_final(0)

        return carry

    lax.fori_loop(0, HEADS_DEV, head_step, 0)

    def beside_one(i):
        share(12, 13, i, TILES, ag_range)
        share(3, 6, i, TILES, rs_range)

    sum_tiles(0, beside_one)

    def cut_step(f, carry):
        ag_wait(HEADS_DEV + f, S)

        def slot_step(slot, inner_carry):
            cut_piece(f, slot)
            share(
                jnp.minimum(13 + 2 * f, 18), jnp.minimum(15 + 2 * f, 18), slot, INNER, ag_range
            )
            share(jnp.maximum(6, 3 + 3 * f), 6 + 3 * f, slot, INNER, rs_range)
            return inner_carry

        lax.fori_loop(0, INNER, slot_step, 0)
        grads(HEADS_DEV + f, cut_turned(f), H2, CUT)
        rs_final(1 + f)
        return carry

    lax.fori_loop(0, CUTS, cut_step, 0)
    sum_sent(0)
    sum_tiles(1, lambda i: share(15, 18, i, TILES, rs_range))
    for i in range(TILES - 2, TILES):
        sib_copy(1, i).wait_send()

    def beside_last(i):
        @pl.when(i == 1)
        def _():
            rs_final(CHUNKS - 1)

    sum_tiles(2, beside_last)
    for i in range(TILES - 2, TILES):
        sib_copy(2, i).wait_send()

    gr_sent(CHUNKS - 1)

    def drain_chunk(k, carry):
        for d in range(1, INNER):
            a2a_copy(k, d).wait_send()
            gr_copy(k, d, True).wait_recv()

        def drain_step(s, inner_carry):
            ag_sends(k, s, lambda copy: copy.wait_send())
            return inner_carry

        lax.fori_loop(1, S + 1, drain_step, 0)
        return carry

    lax.fori_loop(0, CHUNKS, drain_chunk, 0)
    for way in range(2):

        @pl.when(rs_sends(way, S))
        def _():
            rs_copy(CHUNKS - 1, way, S).wait_send()

    for which in range(3):

        def drain_tile(i, carry):
            if which:
                plane_copy(which, i).wait_send()
            plane_copy(which, i).wait_recv()
            return carry

        lax.fori_loop(0, TILES - 2, drain_tile, 0)


def block_call(count, wst, xin, yin, turns, norm_params, bias_h, bias_f):
    outer = count // INNER
    S = outer - 1
    tokens, half = xin.shape
    group = INNER * tokens
    rows = wst.shape[2]
    tile = tokens // 2
    low, high = jnp.bfloat16, jnp.float32
    any_spec = pl.BlockSpec(memory_space=pl.ANY)
    vmem_spec = pl.BlockSpec(memory_space=pltpu.VMEM)
    dma = pltpu.SemaphoreType.DMA
    return pl.pallas_call(
        functools.partial(block_kernel, count),
        out_shape=[
            jax.ShapeDtypeStruct((CHUNKS, INNER, rows, WIDE), low),
            jax.ShapeDtypeStruct((3, INNER - 1, 2, half, tile), low),
            jax.ShapeDtypeStruct((3, 2, half, tile), high),
            jax.ShapeDtypeStruct((HEADS_DEV, 1, 3 * HD), high),
            jax.ShapeDtypeStruct((CUTS, 1, CUT), high),
            jax.ShapeDtypeStruct((CHUNKS, 1, WIDE), high),
            jax.ShapeDtypeStruct((tokens, 128), high),
        ],
        in_specs=[any_spec] * 3 + [vmem_spec] * 4,
        out_specs=[any_spec] * 3 + [vmem_spec] * 4,
        scratch_shapes=[
            pltpu.VMEM((group, D), low),
            pltpu.VMEM((group, D), low),
            pltpu.VMEM((group, D), low),
            pltpu.VMEM((CHUNKS, D, WIDE), low),
            pltpu.VMEM((HEADS_DEV, WIDE, group), low),
            pltpu.VMEM((2, outer, WIDE, INNER * rows), high),
            pltpu.VMEM((2, WIDE, INNER * rows), low),
            pltpu.VMEM((INNER * rows, WIDE), low),
            pltpu.VMEM((2, S, WIDE, INNER * rows), low),
            pltpu.VMEM((2, half, tile), low),
            pltpu.VMEM((4, half, tile), low),
            pltpu.VMEM((2, half, tile), low),
            pltpu.VMEM((half, tile), high),
            dma((CHUNKS, INNER - 1)),
            dma((CHUNKS, INNER - 1)),
            dma((CHUNKS,)),
            dma((CHUNKS, 2, S)),
            dma((CHUNKS, 2, S)),
            dma((2, INNER - 1)),
            dma((2, INNER - 1)),
            dma((2, INNER)),
            dma((2, INNER)),
            dma((CHUNKS, 2, S)),
            dma((CHUNKS, 2, S)),
            dma((CHUNKS, INNER)),
            dma((CHUNKS, INNER - 1)),
            dma((3, 2 * INNER)),
            dma((3, 2 * INNER)),
            dma((3, 2 * INNER)),
            dma((3, 2 * INNER)),
            dma((3,)),
            pltpu.SemaphoreType.REGULAR((2,)),
        ],
        compiler_params=pltpu.CompilerParams(
            collective_id=0, has_side_effects=True, vmem_limit_bytes=64 * 1024 * 1024
        ),
        cost_estimate=pl.CostEstimate(
            flops=80_000_000_000, bytes_accessed=60_000_000, transcendentals=10_000_000
        ),
    )(wst, xin, yin, turns, norm_params, bias_h, bias_f)


SLOT_ROWS = 16


def total_of(values):
    return jnp.sum(jnp.sum(values, axis=0, keepdims=True), axis=1, keepdims=True)


def tail_kernel(
    count,
    gr,
    wq,
    wo,
    w1,
    w2,
    xr,
    xo,
    xin,
    yin,
    st,
    norm_ref,
    pb,
    fcb,
    row_old,
    qc_old,
    or_old,
    f1_old,
    f2_old,
    norm_second,
    bias_second,
    fcb_second,
    cs,
    qb,
    fb,
    out_ref,
    ing_ref,
    row_new,
    qc_new,
    or_new,
    f1_new,
    f2_new,
    norm_grad,
    norm_moment,
    norm_new,
    bias_grad,
    bias_moment,
    bias_new,
    fcb_grad,
    fcb_moment,
    fcb_new,
    coef,
    scaled_buf,
    normed_buf,
    terms,
    terms_in,
    rsum,
    rsum_in,
    pay,
    z_in,
    z_sum,
    p_in,
    p_sum,
    s_in,
    pay2,
    z2_in,
    z2_sum,
    p2_in,
    p2_sum,
    s2_in,
    z_s,
    z_r,
    p_s,
    p_r,
    s_s,
    s_r,
):
    outer = count // INNER
    T, half = xin.shape
    R = gr.shape[2]
    b = lax.axis_index("batch")
    c = lax.axis_index("branch")
    q = lax.rem(b, INNER)
    o = b // INNER
    bx, by = flip(b, 1), flip(b, 2)
    near = (bx, by, flip(bx, 2))
    on_b = (b == 0).astype(jnp.float32)
    on_c = (c == 0).astype(jnp.float32)

    def remote(src, dst, ssem, rsem, to_b, to_c):
        return pltpu.make_async_remote_copy(
            src_ref=src,
            dst_ref=dst,
            send_sem=ssem,
            recv_sem=rsem,
            device_id=(to_b, to_c),
            device_id_type=MESH,
        )

    def chain(d):
        return lax.rem(o + d, outer)

    barrier = pltpu.get_barrier_semaphore()
    for who in near:
        pl.semaphore_signal(barrier, inc=1, device_id=(who, c), device_id_type=MESH)
    pl.semaphore_signal(barrier, inc=1, device_id=(b, 1 - c), device_id_type=MESH)
    for d in range(1, outer):
        pl.semaphore_signal(
            barrier, inc=1, device_id=(chain(d) * INNER + q, c), device_id_type=MESH
        )

    HALF_T = T // 2
    lane_t = lax.broadcasted_iota(jnp.int32, (HALF_T, 128), 1)
    own_half = pl.ds(pl.multiple_of(c * half, 128), half)
    other_half = pl.ds(pl.multiple_of((1 - c) * half, 128), half)
    gain_a = norm_ref[0:1, own_half]
    gain_b = norm_ref[2:3, own_half]
    pay[...] = jnp.zeros_like(pay)
    for i in range(2):
        rows = slice(i * HALF_T, (i + 1) * HALF_T)

        def whole(which):
            return (
                xo[which, i]
                + xr[which, 0, i].astype(jnp.float32)
                + xr[which, 1, i].astype(jnp.float32)
                + xr[which, 2, i].astype(jnp.float32)
            ).T

        values = xin[rows, :].astype(jnp.float32)
        out_ref[rows, :] = (values + whole(2) + pb[3:4, :] + pb[4:5, :]).astype(jnp.bfloat16)
        normed = (values - st[rows, 0:1]) * st[rows, 1:2]
        one = whole(0)
        two = whole(1)
        scaled = one * gain_a + two * gain_b
        scaled_buf[rows, :] = scaled
        normed_buf[rows, :] = normed
        terms[rows, :] = jnp.where(
            lane_t == 0,
            jnp.sum(scaled, axis=1, keepdims=True),
            jnp.where(lane_t == 1, jnp.sum(scaled * normed, axis=1, keepdims=True), 0.0),
        )
        pay[5:6, :] += jnp.sum(one * normed, axis=0, keepdims=True)
        pay[6:7, :] += jnp.sum(one, axis=0, keepdims=True)
        pay[7:8, :] += jnp.sum(two * normed, axis=0, keepdims=True)
        pay[8:9, :] += jnp.sum(two, axis=0, keepdims=True)
        pay[9:10, :] += jnp.sum(yin[rows, :].astype(jnp.float32), axis=0, keepdims=True)
    for k in range(CHUNKS):
        pay[k // 2 : k // 2 + 1, k % 2 * WIDE : (k % 2 + 1) * WIDE] = cs[k]
    for h in range(HEADS_DEV):
        pay[3:4, h * 3 * HD : (h + 1) * 3 * HD] = qb[h]
    for f in range(CUTS):
        pay[4:5, f * CUT : (f + 1) * CUT] = fb[f]
    lane_p = lax.broadcasted_iota(jnp.int32, (1, half), 1)
    biases = jnp.sum(pb[...] * pb[...], axis=1, keepdims=True) * on_b
    scalars = (
        [total_of(w[...] * w[...]) for w in (wq, wo, w1, w2)]
        + [biases[i : i + 1] for i in range(5)]
        + [total_of(fcb[...] * fcb[...]) * on_b]
    )
    line = jnp.zeros((1, half), jnp.float32)
    for place, value in enumerate(scalars):
        line = jnp.where(lane_p == place, value, line)
    pay[10:11, :] = line

    pl.semaphore_wait(barrier, INNER + outer - 1)

    def chain_sends(src, buf, base, what):
        for d in range(1, outer):
            what(
                remote(
                    src,
                    buf.at[o],
                    z_s.at[base, d - 1],
                    z_r.at[base, d - 1],
                    chain(d) * INNER + q,
                    c,
                )
            )

    def chain_waits(src, buf, base):
        for d in range(1, outer):
            source = chain(outer - d)
            remote(
                src,
                buf.at[source],
                z_s.at[base, d - 1],
                z_r.at[base, d - 1],
                source * INNER + q,
                c,
            ).wait_recv()

    def plane_sends(src, buf, base, what):
        for d in range(1, INNER):
            what(remote(src, buf.at[q], p_s.at[base, d - 1], p_r.at[base, d - 1], near[d - 1], c))

    def plane_waits(src, buf, base):
        for d in range(1, INNER):
            remote(
                src,
                buf.at[lax.rem(near[d - 1], INNER)],
                p_s.at[base, d - 1],
                p_r.at[base, d - 1],
                near[d - 1],
                c,
            ).wait_recv()

    def pair_copy(src, dst, place):
        return remote(src, dst, s_s.at[place], s_r.at[place], b, 1 - c)

    start = lambda copy: copy.start()
    chain_sends(pay, z_in, 0, start)
    z_in[o] = pay[...]
    pair_copy(terms, terms_in, 0).start()

    lane_r = lax.broadcasted_iota(jnp.int32, (R, 128), 1)
    head_square = jnp.zeros((R, WIDE), jnp.float32)
    cut_square = jnp.zeros((R, WIDE), jnp.float32)
    for part in range(INNER):
        for k in range(CHUNKS):
            gradient = gr[k, part].astype(jnp.float32)
            if k < HEADS_DEV:
                head_square = head_square + squares(gradient)
            else:
                cut_square = cut_square + squares(gradient)
    pieces = (
        jnp.sum(head_square[:, : 3 * HD], axis=1, keepdims=True),
        jnp.sum(cut_square[:, :CUT], axis=1, keepdims=True),
        jnp.sum(head_square[:, 3 * HD :], axis=1, keepdims=True),
        jnp.sum(cut_square[:, CUT:], axis=1, keepdims=True),
    )
    line = jnp.zeros((R, 128), jnp.float32)
    for place, value in enumerate(pieces):
        line = jnp.where(lane_r == place, value, line)
    rsum[...] = line
    pair_copy(rsum, rsum_in, 1).start()

    pair_copy(terms, terms_in, 0).wait_recv()
    for i in range(2):
        rows = slice(i * HALF_T, (i + 1) * HALF_T)
        both = terms[rows, :] + terms_in[rows, :]
        ing_ref[rows, :] = (
            st[rows, 1:2]
            * (
                scaled_buf[rows, :]
                - both[:, 0:1] / D
                - normed_buf[rows, :] * (both[:, 1:2] / D)
            )
            + yin[rows, :].astype(jnp.float32)
        ).astype(jnp.bfloat16)
    pair_copy(rsum, rsum_in, 1).wait_recv()
    rows_after = renew_stat(row_old[...], (rsum[...] + rsum_in[...])[:, :4])
    row_new[...] = rows_after

    chain_waits(pay, z_in, 0)
    acc = z_in[0]
    for j in range(1, outer):
        acc = acc + z_in[j]
    z_sum[...] = acc
    plane_sends(z_sum, p_in, 0, start)
    p_in[q] = acc
    plane_waits(z_sum, p_in, 0)
    p_sum[...] = p_in[0] + p_in[1] + p_in[2] + p_in[3]
    pair_copy(p_sum, s_in, 2).start()

    inverse_rows = 1.0 / rows_after
    head_acc = [jnp.zeros((R, 3 * HD), jnp.float32), jnp.zeros((R, HD), jnp.float32)]
    cut_acc = [jnp.zeros((R, CUT), jnp.float32), jnp.zeros((R, CUT), jnp.float32)]
    for part in range(INNER):
        sums = p_in[part]
        for h in range(HEADS_DEV):
            gradient = gr[h, part].astype(jnp.float32)
            square = gradient * gradient
            found = sums[h // 2 : h // 2 + 1, h % 2 * WIDE : (h % 2 + 1) * WIDE]
            cols = pl.ds(part * HEADS_DEV * HD + h * HD, HD)
            parts = []
            for p in range(3):
                fresh = renew_stat(qc_old[p : p + 1, cols], found[:, p * HD : (p + 1) * HD])
                qc_new[p : p + 1, cols] = fresh
                parts.append(1.0 / fresh)
            head_acc[0] = head_acc[0] + square[:, : 3 * HD] * jnp.concatenate(parts, axis=1)
            fresh = renew_stat(or_old[:, cols], found[:, 3 * HD :])
            or_new[:, cols] = fresh
            head_acc[1] = head_acc[1] + square[:, 3 * HD :] * (1.0 / fresh)
        for f in range(CUTS):
            k = HEADS_DEV + f
            gradient = gr[k, part].astype(jnp.float32)
            square = gradient * gradient
            found = sums[k // 2 : k // 2 + 1, k % 2 * WIDE : (k % 2 + 1) * WIDE]
            cols = slice(f * CUT, (f + 1) * CUT)
            fresh = renew_stat(f1_old[part : part + 1, cols], found[:, :CUT])
            f1_new[part, :, cols] = fresh
            cut_acc[0] = cut_acc[0] + square[:, :CUT] * (1.0 / fresh)
            fresh = renew_stat(f2_old[part : part + 1, cols], found[:, CUT:])
            f2_new[part, :, cols] = fresh
            cut_acc[1] = cut_acc[1] + square[:, CUT:] * (1.0 / fresh)
    for part in range(INNER):
        for h in range(HEADS_DEV):
            for p in range(3):
                low = h * 3 * HD + p * HD
                bias_grad[p : p + 1, pl.ds(part * HEADS_DEV * HD + h * HD, HD)] = p_in[
                    part, 3:4, low : low + HD
                ]
        fcb_grad[part : part + 1, :] = p_in[part, 4:5, :]
    bias_grad[3:4, :] = p_sum[9:10, :]
    bias_grad[4:5, :] = p_sum[9:10, :]
    bias_after, bias_update = second_step(bias_grad[...], bias_second[...])
    bias_moment[...] = bias_after
    fcb_after, fcb_update = second_step(fcb_grad[...], fcb_second[...])
    fcb_moment[...] = fcb_after
    usq = jnp.sum(bias_update * bias_update, axis=1, keepdims=True) * on_b
    scalars = (
        [
            total_of(rows_after[:, 0:1]) * on_c,
            total_of(head_acc[0] * inverse_rows[:, 0:1]),
            total_of(rows_after[:, 1:2]) * on_c,
            total_of(cut_acc[0] * inverse_rows[:, 1:2]),
            total_of(or_new[...]) * on_b,
            total_of(head_acc[1] * inverse_rows[:, 2:3]),
            sum(total_of(f2_new[part]) for part in range(INNER)) * on_b,
            total_of(cut_acc[1] * inverse_rows[:, 3:4]),
        ]
        + [usq[i : i + 1] for i in range(5)]
        + [total_of(fcb_update * fcb_update) * on_b]
    )
    lane_s = lax.broadcasted_iota(jnp.int32, (8, 128), 1)
    line = jnp.zeros((8, 128), jnp.float32)
    for place, value in enumerate(scalars):
        line = jnp.where(lane_s == place, value, line)
    pay2[...] = line
    chain_sends(pay2, z2_in, 1, start)
    z2_in[o] = line

    pair_copy(p_sum, s_in, 2).wait_recv()
    norm_grad[:, own_half] = p_sum[5:9, :]
    norm_grad[:, other_half] = s_in[5:9, :]
    old = p_sum[10:11, :] + s_in[10:11, :]
    norm_after, norm_update = second_step(norm_grad[...], norm_second[...])
    norm_moment[...] = norm_after

    def moved(vector, update, update_square, old_square, entries):
        clip_factor = jnp.maximum(1.0, jnp.sqrt(update_square / entries))
        step_rate = RATE * jnp.maximum(FLOOR_RATE, jnp.sqrt(old_square / entries))
        return vector - step_rate * update / clip_factor

    norm_values = norm_ref[...]
    norm_new[...] = moved(
        norm_values,
        norm_update,
        jnp.sum(norm_update * norm_update, axis=1, keepdims=True),
        jnp.sum(norm_values * norm_values, axis=1, keepdims=True),
        D,
    )

    chain_waits(pay2, z2_in, 1)
    acc = z2_in[0]
    for j in range(1, outer):
        acc = acc + z2_in[j]
    z2_sum[...] = acc
    plane_sends(z2_sum, p2_in, 1, start)
    p2_in[q] = acc
    plane_waits(z2_sum, p2_in, 1)
    acc = p2_in[0] + p2_in[1] + p2_in[2] + p2_in[3]
    p2_sum[...] = acc
    pair_copy(p2_sum, s2_in, 3).start()
    pair_copy(p2_sum, s2_in, 3).wait_recv()
    sums = (acc + s2_in[...])[0:1, :]

    def scalar(place):
        return sums[:, place : place + 1]

    def factor(total, inverse, place, entries):
        clip_factor = jnp.maximum(1.0, jnp.sqrt(total * inverse / entries))
        rate = RATE * jnp.maximum(FLOOR_RATE, jnp.sqrt(old[:, place : place + 1] / entries))
        return rate * jnp.sqrt(total) / clip_factor

    factors = (
        factor(scalar(0), scalar(1), 0, 3 * D * D),
        factor(scalar(2), scalar(3), 2, D * FF),
        factor(scalar(4), scalar(5), 1, D * D),
        factor(scalar(6), scalar(7), 3, FF * D),
    )
    line = jnp.zeros((8, 128), jnp.float32)
    for place, value in enumerate(factors):
        line = jnp.where(lane_s == place, value, line)
    coef[...] = line
    for i in range(5):
        bias_new[i : i + 1, :] = moved(
            pb[i : i + 1, :], bias_update[i : i + 1], scalar(8 + i), old[:, 4 + i : 5 + i], D
        )
    fcb_new[...] = moved(fcb[...], fcb_update, scalar(13), old[:, 9:10], FF)

    finish = lambda copy: copy.wait_send()
    chain_sends(pay, z_in, 0, finish)
    chain_sends(pay2, z2_in, 1, finish)
    plane_sends(z_sum, p_in, 0, finish)
    plane_sends(z2_sum, p2_in, 1, finish)
    pair_copy(terms, terms_in, 0).wait_send()
    pair_copy(rsum, rsum_in, 1).wait_send()
    pair_copy(p_sum, s_in, 2).wait_send()
    pair_copy(p2_sum, s2_in, 3).wait_send()


def tail_call(count, *args):
    outer = count // INNER
    received, xin = args[0], args[7]
    tokens, half = xin.shape
    rows = received.shape[2]
    high = jnp.float32
    spec = pl.BlockSpec(memory_space=pltpu.VMEM)
    dma = pltpu.SemaphoreType.DMA

    def out(*shape, dtype=high):
        return jax.ShapeDtypeStruct(shape, dtype)

    outs = [
        out(tokens, half, dtype=jnp.bfloat16),
        out(tokens, half, dtype=jnp.bfloat16),
        out(rows, 4),
        out(3, half),
        out(1, half),
        out(INNER, 1, half),
        out(INNER, 1, half),
        out(4, D),
        out(4, D),
        out(4, D),
        out(5, half),
        out(5, half),
        out(5, half),
        out(INNER, half),
        out(INNER, half),
        out(INNER, half),
        out(8, 128),
    ]
    slot = (SLOT_ROWS, half)
    return pl.pallas_call(
        functools.partial(tail_kernel, count),
        out_shape=outs,
        in_specs=[spec] * len(args),
        out_specs=[spec] * len(outs),
        scratch_shapes=[
            pltpu.VMEM((tokens, half), high),
            pltpu.VMEM((tokens, half), high),
            pltpu.VMEM((tokens, 128), high),
            pltpu.VMEM((tokens, 128), high),
            pltpu.VMEM((rows, 128), high),
            pltpu.VMEM((rows, 128), high),
            pltpu.VMEM(slot, high),
            pltpu.VMEM((outer, *slot), high),
            pltpu.VMEM(slot, high),
            pltpu.VMEM((INNER, *slot), high),
            pltpu.VMEM(slot, high),
            pltpu.VMEM(slot, high),
            pltpu.VMEM((8, 128), high),
            pltpu.VMEM((outer, 8, 128), high),
            pltpu.VMEM((8, 128), high),
            pltpu.VMEM((INNER, 8, 128), high),
            pltpu.VMEM((8, 128), high),
            pltpu.VMEM((8, 128), high),
            dma((2, outer - 1)),
            dma((2, outer - 1)),
            dma((2, INNER - 1)),
            dma((2, INNER - 1)),
            dma((4,)),
            dma((4,)),
        ],
        compiler_params=pltpu.CompilerParams(
            collective_id=1, has_side_effects=True, vmem_limit_bytes=58 * 1024 * 1024
        ),
        cost_estimate=pl.CostEstimate(
            flops=50_000_000, bytes_accessed=40_000_000, transcendentals=100_000
        ),
    )(*args)


def update_kernel(
    gr,
    wq,
    wo,
    w1,
    w2,
    row_new,
    qc_new,
    or_new,
    f1_new,
    f2_new,
    coef,
    q_grad,
    q_next,
    q_copy,
    o_grad,
    o_next,
    o_copy,
    f1_grad,
    f1_next,
    f1_copy,
    f2_grad,
    f2_next,
    f2_copy,
):
    side = lax.rsqrt(row_new[...]) * coef[0:1, :4]

    def put(grad_ref, next_ref, copy_ref, where, weight, gradient, update):
        fresh = weight[where] - update
        grad_ref[where] = gradient
        next_ref[where] = fresh
        copy_ref[where] = fresh.astype(jnp.bfloat16)

    for h in range(HEADS_DEV):
        gradient = gr[h, 0].astype(jnp.float32)
        for p in range(3):
            mine = gradient[:, p * HD : (p + 1) * HD]
            update = mine * side[:, 0:1] * lax.rsqrt(qc_new[p : p + 1, h * HD : (h + 1) * HD])
            where = (p, slice(None), slice(h * HD, (h + 1) * HD))
            put(q_grad, q_next, q_copy, where, wq, mine, update)
        mine = gradient[:, 3 * HD :]
        update = mine * side[:, 2:3] * lax.rsqrt(or_new[:, h * HD : (h + 1) * HD])
        where = (slice(h * HD, (h + 1) * HD), slice(None))
        put(o_grad, o_next, o_copy, where, wo, mine.T, update.T)
    for f in range(CUTS):
        gradient = gr[HEADS_DEV + f, 0].astype(jnp.float32)
        cols = slice(f * CUT, (f + 1) * CUT)
        mine = gradient[:, :CUT]
        update = mine * side[:, 1:2] * lax.rsqrt(f1_new[0, :, cols])
        put(f1_grad, f1_next, f1_copy, (slice(None), cols), w1, mine, update)
        mine = gradient[:, CUT:]
        update = mine * side[:, 3:4] * lax.rsqrt(f2_new[0, :, cols])
        put(f2_grad, f2_next, f2_copy, (cols, slice(None)), w2, mine.T, update.T)


def update_call(gr, wq, wo, w1, w2, row_new, qc_new, or_new, f1_new, f2_new, coef):
    rows = gr.shape[2]
    width_q = HEADS_DEV * HD
    hidden_q = CUTS * CUT
    spec = pl.BlockSpec
    q_spec = spec((3, rows, width_q), lambda i: (0, 0, i))
    o_spec = spec((width_q, rows), lambda i: (i, 0))
    f1_spec = spec((rows, hidden_q), lambda i: (0, i))
    f2_spec = spec((hidden_q, rows), lambda i: (i, 0))
    outs, out_specs = [], []
    for array, its in ((wq, q_spec), (wo, o_spec), (w1, f1_spec), (w2, f2_spec)):
        for dtype in (jnp.float32, jnp.float32, jnp.bfloat16):
            outs.append(jax.ShapeDtypeStruct(array.shape, dtype))
            out_specs.append(its)
    return pl.pallas_call(
        update_kernel,
        grid=(INNER,),
        out_shape=outs,
        in_specs=[
            spec((CHUNKS, 1, rows, WIDE), lambda i: (0, i, 0, 0)),
            q_spec,
            o_spec,
            f1_spec,
            f2_spec,
            spec((rows, 4), lambda i: (0, 0)),
            spec((3, width_q), lambda i: (0, i)),
            spec((1, width_q), lambda i: (0, i)),
            spec((1, 1, hidden_q), lambda i: (i, 0, 0)),
            spec((1, 1, hidden_q), lambda i: (i, 0, 0)),
            spec((8, 128), lambda i: (0, 0)),
        ],
        out_specs=out_specs,
        compiler_params=pltpu.CompilerParams(vmem_limit_bytes=48 * 1024 * 1024),
        cost_estimate=pl.CostEstimate(
            flops=20_000_000, bytes_accessed=30_000_000, transcendentals=100_000
        ),
    )(gr, wq, wo, w1, w2, row_new, qc_new, or_new, f1_new, f2_new, coef)


def swap_pairs(count, step):
    return [(i, i ^ step) for i in range(count)]


def block_of(array, index, size, axis=0):
    return lax.dynamic_slice_in_dim(array, index * size, size, axis)


def on_device(
    inputs,
    cotangent,
    segment_ids,
    w_qkv,
    w_out,
    w_fc1,
    w_fc2,
    norm_params,
    proj_bias,
    fc1_bias,
    qkv_rows,
    qkv_cols,
    out_rows,
    out_cols,
    fc1_rows,
    fc1_cols,
    fc2_rows,
    fc2_cols,
    norm_second,
    bias_second,
    fc1b_second,
):
    tokens = inputs.shape[0]
    local_width = inputs.shape[1]
    local_hidden = fc1_bias.shape[0]
    rows = w_qkv.shape[0]
    count = lax.axis_size("batch")
    c = lax.axis_index("branch")
    b = lax.axis_index("batch")
    q = lax.rem(b, INNER)
    group = INNER * tokens
    width_q = local_width // INNER
    hidden_q = local_hidden // INNER
    qkv_low = w_qkv.astype(jnp.bfloat16).reshape(rows, 3, INNER, HEADS_DEV, HD)
    out_low = w_out.astype(jnp.bfloat16).reshape(INNER, HEADS_DEV, HD, rows)
    fc1_low = w_fc1.astype(jnp.bfloat16).reshape(rows, INNER, CUTS, CUT)
    fc2_low = w_fc2.astype(jnp.bfloat16).reshape(INNER, CUTS, CUT, rows)
    heads_low = jnp.concatenate(
        [
            qkv_low.transpose(3, 2, 0, 1, 4).reshape(HEADS_DEV, INNER, rows, 3 * HD),
            out_low.transpose(1, 0, 3, 2),
        ],
        axis=3,
    )
    cuts_low = jnp.concatenate(
        [fc1_low.transpose(2, 1, 0, 3), fc2_low.transpose(1, 0, 3, 2)], axis=3
    )
    wst = jnp.concatenate([heads_low, cuts_low], axis=0)

    segment = jnp.concatenate(
        [segment_ids]
        + [lax.ppermute(segment_ids, "batch", swap_pairs(count, d)) for d in range(1, INNER)],
        axis=0,
    )
    positions_idx = jnp.arange(tokens)
    earlier = jnp.sum((segment[:, None, :] < segment[:, :, None]).astype(jnp.int32), axis=2)
    starts = earlier.astype(jnp.float32).reshape(group, 1)
    places = (positions_idx[None] - earlier).astype(jnp.float32).reshape(group, 1)
    frequency = 10000.0 ** (-2.0 * jnp.arange(ROT // 2, dtype=jnp.float32) / ROT)
    angles = places * frequency[None, :]
    cos_part = jnp.cos(angles)
    sin_part = jnp.sin(angles)
    rest = (group, HD - 2 * ROT)
    turns = jnp.concatenate(
        [cos_part, cos_part, -sin_part, sin_part, jnp.broadcast_to(starts, rest)], axis=1
    )
    bias_h = (
        block_of(proj_bias[0:3], q, width_q, 1)
        .reshape(3, HEADS_DEV, HD)
        .transpose(1, 0, 2)
        .reshape(HEADS_DEV, 1, 3 * HD)
    )
    bias_f = block_of(fc1_bias, q, hidden_q).reshape(CUTS, 1, CUT)
    received, plane_parts, plane_own, head_bias, cut_bias, col_sums, row_moments = block_call(
        count, wst, inputs, cotangent, turns, norm_params, bias_h, bias_f
    )
    by_part = (INNER, hidden_q)
    qkv_parts = w_qkv.transpose(1, 0, 2)
    (
        output,
        input_grad,
        row_stats,
        qkv_cols_new,
        out_rows_new,
        fc1_cols_new,
        fc2_rows_new,
        norm_grad,
        norm_moment,
        norm_new,
        bias_grad,
        bias_moment,
        bias_new,
        fc1b_grad,
        fc1b_moment,
        fc1b_new,
        factors,
    ) = tail_call(
        count,
        received,
        qkv_parts.reshape(3 * rows, local_width),
        w_out,
        w_fc1,
        w_fc2,
        plane_parts,
        plane_own,
        inputs,
        cotangent,
        row_moments,
        norm_params,
        proj_bias,
        fc1_bias.reshape(by_part),
        jnp.stack([qkv_rows, fc1_rows, out_cols, fc2_cols], axis=1),
        qkv_cols,
        out_rows.reshape(1, local_width),
        fc1_cols.reshape(by_part),
        fc2_rows.reshape(by_part),
        norm_second,
        bias_second,
        fc1b_second.reshape(by_part),
        col_sums,
        head_bias,
        cut_bias,
    )
    updated = update_call(
        received,
        qkv_parts,
        w_out,
        w_fc1,
        w_fc2,
        row_stats,
        qkv_cols_new,
        out_rows_new,
        fc1_cols_new,
        fc2_rows_new,
        factors,
    )
    qkv_grad, qkv_next, qkv_copy = (array.transpose(1, 0, 2) for array in updated[0:3])
    out_grad, out_next, out_copy = updated[3:6]
    fc1_grad, fc1_next, fc1_copy = updated[6:9]
    fc2_grad, fc2_next, fc2_copy = updated[9:12]
    return (
        output,
        input_grad,
        qkv_grad,
        qkv_next,
        row_stats[:, 0],
        qkv_cols_new,
        qkv_copy,
        out_grad,
        out_next,
        out_rows_new.reshape(local_width),
        row_stats[:, 2],
        out_copy,
        fc1_grad,
        fc1_next,
        row_stats[:, 1],
        fc1_cols_new.reshape(local_hidden),
        fc1_copy,
        fc2_grad,
        fc2_next,
        fc2_rows_new.reshape(local_hidden),
        row_stats[:, 3],
        fc2_copy,
        norm_grad,
        norm_moment,
        norm_new,
        bias_grad,
        bias_moment,
        bias_new,
        fc1b_grad.reshape(local_hidden),
        fc1b_moment.reshape(local_hidden),
        fc1b_new.reshape(local_hidden),
    )


def solution(mesh):
    in_specs = (
        P("batch", "branch"),
        P("batch", "branch"),
        P("batch", None),
        P("batch", None, "branch"),
        P("branch", "batch"),
        P("batch", "branch"),
        P("branch", "batch"),
        P(),
        P(None, "branch"),
        P("branch"),
        P("batch"),
        P(None, "branch"),
        P("branch"),
        P("batch"),
        P("batch"),
        P("branch"),
        P("branch"),
        P("batch"),
        P(),
        P(None, "branch"),
        P("branch"),
    )
    out_specs = (
        P("batch", "branch"),
        P("batch", "branch"),
        P("batch", None, "branch"),
        P("batch", None, "branch"),
        P("batch"),
        P(None, "branch"),
        P("batch", None, "branch"),
        P("branch", "batch"),
        P("branch", "batch"),
        P("branch"),
        P("batch"),
        P("branch", "batch"),
        P("batch", "branch"),
        P("batch", "branch"),
        P("batch"),
        P("branch"),
        P("batch", "branch"),
        P("branch", "batch"),
        P("branch", "batch"),
        P("branch"),
        P("batch"),
        P("branch", "batch"),
        P(),
        P(),
        P(),
        P(None, "branch"),
        P(None, "branch"),
        P(None, "branch"),
        P("branch"),
        P("branch"),
        P("branch"),
    )
    return jax.shard_map(
        on_device, mesh=mesh, in_specs=in_specs, out_specs=out_specs, check_vma=False
    )
```

```python
import functools

import jax
import jax.numpy as jnp
from jax import lax
from jax.experimental import pallas as pl
from jax.experimental.pallas import tpu as pltpu
from jax.sharding import PartitionSpec as P

D = 2048
HD = 128
ROT = 32
FF = 8192
STEP = 10


EPS_NORM = 1e-05
EPS_SQUARE = 1e-30
RATE = 0.3
FLOOR_RATE = 0.001


def decay_rate():
    return 1.0 - STEP ** (-0.8)


def squares(gradient):
    return gradient * gradient + EPS_SQUARE


def renew_stat(old_stat, new_sum):
    decay = decay_rate()
    return decay * old_stat + (1.0 - decay) * new_sum


def second_step(gradient, second):
    second_new = renew_stat(second, squares(gradient))
    return (second_new, gradient * lax.rsqrt(second_new))


INNER = 4
HEADS_DEV = 2
CUTS = 4
CHUNKS = HEADS_DEV + CUTS
CUT = 256
WIDE = 512
MESH = pl.DeviceIdType.MESH


def flip(index, step):
    return index + step * (1 - 2 * lax.rem(index // step, 2))


def nn(left, right):
    return jnp.dot(left, right, preferred_element_type=jnp.float32)


def nt(left, right):
    return lax.dot_general(
        left, right, (((1,), (1,)), ((), ())), preferred_element_type=jnp.float32
    )


def tn(left, right):
    return lax.dot_general(
        left, right, (((0,), (0,)), ((), ())), preferred_element_type=jnp.float32
    )


def block_kernel(
    count,
    wst,
    xin,
    yin,
    turn_ref,
    norm_ref,
    bias_h,
    bias_f,
    gr,
    xr,
    xo,
    qb,
    fb,
    cs,
    st,
    H1,
    H2,
    DY,
    W,
    TA,
    G,
    sbuf,
    fbuf,
    rsb,
    sib_send,
    sib_land,
    own,
    a2a_s,
    a2a_r,
    loc_s,
    ag_s,
    ag_r,
    x_s,
    x_r,
    sx_s,
    sx_r,
    rs_s,
    rs_r,
    gr_s,
    gr_r,
    sib_s,
    sib_r,
    p_s,
    p_r,
    tmp_s,
    free_s,
):
    outer = count // INNER
    S = outer - 1
    T, half = xin.shape
    R = wst.shape[2]
    block = INNER * R
    QT = T // 2
    b = lax.axis_index("batch")
    c = lax.axis_index("branch")
    q = lax.rem(b, INNER)
    o = b // INNER
    bx, by = flip(b, 1), flip(b, 2)
    bxy = flip(bx, 2)
    near = (bx, by, bxy)
    da = 1 + c
    db = 2 - c
    b_first = bx * (1 - c) + by * c
    b_second = by * (1 - c) + bx * c

    def remote(src, dst, ssem, rsem, to_b, to_c):
        return pltpu.make_async_remote_copy(
            src_ref=src,
            dst_ref=dst,
            send_sem=ssem,
            recv_sem=rsem,
            device_id=(to_b, to_c),
            device_id_type=MESH,
        )

    barrier = pltpu.get_barrier_semaphore()
    for who in near:
        pl.semaphore_signal(barrier, inc=1, device_id=(who, c), device_id_type=MESH)
    pl.semaphore_signal(barrier, inc=1, device_id=(b, 1 - c), device_id_type=MESH)

    @pl.when(o > 0)
    def _():
        pl.semaphore_signal(barrier, inc=1, device_id=(b - INNER, c), device_id_type=MESH)

    @pl.when(o < outer - 1)
    def _():
        pl.semaphore_signal(barrier, inc=1, device_id=(b + INNER, c), device_id_type=MESH)

    pl.semaphore_wait(barrier, 4 + jnp.minimum(o, 1) + jnp.minimum(outer - 1 - o, 1))

    def a2a_copy(k, d, received=False):
        to = near[d - 1]
        row = (to if received else b) * R
        return remote(
            wst.at[k, lax.rem(to, INNER)],
            W.at[k, pl.ds(pl.multiple_of(row, 16), R)],
            a2a_s.at[k, d - 1],
            a2a_r.at[k, d - 1],
            to,
            c,
        )

    def a2a_local(k):
        return pltpu.make_async_copy(
            wst.at[k, q], W.at[k, pl.ds(pl.multiple_of(b * R, 16), R)], loc_s.at[k]
        )

    def a2a_start(k):
        for d in range(1, INNER):
            a2a_copy(k, d).start()
        a2a_local(k).start()

    def a2a_wait(k):
        for d in range(1, INNER):
            a2a_copy(k, d, True).wait_recv()
        a2a_local(k).wait()

    def ag_copy(k, way, s, part):
        rows = pl.ds(pl.multiple_of(part * block, 16), block)
        to = b + INNER if way == 0 else b - INNER
        return remote(
            W.at[k, rows], W.at[k, rows], ag_s.at[k, way, s - 1], ag_r.at[k, way, s - 1], to, c
        )

    def ag_sends(k, s, what):
        @pl.when((o >= s - 1) & (o <= outer - 2))
        def _():
            what(ag_copy(k, 0, s, o - s + 1))

        @pl.when((o >= 1) & (o <= outer - s))
        def _():
            what(ag_copy(k, 1, s, o + s - 1))

    def ag_wait(k, s):
        @pl.when(o >= s)
        def _():
            ag_copy(k, 0, s, o - s).wait_recv()

        @pl.when(o <= outer - 1 - s)
        def _():
            ag_copy(k, 1, s, o + s).wait_recv()

    def ag_range(low, high):
        def step(n, carry):
            k = n // S
            s = lax.rem(n, S) + 1

            @pl.when(s == 1)
            def _():
                a2a_wait(k)

            @pl.when(s > 1)
            def _():
                ag_wait(k, s - 1)

            ag_sends(k, s, lambda copy: copy.start())
            return carry

        lax.fori_loop(low, high, step, 0)

    def ag(low, high):
        ag_range(low * S // 3, high * S // 3)

    def spot(buf, slot):
        return buf.at[
            pl.ds(pl.multiple_of(slot * T, 16), T), pl.ds(pl.multiple_of(c * half, 128), half)
        ]

    def other_spot(buf, slot):
        return buf.at[
            pl.ds(pl.multiple_of(slot * T, 16), T), pl.ds(pl.multiple_of((1 - c) * half, 128), half)
        ]

    def sx_copy(i, buf, slot, src=None):
        place = spot(buf, slot)
        return remote(place if src is None else src, place, sx_s.at[i, slot], sx_r.at[i, slot], b, 1 - c)

    def sx_wait(i, buf, slot):
        remote(
            other_spot(buf, slot), other_spot(buf, slot), sx_s.at[i, slot], sx_r.at[i, slot], b, 1 - c
        ).wait_recv()

    def x_first(i, src, buf):
        return remote(src, spot(buf, da), x_s.at[i, da - 1], x_r.at[i, da - 1], b_first, c)

    def x_second(i, src, buf):
        return remote(src, spot(buf, db), x_s.at[i, db - 1], x_r.at[i, db - 1], b_second, c)

    def x_forward(i, buf):
        return remote(spot(buf, da), spot(buf, 3), x_s.at[i, 2], x_r.at[i, 2], b_second, c)

    def x_diag(i, buf):
        return remote(spot(buf, 3), spot(buf, 3), x_s.at[i, 2], x_r.at[i, 2], b_second, c)

    def x_local(i, src, buf):
        return pltpu.make_async_copy(src, spot(buf, 0), tmp_s.at[i])

    def gather_one(i, src, buf):
        x_first(i, src, buf).start()
        x_local(i, src, buf).start()
        sx_copy(i, buf, 0, src).start()

    def gather_two(i, src, buf):
        x_first(i, src, buf).wait_recv()
        x_second(i, src, buf).start()
        x_forward(i, buf).start()
        sx_copy(i, buf, da).start()

    def gather_three(i, src, buf):
        x_second(i, src, buf).wait_recv()
        sx_copy(i, buf, db).start()
        x_diag(i, buf).wait_recv()
        sx_copy(i, buf, 3).start()

    def gather_sent(i, src, buf):
        x_first(i, src, buf).wait_send()
        x_second(i, src, buf).wait_send()
        x_forward(i, buf).wait_send()
        sx_copy(i, buf, 0, src).wait_send()
        for slot in range(1, INNER):
            sx_copy(i, buf, slot).wait_send()

    lane_n = lax.broadcasted_iota(jnp.int32, (64, 128), 1)

    def norm_rows(slot):
        def step(i, carry):
            rows = pl.ds(pl.multiple_of(slot * T + i * 64, 64), 64)
            values = H1[rows, :].astype(jnp.float32)
            mean = jnp.mean(values, axis=-1, keepdims=True)
            centered = values - mean
            inverse = lax.rsqrt(jnp.mean(centered * centered, axis=-1, keepdims=True) + EPS_NORM)
            normed = centered * inverse
            if slot == 0:
                st[pl.ds(pl.multiple_of(i * 64, 64), 64), :] = jnp.where(lane_n == 0, mean, inverse)
            H1[rows, :] = (normed * norm_ref[0:1, :] + norm_ref[1:2, :]).astype(jnp.bfloat16)
            H2[rows, :] = (normed * norm_ref[2:3, :] + norm_ref[3:4, :]).astype(jnp.bfloat16)
            return carry

        lax.fori_loop(0, T // 64, step, 0)

    lane = lax.broadcasted_iota(jnp.int32, (T, HD), 1)
    scale = HD ** (-0.5)

    def partner(tensor):
        return jnp.where(
            lane < ROT // 2,
            pltpu.roll(tensor, HD - ROT // 2, 1),
            jnp.where(lane < ROT, pltpu.roll(tensor, ROT // 2, 1), 0.0),
        )

    def turns_of(rows):
        table = turn_ref[:, rows].T
        cos_rows = jnp.where(lane < ROT, table, 1.0)
        sin_rows = pltpu.roll(table, HD - ROT, 1)
        return cos_rows, sin_rows, table[:, 2 * ROT : 2 * ROT + 1]

    def project_piece(h, slot):
        rows = pl.ds(pl.multiple_of(slot * T, 128), T)
        cos_rows, sin_rows, _ = turns_of(rows)
        projected = nn(H1[rows, :], W[h, :, : 3 * HD]) + bias_h[h]
        first = projected[:, :HD]
        queries = (first * cos_rows + partner(first) * sin_rows).astype(jnp.bfloat16)
        second = projected[:, HD : 2 * HD]
        keys = (second * cos_rows + partner(second) * sin_rows).astype(jnp.bfloat16)
        values = projected[:, 2 * HD :].astype(jnp.bfloat16)
        start = pl.multiple_of(slot * T, 128)
        TA[h, :, pl.ds(start, HD)] = queries
        TA[h, :, pl.ds(start + HD, HD)] = keys
        TA[h, :, pl.ds(start + 2 * HD, HD)] = values

    def head_piece(h, slot):
        start = pl.multiple_of(slot * T, 128)
        rows = pl.ds(start, T)
        cos_rows, sin_rows, starts = turns_of(rows)
        queries = TA[h, :, pl.ds(start, HD)]
        keys = TA[h, :, pl.ds(start + HD, HD)]
        values = TA[h, :, pl.ds(start + 2 * HD, HD)]
        back = nn(DY[rows, :], W[h, :, 3 * HD :]).astype(jnp.bfloat16)
        contexts, grad_q = [], []
        grad_k, grad_v = [None, None], [None, None]
        for i in range(2):
            seen = QT * (i + 1)
            part = slice(QT * i, QT * (i + 1))
            raw = nt(queries[part], keys[:seen]) * scale
            query_at = lax.broadcasted_iota(jnp.int32, (QT, seen), 0) + QT * i
            key_at = lax.broadcasted_iota(jnp.int32, (QT, seen), 1)
            allowed = (key_at <= query_at) & (key_at.astype(jnp.float32) >= starts[part])
            scores = jnp.where(allowed, raw, -1e30)
            exponent = jnp.exp(scores - jnp.max(scores, axis=-1, keepdims=True))
            probs = exponent * (1.0 / jnp.sum(exponent, axis=-1, keepdims=True))
            soft = probs.astype(jnp.bfloat16)
            contexts.append(nn(soft, values[:seen]).astype(jnp.bfloat16))
            grad_probs = nt(back[part], values[:seen])
            inner = jnp.sum(probs * grad_probs, axis=-1, keepdims=True)
            grad_scores = (probs * (grad_probs - inner)).astype(jnp.bfloat16)
            grad_q.append((nn(grad_scores, keys[:seen]) * scale).astype(jnp.bfloat16))
            for j in range(i + 1):
                cut = slice(QT * j, QT * (j + 1))
                term_v = tn(soft[:, cut], back[part])
                term_k = tn(grad_scores[:, cut], queries[part])
                grad_v[j] = term_v if grad_v[j] is None else grad_v[j] + term_v
                grad_k[j] = term_k if grad_k[j] is None else grad_k[j] + term_k
        context = jnp.concatenate(contexts, axis=0)
        dq = jnp.concatenate(grad_q, axis=0).astype(jnp.float32)
        dk = (jnp.concatenate(grad_k, axis=0) * scale).astype(jnp.bfloat16).astype(jnp.float32)
        dv = jnp.concatenate(grad_v, axis=0)
        turned = jnp.concatenate(
            [
                dq * cos_rows - partner(dq) * sin_rows,
                dk * cos_rows - partner(dk) * sin_rows,
                dv,
            ],
            axis=1,
        ).astype(jnp.bfloat16)
        TA[h, : 3 * HD, rows] = turned.T
        TA[h, 3 * HD :, rows] = context.T
        total = jnp.sum(turned.astype(jnp.float32), axis=0, keepdims=True)
        qb[h] = jnp.where(slot == 0, total, qb[h] + total)

    def cut_piece(f, slot):
        rows = pl.ds(pl.multiple_of(slot * T, 128), T)
        k = HEADS_DEV + f
        pre = nn(H2[rows, :], W[k, :, :CUT]) + bias_f[f]
        grad = nn(DY[rows, :], W[k, :, CUT:])
        normal = 0.5 * (1.0 + lax.erf(pre * (0.5**0.5)))
        slope = normal + pre * (jnp.exp(-0.5 * pre * pre) * (0.5 * 0.7978845608028654))
        active = (pre * normal).astype(jnp.bfloat16)
        pulled = (grad * slope).astype(jnp.bfloat16)
        low = pl.multiple_of(f * WIDE, WIDE)
        H1[pl.ds(low, CUT), rows] = pulled.T
        H1[pl.ds(low + CUT, CUT), rows] = active.T
        total = jnp.sum(pulled.astype(jnp.float32), axis=0, keepdims=True)
        fb[f] = jnp.where(slot == 0, total, fb[f] + total)

    def grads(k, turned, left, edge):
        def step(j, carry):
            cols = pl.ds(pl.multiple_of(j * block, 128), block)
            G[lax.rem(k, 2), j, :edge, :] = nn(turned(0, edge), left[:, cols])
            G[lax.rem(k, 2), j, edge:, :] = nn(turned(edge, WIDE - edge), DY[:, cols])
            return carry

        lax.fori_loop(0, outer, step, 0)

    def head_turned(h):
        return lambda low, size: TA[h, pl.ds(low, size), :]

    def cut_turned(f):
        return lambda low, size: H1[pl.ds(pl.multiple_of(f * WIDE + low, 128), size), :]

    def rs_copy(k, way, t):
        to = b + INNER if way == 0 else b - INNER
        return remote(
            sbuf.at[way],
            rsb.at[way, t - 1],
            rs_s.at[k, way, t - 1],
            rs_r.at[k, way, t - 1],
            to,
            c,
        )

    def rs_sends(way, t):
        if way == 0:
            return (o <= t - 1) & (o <= outer - 2)
        return (o >= outer - t) & (o >= 1)

    def rs_receives(way, t):
        if way == 0:
            return (o >= 1) & (o <= t)
        return (o <= outer - 2) & (o >= outer - 1 - t)

    def rs_fetch(k, way, t):
        rs_copy(k, way, t).wait_recv()
        return rsb[way, t - 1].astype(jnp.float32)

    def rs_step(k, t):
        n = k * S + t - 1

        @pl.when((t == 1) & (k >= 1) & (o < outer - 1))
        def _():
            pl.semaphore_wait(free_s.at[0], 1)

        @pl.when((t == 1) & (k >= 1) & (o > 0))
        def _():
            pl.semaphore_wait(free_s.at[1], 1)

        before = jnp.maximum(n - 1, 0)
        k_before = before // S
        t_before = lax.rem(before, S) + 1
        for way in range(2):
            owner = o + outer - t if way == 0 else o - outer + t

            @pl.when((n >= 1) & rs_sends(way, t_before))
            def _():
                rs_copy(k_before, way, t_before).wait_send()

            @pl.when(rs_sends(way, t))
            def _():
                @pl.when(rs_receives(way, t - 1) & (t > 1))
                def _():
                    sbuf[way] = (
                        G[lax.rem(k, 2), owner] + rs_fetch(k, way, t - 1)
                    ).astype(jnp.bfloat16)

                @pl.when(jnp.logical_not(rs_receives(way, t - 1) & (t > 1)))
                def _():
                    sbuf[way] = G[lax.rem(k, 2), owner].astype(jnp.bfloat16)

                rs_copy(k, way, t).start()

    def gr_copy(k, d, received=False):
        to = near[d - 1]
        slot = lax.rem(to, INNER)
        return remote(
            fbuf.at[pl.ds(pl.multiple_of(slot * R, 16), R)],
            gr.at[k, slot if received else q],
            gr_s.at[k, d - 1],
            gr_r.at[k, d - 1],
            to,
            c,
        )

    def gr_local(k):
        return pltpu.make_async_copy(
            fbuf.at[pl.ds(pl.multiple_of(q * R, 16), R)],
            gr.at[k, q],
            gr_s.at[k, 3],
        )

    def gr_sent(k):
        for d in range(1, INNER):
            gr_copy(k, d).wait_send()
        gr_local(k).wait()

    def rs_final(k):
        for way in range(2):

            @pl.when(rs_receives(way, S))
            def _():
                G[lax.rem(k, 2), o] = G[lax.rem(k, 2), o] + rs_fetch(k, way, S)

        @pl.when((k < CHUNKS - 1) & (o > 0))
        def _():
            pl.semaphore_signal(
                free_s.at[0], inc=1, device_id=(b - INNER, c), device_id_type=MESH
            )

        @pl.when((k < CHUNKS - 1) & (o < outer - 1))
        def _():
            pl.semaphore_signal(
                free_s.at[1], inc=1, device_id=(b + INNER, c), device_id_type=MESH
            )

        @pl.when(k >= 1)
        def _():
            gr_sent(k - 1)

        final = G[lax.rem(k, 2), o].T
        cs[k] = jnp.sum(squares(final), axis=0, keepdims=True)
        fbuf[...] = final.astype(jnp.bfloat16)
        for d in range(1, INNER):
            gr_copy(k, d).start()
        gr_local(k).start()

    def rs_range(low, high):
        def step(n, carry):
            k = n // (S + 1)
            t = lax.rem(n, S + 1) + 1

            @pl.when(t <= S)
            def _():
                rs_step(k, t)

            @pl.when(t == S + 1)
            def _():
                rs_final(k)

            return carry

        lax.fori_loop(low, high, step, 0)

    TILE = T // 2
    TILES = 2 * INNER
    PER_ROW = D // TILE

    def tile_slot(i):
        return INNER - 1 - i // 2

    def product(which, i, side):
        at = pl.multiple_of(tile_slot(i) * T + lax.rem(i, 2) * TILE, 128)
        toks = pl.ds(at, TILE)
        features = pl.ds(pl.multiple_of(side * half, 128), half)
        terms = []
        if which == 0:
            for h in range(HEADS_DEV):
                terms.append((h, slice(0, 3 * HD), lambda h=h: TA[h, : 3 * HD, toks]))
        elif which == 1:
            for f in range(CUTS):
                low = f * WIDE
                terms.append(
                    (HEADS_DEV + f, slice(0, CUT), lambda low=low: H1[low : low + CUT, toks])
                )
        else:
            for h in range(HEADS_DEV):
                terms.append((h, slice(3 * HD, WIDE), lambda h=h: TA[h, 3 * HD :, toks]))
            for f in range(CUTS):
                low = f * WIDE + CUT
                terms.append(
                    (HEADS_DEV + f, slice(CUT, WIDE), lambda low=low: H1[low : low + CUT, toks])
                )
        for place, (k, cols, right) in enumerate(terms):
            term = nn(W[k, features, cols], right())
            own[...] = term if place == 0 else own[...] + term

    def sib_copy(which, i):
        return remote(
            sib_send.at[lax.rem(i, 2)],
            sib_land.at[lax.rem(i, 4)],
            sib_s.at[which, i],
            sib_r.at[which, i],
            b,
            1 - c,
        )

    def stage(which, i):
        if which == 0:
            return H1.at[pl.ds(half, half), pl.ds(pl.multiple_of(i * TILE, 128), TILE)]
        t = (which - 1) * (TILES - 2) + i
        return H2.at[
            pl.ds(pl.multiple_of(t // PER_ROW * half, 128), half),
            pl.ds(pl.multiple_of(lax.rem(t, PER_ROW) * TILE, 128), TILE),
        ]

    def plane_copy(which, i):
        slot = tile_slot(i)
        low, high = lax.rem(slot, 2), slot // 2
        to = b + low * (1 - 2 * lax.rem(b, 2)) + high * 2 * (1 - 2 * lax.rem(b // 2, 2))
        src = stage(which, i)
        return remote(
            src,
            xr.at[which, slot - 1, lax.rem(i, 2)],
            p_s.at[which, i],
            p_r.at[which, i],
            to,
            c,
        )

    def tile_a(which, i):
        @pl.when(i >= 2)
        def _():
            sib_copy(which, i - 2).wait_send()

        product(which, i, 1 - c)
        sib_send[lax.rem(i, 2)] = own[...].astype(jnp.bfloat16)
        sib_copy(which, i).start()

    def tile_b(which, i):
        product(which, i, c)
        sib_copy(which, i).wait_recv()

        @pl.when(i < TILES - 2)
        def _():
            total = (own[...] + sib_land[lax.rem(i, 4)].astype(jnp.float32)).astype(jnp.bfloat16)
            stage(which, i)[...] = total
            plane_copy(which, i).start()

        @pl.when(i >= TILES - 2)
        def _():
            own[...] = own[...] + sib_land[lax.rem(i, 4)].astype(jnp.float32)
            keep = pltpu.make_async_copy(own, xo.at[which, lax.rem(i, 2)], tmp_s.at[2])
            keep.start()
            keep.wait()

    def sum_tiles(which, beside):
        tile_a(which, 0)

        def step(i, carry):
            @pl.when(i < TILES - 1)
            def _():
                tile_a(which, i + 1)

            tile_b(which, i)
            beside(i)
            return carry

        lax.fori_loop(0, TILES, step, 0)

    def sib_sent(which):
        for i in range(TILES - 2, TILES):
            sib_copy(which, i).wait_send()

    def spread(first, last, i, pieces, run):
        steps = last - first
        run(
            first + (steps * i + pieces - 1) // pieces,
            first + (steps * (i + 1) + pieces - 1) // pieces,
        )

    def ag_share(low, high, i, pieces):
        spread(low * S // 3, high * S // 3, i, pieces, ag_range)

    def rs_share(low, high, i, pieces):
        spread(low * (S + 1) // 4, high * (S + 1) // 4, i, pieces, rs_range)

    a2a_start(0)
    gather_one(0, xin, H1)
    gather_one(1, yin, DY)
    ag(0, 1)
    a2a_start(1)
    gather_two(0, xin, H1)
    gather_two(1, yin, DY)
    ag(1, 2)
    a2a_start(2)
    x_local(0, xin, H1).wait()
    sx_wait(0, H1, 0)
    norm_rows(0)
    ag(2, 3)
    gather_three(0, xin, H1)
    gather_sent(0, xin, H1)
    for k in range(3, CHUNKS):
        a2a_start(k)
    for slot in range(1, INNER):
        sx_wait(0, H1, slot)
        norm_rows(slot)
        if slot < 3:
            ag(2 + slot, 3 + slot)

    def project_step(h):
        ag_wait(h, S)

        def slot_step(slot, inner_carry):
            project_piece(h, slot)
            return inner_carry

        lax.fori_loop(0, INNER, slot_step, 0)
        ag(5 + h, 6 + h)

    project_step(0)
    gather_three(1, yin, DY)
    project_step(1)
    x_local(1, yin, DY).wait()
    for slot in range(INNER):
        sx_wait(1, DY, slot)
    gather_sent(1, yin, DY)

    def head_step(h, carry):
        def slot_step(slot, inner_carry):
            head_piece(h, slot)
            ag_share(7 + 3 * h, 10 + 3 * h, slot, INNER)
            rs_share(0, 3 * h, slot, INNER)
            return inner_carry

        lax.fori_loop(0, INNER, slot_step, 0)
        grads(h, head_turned(h), H1, 3 * HD)
        return carry

    lax.fori_loop(0, HEADS_DEV, head_step, 0)
    rs_share(3, 4, 0, 1)

    def beside_one(i):
        ag_share(13, 15, i, TILES)
        rs_share(4, 7, i, TILES)

    sum_tiles(0, beside_one)

    def cut_step(f, carry):
        ag_wait(HEADS_DEV + f, S)

        @pl.when(f == CUTS // 2)
        def _():
            for i in range(TILES - 2):
                plane_copy(0, i).wait_send()

        def slot_step(slot, inner_carry):
            cut_piece(f, slot)
            ag_share(
                jnp.minimum(15 + 2 * f, 18), jnp.minimum(17 + 2 * f, 18), slot, INNER
            )
            rs_share(
                jnp.where(f == 0, 7, 5 + 3 * f),
                jnp.where(f == 3, 18, 8 + 3 * f),
                slot,
                INNER,
            )
            return inner_carry

        lax.fori_loop(0, INNER, slot_step, 0)
        grads(HEADS_DEV + f, cut_turned(f), H2, CUT)
        return carry

    lax.fori_loop(0, CUTS, cut_step, 0)
    sib_sent(0)
    sum_tiles(1, lambda i: rs_share(18, 22, i, TILES))
    sib_sent(1)
    sum_tiles(2, lambda i: rs_share(22, 24, i, TILES))
    sib_sent(2)

    gr_sent(CHUNKS - 1)

    def drain_chunk(k, carry):
        for d in range(1, INNER):
            a2a_copy(k, d).wait_send()
            gr_copy(k, d, True).wait_recv()

        def drain_step(s, inner_carry):
            ag_sends(k, s, lambda copy: copy.wait_send())
            return inner_carry

        lax.fori_loop(1, S + 1, drain_step, 0)
        return carry

    lax.fori_loop(0, CHUNKS, drain_chunk, 0)
    for way in range(2):

        @pl.when(rs_sends(way, S))
        def _():
            rs_copy(CHUNKS - 1, way, S).wait_send()

    for which in range(3):

        def drain_tile(i, carry):
            if which:
                plane_copy(which, i).wait_send()
            plane_copy(which, i).wait_recv()
            return carry

        lax.fori_loop(0, TILES - 2, drain_tile, 0)


def block_call(count, wst, xin, yin, turns, norm_params, bias_h, bias_f):
    outer = count // INNER
    S = outer - 1
    tokens, half = xin.shape
    group = INNER * tokens
    rows = wst.shape[2]
    tile = tokens // 2
    low, high = jnp.bfloat16, jnp.float32
    any_spec = pl.BlockSpec(memory_space=pl.ANY)
    vmem_spec = pl.BlockSpec(memory_space=pltpu.VMEM)
    dma = pltpu.SemaphoreType.DMA
    return pl.pallas_call(
        functools.partial(block_kernel, count),
        out_shape=[
            jax.ShapeDtypeStruct((CHUNKS, INNER, rows, WIDE), low),
            jax.ShapeDtypeStruct((3, INNER - 1, 2, half, tile), low),
            jax.ShapeDtypeStruct((3, 2, half, tile), high),
            jax.ShapeDtypeStruct((HEADS_DEV, 1, 3 * HD), high),
            jax.ShapeDtypeStruct((CUTS, 1, CUT), high),
            jax.ShapeDtypeStruct((CHUNKS, 1, WIDE), high),
            jax.ShapeDtypeStruct((tokens, 128), high),
        ],
        in_specs=[any_spec] * 3 + [vmem_spec] * 4,
        out_specs=[any_spec] * 3 + [vmem_spec] * 4,
        scratch_shapes=[
            pltpu.VMEM((group, D), low),
            pltpu.VMEM((group, D), low),
            pltpu.VMEM((group, D), low),
            pltpu.VMEM((CHUNKS, D, WIDE), low),
            pltpu.VMEM((HEADS_DEV, WIDE, group), low),
            pltpu.VMEM((2, outer, WIDE, INNER * rows), high),
            pltpu.VMEM((2, WIDE, INNER * rows), low),
            pltpu.VMEM((INNER * rows, WIDE), low),
            pltpu.VMEM((2, S, WIDE, INNER * rows), low),
            pltpu.VMEM((2, half, tile), low),
            pltpu.VMEM((4, half, tile), low),
            pltpu.VMEM((half, tile), high),
            dma((CHUNKS, INNER - 1)),
            dma((CHUNKS, INNER - 1)),
            dma((CHUNKS,)),
            dma((CHUNKS, 2, S)),
            dma((CHUNKS, 2, S)),
            dma((2, INNER - 1)),
            dma((2, INNER - 1)),
            dma((2, INNER)),
            dma((2, INNER)),
            dma((CHUNKS, 2, S)),
            dma((CHUNKS, 2, S)),
            dma((CHUNKS, INNER)),
            dma((CHUNKS, INNER - 1)),
            dma((3, 2 * INNER)),
            dma((3, 2 * INNER)),
            dma((3, 2 * INNER)),
            dma((3, 2 * INNER)),
            dma((3,)),
            pltpu.SemaphoreType.REGULAR((2,)),
        ],
        compiler_params=pltpu.CompilerParams(
            collective_id=0, has_side_effects=True, vmem_limit_bytes=64 * 1024 * 1024
        ),
        cost_estimate=pl.CostEstimate(
            flops=80_000_000_000, bytes_accessed=60_000_000, transcendentals=10_000_000
        ),
    )(wst, xin, yin, turns, norm_params, bias_h, bias_f)


SLOT_ROWS = 16


def total_of(values):
    return jnp.sum(jnp.sum(values, axis=0, keepdims=True), axis=1, keepdims=True)


def tail_kernel(
    count,
    gr,
    wq,
    wo,
    w1,
    w2,
    xr,
    xo,
    xin,
    yin,
    st,
    norm_ref,
    pb,
    fcb,
    row_old,
    qc_old,
    or_old,
    f1_old,
    f2_old,
    norm_second,
    bias_second,
    fcb_second,
    cs,
    qb,
    fb,
    out_ref,
    ing_ref,
    row_new,
    qc_new,
    or_new,
    f1_new,
    f2_new,
    norm_grad,
    norm_moment,
    norm_new,
    bias_grad,
    bias_moment,
    bias_new,
    fcb_grad,
    fcb_moment,
    fcb_new,
    coef,
    scaled_buf,
    normed_buf,
    terms,
    terms_in,
    rsum,
    rsum_in,
    pay,
    z_in,
    z_sum,
    p_in,
    p_sum,
    s_in,
    pay2,
    z2_in,
    z2_sum,
    p2_in,
    p2_sum,
    s2_in,
    z_s,
    z_r,
    p_s,
    p_r,
    s_s,
    s_r,
):
    outer = count // INNER
    T, half = xin.shape
    R = gr.shape[2]
    b = lax.axis_index("batch")
    c = lax.axis_index("branch")
    q = lax.rem(b, INNER)
    o = b // INNER
    bx, by = flip(b, 1), flip(b, 2)
    near = (bx, by, flip(bx, 2))
    on_b = (b == 0).astype(jnp.float32)
    on_c = (c == 0).astype(jnp.float32)

    def remote(src, dst, ssem, rsem, to_b, to_c):
        return pltpu.make_async_remote_copy(
            src_ref=src,
            dst_ref=dst,
            send_sem=ssem,
            recv_sem=rsem,
            device_id=(to_b, to_c),
            device_id_type=MESH,
        )

    def chain(d):
        return lax.rem(o + d, outer)

    barrier = pltpu.get_barrier_semaphore()
    for who in near:
        pl.semaphore_signal(barrier, inc=1, device_id=(who, c), device_id_type=MESH)
    pl.semaphore_signal(barrier, inc=1, device_id=(b, 1 - c), device_id_type=MESH)
    for d in range(1, outer):
        pl.semaphore_signal(
            barrier, inc=1, device_id=(chain(d) * INNER + q, c), device_id_type=MESH
        )

    HALF_T = T // 2
    lane_t = lax.broadcasted_iota(jnp.int32, (HALF_T, 128), 1)
    own_half = pl.ds(pl.multiple_of(c * half, 128), half)
    other_half = pl.ds(pl.multiple_of((1 - c) * half, 128), half)
    gain_a = norm_ref[0:1, own_half]
    gain_b = norm_ref[2:3, own_half]
    pay[...] = jnp.zeros_like(pay)
    for i in range(2):
        rows = slice(i * HALF_T, (i + 1) * HALF_T)

        def whole(which):
            return (
                xo[which, i]
                + xr[which, 0, i].astype(jnp.float32)
                + xr[which, 1, i].astype(jnp.float32)
                + xr[which, 2, i].astype(jnp.float32)
            ).T

        values = xin[rows, :].astype(jnp.float32)
        out_ref[rows, :] = (values + whole(2) + pb[3:4, :] + pb[4:5, :]).astype(jnp.bfloat16)
        normed = (values - st[rows, 0:1]) * st[rows, 1:2]
        one = whole(0)
        two = whole(1)
        scaled = one * gain_a + two * gain_b
        scaled_buf[rows, :] = scaled
        normed_buf[rows, :] = normed
        terms[rows, :] = jnp.where(
            lane_t == 0,
            jnp.sum(scaled, axis=1, keepdims=True),
            jnp.where(lane_t == 1, jnp.sum(scaled * normed, axis=1, keepdims=True), 0.0),
        )
        pay[5:6, :] += jnp.sum(one * normed, axis=0, keepdims=True)
        pay[6:7, :] += jnp.sum(one, axis=0, keepdims=True)
        pay[7:8, :] += jnp.sum(two * normed, axis=0, keepdims=True)
        pay[8:9, :] += jnp.sum(two, axis=0, keepdims=True)
        pay[9:10, :] += jnp.sum(yin[rows, :].astype(jnp.float32), axis=0, keepdims=True)
    for k in range(CHUNKS):
        pay[k // 2 : k // 2 + 1, k % 2 * WIDE : (k % 2 + 1) * WIDE] = cs[k]
    for h in range(HEADS_DEV):
        pay[3:4, h * 3 * HD : (h + 1) * 3 * HD] = qb[h]
    for f in range(CUTS):
        pay[4:5, f * CUT : (f + 1) * CUT] = fb[f]
    lane_p = lax.broadcasted_iota(jnp.int32, (1, half), 1)
    biases = jnp.sum(pb[...] * pb[...], axis=1, keepdims=True) * on_b
    scalars = (
        [total_of(w[...] * w[...]) for w in (wq, wo, w1, w2)]
        + [biases[i : i + 1] for i in range(5)]
        + [total_of(fcb[...] * fcb[...]) * on_b]
    )
    line = jnp.zeros((1, half), jnp.float32)
    for place, value in enumerate(scalars):
        line = jnp.where(lane_p == place, value, line)
    pay[10:11, :] = line

    pl.semaphore_wait(barrier, INNER + outer - 1)

    def chain_sends(src, buf, base, what):
        for d in range(1, outer):
            what(
                remote(
                    src,
                    buf.at[o],
                    z_s.at[base, d - 1],
                    z_r.at[base, d - 1],
                    chain(d) * INNER + q,
                    c,
                )
            )

    def chain_waits(src, buf, base):
        for d in range(1, outer):
            source = chain(outer - d)
            remote(
                src,
                buf.at[source],
                z_s.at[base, d - 1],
                z_r.at[base, d - 1],
                source * INNER + q,
                c,
            ).wait_recv()

    def plane_sends(src, buf, base, what):
        for d in range(1, INNER):
            what(remote(src, buf.at[q], p_s.at[base, d - 1], p_r.at[base, d - 1], near[d - 1], c))

    def plane_waits(src, buf, base):
        for d in range(1, INNER):
            remote(
                src,
                buf.at[lax.rem(near[d - 1], INNER)],
                p_s.at[base, d - 1],
                p_r.at[base, d - 1],
                near[d - 1],
                c,
            ).wait_recv()

    def pair_copy(src, dst, place):
        return remote(src, dst, s_s.at[place], s_r.at[place], b, 1 - c)

    start = lambda copy: copy.start()
    chain_sends(pay, z_in, 0, start)
    z_in[o] = pay[...]
    pair_copy(terms, terms_in, 0).start()

    lane_r = lax.broadcasted_iota(jnp.int32, (R, 128), 1)
    head_square = jnp.zeros((R, WIDE), jnp.float32)
    cut_square = jnp.zeros((R, WIDE), jnp.float32)
    for part in range(INNER):
        for k in range(CHUNKS):
            gradient = gr[k, part].astype(jnp.float32)
            if k < HEADS_DEV:
                head_square = head_square + squares(gradient)
            else:
                cut_square = cut_square + squares(gradient)
    pieces = (
        jnp.sum(head_square[:, : 3 * HD], axis=1, keepdims=True),
        jnp.sum(cut_square[:, :CUT], axis=1, keepdims=True),
        jnp.sum(head_square[:, 3 * HD :], axis=1, keepdims=True),
        jnp.sum(cut_square[:, CUT:], axis=1, keepdims=True),
    )
    line = jnp.zeros((R, 128), jnp.float32)
    for place, value in enumerate(pieces):
        line = jnp.where(lane_r == place, value, line)
    rsum[...] = line
    pair_copy(rsum, rsum_in, 1).start()

    pair_copy(terms, terms_in, 0).wait_recv()
    for i in range(2):
        rows = slice(i * HALF_T, (i + 1) * HALF_T)
        both = terms[rows, :] + terms_in[rows, :]
        ing_ref[rows, :] = (
            st[rows, 1:2]
            * (
                scaled_buf[rows, :]
                - both[:, 0:1] / D
                - normed_buf[rows, :] * (both[:, 1:2] / D)
            )
            + yin[rows, :].astype(jnp.float32)
        ).astype(jnp.bfloat16)
    pair_copy(rsum, rsum_in, 1).wait_recv()
    rows_after = renew_stat(row_old[...], (rsum[...] + rsum_in[...])[:, :4])
    row_new[...] = jnp.concatenate(
        [rows_after, jnp.zeros((R, 128 - 4), jnp.float32)], axis=1
    )

    chain_waits(pay, z_in, 0)
    acc = z_in[0]
    for j in range(1, outer):
        acc = acc + z_in[j]
    z_sum[...] = acc
    plane_sends(z_sum, p_in, 0, start)
    p_in[q] = acc
    plane_waits(z_sum, p_in, 0)
    p_sum[...] = p_in[0] + p_in[1] + p_in[2] + p_in[3]
    pair_copy(p_sum, s_in, 2).start()

    inverse_rows = 1.0 / rows_after
    head_acc = [jnp.zeros((R, 3 * HD), jnp.float32), jnp.zeros((R, HD), jnp.float32)]
    cut_acc = [jnp.zeros((R, CUT), jnp.float32), jnp.zeros((R, CUT), jnp.float32)]
    for part in range(INNER):
        sums = p_in[part]
        for h in range(HEADS_DEV):
            gradient = gr[h, part].astype(jnp.float32)
            square = gradient * gradient
            found = sums[h // 2 : h // 2 + 1, h % 2 * WIDE : (h % 2 + 1) * WIDE]
            cols = pl.ds(part * HEADS_DEV * HD + h * HD, HD)
            parts = []
            for p in range(3):
                fresh = renew_stat(qc_old[p : p + 1, cols], found[:, p * HD : (p + 1) * HD])
                qc_new[p : p + 1, cols] = fresh
                parts.append(1.0 / fresh)
            head_acc[0] = head_acc[0] + square[:, : 3 * HD] * jnp.concatenate(parts, axis=1)
            fresh = renew_stat(or_old[:, cols], found[:, 3 * HD :])
            or_new[:, cols] = fresh
            head_acc[1] = head_acc[1] + square[:, 3 * HD :] * (1.0 / fresh)
        for f in range(CUTS):
            k = HEADS_DEV + f
            gradient = gr[k, part].astype(jnp.float32)
            square = gradient * gradient
            found = sums[k // 2 : k // 2 + 1, k % 2 * WIDE : (k % 2 + 1) * WIDE]
            cols = slice(f * CUT, (f + 1) * CUT)
            fresh = renew_stat(f1_old[part : part + 1, cols], found[:, :CUT])
            f1_new[part, :, cols] = fresh
            cut_acc[0] = cut_acc[0] + square[:, :CUT] * (1.0 / fresh)
            fresh = renew_stat(f2_old[part : part + 1, cols], found[:, CUT:])
            f2_new[part, :, cols] = fresh
            cut_acc[1] = cut_acc[1] + square[:, CUT:] * (1.0 / fresh)
    for part in range(INNER):
        for h in range(HEADS_DEV):
            for p in range(3):
                low = h * 3 * HD + p * HD
                bias_grad[p : p + 1, pl.ds(part * HEADS_DEV * HD + h * HD, HD)] = p_in[
                    part, 3:4, low : low + HD
                ]
        fcb_grad[part : part + 1, :] = p_in[part, 4:5, :]
    bias_grad[3:4, :] = p_sum[9:10, :]
    bias_grad[4:5, :] = p_sum[9:10, :]
    bias_after, bias_update = second_step(bias_grad[...], bias_second[...])
    bias_moment[...] = bias_after
    fcb_after, fcb_update = second_step(fcb_grad[...], fcb_second[...])
    fcb_moment[...] = fcb_after
    usq = jnp.sum(bias_update * bias_update, axis=1, keepdims=True) * on_b
    scalars = (
        [
            total_of(rows_after[:, 0:1]) * on_c,
            total_of(head_acc[0] * inverse_rows[:, 0:1]),
            total_of(rows_after[:, 1:2]) * on_c,
            total_of(cut_acc[0] * inverse_rows[:, 1:2]),
            total_of(or_new[...]) * on_b,
            total_of(head_acc[1] * inverse_rows[:, 2:3]),
            sum(total_of(f2_new[part]) for part in range(INNER)) * on_b,
            total_of(cut_acc[1] * inverse_rows[:, 3:4]),
        ]
        + [usq[i : i + 1] for i in range(5)]
        + [total_of(fcb_update * fcb_update) * on_b]
    )
    lane_s = lax.broadcasted_iota(jnp.int32, (8, 128), 1)
    line = jnp.zeros((8, 128), jnp.float32)
    for place, value in enumerate(scalars):
        line = jnp.where(lane_s == place, value, line)
    pay2[...] = line
    chain_sends(pay2, z2_in, 1, start)
    z2_in[o] = line

    pair_copy(p_sum, s_in, 2).wait_recv()
    norm_grad[:, own_half] = p_sum[5:9, :]
    norm_grad[:, other_half] = s_in[5:9, :]
    old = p_sum[10:11, :] + s_in[10:11, :]
    norm_after, norm_update = second_step(norm_grad[...], norm_second[...])
    norm_moment[...] = norm_after

    def moved(vector, update, update_square, old_square, entries):
        clip_factor = jnp.maximum(1.0, jnp.sqrt(update_square / entries))
        step_rate = RATE * jnp.maximum(FLOOR_RATE, jnp.sqrt(old_square / entries))
        return vector - step_rate * update / clip_factor

    norm_values = norm_ref[...]
    norm_new[...] = moved(
        norm_values,
        norm_update,
        jnp.sum(norm_update * norm_update, axis=1, keepdims=True),
        jnp.sum(norm_values * norm_values, axis=1, keepdims=True),
        D,
    )

    chain_waits(pay2, z2_in, 1)
    acc = z2_in[0]
    for j in range(1, outer):
        acc = acc + z2_in[j]
    z2_sum[...] = acc
    plane_sends(z2_sum, p2_in, 1, start)
    p2_in[q] = acc
    plane_waits(z2_sum, p2_in, 1)
    acc = p2_in[0] + p2_in[1] + p2_in[2] + p2_in[3]
    p2_sum[...] = acc
    pair_copy(p2_sum, s2_in, 3).start()
    pair_copy(p2_sum, s2_in, 3).wait_recv()
    sums = (acc + s2_in[...])[0:1, :]

    def scalar(place):
        return sums[:, place : place + 1]

    def factor(total, inverse, place, entries):
        clip_factor = jnp.maximum(1.0, jnp.sqrt(total * inverse / entries))
        rate = RATE * jnp.maximum(FLOOR_RATE, jnp.sqrt(old[:, place : place + 1] / entries))
        return rate * jnp.sqrt(total) / clip_factor

    factors = (
        factor(scalar(0), scalar(1), 0, 3 * D * D),
        factor(scalar(2), scalar(3), 2, D * FF),
        factor(scalar(4), scalar(5), 1, D * D),
        factor(scalar(6), scalar(7), 3, FF * D),
    )
    line = jnp.zeros((8, 128), jnp.float32)
    for place, value in enumerate(factors):
        line = jnp.where(lane_s == place, value, line)
    coef[...] = line
    for i in range(5):
        bias_new[i : i + 1, :] = moved(
            pb[i : i + 1, :], bias_update[i : i + 1], scalar(8 + i), old[:, 4 + i : 5 + i], D
        )
    fcb_new[...] = moved(fcb[...], fcb_update, scalar(13), old[:, 9:10], FF)

    finish = lambda copy: copy.wait_send()
    chain_sends(pay, z_in, 0, finish)
    chain_sends(pay2, z2_in, 1, finish)
    plane_sends(z_sum, p_in, 0, finish)
    plane_sends(z2_sum, p2_in, 1, finish)
    pair_copy(terms, terms_in, 0).wait_send()
    pair_copy(rsum, rsum_in, 1).wait_send()
    pair_copy(p_sum, s_in, 2).wait_send()
    pair_copy(p2_sum, s2_in, 3).wait_send()


def tail_call(count, *args):
    outer = count // INNER
    received, xin = args[0], args[7]
    tokens, half = xin.shape
    rows = received.shape[2]
    high = jnp.float32
    spec = pl.BlockSpec(memory_space=pltpu.VMEM)
    dma = pltpu.SemaphoreType.DMA

    def out(*shape, dtype=high):
        return jax.ShapeDtypeStruct(shape, dtype)

    outs = [
        out(tokens, half, dtype=jnp.bfloat16),
        out(tokens, half, dtype=jnp.bfloat16),
        out(rows, 128),
        out(3, half),
        out(1, half),
        out(INNER, 1, half),
        out(INNER, 1, half),
        out(4, D),
        out(4, D),
        out(4, D),
        out(5, half),
        out(5, half),
        out(5, half),
        out(INNER, half),
        out(INNER, half),
        out(INNER, half),
        out(8, 128),
    ]
    slot = (SLOT_ROWS, half)
    return pl.pallas_call(
        functools.partial(tail_kernel, count),
        out_shape=outs,
        in_specs=[spec] * len(args),
        out_specs=[spec] * len(outs),
        scratch_shapes=[
            pltpu.VMEM((tokens, half), high),
            pltpu.VMEM((tokens, half), high),
            pltpu.VMEM((tokens, 128), high),
            pltpu.VMEM((tokens, 128), high),
            pltpu.VMEM((rows, 128), high),
            pltpu.VMEM((rows, 128), high),
            pltpu.VMEM(slot, high),
            pltpu.VMEM((outer, *slot), high),
            pltpu.VMEM(slot, high),
            pltpu.VMEM((INNER, *slot), high),
            pltpu.VMEM(slot, high),
            pltpu.VMEM(slot, high),
            pltpu.VMEM((8, 128), high),
            pltpu.VMEM((outer, 8, 128), high),
            pltpu.VMEM((8, 128), high),
            pltpu.VMEM((INNER, 8, 128), high),
            pltpu.VMEM((8, 128), high),
            pltpu.VMEM((8, 128), high),
            dma((2, outer - 1)),
            dma((2, outer - 1)),
            dma((2, INNER - 1)),
            dma((2, INNER - 1)),
            dma((4,)),
            dma((4,)),
        ],
        compiler_params=pltpu.CompilerParams(
            collective_id=1, has_side_effects=True, vmem_limit_bytes=58 * 1024 * 1024
        ),
        cost_estimate=pl.CostEstimate(
            flops=50_000_000, bytes_accessed=40_000_000, transcendentals=100_000
        ),
    )(*args)


def update_kernel(*refs):
    gr, wq, wo, w1, w2, row_new, coef = refs[:7]
    small = refs[7:22]
    qc_new, or_new, f1_new, f2_new = small[2:6]
    q_grad, q_next, q_copy, o_grad, o_next, o_copy = refs[22:28]
    f1_grad, f1_next, f1_copy, f2_grad, f2_next, f2_copy = refs[28:34]
    row_out, small_out = refs[34:38], refs[38:]
    part = pl.program_id(0)
    side = lax.rsqrt(row_new[:, :4]) * coef[0:1, :4]
    width_q = HEADS_DEV * HD

    @pl.when(part == 0)
    def _():
        for source, target in zip(small, small_out):
            target[...] = source[...]
        turned = row_new[...].T
        for place in range(4):
            row_out[place][...] = turned[place : place + 1, :]

    def put(grad_ref, next_ref, copy_ref, where, weight, gradient, update):
        fresh = weight[where] - update
        grad_ref[where] = gradient
        next_ref[where] = fresh
        copy_ref[where] = fresh.astype(jnp.bfloat16)

    for h in range(HEADS_DEV):
        gradient = gr[h, 0].astype(jnp.float32)
        cols = pl.ds(pl.multiple_of(part * width_q + h * HD, HD), HD)
        for p in range(3):
            mine = gradient[:, p * HD : (p + 1) * HD]
            update = mine * side[:, 0:1] * lax.rsqrt(qc_new[p : p + 1, cols])
            where = (p, slice(None), slice(h * HD, (h + 1) * HD))
            put(q_grad, q_next, q_copy, where, wq, mine, update)
        mine = gradient[:, 3 * HD :]
        update = mine * side[:, 2:3] * lax.rsqrt(or_new[:, cols])
        where = (slice(h * HD, (h + 1) * HD), slice(None))
        put(o_grad, o_next, o_copy, where, wo, mine.T, update.T)
    for f in range(CUTS):
        gradient = gr[HEADS_DEV + f, 0].astype(jnp.float32)
        cols = slice(f * CUT, (f + 1) * CUT)
        mine = gradient[:, :CUT]
        update = mine * side[:, 1:2] * lax.rsqrt(f1_new[part, :, cols])
        put(f1_grad, f1_next, f1_copy, (slice(None), cols), w1, mine, update)
        mine = gradient[:, CUT:]
        update = mine * side[:, 3:4] * lax.rsqrt(f2_new[part, :, cols])
        put(f2_grad, f2_next, f2_copy, (cols, slice(None)), w2, mine.T, update.T)


def update_call(gr, wq, wo, w1, w2, row_new, coef, *small):
    rows = gr.shape[2]
    width_q = HEADS_DEV * HD
    hidden_q = CUTS * CUT
    spec = pl.BlockSpec
    q_spec = spec((3, rows, width_q), lambda i: (0, 0, i))
    o_spec = spec((width_q, rows), lambda i: (i, 0))
    f1_spec = spec((rows, hidden_q), lambda i: (0, i))
    f2_spec = spec((hidden_q, rows), lambda i: (i, 0))
    outs, out_specs = [], []
    for array, its in ((wq, q_spec), (wo, o_spec), (w1, f1_spec), (w2, f2_spec)):
        for dtype in (jnp.float32, jnp.float32, jnp.bfloat16):
            outs.append(jax.ShapeDtypeStruct(array.shape, dtype))
            out_specs.append(its)

    def fixed(shape):
        return spec(shape, lambda i: (0,) * len(shape))

    for _ in range(4):
        outs.append(jax.ShapeDtypeStruct((1, rows), jnp.float32))
        out_specs.append(fixed((1, rows)))
    for array in small:
        outs.append(jax.ShapeDtypeStruct(array.shape, array.dtype))
        out_specs.append(fixed(array.shape))
    return pl.pallas_call(
        update_kernel,
        grid=(INNER,),
        out_shape=outs,
        in_specs=[
            spec((CHUNKS, 1, rows, WIDE), lambda i: (0, i, 0, 0)),
            q_spec,
            o_spec,
            f1_spec,
            f2_spec,
            fixed((rows, 128)),
            fixed((8, 128)),
        ]
        + [fixed(array.shape) for array in small],
        out_specs=out_specs,
        compiler_params=pltpu.CompilerParams(vmem_limit_bytes=48 * 1024 * 1024),
        cost_estimate=pl.CostEstimate(
            flops=20_000_000, bytes_accessed=30_000_000, transcendentals=100_000
        ),
    )(gr, wq, wo, w1, w2, row_new, coef, *small)


def swap_pairs(count, step):
    return [(i, i ^ step) for i in range(count)]


def block_of(array, index, size, axis=0):
    return lax.dynamic_slice_in_dim(array, index * size, size, axis)


def on_device(
    inputs,
    cotangent,
    segment_ids,
    w_qkv,
    w_out,
    w_fc1,
    w_fc2,
    norm_params,
    proj_bias,
    fc1_bias,
    qkv_rows,
    qkv_cols,
    out_rows,
    out_cols,
    fc1_rows,
    fc1_cols,
    fc2_rows,
    fc2_cols,
    norm_second,
    bias_second,
    fc1b_second,
):
    tokens = inputs.shape[0]
    local_width = inputs.shape[1]
    local_hidden = fc1_bias.shape[0]
    rows = w_qkv.shape[0]
    count = lax.axis_size("batch")
    c = lax.axis_index("branch")
    b = lax.axis_index("batch")
    q = lax.rem(b, INNER)
    group = INNER * tokens
    width_q = local_width // INNER
    hidden_q = local_hidden // INNER
    qkv_low = w_qkv.astype(jnp.bfloat16).reshape(rows, 3, INNER, HEADS_DEV, HD)
    out_low = w_out.astype(jnp.bfloat16).reshape(INNER, HEADS_DEV, HD, rows)
    fc1_low = w_fc1.astype(jnp.bfloat16).reshape(rows, INNER, CUTS, CUT)
    fc2_low = w_fc2.astype(jnp.bfloat16).reshape(INNER, CUTS, CUT, rows)
    heads_low = jnp.concatenate(
        [
            qkv_low.transpose(3, 2, 0, 1, 4).reshape(HEADS_DEV, INNER, rows, 3 * HD),
            out_low.transpose(1, 0, 3, 2),
        ],
        axis=3,
    )
    cuts_low = jnp.concatenate(
        [fc1_low.transpose(2, 1, 0, 3), fc2_low.transpose(1, 0, 3, 2)], axis=3
    )
    wst = jnp.concatenate([heads_low, cuts_low], axis=0)

    segment = jnp.concatenate(
        [segment_ids]
        + [lax.ppermute(segment_ids, "batch", swap_pairs(count, d)) for d in range(1, INNER)],
        axis=0,
    )
    positions_idx = jnp.arange(tokens)
    earlier = jnp.sum((segment[:, None, :] < segment[:, :, None]).astype(jnp.int32), axis=2)
    starts = earlier.astype(jnp.float32).reshape(1, group)
    places = (positions_idx[None] - earlier).astype(jnp.float32).reshape(1, group)
    frequency = 10000.0 ** (-2.0 * jnp.arange(ROT // 2, dtype=jnp.float32) / ROT)
    angles = frequency[:, None] * places
    cos_part = jnp.cos(angles)
    sin_part = jnp.sin(angles)
    turns = jnp.concatenate(
        [
            cos_part,
            cos_part,
            -sin_part,
            sin_part,
            jnp.broadcast_to(starts, (HD - 2 * ROT, group)),
        ],
        axis=0,
    )
    bias_h = (
        block_of(proj_bias[0:3], q, width_q, 1)
        .reshape(3, HEADS_DEV, HD)
        .transpose(1, 0, 2)
        .reshape(HEADS_DEV, 1, 3 * HD)
    )
    bias_f = block_of(fc1_bias, q, hidden_q).reshape(CUTS, 1, CUT)
    received, plane_parts, plane_own, head_bias, cut_bias, col_sums, row_moments = block_call(
        count, wst, inputs, cotangent, turns, norm_params, bias_h, bias_f
    )
    by_part = (INNER, hidden_q)
    qkv_parts = w_qkv.transpose(1, 0, 2)
    (
        output,
        input_grad,
        row_stats,
        qkv_cols_new,
        out_rows_new,
        fc1_cols_new,
        fc2_rows_new,
        norm_grad,
        norm_moment,
        norm_new,
        bias_grad,
        bias_moment,
        bias_new,
        fc1b_grad,
        fc1b_moment,
        fc1b_new,
        factors,
    ) = tail_call(
        count,
        received,
        qkv_parts.reshape(3 * rows, local_width),
        w_out,
        w_fc1,
        w_fc2,
        plane_parts,
        plane_own,
        inputs,
        cotangent,
        row_moments,
        norm_params,
        proj_bias,
        fc1_bias.reshape(by_part),
        jnp.stack([qkv_rows, fc1_rows, out_cols, fc2_cols], axis=1),
        qkv_cols,
        out_rows.reshape(1, local_width),
        fc1_cols.reshape(by_part),
        fc2_rows.reshape(by_part),
        norm_second,
        bias_second,
        fc1b_second.reshape(by_part),
        col_sums,
        head_bias,
        cut_bias,
    )
    small = (
        output,
        input_grad,
        qkv_cols_new,
        out_rows_new,
        fc1_cols_new,
        fc2_rows_new,
        norm_grad,
        norm_moment,
        norm_new,
        bias_grad,
        bias_moment,
        bias_new,
        fc1b_grad,
        fc1b_moment,
        fc1b_new,
    )
    updated = update_call(
        received, qkv_parts, w_out, w_fc1, w_fc2, row_stats, factors, *small
    )
    qkv_grad, qkv_next, qkv_copy = (array.transpose(1, 0, 2) for array in updated[0:3])
    out_grad, out_next, out_copy = updated[3:6]
    fc1_grad, fc1_next, fc1_copy = updated[6:9]
    fc2_grad, fc2_next, fc2_copy = updated[9:12]
    qkv_rows_new, fc1_rows_new, out_cols_new, fc2_cols_new = (
        array.reshape(rows) for array in updated[12:16]
    )
    (
        output,
        input_grad,
        qkv_cols_new,
        out_rows_new,
        fc1_cols_new,
        fc2_rows_new,
        norm_grad,
        norm_moment,
        norm_new,
        bias_grad,
        bias_moment,
        bias_new,
        fc1b_grad,
        fc1b_moment,
        fc1b_new,
    ) = updated[16:]
    return (
        output,
        input_grad,
        qkv_grad,
        qkv_next,
        qkv_rows_new,
        qkv_cols_new,
        qkv_copy,
        out_grad,
        out_next,
        out_rows_new.reshape(local_width),
        out_cols_new,
        out_copy,
        fc1_grad,
        fc1_next,
        fc1_rows_new,
        fc1_cols_new.reshape(local_hidden),
        fc1_copy,
        fc2_grad,
        fc2_next,
        fc2_rows_new.reshape(local_hidden),
        fc2_cols_new,
        fc2_copy,
        norm_grad,
        norm_moment,
        norm_new,
        bias_grad,
        bias_moment,
        bias_new,
        fc1b_grad.reshape(local_hidden),
        fc1b_moment.reshape(local_hidden),
        fc1b_new.reshape(local_hidden),
    )


def solution(mesh):
    in_specs = (
        P("batch", "branch"),
        P("batch", "branch"),
        P("batch", None),
        P("batch", None, "branch"),
        P("branch", "batch"),
        P("batch", "branch"),
        P("branch", "batch"),
        P(),
        P(None, "branch"),
        P("branch"),
        P("batch"),
        P(None, "branch"),
        P("branch"),
        P("batch"),
        P("batch"),
        P("branch"),
        P("branch"),
        P("batch"),
        P(),
        P(None, "branch"),
        P("branch"),
    )
    out_specs = (
        P("batch", "branch"),
        P("batch", "branch"),
        P("batch", None, "branch"),
        P("batch", None, "branch"),
        P("batch"),
        P(None, "branch"),
        P("batch", None, "branch"),
        P("branch", "batch"),
        P("branch", "batch"),
        P("branch"),
        P("batch"),
        P("branch", "batch"),
        P("batch", "branch"),
        P("batch", "branch"),
        P("batch"),
        P("branch"),
        P("batch", "branch"),
        P("branch", "batch"),
        P("branch", "batch"),
        P("branch"),
        P("batch"),
        P("branch", "batch"),
        P(),
        P(),
        P(),
        P(None, "branch"),
        P(None, "branch"),
        P(None, "branch"),
        P("branch"),
        P("branch"),
        P("branch"),
    )
    return jax.shard_map(
        on_device, mesh=mesh, in_specs=in_specs, out_specs=out_specs, check_vma=False
    )
```

```python
import functools

import jax
import jax.numpy as jnp
from jax import lax
from jax.experimental import pallas as pl
from jax.experimental.pallas import tpu as pltpu
from jax.sharding import PartitionSpec as P

D = 2048
HD = 128
ROT = 32
FF = 8192
STEP = 10


EPS_NORM = 1e-05
EPS_SQUARE = 1e-30
RATE = 0.3
FLOOR_RATE = 0.001


def decay_rate():
    return 1.0 - STEP ** (-0.8)


def squares(gradient):
    return gradient * gradient + EPS_SQUARE


def renew_stat(old_stat, new_sum):
    decay = decay_rate()
    return decay * old_stat + (1.0 - decay) * new_sum


def second_step(gradient, second):
    second_new = renew_stat(second, squares(gradient))
    return (second_new, gradient * lax.rsqrt(second_new))


INNER = 4
HEADS_DEV = 2
CUTS = 4
CHUNKS = HEADS_DEV + CUTS
CUT = 256
WIDE = 512
MESH = pl.DeviceIdType.MESH


def flip(index, step):
    return index + step * (1 - 2 * lax.rem(index // step, 2))


def nn(left, right):
    return jnp.dot(left, right, preferred_element_type=jnp.float32)


def nt(left, right):
    return lax.dot_general(
        left, right, (((1,), (1,)), ((), ())), preferred_element_type=jnp.float32
    )


def tn(left, right):
    return lax.dot_general(
        left, right, (((0,), (0,)), ((), ())), preferred_element_type=jnp.float32
    )


def block_kernel(
    count,
    wst,
    xin,
    yin,
    turn_ref,
    norm_ref,
    bias_h,
    bias_f,
    gr,
    xr,
    xo,
    qb,
    fb,
    cs,
    st,
    H1,
    H2,
    DY,
    W,
    TA,
    G,
    sbuf,
    fbuf,
    rsb,
    sib_send,
    sib_land,
    own,
    a2a_s,
    a2a_r,
    loc_s,
    ag_s,
    ag_r,
    x_s,
    x_r,
    sx_s,
    sx_r,
    rs_s,
    rs_r,
    gr_s,
    gr_r,
    sib_s,
    sib_r,
    p_s,
    p_r,
    tmp_s,
    free_s,
):
    outer = count // INNER
    S = outer - 1
    T, half = xin.shape
    R = wst.shape[2]
    block = INNER * R
    QT = T // 2
    b = lax.axis_index("batch")
    c = lax.axis_index("branch")
    q = lax.rem(b, INNER)
    o = b // INNER
    bx, by = flip(b, 1), flip(b, 2)
    bxy = flip(bx, 2)
    near = (bx, by, bxy)
    da = 1 + c
    db = 2 - c
    b_first = bx * (1 - c) + by * c
    b_second = by * (1 - c) + bx * c

    def remote(src, dst, ssem, rsem, to_b, to_c):
        return pltpu.make_async_remote_copy(
            src_ref=src,
            dst_ref=dst,
            send_sem=ssem,
            recv_sem=rsem,
            device_id=(to_b, to_c),
            device_id_type=MESH,
        )

    barrier = pltpu.get_barrier_semaphore()
    for who in near:
        pl.semaphore_signal(barrier, inc=1, device_id=(who, c), device_id_type=MESH)
    pl.semaphore_signal(barrier, inc=1, device_id=(b, 1 - c), device_id_type=MESH)

    @pl.when(o > 0)
    def _():
        pl.semaphore_signal(barrier, inc=1, device_id=(b - INNER, c), device_id_type=MESH)

    @pl.when(o < outer - 1)
    def _():
        pl.semaphore_signal(barrier, inc=1, device_id=(b + INNER, c), device_id_type=MESH)

    pl.semaphore_wait(barrier, 4 + jnp.minimum(o, 1) + jnp.minimum(outer - 1 - o, 1))

    def a2a_copy(k, d, received=False):
        to = near[d - 1]
        row = (to if received else b) * R
        return remote(
            wst.at[k, lax.rem(to, INNER)],
            W.at[k, pl.ds(pl.multiple_of(row, 16), R)],
            a2a_s.at[k, d - 1],
            a2a_r.at[k, d - 1],
            to,
            c,
        )

    def a2a_local(k):
        return pltpu.make_async_copy(
            wst.at[k, q], W.at[k, pl.ds(pl.multiple_of(b * R, 16), R)], loc_s.at[k]
        )

    def a2a_start(k):
        for d in range(1, INNER):
            a2a_copy(k, d).start()
        a2a_local(k).start()

    def a2a_wait(k):
        for d in range(1, INNER):
            a2a_copy(k, d, True).wait_recv()
        a2a_local(k).wait()

    def ag_copy(k, way, s, part):
        rows = pl.ds(pl.multiple_of(part * block, 16), block)
        to = b + INNER if way == 0 else b - INNER
        return remote(
            W.at[k, rows], W.at[k, rows], ag_s.at[k, way, s - 1], ag_r.at[k, way, s - 1], to, c
        )

    def ag_sends(k, s, what):
        @pl.when((o >= s - 1) & (o <= outer - 2))
        def _():
            what(ag_copy(k, 0, s, o - s + 1))

        @pl.when((o >= 1) & (o <= outer - s))
        def _():
            what(ag_copy(k, 1, s, o + s - 1))

    def ag_wait(k, s):
        @pl.when(o >= s)
        def _():
            ag_copy(k, 0, s, o - s).wait_recv()

        @pl.when(o <= outer - 1 - s)
        def _():
            ag_copy(k, 1, s, o + s).wait_recv()

    def ag_range(low, high):
        def step(n, carry):
            k = n // S
            s = lax.rem(n, S) + 1

            @pl.when(s == 1)
            def _():
                a2a_wait(k)

            @pl.when(s > 1)
            def _():
                ag_wait(k, s - 1)

            ag_sends(k, s, lambda copy: copy.start())
            return carry

        lax.fori_loop(low, high, step, 0)

    def ag(low, high):
        ag_range(low * S // 3, high * S // 3)

    def spot(buf, slot):
        return buf.at[
            pl.ds(pl.multiple_of(slot * T, 16), T), pl.ds(pl.multiple_of(c * half, 128), half)
        ]

    def other_spot(buf, slot):
        return buf.at[
            pl.ds(pl.multiple_of(slot * T, 16), T), pl.ds(pl.multiple_of((1 - c) * half, 128), half)
        ]

    def sx_copy(i, buf, slot, src=None):
        place = spot(buf, slot)
        return remote(place if src is None else src, place, sx_s.at[i, slot], sx_r.at[i, slot], b, 1 - c)

    def sx_wait(i, buf, slot):
        remote(
            other_spot(buf, slot), other_spot(buf, slot), sx_s.at[i, slot], sx_r.at[i, slot], b, 1 - c
        ).wait_recv()

    def x_first(i, src, buf):
        return remote(src, spot(buf, da), x_s.at[i, da - 1], x_r.at[i, da - 1], b_first, c)

    def x_second(i, src, buf):
        return remote(src, spot(buf, db), x_s.at[i, db - 1], x_r.at[i, db - 1], b_second, c)

    def x_forward(i, buf):
        return remote(spot(buf, da), spot(buf, 3), x_s.at[i, 2], x_r.at[i, 2], b_second, c)

    def x_diag(i, buf):
        return remote(spot(buf, 3), spot(buf, 3), x_s.at[i, 2], x_r.at[i, 2], b_second, c)

    def x_local(i, src, buf):
        return pltpu.make_async_copy(src, spot(buf, 0), tmp_s.at[i])

    def gather_one(i, src, buf):
        x_first(i, src, buf).start()
        x_local(i, src, buf).start()
        sx_copy(i, buf, 0, src).start()

    def gather_two(i, src, buf):
        x_first(i, src, buf).wait_recv()
        x_second(i, src, buf).start()
        x_forward(i, buf).start()
        sx_copy(i, buf, da).start()

    def gather_three(i, src, buf):
        x_second(i, src, buf).wait_recv()
        sx_copy(i, buf, db).start()
        x_diag(i, buf).wait_recv()
        sx_copy(i, buf, 3).start()

    def gather_sent(i, src, buf):
        x_first(i, src, buf).wait_send()
        x_second(i, src, buf).wait_send()
        x_forward(i, buf).wait_send()
        sx_copy(i, buf, 0, src).wait_send()
        for slot in range(1, INNER):
            sx_copy(i, buf, slot).wait_send()

    lane_n = lax.broadcasted_iota(jnp.int32, (64, 128), 1)

    def norm_rows(slot):
        def step(i, carry):
            rows = pl.ds(pl.multiple_of(slot * T + i * 64, 64), 64)
            values = H1[rows, :].astype(jnp.float32)
            mean = jnp.mean(values, axis=-1, keepdims=True)
            centered = values - mean
            inverse = lax.rsqrt(jnp.mean(centered * centered, axis=-1, keepdims=True) + EPS_NORM)
            normed = centered * inverse
            if slot == 0:
                st[pl.ds(pl.multiple_of(i * 64, 64), 64), :] = jnp.where(lane_n == 0, mean, inverse)
            H1[rows, :] = (normed * norm_ref[0:1, :] + norm_ref[1:2, :]).astype(jnp.bfloat16)
            H2[rows, :] = (normed * norm_ref[2:3, :] + norm_ref[3:4, :]).astype(jnp.bfloat16)
            return carry

        lax.fori_loop(0, T // 64, step, 0)

    lane = lax.broadcasted_iota(jnp.int32, (T, HD), 1)
    scale = HD ** (-0.5)

    def partner(tensor):
        return jnp.where(
            lane < ROT // 2,
            pltpu.roll(tensor, HD - ROT // 2, 1),
            jnp.where(lane < ROT, pltpu.roll(tensor, ROT // 2, 1), 0.0),
        )

    def turns_of(rows):
        table = turn_ref[:, rows].T
        cos_rows = jnp.where(lane < ROT, table, 1.0)
        sin_rows = pltpu.roll(table, HD - ROT, 1)
        return cos_rows, sin_rows, table[:, 2 * ROT : 2 * ROT + 1]

    def probs_at(h, slot, i):
        seen = QT * (i + 1)
        wide = min(block, seen)
        part = slice(QT * i, QT * (i + 1))
        base = slot * (outer // INNER)
        return [(h, base + j, part, slice(0, wide)) for j in range(seen // wide)]

    def forward_piece(h, slot):
        start = pl.multiple_of(slot * T, 128)
        rows = pl.ds(start, T)
        cos_rows, sin_rows, starts = turns_of(rows)
        projected = nn(H1[rows, :], W[h, :, : 3 * HD]) + bias_h[h]
        first = projected[:, :HD]
        queries = (first * cos_rows + partner(first) * sin_rows).astype(jnp.bfloat16)
        second = projected[:, HD : 2 * HD]
        keys = (second * cos_rows + partner(second) * sin_rows).astype(jnp.bfloat16)
        values = projected[:, 2 * HD :].astype(jnp.bfloat16)
        TA[h, :, pl.ds(start, HD)] = queries
        TA[h, :, pl.ds(start + HD, HD)] = keys
        TA[h, :, pl.ds(start + 2 * HD, HD)] = values
        for i in range(2):
            seen = QT * (i + 1)
            part = slice(QT * i, QT * (i + 1))
            raw = nt(queries[part], keys[:seen]) * scale
            query_at = lax.broadcasted_iota(jnp.int32, (QT, seen), 0) + QT * i
            key_at = lax.broadcasted_iota(jnp.int32, (QT, seen), 1)
            allowed = (key_at <= query_at) & (key_at.astype(jnp.float32) >= starts[part])
            scores = jnp.where(allowed, raw, -1e30)
            exponent = jnp.exp(scores - jnp.max(scores, axis=-1, keepdims=True))
            probs = exponent * (1.0 / jnp.sum(exponent, axis=-1, keepdims=True))
            for j, place in enumerate(probs_at(h, slot, i)):
                wide = min(block, seen)
                G[place] = probs[:, j * wide : (j + 1) * wide]
            TA[h, part, pl.ds(start + 3 * HD, HD)] = nn(
                probs.astype(jnp.bfloat16), values[:seen]
            ).astype(jnp.bfloat16)

    def head_piece(h, slot):
        start = pl.multiple_of(slot * T, 128)
        rows = pl.ds(start, T)
        cos_rows, sin_rows, _ = turns_of(rows)
        queries = TA[h, :, pl.ds(start, HD)]
        keys = TA[h, :, pl.ds(start + HD, HD)]
        values = TA[h, :, pl.ds(start + 2 * HD, HD)]
        context = TA[h, :, pl.ds(start + 3 * HD, HD)]
        back = nn(DY[rows, :], W[h, :, 3 * HD :]).astype(jnp.bfloat16)
        grad_q = []
        grad_k, grad_v = [None, None], [None, None]
        for i in range(2):
            seen = QT * (i + 1)
            part = slice(QT * i, QT * (i + 1))
            probs = [G[place] for place in probs_at(h, slot, i)]
            probs = probs[0] if len(probs) == 1 else jnp.concatenate(probs, axis=1)
            soft = probs.astype(jnp.bfloat16)
            grad_probs = nt(back[part], values[:seen])
            inner = jnp.sum(probs * grad_probs, axis=-1, keepdims=True)
            grad_scores = (probs * (grad_probs - inner)).astype(jnp.bfloat16)
            grad_q.append((nn(grad_scores, keys[:seen]) * scale).astype(jnp.bfloat16))
            for j in range(i + 1):
                cut = slice(QT * j, QT * (j + 1))
                term_v = tn(soft[:, cut], back[part])
                term_k = tn(grad_scores[:, cut], queries[part])
                grad_v[j] = term_v if grad_v[j] is None else grad_v[j] + term_v
                grad_k[j] = term_k if grad_k[j] is None else grad_k[j] + term_k
        dq = jnp.concatenate(grad_q, axis=0).astype(jnp.float32)
        dk = (jnp.concatenate(grad_k, axis=0) * scale).astype(jnp.bfloat16).astype(jnp.float32)
        dv = jnp.concatenate(grad_v, axis=0)
        turned = jnp.concatenate(
            [
                dq * cos_rows - partner(dq) * sin_rows,
                dk * cos_rows - partner(dk) * sin_rows,
                dv,
            ],
            axis=1,
        ).astype(jnp.bfloat16)
        TA[h, : 3 * HD, rows] = turned.T
        TA[h, 3 * HD :, rows] = context.T
        total = jnp.sum(turned.astype(jnp.float32), axis=0, keepdims=True)
        qb[h] = jnp.where(slot == 0, total, qb[h] + total)

    def cut_piece(f, slot):
        rows = pl.ds(pl.multiple_of(slot * T, 128), T)
        k = HEADS_DEV + f
        pre = nn(H2[rows, :], W[k, :, :CUT]) + bias_f[f]
        grad = nn(DY[rows, :], W[k, :, CUT:])
        normal = 0.5 * (1.0 + lax.erf(pre * (0.5**0.5)))
        slope = normal + pre * (jnp.exp(-0.5 * pre * pre) * (0.5 * 0.7978845608028654))
        active = (pre * normal).astype(jnp.bfloat16)
        pulled = (grad * slope).astype(jnp.bfloat16)
        low = pl.multiple_of(f * WIDE, WIDE)
        H1[pl.ds(low, CUT), rows] = pulled.T
        H1[pl.ds(low + CUT, CUT), rows] = active.T
        total = jnp.sum(pulled.astype(jnp.float32), axis=0, keepdims=True)
        fb[f] = jnp.where(slot == 0, total, fb[f] + total)

    def grads(k, turned, left, edge):
        def step(j, carry):
            cols = pl.ds(pl.multiple_of(j * block, 128), block)
            G[lax.rem(k, 2), j, :edge, :] = nn(turned(0, edge), left[:, cols])
            G[lax.rem(k, 2), j, edge:, :] = nn(turned(edge, WIDE - edge), DY[:, cols])
            return carry

        lax.fori_loop(0, outer, step, 0)

    def head_turned(h):
        return lambda low, size: TA[h, pl.ds(low, size), :]

    def cut_turned(f):
        return lambda low, size: H1[pl.ds(pl.multiple_of(f * WIDE + low, 128), size), :]

    def rs_copy(k, way, t):
        to = b + INNER if way == 0 else b - INNER
        return remote(
            sbuf.at[way],
            rsb.at[way, t - 1],
            rs_s.at[k, way, t - 1],
            rs_r.at[k, way, t - 1],
            to,
            c,
        )

    def rs_sends(way, t):
        if way == 0:
            return (o <= t - 1) & (o <= outer - 2)
        return (o >= outer - t) & (o >= 1)

    def rs_receives(way, t):
        if way == 0:
            return (o >= 1) & (o <= t)
        return (o <= outer - 2) & (o >= outer - 1 - t)

    def rs_fetch(k, way, t):
        rs_copy(k, way, t).wait_recv()
        return rsb[way, t - 1].astype(jnp.float32)

    def rs_step(k, t):
        n = k * S + t - 1

        @pl.when((t == 1) & (k >= 1) & (o < outer - 1))
        def _():
            pl.semaphore_wait(free_s.at[0], 1)

        @pl.when((t == 1) & (k >= 1) & (o > 0))
        def _():
            pl.semaphore_wait(free_s.at[1], 1)

        before = jnp.maximum(n - 1, 0)
        k_before = before // S
        t_before = lax.rem(before, S) + 1
        for way in range(2):
            owner = o + outer - t if way == 0 else o - outer + t

            @pl.when((n >= 1) & rs_sends(way, t_before))
            def _():
                rs_copy(k_before, way, t_before).wait_send()

            @pl.when(rs_sends(way, t))
            def _():
                @pl.when(rs_receives(way, t - 1) & (t > 1))
                def _():
                    sbuf[way] = (
                        G[lax.rem(k, 2), owner] + rs_fetch(k, way, t - 1)
                    ).astype(jnp.bfloat16)

                @pl.when(jnp.logical_not(rs_receives(way, t - 1) & (t > 1)))
                def _():
                    sbuf[way] = G[lax.rem(k, 2), owner].astype(jnp.bfloat16)

                rs_copy(k, way, t).start()

    def gr_copy(k, d, received=False):
        to = near[d - 1]
        slot = lax.rem(to, INNER)
        return remote(
            fbuf.at[pl.ds(pl.multiple_of(slot * R, 16), R)],
            gr.at[k, slot if received else q],
            gr_s.at[k, d - 1],
            gr_r.at[k, d - 1],
            to,
            c,
        )

    def gr_local(k):
        return pltpu.make_async_copy(
            fbuf.at[pl.ds(pl.multiple_of(q * R, 16), R)],
            gr.at[k, q],
            gr_s.at[k, 3],
        )

    def gr_sent(k):
        for d in range(1, INNER):
            gr_copy(k, d).wait_send()
        gr_local(k).wait()

    def rs_final(k):
        for way in range(2):

            @pl.when(rs_receives(way, S))
            def _():
                G[lax.rem(k, 2), o] = G[lax.rem(k, 2), o] + rs_fetch(k, way, S)

        @pl.when((k < CHUNKS - 1) & (o > 0))
        def _():
            pl.semaphore_signal(
                free_s.at[0], inc=1, device_id=(b - INNER, c), device_id_type=MESH
            )

        @pl.when((k < CHUNKS - 1) & (o < outer - 1))
        def _():
            pl.semaphore_signal(
                free_s.at[1], inc=1, device_id=(b + INNER, c), device_id_type=MESH
            )

        @pl.when(k >= 1)
        def _():
            gr_sent(k - 1)

        final = G[lax.rem(k, 2), o].T
        cs[k] = jnp.sum(squares(final), axis=0, keepdims=True)
        fbuf[...] = final.astype(jnp.bfloat16)
        for d in range(1, INNER):
            gr_copy(k, d).start()
        gr_local(k).start()

    def rs_range(low, high):
        def step(n, carry):
            k = n // (S + 1)
            t = lax.rem(n, S + 1) + 1

            @pl.when(t <= S)
            def _():
                rs_step(k, t)

            @pl.when(t == S + 1)
            def _():
                rs_final(k)

            return carry

        lax.fori_loop(low, high, step, 0)

    TILE = T // 2
    TILES = 2 * INNER
    PER_ROW = D // TILE

    def tile_slot(i):
        return INNER - 1 - i // 2

    def product(which, i, side):
        at = pl.multiple_of(tile_slot(i) * T + lax.rem(i, 2) * TILE, 128)
        toks = pl.ds(at, TILE)
        features = pl.ds(pl.multiple_of(side * half, 128), half)
        terms = []
        if which == 0:
            for h in range(HEADS_DEV):
                terms.append((h, slice(0, 3 * HD), lambda h=h: TA[h, : 3 * HD, toks]))
        elif which == 1:
            for f in range(CUTS):
                low = f * WIDE
                terms.append(
                    (HEADS_DEV + f, slice(0, CUT), lambda low=low: H1[low : low + CUT, toks])
                )
        else:
            for h in range(HEADS_DEV):
                terms.append((h, slice(3 * HD, WIDE), lambda h=h: TA[h, 3 * HD :, toks]))
            for f in range(CUTS):
                low = f * WIDE + CUT
                terms.append(
                    (HEADS_DEV + f, slice(CUT, WIDE), lambda low=low: H1[low : low + CUT, toks])
                )
        for place, (k, cols, right) in enumerate(terms):
            term = nn(W[k, features, cols], right())
            own[...] = term if place == 0 else own[...] + term

    def sib_copy(which, i):
        return remote(
            sib_send.at[lax.rem(i, 2)],
            sib_land.at[lax.rem(i, 4)],
            sib_s.at[which, i],
            sib_r.at[which, i],
            b,
            1 - c,
        )

    def stage(which, i):
        if which == 0:
            return H1.at[pl.ds(half, half), pl.ds(pl.multiple_of(i * TILE, 128), TILE)]
        t = (which - 1) * (TILES - 2) + i
        return H2.at[
            pl.ds(pl.multiple_of(t // PER_ROW * half, 128), half),
            pl.ds(pl.multiple_of(lax.rem(t, PER_ROW) * TILE, 128), TILE),
        ]

    def plane_copy(which, i):
        slot = tile_slot(i)
        low, high = lax.rem(slot, 2), slot // 2
        to = b + low * (1 - 2 * lax.rem(b, 2)) + high * 2 * (1 - 2 * lax.rem(b // 2, 2))
        src = stage(which, i)
        return remote(
            src,
            xr.at[which, slot - 1, lax.rem(i, 2)],
            p_s.at[which, i],
            p_r.at[which, i],
            to,
            c,
        )

    def tile_a(which, i):
        @pl.when(i >= 2)
        def _():
            sib_copy(which, i - 2).wait_send()

        product(which, i, 1 - c)
        sib_send[lax.rem(i, 2)] = own[...].astype(jnp.bfloat16)
        sib_copy(which, i).start()

    def tile_b(which, i):
        product(which, i, c)
        sib_copy(which, i).wait_recv()

        @pl.when(i < TILES - 2)
        def _():
            total = (own[...] + sib_land[lax.rem(i, 4)].astype(jnp.float32)).astype(jnp.bfloat16)
            stage(which, i)[...] = total
            plane_copy(which, i).start()

        @pl.when(i >= TILES - 2)
        def _():
            own[...] = own[...] + sib_land[lax.rem(i, 4)].astype(jnp.float32)
            keep = pltpu.make_async_copy(own, xo.at[which, lax.rem(i, 2)], tmp_s.at[2])
            keep.start()
            keep.wait()

    def sum_tiles(which, beside):
        tile_a(which, 0)

        def step(i, carry):
            @pl.when(i < TILES - 1)
            def _():
                tile_a(which, i + 1)

            tile_b(which, i)
            beside(i)
            return carry

        lax.fori_loop(0, TILES, step, 0)

    def sib_sent(which):
        for i in range(TILES - 2, TILES):
            sib_copy(which, i).wait_send()

    def spread(first, last, i, pieces, run):
        steps = last - first
        run(
            first + (steps * i + pieces - 1) // pieces,
            first + (steps * (i + 1) + pieces - 1) // pieces,
        )

    def ag_share(low, high, i, pieces):
        spread(low * S // 3, high * S // 3, i, pieces, ag_range)

    def rs_share(low, high, i, pieces):
        spread(low * (S + 1) // 4, high * (S + 1) // 4, i, pieces, rs_range)

    a2a_start(0)
    gather_one(0, xin, H1)
    gather_one(1, yin, DY)
    ag(0, 1)
    a2a_start(1)
    gather_two(0, xin, H1)
    gather_two(1, yin, DY)
    ag(1, 2)
    a2a_start(2)
    x_local(0, xin, H1).wait()
    sx_wait(0, H1, 0)
    norm_rows(0)
    ag(2, 3)
    gather_three(0, xin, H1)
    gather_sent(0, xin, H1)
    for k in range(3, CHUNKS):
        a2a_start(k)
    for slot in range(1, INNER):
        sx_wait(0, H1, slot)
        norm_rows(slot)
        if slot < 3:
            ag(2 + slot, 3 + slot)

    def project_step(h):
        ag_wait(h, S)

        def slot_step(slot, inner_carry):
            forward_piece(h, slot)
            return inner_carry

        lax.fori_loop(0, INNER, slot_step, 0)
        ag(5 + h, 6 + h)

    project_step(0)
    gather_three(1, yin, DY)
    project_step(1)
    x_local(1, yin, DY).wait()
    for slot in range(INNER):
        sx_wait(1, DY, slot)
    gather_sent(1, yin, DY)

    def head_step(h, carry):
        def slot_step(slot, inner_carry):
            head_piece(h, slot)
            ag_share(7 + 2 * h, 9 + 2 * h, slot, INNER)
            rs_share(0, 2 * h, slot, INNER)
            return inner_carry

        lax.fori_loop(0, INNER, slot_step, 0)
        grads(h, head_turned(h), H1, 3 * HD)
        return carry

    lax.fori_loop(0, HEADS_DEV, head_step, 0)

    def beside_one(i):
        ag_share(13, 15, i, TILES)
        rs_share(4, 7, i, TILES)

    def cut_step(f, carry):
        ag_wait(HEADS_DEV + f, S)

        @pl.when(f == CUTS // 2)
        def _():
            for i in range(TILES - 2):
                plane_copy(0, i).wait_send()

        def slot_step(slot, inner_carry):
            cut_piece(f, slot)
            ag_share(
                jnp.where(f == 0, 11, jnp.minimum(13 + 2 * f, 18)),
                jnp.where(f == 0, 13, jnp.minimum(15 + 2 * f, 18)),
                slot,
                INNER,
            )
            rs_share(
                jnp.where(f == 0, 2, jnp.where(f == 1, 7, 2 + 4 * f)),
                jnp.where(f == 0, 4, 6 + 4 * f),
                slot,
                INNER,
            )
            return inner_carry

        lax.fori_loop(0, INNER, slot_step, 0)
        grads(HEADS_DEV + f, cut_turned(f), H2, CUT)

        @pl.when(f == 0)
        def _():
            sum_tiles(0, beside_one)

        return carry

    lax.fori_loop(0, CUTS, cut_step, 0)
    sib_sent(0)
    sum_tiles(1, lambda i: rs_share(18, 22, i, TILES))
    sib_sent(1)
    sum_tiles(2, lambda i: rs_share(22, 24, i, TILES))
    sib_sent(2)

    gr_sent(CHUNKS - 1)

    def drain_chunk(k, carry):
        for d in range(1, INNER):
            a2a_copy(k, d).wait_send()
            gr_copy(k, d, True).wait_recv()

        def drain_step(s, inner_carry):
            ag_sends(k, s, lambda copy: copy.wait_send())
            return inner_carry

        lax.fori_loop(1, S + 1, drain_step, 0)
        return carry

    lax.fori_loop(0, CHUNKS, drain_chunk, 0)
    for way in range(2):

        @pl.when(rs_sends(way, S))
        def _():
            rs_copy(CHUNKS - 1, way, S).wait_send()

    for which in range(3):

        def drain_tile(i, carry):
            if which:
                plane_copy(which, i).wait_send()
            plane_copy(which, i).wait_recv()
            return carry

        lax.fori_loop(0, TILES - 2, drain_tile, 0)


def block_call(count, wst, xin, yin, turns, norm_params, bias_h, bias_f):
    outer = count // INNER
    S = outer - 1
    tokens, half = xin.shape
    group = INNER * tokens
    rows = wst.shape[2]
    tile = tokens // 2
    low, high = jnp.bfloat16, jnp.float32
    any_spec = pl.BlockSpec(memory_space=pl.ANY)
    vmem_spec = pl.BlockSpec(memory_space=pltpu.VMEM)
    dma = pltpu.SemaphoreType.DMA
    return pl.pallas_call(
        functools.partial(block_kernel, count),
        out_shape=[
            jax.ShapeDtypeStruct((CHUNKS, INNER, rows, WIDE), low),
            jax.ShapeDtypeStruct((3, INNER - 1, 2, half, tile), low),
            jax.ShapeDtypeStruct((3, 2, half, tile), high),
            jax.ShapeDtypeStruct((HEADS_DEV, 1, 3 * HD), high),
            jax.ShapeDtypeStruct((CUTS, 1, CUT), high),
            jax.ShapeDtypeStruct((CHUNKS, 1, WIDE), high),
            jax.ShapeDtypeStruct((tokens, 128), high),
        ],
        in_specs=[any_spec] * 3 + [vmem_spec] * 4,
        out_specs=[any_spec] * 3 + [vmem_spec] * 4,
        scratch_shapes=[
            pltpu.VMEM((group, D), low),
            pltpu.VMEM((group, D), low),
            pltpu.VMEM((group, D), low),
            pltpu.VMEM((CHUNKS, D, WIDE), low),
            pltpu.VMEM((HEADS_DEV, WIDE, group), low),
            pltpu.VMEM((2, outer, WIDE, INNER * rows), high),
            pltpu.VMEM((2, WIDE, INNER * rows), low),
            pltpu.VMEM((INNER * rows, WIDE), low),
            pltpu.VMEM((2, S, WIDE, INNER * rows), low),
            pltpu.VMEM((2, half, tile), low),
            pltpu.VMEM((4, half, tile), low),
            pltpu.VMEM((half, tile), high),
            dma((CHUNKS, INNER - 1)),
            dma((CHUNKS, INNER - 1)),
            dma((CHUNKS,)),
            dma((CHUNKS, 2, S)),
            dma((CHUNKS, 2, S)),
            dma((2, INNER - 1)),
            dma((2, INNER - 1)),
            dma((2, INNER)),
            dma((2, INNER)),
            dma((CHUNKS, 2, S)),
            dma((CHUNKS, 2, S)),
            dma((CHUNKS, INNER)),
            dma((CHUNKS, INNER - 1)),
            dma((3, 2 * INNER)),
            dma((3, 2 * INNER)),
            dma((3, 2 * INNER)),
            dma((3, 2 * INNER)),
            dma((3,)),
            pltpu.SemaphoreType.REGULAR((2,)),
        ],
        compiler_params=pltpu.CompilerParams(
            collective_id=0, has_side_effects=True, vmem_limit_bytes=64 * 1024 * 1024
        ),
        cost_estimate=pl.CostEstimate(
            flops=80_000_000_000, bytes_accessed=60_000_000, transcendentals=10_000_000
        ),
    )(wst, xin, yin, turns, norm_params, bias_h, bias_f)


SLOT_ROWS = 16
PACK_ROWS = 40
PACK_ENDS = (0, 3, 4, 8, 12, 17, 22, 27, 31, 35, 39)


def total_of(values):
    return jnp.sum(jnp.sum(values, axis=0, keepdims=True), axis=1, keepdims=True)


def tail_kernel(
    count,
    gr,
    wq,
    wo,
    w1,
    w2,
    xr,
    xo,
    xin,
    yin,
    st,
    norm_ref,
    pb,
    fcb,
    row_old,
    qc_old,
    or_old,
    f1_old,
    f2_old,
    norm_second,
    bias_second,
    fcb_second,
    cs,
    qb,
    fb,
    out_ref,
    ing_ref,
    row_new,
    pack,
    norm_pack,
    qc_new,
    or_new,
    f1_new,
    f2_new,
    norm_grad,
    bias_grad,
    fcb_grad,
    scaled_buf,
    normed_buf,
    terms,
    terms_in,
    rsum,
    rsum_in,
    pay,
    z_in,
    z_sum,
    p_in,
    p_sum,
    s_in,
    pay2,
    z2_in,
    z2_sum,
    p2_in,
    p2_sum,
    s2_in,
    z_s,
    z_r,
    p_s,
    p_r,
    s_s,
    s_r,
):
    outer = count // INNER
    T, half = xin.shape
    R = gr.shape[2]
    b = lax.axis_index("batch")
    c = lax.axis_index("branch")
    q = lax.rem(b, INNER)
    o = b // INNER
    bx, by = flip(b, 1), flip(b, 2)
    near = (bx, by, flip(bx, 2))
    on_b = (b == 0).astype(jnp.float32)
    on_c = (c == 0).astype(jnp.float32)

    def remote(src, dst, ssem, rsem, to_b, to_c):
        return pltpu.make_async_remote_copy(
            src_ref=src,
            dst_ref=dst,
            send_sem=ssem,
            recv_sem=rsem,
            device_id=(to_b, to_c),
            device_id_type=MESH,
        )

    def chain(d):
        return lax.rem(o + d, outer)

    barrier = pltpu.get_barrier_semaphore()
    for who in near:
        pl.semaphore_signal(barrier, inc=1, device_id=(who, c), device_id_type=MESH)
    pl.semaphore_signal(barrier, inc=1, device_id=(b, 1 - c), device_id_type=MESH)
    for d in range(1, outer):
        pl.semaphore_signal(
            barrier, inc=1, device_id=(chain(d) * INNER + q, c), device_id_type=MESH
        )

    HALF_T = T // 2
    lane_t = lax.broadcasted_iota(jnp.int32, (HALF_T, 128), 1)
    own_half = pl.ds(pl.multiple_of(c * half, 128), half)
    other_half = pl.ds(pl.multiple_of((1 - c) * half, 128), half)
    gain_a = norm_ref[0:1, own_half]
    gain_b = norm_ref[2:3, own_half]
    pay[...] = jnp.zeros_like(pay)
    for i in range(2):
        rows = slice(i * HALF_T, (i + 1) * HALF_T)

        def whole(which):
            return (
                xo[which, i]
                + xr[which, 0, i].astype(jnp.float32)
                + xr[which, 1, i].astype(jnp.float32)
                + xr[which, 2, i].astype(jnp.float32)
            ).T

        values = xin[rows, :].astype(jnp.float32)
        out_ref[rows, :] = (values + whole(2) + pb[3:4, :] + pb[4:5, :]).astype(jnp.bfloat16)
        normed = (values - st[rows, 0:1]) * st[rows, 1:2]
        one = whole(0)
        two = whole(1)
        scaled = one * gain_a + two * gain_b
        scaled_buf[rows, :] = scaled
        normed_buf[rows, :] = normed
        terms[rows, :] = jnp.where(
            lane_t == 0,
            jnp.sum(scaled, axis=1, keepdims=True),
            jnp.where(lane_t == 1, jnp.sum(scaled * normed, axis=1, keepdims=True), 0.0),
        )
        pay[5:6, :] += jnp.sum(one * normed, axis=0, keepdims=True)
        pay[6:7, :] += jnp.sum(one, axis=0, keepdims=True)
        pay[7:8, :] += jnp.sum(two * normed, axis=0, keepdims=True)
        pay[8:9, :] += jnp.sum(two, axis=0, keepdims=True)
        pay[9:10, :] += jnp.sum(yin[rows, :].astype(jnp.float32), axis=0, keepdims=True)
    for k in range(CHUNKS):
        pay[k // 2 : k // 2 + 1, k % 2 * WIDE : (k % 2 + 1) * WIDE] = cs[k]
    for h in range(HEADS_DEV):
        pay[3:4, h * 3 * HD : (h + 1) * 3 * HD] = qb[h]
    for f in range(CUTS):
        pay[4:5, f * CUT : (f + 1) * CUT] = fb[f]
    lane_p = lax.broadcasted_iota(jnp.int32, (1, half), 1)
    biases = jnp.sum(pb[...] * pb[...], axis=1, keepdims=True) * on_b
    scalars = (
        [total_of(w[...] * w[...]) for w in (wq, wo, w1, w2)]
        + [biases[i : i + 1] for i in range(5)]
        + [total_of(fcb[...] * fcb[...]) * on_b]
    )
    line = jnp.zeros((1, half), jnp.float32)
    for place, value in enumerate(scalars):
        line = jnp.where(lane_p == place, value, line)
    pay[10:11, :] = line

    pl.semaphore_wait(barrier, INNER + outer - 1)

    def chain_sends(src, buf, base, what):
        for d in range(1, outer):
            what(
                remote(
                    src,
                    buf.at[o],
                    z_s.at[base, d - 1],
                    z_r.at[base, d - 1],
                    chain(d) * INNER + q,
                    c,
                )
            )

    def chain_waits(src, buf, base):
        for d in range(1, outer):
            source = chain(outer - d)
            remote(
                src,
                buf.at[source],
                z_s.at[base, d - 1],
                z_r.at[base, d - 1],
                source * INNER + q,
                c,
            ).wait_recv()

    def plane_sends(src, buf, base, what):
        for d in range(1, INNER):
            what(remote(src, buf.at[q], p_s.at[base, d - 1], p_r.at[base, d - 1], near[d - 1], c))

    def plane_waits(src, buf, base):
        for d in range(1, INNER):
            remote(
                src,
                buf.at[lax.rem(near[d - 1], INNER)],
                p_s.at[base, d - 1],
                p_r.at[base, d - 1],
                near[d - 1],
                c,
            ).wait_recv()

    def pair_copy(src, dst, place):
        return remote(src, dst, s_s.at[place], s_r.at[place], b, 1 - c)

    start = lambda copy: copy.start()
    chain_sends(pay, z_in, 0, start)
    z_in[o] = pay[...]
    pair_copy(terms, terms_in, 0).start()

    lane_r = lax.broadcasted_iota(jnp.int32, (R, 128), 1)
    head_square = jnp.zeros((R, WIDE), jnp.float32)
    cut_square = jnp.zeros((R, WIDE), jnp.float32)
    for part in range(INNER):
        for k in range(CHUNKS):
            gradient = gr[k, part].astype(jnp.float32)
            if k < HEADS_DEV:
                head_square = head_square + squares(gradient)
            else:
                cut_square = cut_square + squares(gradient)
    pieces = (
        jnp.sum(head_square[:, : 3 * HD], axis=1, keepdims=True),
        jnp.sum(cut_square[:, :CUT], axis=1, keepdims=True),
        jnp.sum(head_square[:, 3 * HD :], axis=1, keepdims=True),
        jnp.sum(cut_square[:, CUT:], axis=1, keepdims=True),
    )
    line = jnp.zeros((R, 128), jnp.float32)
    for place, value in enumerate(pieces):
        line = jnp.where(lane_r == place, value, line)
    rsum[...] = line
    pair_copy(rsum, rsum_in, 1).start()

    pair_copy(terms, terms_in, 0).wait_recv()
    for i in range(2):
        rows = slice(i * HALF_T, (i + 1) * HALF_T)
        both = terms[rows, :] + terms_in[rows, :]
        ing_ref[rows, :] = (
            st[rows, 1:2]
            * (
                scaled_buf[rows, :]
                - both[:, 0:1] / D
                - normed_buf[rows, :] * (both[:, 1:2] / D)
            )
            + yin[rows, :].astype(jnp.float32)
        ).astype(jnp.bfloat16)
    pair_copy(rsum, rsum_in, 1).wait_recv()
    rows_after = renew_stat(row_old[...], (rsum[...] + rsum_in[...])[:, :4])
    row_new[...] = jnp.concatenate(
        [rows_after, jnp.zeros((R, 128 - 4), jnp.float32)], axis=1
    )

    chain_waits(pay, z_in, 0)
    acc = z_in[0]
    for j in range(1, outer):
        acc = acc + z_in[j]
    z_sum[...] = acc
    plane_sends(z_sum, p_in, 0, start)
    p_in[q] = acc
    plane_waits(z_sum, p_in, 0)
    p_sum[...] = p_in[0] + p_in[1] + p_in[2] + p_in[3]
    pair_copy(p_sum, s_in, 2).start()

    inverse_rows = 1.0 / rows_after
    head_acc = [jnp.zeros((R, 3 * HD), jnp.float32), jnp.zeros((R, HD), jnp.float32)]
    cut_acc = [jnp.zeros((R, CUT), jnp.float32), jnp.zeros((R, CUT), jnp.float32)]
    for part in range(INNER):
        sums = p_in[part]
        for h in range(HEADS_DEV):
            gradient = gr[h, part].astype(jnp.float32)
            square = gradient * gradient
            found = sums[h // 2 : h // 2 + 1, h % 2 * WIDE : (h % 2 + 1) * WIDE]
            cols = pl.ds(part * HEADS_DEV * HD + h * HD, HD)
            parts = []
            for p in range(3):
                fresh = renew_stat(qc_old[p : p + 1, cols], found[:, p * HD : (p + 1) * HD])
                qc_new[p : p + 1, cols] = fresh
                parts.append(1.0 / fresh)
            head_acc[0] = head_acc[0] + square[:, : 3 * HD] * jnp.concatenate(parts, axis=1)
            fresh = renew_stat(or_old[:, cols], found[:, 3 * HD :])
            or_new[:, cols] = fresh
            head_acc[1] = head_acc[1] + square[:, 3 * HD :] * (1.0 / fresh)
        for f in range(CUTS):
            k = HEADS_DEV + f
            gradient = gr[k, part].astype(jnp.float32)
            square = gradient * gradient
            found = sums[k // 2 : k // 2 + 1, k % 2 * WIDE : (k % 2 + 1) * WIDE]
            cols = slice(f * CUT, (f + 1) * CUT)
            fresh = renew_stat(f1_old[part : part + 1, cols], found[:, :CUT])
            f1_new[part, :, cols] = fresh
            cut_acc[0] = cut_acc[0] + square[:, :CUT] * (1.0 / fresh)
            fresh = renew_stat(f2_old[part : part + 1, cols], found[:, CUT:])
            f2_new[part, :, cols] = fresh
            cut_acc[1] = cut_acc[1] + square[:, CUT:] * (1.0 / fresh)
    for part in range(INNER):
        for h in range(HEADS_DEV):
            for p in range(3):
                low = h * 3 * HD + p * HD
                bias_grad[p : p + 1, pl.ds(part * HEADS_DEV * HD + h * HD, HD)] = p_in[
                    part, 3:4, low : low + HD
                ]
        fcb_grad[part : part + 1, :] = p_in[part, 4:5, :]
    bias_grad[3:4, :] = p_sum[9:10, :]
    bias_grad[4:5, :] = p_sum[9:10, :]
    bias_after, bias_update = second_step(bias_grad[...], bias_second[...])
    pack[17:22, :] = bias_after
    fcb_after, fcb_update = second_step(fcb_grad[...], fcb_second[...])
    pack[31:35, :] = fcb_after
    usq = jnp.sum(bias_update * bias_update, axis=1, keepdims=True) * on_b
    scalars = (
        [
            total_of(rows_after[:, 0:1]) * on_c,
            total_of(head_acc[0] * inverse_rows[:, 0:1]),
            total_of(rows_after[:, 1:2]) * on_c,
            total_of(cut_acc[0] * inverse_rows[:, 1:2]),
            total_of(or_new[...]) * on_b,
            total_of(head_acc[1] * inverse_rows[:, 2:3]),
            sum(total_of(f2_new[part]) for part in range(INNER)) * on_b,
            total_of(cut_acc[1] * inverse_rows[:, 3:4]),
        ]
        + [usq[i : i + 1] for i in range(5)]
        + [total_of(fcb_update * fcb_update) * on_b]
    )
    lane_s = lax.broadcasted_iota(jnp.int32, (8, 128), 1)
    line = jnp.zeros((8, 128), jnp.float32)
    for place, value in enumerate(scalars):
        line = jnp.where(lane_s == place, value, line)
    pay2[...] = line
    chain_sends(pay2, z2_in, 1, start)
    z2_in[o] = line
    pack[0:3, :] = qc_new[...]
    pack[3:4, :] = or_new[...]
    for part in range(INNER):
        pack[4 + part : 5 + part, :] = f1_new[part]
        pack[8 + part : 9 + part, :] = f2_new[part]
    pack[12:17, :] = bias_grad[...]
    pack[27:31, :] = fcb_grad[...]

    pair_copy(p_sum, s_in, 2).wait_recv()
    norm_grad[:, own_half] = p_sum[5:9, :]
    norm_grad[:, other_half] = s_in[5:9, :]
    old = p_sum[10:11, :] + s_in[10:11, :]
    norm_after, norm_update = second_step(norm_grad[...], norm_second[...])
    norm_pack[0:4, :] = norm_grad[...]
    norm_pack[4:8, :] = norm_after

    def moved(vector, update, update_square, old_square, entries):
        clip_factor = jnp.maximum(1.0, jnp.sqrt(update_square / entries))
        step_rate = RATE * jnp.maximum(FLOOR_RATE, jnp.sqrt(old_square / entries))
        return vector - step_rate * update / clip_factor

    norm_values = norm_ref[...]
    norm_pack[8:12, :] = moved(
        norm_values,
        norm_update,
        jnp.sum(norm_update * norm_update, axis=1, keepdims=True),
        jnp.sum(norm_values * norm_values, axis=1, keepdims=True),
        D,
    )

    chain_waits(pay2, z2_in, 1)
    acc = z2_in[0]
    for j in range(1, outer):
        acc = acc + z2_in[j]
    z2_sum[...] = acc
    plane_sends(z2_sum, p2_in, 1, start)
    p2_in[q] = acc
    plane_waits(z2_sum, p2_in, 1)
    acc = p2_in[0] + p2_in[1] + p2_in[2] + p2_in[3]
    p2_sum[...] = acc
    pair_copy(p2_sum, s2_in, 3).start()
    pair_copy(p2_sum, s2_in, 3).wait_recv()
    sums = (acc + s2_in[...])[0:1, :]

    def scalar(place):
        return sums[:, place : place + 1]

    def factor(total, inverse, place, entries):
        clip_factor = jnp.maximum(1.0, jnp.sqrt(total * inverse / entries))
        rate = RATE * jnp.maximum(FLOOR_RATE, jnp.sqrt(old[:, place : place + 1] / entries))
        return rate * jnp.sqrt(total) / clip_factor

    factors = (
        factor(scalar(0), scalar(1), 0, 3 * D * D),
        factor(scalar(2), scalar(3), 2, D * FF),
        factor(scalar(4), scalar(5), 1, D * D),
        factor(scalar(6), scalar(7), 3, FF * D),
    )
    line = jnp.zeros((8, 128), jnp.float32)
    for place, value in enumerate(factors):
        line = jnp.where(lane_s == place, value, line)
    pack[39:40, :] = jnp.concatenate(
        [line[0:1, :], jnp.zeros((1, half - 128), jnp.float32)], axis=1
    )
    for i in range(5):
        pack[22 + i : 23 + i, :] = moved(
            pb[i : i + 1, :], bias_update[i : i + 1], scalar(8 + i), old[:, 4 + i : 5 + i], D
        )
    pack[35:39, :] = moved(fcb[...], fcb_update, scalar(13), old[:, 9:10], FF)

    finish = lambda copy: copy.wait_send()
    chain_sends(pay, z_in, 0, finish)
    chain_sends(pay2, z2_in, 1, finish)
    plane_sends(z_sum, p_in, 0, finish)
    plane_sends(z2_sum, p2_in, 1, finish)
    pair_copy(terms, terms_in, 0).wait_send()
    pair_copy(rsum, rsum_in, 1).wait_send()
    pair_copy(p_sum, s_in, 2).wait_send()
    pair_copy(p2_sum, s2_in, 3).wait_send()


def tail_call(count, *args):
    outer = count // INNER
    received, xin = args[0], args[7]
    tokens, half = xin.shape
    rows = received.shape[2]
    high = jnp.float32
    spec = pl.BlockSpec(memory_space=pltpu.VMEM)
    dma = pltpu.SemaphoreType.DMA

    def out(*shape, dtype=high):
        return jax.ShapeDtypeStruct(shape, dtype)

    outs = [
        out(tokens, half, dtype=jnp.bfloat16),
        out(tokens, half, dtype=jnp.bfloat16),
        out(rows, 128),
        out(PACK_ROWS, half),
        out(12, D),
    ]
    slot = (SLOT_ROWS, half)
    return pl.pallas_call(
        functools.partial(tail_kernel, count),
        out_shape=outs,
        in_specs=[spec] * len(args),
        out_specs=[spec] * len(outs),
        scratch_shapes=[
            pltpu.VMEM((3, half), high),
            pltpu.VMEM((1, half), high),
            pltpu.VMEM((INNER, 1, half), high),
            pltpu.VMEM((INNER, 1, half), high),
            pltpu.VMEM((4, D), high),
            pltpu.VMEM((5, half), high),
            pltpu.VMEM((INNER, half), high),
            pltpu.VMEM((tokens, half), high),
            pltpu.VMEM((tokens, half), high),
            pltpu.VMEM((tokens, 128), high),
            pltpu.VMEM((tokens, 128), high),
            pltpu.VMEM((rows, 128), high),
            pltpu.VMEM((rows, 128), high),
            pltpu.VMEM(slot, high),
            pltpu.VMEM((outer, *slot), high),
            pltpu.VMEM(slot, high),
            pltpu.VMEM((INNER, *slot), high),
            pltpu.VMEM(slot, high),
            pltpu.VMEM(slot, high),
            pltpu.VMEM((8, 128), high),
            pltpu.VMEM((outer, 8, 128), high),
            pltpu.VMEM((8, 128), high),
            pltpu.VMEM((INNER, 8, 128), high),
            pltpu.VMEM((8, 128), high),
            pltpu.VMEM((8, 128), high),
            dma((2, outer - 1)),
            dma((2, outer - 1)),
            dma((2, INNER - 1)),
            dma((2, INNER - 1)),
            dma((4,)),
            dma((4,)),
        ],
        compiler_params=pltpu.CompilerParams(
            collective_id=1, has_side_effects=True, vmem_limit_bytes=58 * 1024 * 1024
        ),
        cost_estimate=pl.CostEstimate(
            flops=50_000_000, bytes_accessed=40_000_000, transcendentals=100_000
        ),
    )(*args)


def update_kernel(*refs):
    gr, wq, wo, w1, w2, row_new, pack, norm_pack, output, input_grad = refs[:10]
    q_grad, q_next, q_copy, o_grad, o_next, o_copy = refs[10:16]
    f1_grad, f1_next, f1_copy, f2_grad, f2_next, f2_copy = refs[16:22]
    row_out, whole_out, pack_out, norm_out = refs[22:26], refs[26:28], refs[28:38], refs[38:]
    part = pl.program_id(0)
    side = lax.rsqrt(row_new[:, :4]) * pack[39:40, :4]
    width_q = HEADS_DEV * HD

    @pl.when(part == 0)
    def _():
        whole_out[0][...] = output[...]
        whole_out[1][...] = input_grad[...]
        for place, target in enumerate(pack_out):
            target[...] = pack[PACK_ENDS[place] : PACK_ENDS[place + 1], :]
        for place, target in enumerate(norm_out):
            target[...] = norm_pack[4 * place : 4 * place + 4, :]
        turned = row_new[...].T
        for place in range(4):
            row_out[place][...] = turned[place : place + 1, :]

    def put(grad_ref, next_ref, copy_ref, where, weight, gradient, update):
        fresh = weight[where] - update
        grad_ref[where] = gradient
        next_ref[where] = fresh
        copy_ref[where] = fresh.astype(jnp.bfloat16)

    for h in range(HEADS_DEV):
        gradient = gr[h, 0].astype(jnp.float32)
        cols = pl.ds(pl.multiple_of(part * width_q + h * HD, HD), HD)
        for p in range(3):
            mine = gradient[:, p * HD : (p + 1) * HD]
            update = mine * side[:, 0:1] * lax.rsqrt(pack[p : p + 1, cols])
            where = (p, slice(None), slice(h * HD, (h + 1) * HD))
            put(q_grad, q_next, q_copy, where, wq, mine, update)
        mine = gradient[:, 3 * HD :]
        update = mine * side[:, 2:3] * lax.rsqrt(pack[3:4, cols])
        where = (slice(h * HD, (h + 1) * HD), slice(None))
        put(o_grad, o_next, o_copy, where, wo, mine.T, update.T)
    for f in range(CUTS):
        gradient = gr[HEADS_DEV + f, 0].astype(jnp.float32)
        cols = slice(f * CUT, (f + 1) * CUT)
        mine = gradient[:, :CUT]
        update = mine * side[:, 1:2] * lax.rsqrt(pack[pl.ds(4 + part, 1), cols])
        put(f1_grad, f1_next, f1_copy, (slice(None), cols), w1, mine, update)
        mine = gradient[:, CUT:]
        update = mine * side[:, 3:4] * lax.rsqrt(pack[pl.ds(8 + part, 1), cols])
        put(f2_grad, f2_next, f2_copy, (cols, slice(None)), w2, mine.T, update.T)


def update_call(gr, wq, wo, w1, w2, row_new, pack, norm_pack, output, input_grad):
    rows = gr.shape[2]
    half = pack.shape[1]
    width_q = HEADS_DEV * HD
    hidden_q = CUTS * CUT
    spec = pl.BlockSpec
    q_spec = spec((3, rows, width_q), lambda i: (0, 0, i))
    o_spec = spec((width_q, rows), lambda i: (i, 0))
    f1_spec = spec((rows, hidden_q), lambda i: (0, i))
    f2_spec = spec((hidden_q, rows), lambda i: (i, 0))
    outs, out_specs = [], []
    for array, its in ((wq, q_spec), (wo, o_spec), (w1, f1_spec), (w2, f2_spec)):
        for dtype in (jnp.float32, jnp.float32, jnp.bfloat16):
            outs.append(jax.ShapeDtypeStruct(array.shape, dtype))
            out_specs.append(its)

    def fixed(shape):
        return spec(shape, lambda i: (0,) * len(shape))

    shapes = [((1, rows), jnp.float32)] * 4 + [(output.shape, output.dtype)] * 2
    for place in range(len(PACK_ENDS) - 1):
        shapes.append(((PACK_ENDS[place + 1] - PACK_ENDS[place], half), jnp.float32))
    shapes += [((4, D), jnp.float32)] * 3
    for shape, dtype in shapes:
        outs.append(jax.ShapeDtypeStruct(shape, dtype))
        out_specs.append(fixed(shape))
    small = (row_new, pack, norm_pack, output, input_grad)
    return pl.pallas_call(
        update_kernel,
        grid=(INNER,),
        out_shape=outs,
        in_specs=[
            spec((CHUNKS, 1, rows, WIDE), lambda i: (0, i, 0, 0)),
            q_spec,
            o_spec,
            f1_spec,
            f2_spec,
        ]
        + [fixed(array.shape) for array in small],
        out_specs=out_specs,
        compiler_params=pltpu.CompilerParams(vmem_limit_bytes=48 * 1024 * 1024),
        cost_estimate=pl.CostEstimate(
            flops=20_000_000, bytes_accessed=30_000_000, transcendentals=100_000
        ),
    )(gr, wq, wo, w1, w2, *small)


def swap_pairs(count, step):
    return [(i, i ^ step) for i in range(count)]


def block_of(array, index, size, axis=0):
    return lax.dynamic_slice_in_dim(array, index * size, size, axis)


def on_device(
    inputs,
    cotangent,
    segment_ids,
    w_qkv,
    w_out,
    w_fc1,
    w_fc2,
    norm_params,
    proj_bias,
    fc1_bias,
    qkv_rows,
    qkv_cols,
    out_rows,
    out_cols,
    fc1_rows,
    fc1_cols,
    fc2_rows,
    fc2_cols,
    norm_second,
    bias_second,
    fc1b_second,
):
    tokens = inputs.shape[0]
    local_width = inputs.shape[1]
    local_hidden = fc1_bias.shape[0]
    rows = w_qkv.shape[0]
    count = lax.axis_size("batch")
    c = lax.axis_index("branch")
    b = lax.axis_index("batch")
    q = lax.rem(b, INNER)
    group = INNER * tokens
    width_q = local_width // INNER
    hidden_q = local_hidden // INNER
    qkv_low = w_qkv.astype(jnp.bfloat16).reshape(rows, 3, INNER, HEADS_DEV, HD)
    out_low = w_out.astype(jnp.bfloat16).reshape(INNER, HEADS_DEV, HD, rows)
    fc1_low = w_fc1.astype(jnp.bfloat16).reshape(rows, INNER, CUTS, CUT)
    fc2_low = w_fc2.astype(jnp.bfloat16).reshape(INNER, CUTS, CUT, rows)
    heads_low = jnp.concatenate(
        [
            qkv_low.transpose(3, 2, 0, 1, 4).reshape(HEADS_DEV, INNER, rows, 3 * HD),
            out_low.transpose(1, 0, 3, 2),
        ],
        axis=3,
    )
    cuts_low = jnp.concatenate(
        [fc1_low.transpose(2, 1, 0, 3), fc2_low.transpose(1, 0, 3, 2)], axis=3
    )
    wst = jnp.concatenate([heads_low, cuts_low], axis=0)

    segment = jnp.concatenate(
        [segment_ids]
        + [lax.ppermute(segment_ids, "batch", swap_pairs(count, d)) for d in range(1, INNER)],
        axis=0,
    )
    positions_idx = jnp.arange(tokens)
    earlier = jnp.sum((segment[:, None, :] < segment[:, :, None]).astype(jnp.int32), axis=2)
    starts = earlier.astype(jnp.float32).reshape(1, group)
    places = (positions_idx[None] - earlier).astype(jnp.float32).reshape(1, group)
    frequency = 10000.0 ** (-2.0 * jnp.arange(ROT // 2, dtype=jnp.float32) / ROT)
    angles = frequency[:, None] * places
    cos_part = jnp.cos(angles)
    sin_part = jnp.sin(angles)
    turns = jnp.concatenate(
        [
            cos_part,
            cos_part,
            -sin_part,
            sin_part,
            jnp.broadcast_to(starts, (HD - 2 * ROT, group)),
        ],
        axis=0,
    )
    bias_h = (
        block_of(proj_bias[0:3], q, width_q, 1)
        .reshape(3, HEADS_DEV, HD)
        .transpose(1, 0, 2)
        .reshape(HEADS_DEV, 1, 3 * HD)
    )
    bias_f = block_of(fc1_bias, q, hidden_q).reshape(CUTS, 1, CUT)
    received, plane_parts, plane_own, head_bias, cut_bias, col_sums, row_moments = block_call(
        count, wst, inputs, cotangent, turns, norm_params, bias_h, bias_f
    )
    by_part = (INNER, hidden_q)
    qkv_parts = w_qkv.transpose(1, 0, 2)
    output, input_grad, row_stats, pack, norm_pack = tail_call(
        count,
        received,
        qkv_parts.reshape(3 * rows, local_width),
        w_out,
        w_fc1,
        w_fc2,
        plane_parts,
        plane_own,
        inputs,
        cotangent,
        row_moments,
        norm_params,
        proj_bias,
        fc1_bias.reshape(by_part),
        jnp.stack([qkv_rows, fc1_rows, out_cols, fc2_cols], axis=1),
        qkv_cols,
        out_rows.reshape(1, local_width),
        fc1_cols.reshape(by_part),
        fc2_rows.reshape(by_part),
        norm_second,
        bias_second,
        fc1b_second.reshape(by_part),
        col_sums,
        head_bias,
        cut_bias,
    )
    updated = update_call(
        received,
        qkv_parts,
        w_out,
        w_fc1,
        w_fc2,
        row_stats,
        pack,
        norm_pack,
        output,
        input_grad,
    )
    qkv_grad, qkv_next, qkv_copy = (array.transpose(1, 0, 2) for array in updated[0:3])
    out_grad, out_next, out_copy = updated[3:6]
    fc1_grad, fc1_next, fc1_copy = updated[6:9]
    fc2_grad, fc2_next, fc2_copy = updated[9:12]
    qkv_rows_new, fc1_rows_new, out_cols_new, fc2_cols_new = (
        array.reshape(rows) for array in updated[12:16]
    )
    (
        output,
        input_grad,
        qkv_cols_new,
        out_rows_new,
        fc1_cols_new,
        fc2_rows_new,
        bias_grad,
        bias_moment,
        bias_new,
        fc1b_grad,
        fc1b_moment,
        fc1b_new,
        norm_grad,
        norm_moment,
        norm_new,
    ) = updated[16:]
    return (
        output,
        input_grad,
        qkv_grad,
        qkv_next,
        qkv_rows_new,
        qkv_cols_new,
        qkv_copy,
        out_grad,
        out_next,
        out_rows_new.reshape(local_width),
        out_cols_new,
        out_copy,
        fc1_grad,
        fc1_next,
        fc1_rows_new,
        fc1_cols_new.reshape(local_hidden),
        fc1_copy,
        fc2_grad,
        fc2_next,
        fc2_rows_new.reshape(local_hidden),
        fc2_cols_new,
        fc2_copy,
        norm_grad,
        norm_moment,
        norm_new,
        bias_grad,
        bias_moment,
        bias_new,
        fc1b_grad.reshape(local_hidden),
        fc1b_moment.reshape(local_hidden),
        fc1b_new.reshape(local_hidden),
    )


def solution(mesh):
    in_specs = (
        P("batch", "branch"),
        P("batch", "branch"),
        P("batch", None),
        P("batch", None, "branch"),
        P("branch", "batch"),
        P("batch", "branch"),
        P("branch", "batch"),
        P(),
        P(None, "branch"),
        P("branch"),
        P("batch"),
        P(None, "branch"),
        P("branch"),
        P("batch"),
        P("batch"),
        P("branch"),
        P("branch"),
        P("batch"),
        P(),
        P(None, "branch"),
        P("branch"),
    )
    out_specs = (
        P("batch", "branch"),
        P("batch", "branch"),
        P("batch", None, "branch"),
        P("batch", None, "branch"),
        P("batch"),
        P(None, "branch"),
        P("batch", None, "branch"),
        P("branch", "batch"),
        P("branch", "batch"),
        P("branch"),
        P("batch"),
        P("branch", "batch"),
        P("batch", "branch"),
        P("batch", "branch"),
        P("batch"),
        P("branch"),
        P("batch", "branch"),
        P("branch", "batch"),
        P("branch", "batch"),
        P("branch"),
        P("batch"),
        P("branch", "batch"),
        P(),
        P(),
        P(),
        P(None, "branch"),
        P(None, "branch"),
        P(None, "branch"),
        P("branch"),
        P("branch"),
        P("branch"),
    )
    return jax.shard_map(
        on_device, mesh=mesh, in_specs=in_specs, out_specs=out_specs, check_vma=False
    )
```

```python
import functools

import jax
import jax.numpy as jnp
from jax import lax
from jax.experimental import pallas as pl
from jax.experimental.pallas import tpu as pltpu
from jax.sharding import PartitionSpec as P

D = 2048
HD = 128
ROT = 32
FF = 8192
STEP = 10


EPS_NORM = 1e-05
EPS_SQUARE = 1e-30
RATE = 0.3
FLOOR_RATE = 0.001


def decay_rate():
    return 1.0 - STEP ** (-0.8)


def squares(gradient):
    return gradient * gradient + EPS_SQUARE


def renew_stat(old_stat, new_sum):
    decay = decay_rate()
    return decay * old_stat + (1.0 - decay) * new_sum


def second_step(gradient, second):
    second_new = renew_stat(second, squares(gradient))
    return (second_new, gradient * lax.rsqrt(second_new))


INNER = 4
HEADS_DEV = 2
CUTS = 4
CHUNKS = HEADS_DEV + CUTS
CUT = 256
WIDE = 512
MESH = pl.DeviceIdType.MESH


def flip(index, step):
    return index + step * (1 - 2 * lax.rem(index // step, 2))


def nn(left, right):
    return jnp.dot(left, right, preferred_element_type=jnp.float32)


def nt(left, right):
    return lax.dot_general(
        left, right, (((1,), (1,)), ((), ())), preferred_element_type=jnp.float32
    )


def tn(left, right):
    return lax.dot_general(
        left, right, (((0,), (0,)), ((), ())), preferred_element_type=jnp.float32
    )


def block_kernel(
    count,
    wst,
    xin,
    yin,
    turn_ref,
    norm_ref,
    bias_h,
    bias_f,
    gr,
    xr,
    xo,
    qb,
    fb,
    cs,
    st,
    H1,
    H2,
    DY,
    W,
    TA,
    G,
    sbuf,
    fbuf,
    rsb,
    sib_send,
    sib_land,
    own,
    a2a_s,
    a2a_r,
    loc_s,
    ag_s,
    ag_r,
    x_s,
    x_r,
    sx_s,
    sx_r,
    rs_s,
    rs_r,
    gr_s,
    gr_r,
    sib_s,
    sib_r,
    p_s,
    p_r,
    tmp_s,
    free_s,
):
    outer = count // INNER
    S = outer - 1
    T, half = xin.shape
    R = wst.shape[2]
    block = INNER * R
    QT = T // 2
    b = lax.axis_index("batch")
    c = lax.axis_index("branch")
    q = lax.rem(b, INNER)
    o = b // INNER
    bx, by = flip(b, 1), flip(b, 2)
    bxy = flip(bx, 2)
    near = (bx, by, bxy)
    da = 1 + c
    db = 2 - c
    b_first = bx * (1 - c) + by * c
    b_second = by * (1 - c) + bx * c

    def remote(src, dst, ssem, rsem, to_b, to_c):
        return pltpu.make_async_remote_copy(
            src_ref=src,
            dst_ref=dst,
            send_sem=ssem,
            recv_sem=rsem,
            device_id=(to_b, to_c),
            device_id_type=MESH,
        )

    barrier = pltpu.get_barrier_semaphore()
    for who in near:
        pl.semaphore_signal(barrier, inc=1, device_id=(who, c), device_id_type=MESH)
    pl.semaphore_signal(barrier, inc=1, device_id=(b, 1 - c), device_id_type=MESH)

    @pl.when(o > 0)
    def _():
        pl.semaphore_signal(barrier, inc=1, device_id=(b - INNER, c), device_id_type=MESH)

    @pl.when(o < outer - 1)
    def _():
        pl.semaphore_signal(barrier, inc=1, device_id=(b + INNER, c), device_id_type=MESH)

    pl.semaphore_wait(barrier, 4 + jnp.minimum(o, 1) + jnp.minimum(outer - 1 - o, 1))

    def a2a_copy(k, d, received=False):
        to = near[d - 1]
        row = (to if received else b) * R
        return remote(
            wst.at[k, lax.rem(to, INNER)],
            W.at[k, pl.ds(pl.multiple_of(row, 16), R)],
            a2a_s.at[k, d - 1],
            a2a_r.at[k, d - 1],
            to,
            c,
        )

    def a2a_local(k):
        return pltpu.make_async_copy(
            wst.at[k, q], W.at[k, pl.ds(pl.multiple_of(b * R, 16), R)], loc_s.at[k]
        )

    def a2a_start(k):
        for d in range(1, INNER):
            a2a_copy(k, d).start()
        a2a_local(k).start()

    def a2a_wait(k):
        for d in range(1, INNER):
            a2a_copy(k, d, True).wait_recv()
        a2a_local(k).wait()

    def ag_copy(k, way, s, part):
        rows = pl.ds(pl.multiple_of(part * block, 16), block)
        to = b + INNER if way == 0 else b - INNER
        return remote(
            W.at[k, rows], W.at[k, rows], ag_s.at[k, way, s - 1], ag_r.at[k, way, s - 1], to, c
        )

    def ag_sends(k, s, what):
        @pl.when((o >= s - 1) & (o <= outer - 2))
        def _():
            what(ag_copy(k, 0, s, o - s + 1))

        @pl.when((o >= 1) & (o <= outer - s))
        def _():
            what(ag_copy(k, 1, s, o + s - 1))

    def ag_wait(k, s):
        @pl.when(o >= s)
        def _():
            ag_copy(k, 0, s, o - s).wait_recv()

        @pl.when(o <= outer - 1 - s)
        def _():
            ag_copy(k, 1, s, o + s).wait_recv()

    def ag_range(low, high):
        def step(n, carry):
            k = n // S
            s = lax.rem(n, S) + 1

            @pl.when(s == 1)
            def _():
                a2a_wait(k)

            @pl.when(s > 1)
            def _():
                ag_wait(k, s - 1)

            ag_sends(k, s, lambda copy: copy.start())
            return carry

        lax.fori_loop(low, high, step, 0)

    def ag(low, high):
        ag_range(low * S // 3, high * S // 3)

    def spot(buf, slot):
        return buf.at[
            pl.ds(pl.multiple_of(slot * T, 16), T), pl.ds(pl.multiple_of(c * half, 128), half)
        ]

    def other_spot(buf, slot):
        return buf.at[
            pl.ds(pl.multiple_of(slot * T, 16), T), pl.ds(pl.multiple_of((1 - c) * half, 128), half)
        ]

    def sx_copy(i, buf, slot, src=None):
        place = spot(buf, slot)
        return remote(place if src is None else src, place, sx_s.at[i, slot], sx_r.at[i, slot], b, 1 - c)

    def sx_wait(i, buf, slot):
        remote(
            other_spot(buf, slot), other_spot(buf, slot), sx_s.at[i, slot], sx_r.at[i, slot], b, 1 - c
        ).wait_recv()

    def x_first(i, src, buf):
        return remote(src, spot(buf, da), x_s.at[i, da - 1], x_r.at[i, da - 1], b_first, c)

    def x_second(i, src, buf):
        return remote(src, spot(buf, db), x_s.at[i, db - 1], x_r.at[i, db - 1], b_second, c)

    def x_forward(i, buf):
        return remote(spot(buf, da), spot(buf, 3), x_s.at[i, 2], x_r.at[i, 2], b_second, c)

    def x_diag(i, buf):
        return remote(spot(buf, 3), spot(buf, 3), x_s.at[i, 2], x_r.at[i, 2], b_second, c)

    def x_local(i, src, buf):
        return pltpu.make_async_copy(src, spot(buf, 0), tmp_s.at[i])

    def gather_one(i, src, buf):
        x_first(i, src, buf).start()
        x_local(i, src, buf).start()
        sx_copy(i, buf, 0, src).start()

    def gather_two(i, src, buf):
        x_first(i, src, buf).wait_recv()
        x_second(i, src, buf).start()
        x_forward(i, buf).start()
        sx_copy(i, buf, da).start()

    def gather_three(i, src, buf):
        x_second(i, src, buf).wait_recv()
        sx_copy(i, buf, db).start()
        x_diag(i, buf).wait_recv()
        sx_copy(i, buf, 3).start()

    def gather_sent(i, src, buf):
        x_first(i, src, buf).wait_send()
        x_second(i, src, buf).wait_send()
        x_forward(i, buf).wait_send()
        sx_copy(i, buf, 0, src).wait_send()
        for slot in range(1, INNER):
            sx_copy(i, buf, slot).wait_send()

    lane_n = lax.broadcasted_iota(jnp.int32, (64, 128), 1)

    def norm_rows(slot):
        def step(i, carry):
            rows = pl.ds(pl.multiple_of(slot * T + i * 64, 64), 64)
            values = H1[rows, :].astype(jnp.float32)
            mean = jnp.mean(values, axis=-1, keepdims=True)
            centered = values - mean
            inverse = lax.rsqrt(jnp.mean(centered * centered, axis=-1, keepdims=True) + EPS_NORM)
            normed = centered * inverse
            if slot == 0:
                st[pl.ds(pl.multiple_of(i * 64, 64), 64), :] = jnp.where(lane_n == 0, mean, inverse)
            H1[rows, :] = (normed * norm_ref[0:1, :] + norm_ref[1:2, :]).astype(jnp.bfloat16)
            H2[rows, :] = (normed * norm_ref[2:3, :] + norm_ref[3:4, :]).astype(jnp.bfloat16)
            return carry

        lax.fori_loop(0, T // 64, step, 0)

    lane = lax.broadcasted_iota(jnp.int32, (T, HD), 1)
    scale = HD ** (-0.5)

    def partner(tensor):
        return jnp.where(
            lane < ROT // 2,
            pltpu.roll(tensor, HD - ROT // 2, 1),
            jnp.where(lane < ROT, pltpu.roll(tensor, ROT // 2, 1), 0.0),
        )

    def turns_of(rows):
        table = turn_ref[:, rows].T
        cos_rows = jnp.where(lane < ROT, table, 1.0)
        sin_rows = pltpu.roll(table, HD - ROT, 1)
        return cos_rows, sin_rows, table[:, 2 * ROT : 2 * ROT + 1]

    def probs_at(h, slot, i):
        seen = QT * (i + 1)
        wide = min(block, seen)
        part = slice(QT * i, QT * (i + 1))
        base = slot * (outer // INNER)
        return [(h, base + j, part, slice(0, wide)) for j in range(seen // wide)]

    def forward_piece(h, slot):
        start = pl.multiple_of(slot * T, 128)
        rows = pl.ds(start, T)
        cos_rows, sin_rows, starts = turns_of(rows)
        projected = nn(H1[rows, :], W[h, :, : 3 * HD]) + bias_h[h]
        first = projected[:, :HD]
        queries = (first * cos_rows + partner(first) * sin_rows).astype(jnp.bfloat16)
        second = projected[:, HD : 2 * HD]
        keys = (second * cos_rows + partner(second) * sin_rows).astype(jnp.bfloat16)
        values = projected[:, 2 * HD :].astype(jnp.bfloat16)
        TA[h, :, pl.ds(start, HD)] = queries
        TA[h, :, pl.ds(start + HD, HD)] = keys
        TA[h, :, pl.ds(start + 2 * HD, HD)] = values
        for i in range(2):
            seen = QT * (i + 1)
            part = slice(QT * i, QT * (i + 1))
            raw = nt(queries[part], keys[:seen]) * scale
            query_at = lax.broadcasted_iota(jnp.int32, (QT, seen), 0) + QT * i
            key_at = lax.broadcasted_iota(jnp.int32, (QT, seen), 1)
            allowed = (key_at <= query_at) & (key_at.astype(jnp.float32) >= starts[part])
            scores = jnp.where(allowed, raw, -1e30)
            exponent = jnp.exp(scores - jnp.max(scores, axis=-1, keepdims=True))
            probs = exponent * (1.0 / jnp.sum(exponent, axis=-1, keepdims=True))
            for j, place in enumerate(probs_at(h, slot, i)):
                wide = min(block, seen)
                G[place] = probs[:, j * wide : (j + 1) * wide]
            TA[h, part, pl.ds(start + 3 * HD, HD)] = nn(
                probs.astype(jnp.bfloat16), values[:seen]
            ).astype(jnp.bfloat16)

    def head_piece(h, slot):
        start = pl.multiple_of(slot * T, 128)
        rows = pl.ds(start, T)
        cos_rows, sin_rows, _ = turns_of(rows)
        queries = TA[h, :, pl.ds(start, HD)]
        keys = TA[h, :, pl.ds(start + HD, HD)]
        values = TA[h, :, pl.ds(start + 2 * HD, HD)]
        context = TA[h, :, pl.ds(start + 3 * HD, HD)]
        back = nn(DY[rows, :], W[h, :, 3 * HD :]).astype(jnp.bfloat16)
        grad_q = []
        grad_k, grad_v = [None, None], [None, None]
        for i in range(2):
            seen = QT * (i + 1)
            part = slice(QT * i, QT * (i + 1))
            probs = [G[place] for place in probs_at(h, slot, i)]
            probs = probs[0] if len(probs) == 1 else jnp.concatenate(probs, axis=1)
            soft = probs.astype(jnp.bfloat16)
            grad_probs = nt(back[part], values[:seen])
            inner = jnp.sum(probs * grad_probs, axis=-1, keepdims=True)
            grad_scores = (probs * (grad_probs - inner)).astype(jnp.bfloat16)
            grad_q.append((nn(grad_scores, keys[:seen]) * scale).astype(jnp.bfloat16))
            for j in range(i + 1):
                cut = slice(QT * j, QT * (j + 1))
                term_v = tn(soft[:, cut], back[part])
                term_k = tn(grad_scores[:, cut], queries[part])
                grad_v[j] = term_v if grad_v[j] is None else grad_v[j] + term_v
                grad_k[j] = term_k if grad_k[j] is None else grad_k[j] + term_k
        dq = jnp.concatenate(grad_q, axis=0).astype(jnp.float32)
        dk = (jnp.concatenate(grad_k, axis=0) * scale).astype(jnp.bfloat16).astype(jnp.float32)
        dv = jnp.concatenate(grad_v, axis=0)
        turned = jnp.concatenate(
            [
                dq * cos_rows - partner(dq) * sin_rows,
                dk * cos_rows - partner(dk) * sin_rows,
                dv,
            ],
            axis=1,
        ).astype(jnp.bfloat16)
        TA[h, : 3 * HD, rows] = turned.T
        TA[h, 3 * HD :, rows] = context.T
        total = jnp.sum(turned.astype(jnp.float32), axis=0, keepdims=True)
        qb[h] = jnp.where(slot == 0, total, qb[h] + total)

    def cut_piece(f, slot):
        rows = pl.ds(pl.multiple_of(slot * T, 128), T)
        k = HEADS_DEV + f
        pre = nn(H2[rows, :], W[k, :, :CUT]) + bias_f[f]
        grad = nn(DY[rows, :], W[k, :, CUT:])
        normal = 0.5 * (1.0 + lax.erf(pre * (0.5**0.5)))
        slope = normal + pre * (jnp.exp(-0.5 * pre * pre) * (0.5 * 0.7978845608028654))
        active = (pre * normal).astype(jnp.bfloat16)
        pulled = (grad * slope).astype(jnp.bfloat16)
        low = pl.multiple_of(f * WIDE, WIDE)
        H1[pl.ds(low, CUT), rows] = pulled.T
        H1[pl.ds(low + CUT, CUT), rows] = active.T
        total = jnp.sum(pulled.astype(jnp.float32), axis=0, keepdims=True)
        fb[f] = jnp.where(slot == 0, total, fb[f] + total)

    def grads(k, turned, left, edge):
        def step(j, carry):
            cols = pl.ds(pl.multiple_of(j * block, 128), block)
            G[lax.rem(k, 2), j, :edge, :] = nn(turned(0, edge), left[:, cols])
            G[lax.rem(k, 2), j, edge:, :] = nn(turned(edge, WIDE - edge), DY[:, cols])
            return carry

        lax.fori_loop(0, outer, step, 0)

    def head_turned(h):
        return lambda low, size: TA[h, pl.ds(low, size), :]

    def cut_turned(f):
        return lambda low, size: H1[pl.ds(pl.multiple_of(f * WIDE + low, 128), size), :]

    def rs_copy(k, way, t):
        to = b + INNER if way == 0 else b - INNER
        return remote(
            sbuf.at[way],
            rsb.at[way, t - 1],
            rs_s.at[k, way, t - 1],
            rs_r.at[k, way, t - 1],
            to,
            c,
        )

    def rs_sends(way, t):
        if way == 0:
            return (o <= t - 1) & (o <= outer - 2)
        return (o >= outer - t) & (o >= 1)

    def rs_receives(way, t):
        if way == 0:
            return (o >= 1) & (o <= t)
        return (o <= outer - 2) & (o >= outer - 1 - t)

    def rs_fetch(k, way, t):
        rs_copy(k, way, t).wait_recv()
        return rsb[way, t - 1].astype(jnp.float32)

    def rs_step(k, t):
        n = k * S + t - 1

        @pl.when((t == 1) & (k >= 1) & (o < outer - 1))
        def _():
            pl.semaphore_wait(free_s.at[0], 1)

        @pl.when((t == 1) & (k >= 1) & (o > 0))
        def _():
            pl.semaphore_wait(free_s.at[1], 1)

        before = jnp.maximum(n - 1, 0)
        k_before = before // S
        t_before = lax.rem(before, S) + 1
        for way in range(2):
            owner = o + outer - t if way == 0 else o - outer + t

            @pl.when((n >= 1) & rs_sends(way, t_before))
            def _():
                rs_copy(k_before, way, t_before).wait_send()

            @pl.when(rs_sends(way, t))
            def _():
                @pl.when(rs_receives(way, t - 1) & (t > 1))
                def _():
                    sbuf[way] = (
                        G[lax.rem(k, 2), owner] + rs_fetch(k, way, t - 1)
                    ).astype(jnp.bfloat16)

                @pl.when(jnp.logical_not(rs_receives(way, t - 1) & (t > 1)))
                def _():
                    sbuf[way] = G[lax.rem(k, 2), owner].astype(jnp.bfloat16)

                rs_copy(k, way, t).start()

    def gr_copy(k, d, received=False):
        to = near[d - 1]
        slot = lax.rem(to, INNER)
        return remote(
            fbuf.at[pl.ds(pl.multiple_of(slot * R, 16), R)],
            gr.at[k, slot if received else q],
            gr_s.at[k, d - 1],
            gr_r.at[k, d - 1],
            to,
            c,
        )

    def gr_local(k):
        return pltpu.make_async_copy(
            fbuf.at[pl.ds(pl.multiple_of(q * R, 16), R)],
            gr.at[k, q],
            gr_s.at[k, 3],
        )

    def gr_sent(k):
        for d in range(1, INNER):
            gr_copy(k, d).wait_send()
        gr_local(k).wait()

    def rs_final(k):
        for way in range(2):

            @pl.when(rs_receives(way, S))
            def _():
                G[lax.rem(k, 2), o] = G[lax.rem(k, 2), o] + rs_fetch(k, way, S)

        @pl.when((k < CHUNKS - 1) & (o > 0))
        def _():
            pl.semaphore_signal(
                free_s.at[0], inc=1, device_id=(b - INNER, c), device_id_type=MESH
            )

        @pl.when((k < CHUNKS - 1) & (o < outer - 1))
        def _():
            pl.semaphore_signal(
                free_s.at[1], inc=1, device_id=(b + INNER, c), device_id_type=MESH
            )

        @pl.when(k >= 1)
        def _():
            gr_sent(k - 1)

        final = G[lax.rem(k, 2), o].T
        cs[k] = jnp.sum(squares(final), axis=0, keepdims=True)
        fbuf[...] = final.astype(jnp.bfloat16)
        for d in range(1, INNER):
            gr_copy(k, d).start()
        gr_local(k).start()

    def rs_range(low, high):
        def step(n, carry):
            k = n // (S + 1)
            t = lax.rem(n, S + 1) + 1

            @pl.when(t <= S)
            def _():
                rs_step(k, t)

            @pl.when(t == S + 1)
            def _():
                rs_final(k)

            return carry

        lax.fori_loop(low, high, step, 0)

    TILE = T // 2
    TILES = 2 * INNER
    PER_ROW = D // TILE

    def tile_slot(i):
        return INNER - 1 - i // 2

    def product(which, i, side):
        at = pl.multiple_of(tile_slot(i) * T + lax.rem(i, 2) * TILE, 128)
        toks = pl.ds(at, TILE)
        features = pl.ds(pl.multiple_of(side * half, 128), half)
        terms = []
        if which == 0:
            for h in range(HEADS_DEV):
                terms.append((h, slice(0, 3 * HD), lambda h=h: TA[h, : 3 * HD, toks]))
        elif which == 1:
            for f in range(CUTS):
                low = f * WIDE
                terms.append(
                    (HEADS_DEV + f, slice(0, CUT), lambda low=low: H1[low : low + CUT, toks])
                )
        else:
            for h in range(HEADS_DEV):
                terms.append((h, slice(3 * HD, WIDE), lambda h=h: TA[h, 3 * HD :, toks]))
            for f in range(CUTS):
                low = f * WIDE + CUT
                terms.append(
                    (HEADS_DEV + f, slice(CUT, WIDE), lambda low=low: H1[low : low + CUT, toks])
                )
        for place, (k, cols, right) in enumerate(terms):
            term = nn(W[k, features, cols], right())
            own[...] = term if place == 0 else own[...] + term

    def sib_copy(which, i):
        return remote(
            sib_send.at[lax.rem(i, 2)],
            sib_land.at[lax.rem(i, 4)],
            sib_s.at[which, i],
            sib_r.at[which, i],
            b,
            1 - c,
        )

    def stage(which, i):
        if which == 0:
            return H1.at[pl.ds(half, half), pl.ds(pl.multiple_of(i * TILE, 128), TILE)]
        t = (which - 1) * (TILES - 2) + i
        return H2.at[
            pl.ds(pl.multiple_of(t // PER_ROW * half, 128), half),
            pl.ds(pl.multiple_of(lax.rem(t, PER_ROW) * TILE, 128), TILE),
        ]

    def plane_copy(which, i):
        slot = tile_slot(i)
        low, high = lax.rem(slot, 2), slot // 2
        to = b + low * (1 - 2 * lax.rem(b, 2)) + high * 2 * (1 - 2 * lax.rem(b // 2, 2))
        src = stage(which, i)
        return remote(
            src,
            xr.at[which, slot - 1, lax.rem(i, 2)],
            p_s.at[which, i],
            p_r.at[which, i],
            to,
            c,
        )

    def tile_a(which, i):
        @pl.when(i >= 2)
        def _():
            sib_copy(which, i - 2).wait_send()

        product(which, i, 1 - c)
        sib_send[lax.rem(i, 2)] = own[...].astype(jnp.bfloat16)
        sib_copy(which, i).start()

    def tile_b(which, i):
        product(which, i, c)
        sib_copy(which, i).wait_recv()

        @pl.when(i < TILES - 2)
        def _():
            total = (own[...] + sib_land[lax.rem(i, 4)].astype(jnp.float32)).astype(jnp.bfloat16)
            stage(which, i)[...] = total
            plane_copy(which, i).start()

        @pl.when(i >= TILES - 2)
        def _():
            own[...] = own[...] + sib_land[lax.rem(i, 4)].astype(jnp.float32)
            keep = pltpu.make_async_copy(own, xo.at[which, lax.rem(i, 2)], tmp_s.at[2])
            keep.start()
            keep.wait()

    def sum_tiles(which, beside):
        tile_a(which, 0)

        def step(i, carry):
            @pl.when(i < TILES - 1)
            def _():
                tile_a(which, i + 1)

            tile_b(which, i)
            beside(i)
            return carry

        lax.fori_loop(0, TILES, step, 0)

    def sib_sent(which):
        for i in range(TILES - 2, TILES):
            sib_copy(which, i).wait_send()

    def spread(first, last, i, pieces, run):
        steps = last - first
        run(
            first + (steps * i + pieces - 1) // pieces,
            first + (steps * (i + 1) + pieces - 1) // pieces,
        )

    def ag_share(low, high, i, pieces):
        spread(low * S // 3, high * S // 3, i, pieces, ag_range)

    def rs_share(low, high, i, pieces):
        spread(low * (S + 1) // 4, high * (S + 1) // 4, i, pieces, rs_range)

    a2a_start(0)
    gather_one(0, xin, H1)
    gather_one(1, yin, DY)
    ag(0, 1)
    a2a_start(1)
    gather_two(0, xin, H1)
    gather_two(1, yin, DY)
    ag(1, 2)
    a2a_start(2)
    x_local(0, xin, H1).wait()
    sx_wait(0, H1, 0)
    norm_rows(0)
    ag(2, 3)
    gather_three(0, xin, H1)
    gather_sent(0, xin, H1)
    for k in range(3, CHUNKS):
        a2a_start(k)
    for slot in range(1, INNER):
        sx_wait(0, H1, slot)
        norm_rows(slot)
        if slot < 3:
            ag(2 + slot, 3 + slot)

    def project_step(h):
        ag_wait(h, S)

        def slot_step(slot, inner_carry):
            forward_piece(h, slot)
            ag_share(5 + 2 * h, 7 + 2 * h, slot, INNER)
            return inner_carry

        lax.fori_loop(0, INNER, slot_step, 0)

    project_step(0)
    gather_three(1, yin, DY)
    project_step(1)
    x_local(1, yin, DY).wait()
    for slot in range(INNER):
        sx_wait(1, DY, slot)
    gather_sent(1, yin, DY)

    def head_step(h, carry):
        def slot_step(slot, inner_carry):
            head_piece(h, slot)
            ag_share(9 + 2 * h, 11 + 2 * h, slot, INNER)
            rs_share(0, 3 * h, slot, INNER)
            return inner_carry

        lax.fori_loop(0, INNER, slot_step, 0)
        grads(h, head_turned(h), H1, 3 * HD)
        return carry

    lax.fori_loop(0, HEADS_DEV, head_step, 0)

    def beside_one(i):
        ag_share(15, 17, i, TILES)
        rs_share(6, 10, i, TILES)

    def cut_step(f, carry):
        ag_wait(HEADS_DEV + f, S)

        @pl.when(f == CUTS // 2)
        def _():
            for i in range(TILES - 2):
                plane_copy(0, i).wait_send()

        def slot_step(slot, inner_carry):
            cut_piece(f, slot)
            ag_share(
                jnp.where(f == 0, 13, jnp.where(f == 1, 17, 18)),
                jnp.where(f == 0, 15, 18),
                slot,
                INNER,
            )
            rs_share(
                jnp.where(f == 0, 3, jnp.where(f == 1, 10, 6 + 3 * f)),
                jnp.where(f == 0, 6, jnp.where(f == 1, 12, 9 + 3 * f)),
                slot,
                INNER,
            )
            return inner_carry

        lax.fori_loop(0, INNER, slot_step, 0)
        grads(HEADS_DEV + f, cut_turned(f), H2, CUT)

        @pl.when(f == 0)
        def _():
            sum_tiles(0, beside_one)

        return carry

    lax.fori_loop(0, CUTS, cut_step, 0)
    sib_sent(0)
    sum_tiles(1, lambda i: rs_share(18, 22, i, TILES))
    sib_sent(1)
    sum_tiles(2, lambda i: rs_share(22, 24, i, TILES))
    sib_sent(2)

    gr_sent(CHUNKS - 1)

    def drain_chunk(k, carry):
        for d in range(1, INNER):
            a2a_copy(k, d).wait_send()
            gr_copy(k, d, True).wait_recv()

        def drain_step(s, inner_carry):
            ag_sends(k, s, lambda copy: copy.wait_send())
            return inner_carry

        lax.fori_loop(1, S + 1, drain_step, 0)
        return carry

    lax.fori_loop(0, CHUNKS, drain_chunk, 0)
    for way in range(2):

        @pl.when(rs_sends(way, S))
        def _():
            rs_copy(CHUNKS - 1, way, S).wait_send()

    for which in range(3):

        def drain_tile(i, carry):
            if which:
                plane_copy(which, i).wait_send()
            plane_copy(which, i).wait_recv()
            return carry

        lax.fori_loop(0, TILES - 2, drain_tile, 0)


def block_call(count, wst, xin, yin, turns, norm_params, bias_h, bias_f):
    outer = count // INNER
    S = outer - 1
    tokens, half = xin.shape
    group = INNER * tokens
    rows = wst.shape[2]
    tile = tokens // 2
    low, high = jnp.bfloat16, jnp.float32
    any_spec = pl.BlockSpec(memory_space=pl.ANY)
    vmem_spec = pl.BlockSpec(memory_space=pltpu.VMEM)
    dma = pltpu.SemaphoreType.DMA
    return pl.pallas_call(
        functools.partial(block_kernel, count),
        out_shape=[
            jax.ShapeDtypeStruct((CHUNKS, INNER, rows, WIDE), low),
            jax.ShapeDtypeStruct((3, INNER - 1, 2, half, tile), low),
            jax.ShapeDtypeStruct((3, 2, half, tile), high),
            jax.ShapeDtypeStruct((HEADS_DEV, 1, 3 * HD), high),
            jax.ShapeDtypeStruct((CUTS, 1, CUT), high),
            jax.ShapeDtypeStruct((CHUNKS, 1, WIDE), high),
            jax.ShapeDtypeStruct((tokens, 128), high),
        ],
        in_specs=[any_spec] * 3 + [vmem_spec] * 4,
        out_specs=[any_spec] * 3 + [vmem_spec] * 4,
        scratch_shapes=[
            pltpu.VMEM((group, D), low),
            pltpu.VMEM((group, D), low),
            pltpu.VMEM((group, D), low),
            pltpu.VMEM((CHUNKS, D, WIDE), low),
            pltpu.VMEM((HEADS_DEV, WIDE, group), low),
            pltpu.VMEM((2, outer, WIDE, INNER * rows), high),
            pltpu.VMEM((2, WIDE, INNER * rows), low),
            pltpu.VMEM((INNER * rows, WIDE), low),
            pltpu.VMEM((2, S, WIDE, INNER * rows), low),
            pltpu.VMEM((2, half, tile), low),
            pltpu.VMEM((4, half, tile), low),
            pltpu.VMEM((half, tile), high),
            dma((CHUNKS, INNER - 1)),
            dma((CHUNKS, INNER - 1)),
            dma((CHUNKS,)),
            dma((CHUNKS, 2, S)),
            dma((CHUNKS, 2, S)),
            dma((2, INNER - 1)),
            dma((2, INNER - 1)),
            dma((2, INNER)),
            dma((2, INNER)),
            dma((CHUNKS, 2, S)),
            dma((CHUNKS, 2, S)),
            dma((CHUNKS, INNER)),
            dma((CHUNKS, INNER - 1)),
            dma((3, 2 * INNER)),
            dma((3, 2 * INNER)),
            dma((3, 2 * INNER)),
            dma((3, 2 * INNER)),
            dma((3,)),
            pltpu.SemaphoreType.REGULAR((2,)),
        ],
        compiler_params=pltpu.CompilerParams(
            collective_id=0, has_side_effects=True, vmem_limit_bytes=64 * 1024 * 1024
        ),
        cost_estimate=pl.CostEstimate(
            flops=80_000_000_000, bytes_accessed=60_000_000, transcendentals=10_000_000
        ),
    )(wst, xin, yin, turns, norm_params, bias_h, bias_f)


SLOT_ROWS = 16
PACK_ROWS = 40
PACK_ENDS = (0, 3, 4, 8, 12, 17, 22, 27, 31, 35, 39)


def total_of(values):
    return jnp.sum(jnp.sum(values, axis=0, keepdims=True), axis=1, keepdims=True)


def tail_kernel(
    count,
    gr,
    wq,
    wo,
    w1,
    w2,
    xr,
    xo,
    xin,
    yin,
    st,
    norm_ref,
    pb,
    fcb,
    row_old,
    qc_old,
    or_old,
    f1_old,
    f2_old,
    norm_second,
    bias_second,
    fcb_second,
    cs,
    qb,
    fb,
    out_ref,
    ing_ref,
    row_new,
    pack,
    norm_pack,
    qc_new,
    or_new,
    f1_new,
    f2_new,
    norm_grad,
    bias_grad,
    fcb_grad,
    scaled_buf,
    normed_buf,
    terms,
    terms_in,
    rsum,
    rsum_in,
    pay,
    z_in,
    z_sum,
    p_in,
    p_sum,
    s_in,
    pay2,
    z2_in,
    z2_sum,
    p2_in,
    p2_sum,
    s2_in,
    z_s,
    z_r,
    p_s,
    p_r,
    s_s,
    s_r,
):
    outer = count // INNER
    T, half = xin.shape
    R = gr.shape[2]
    b = lax.axis_index("batch")
    c = lax.axis_index("branch")
    q = lax.rem(b, INNER)
    o = b // INNER
    bx, by = flip(b, 1), flip(b, 2)
    near = (bx, by, flip(bx, 2))
    on_b = (b == 0).astype(jnp.float32)
    on_c = (c == 0).astype(jnp.float32)

    def remote(src, dst, ssem, rsem, to_b, to_c):
        return pltpu.make_async_remote_copy(
            src_ref=src,
            dst_ref=dst,
            send_sem=ssem,
            recv_sem=rsem,
            device_id=(to_b, to_c),
            device_id_type=MESH,
        )

    def chain(d):
        return lax.rem(o + d, outer)

    barrier = pltpu.get_barrier_semaphore()
    for who in near:
        pl.semaphore_signal(barrier, inc=1, device_id=(who, c), device_id_type=MESH)
    pl.semaphore_signal(barrier, inc=1, device_id=(b, 1 - c), device_id_type=MESH)
    for d in range(1, outer):
        pl.semaphore_signal(
            barrier, inc=1, device_id=(chain(d) * INNER + q, c), device_id_type=MESH
        )

    HALF_T = T // 2
    lane_t = lax.broadcasted_iota(jnp.int32, (HALF_T, 128), 1)
    own_half = pl.ds(pl.multiple_of(c * half, 128), half)
    other_half = pl.ds(pl.multiple_of((1 - c) * half, 128), half)
    gain_a = norm_ref[0:1, own_half]
    gain_b = norm_ref[2:3, own_half]
    pay[...] = jnp.zeros_like(pay)
    for i in range(2):
        rows = slice(i * HALF_T, (i + 1) * HALF_T)

        def whole(which):
            return (
                xo[which, i]
                + xr[which, 0, i].astype(jnp.float32)
                + xr[which, 1, i].astype(jnp.float32)
                + xr[which, 2, i].astype(jnp.float32)
            ).T

        values = xin[rows, :].astype(jnp.float32)
        out_ref[rows, :] = (values + whole(2) + pb[3:4, :] + pb[4:5, :]).astype(jnp.bfloat16)
        normed = (values - st[rows, 0:1]) * st[rows, 1:2]
        one = whole(0)
        two = whole(1)
        scaled = one * gain_a + two * gain_b
        scaled_buf[rows, :] = scaled
        normed_buf[rows, :] = normed
        terms[rows, :] = jnp.where(
            lane_t == 0,
            jnp.sum(scaled, axis=1, keepdims=True),
            jnp.where(lane_t == 1, jnp.sum(scaled * normed, axis=1, keepdims=True), 0.0),
        )
        pay[5:6, :] += jnp.sum(one * normed, axis=0, keepdims=True)
        pay[6:7, :] += jnp.sum(one, axis=0, keepdims=True)
        pay[7:8, :] += jnp.sum(two * normed, axis=0, keepdims=True)
        pay[8:9, :] += jnp.sum(two, axis=0, keepdims=True)
        pay[9:10, :] += jnp.sum(yin[rows, :].astype(jnp.float32), axis=0, keepdims=True)
    for k in range(CHUNKS):
        pay[k // 2 : k // 2 + 1, k % 2 * WIDE : (k % 2 + 1) * WIDE] = cs[k]
    for h in range(HEADS_DEV):
        pay[3:4, h * 3 * HD : (h + 1) * 3 * HD] = qb[h]
    for f in range(CUTS):
        pay[4:5, f * CUT : (f + 1) * CUT] = fb[f]
    lane_p = lax.broadcasted_iota(jnp.int32, (1, half), 1)
    biases = jnp.sum(pb[...] * pb[...], axis=1, keepdims=True) * on_b
    scalars = (
        [total_of(w[...] * w[...]) for w in (wq, wo, w1, w2)]
        + [biases[i : i + 1] for i in range(5)]
        + [total_of(fcb[...] * fcb[...]) * on_b]
    )
    line = jnp.zeros((1, half), jnp.float32)
    for place, value in enumerate(scalars):
        line = jnp.where(lane_p == place, value, line)
    pay[10:11, :] = line

    pl.semaphore_wait(barrier, INNER + outer - 1)

    def chain_sends(src, buf, base, what):
        for d in range(1, outer):
            what(
                remote(
                    src,
                    buf.at[o],
                    z_s.at[base, d - 1],
                    z_r.at[base, d - 1],
                    chain(d) * INNER + q,
                    c,
                )
            )

    def chain_waits(src, buf, base):
        for d in range(1, outer):
            source = chain(outer - d)
            remote(
                src,
                buf.at[source],
                z_s.at[base, d - 1],
                z_r.at[base, d - 1],
                source * INNER + q,
                c,
            ).wait_recv()

    def plane_sends(src, buf, base, what):
        for d in range(1, INNER):
            what(remote(src, buf.at[q], p_s.at[base, d - 1], p_r.at[base, d - 1], near[d - 1], c))

    def plane_waits(src, buf, base):
        for d in range(1, INNER):
            remote(
                src,
                buf.at[lax.rem(near[d - 1], INNER)],
                p_s.at[base, d - 1],
                p_r.at[base, d - 1],
                near[d - 1],
                c,
            ).wait_recv()

    def pair_copy(src, dst, place):
        return remote(src, dst, s_s.at[place], s_r.at[place], b, 1 - c)

    start = lambda copy: copy.start()
    chain_sends(pay, z_in, 0, start)
    z_in[o] = pay[...]
    pair_copy(terms, terms_in, 0).start()

    lane_r = lax.broadcasted_iota(jnp.int32, (R, 128), 1)
    head_square = jnp.zeros((R, WIDE), jnp.float32)
    cut_square = jnp.zeros((R, WIDE), jnp.float32)
    for part in range(INNER):
        for k in range(CHUNKS):
            gradient = gr[k, part].astype(jnp.float32)
            if k < HEADS_DEV:
                head_square = head_square + squares(gradient)
            else:
                cut_square = cut_square + squares(gradient)
    pieces = (
        jnp.sum(head_square[:, : 3 * HD], axis=1, keepdims=True),
        jnp.sum(cut_square[:, :CUT], axis=1, keepdims=True),
        jnp.sum(head_square[:, 3 * HD :], axis=1, keepdims=True),
        jnp.sum(cut_square[:, CUT:], axis=1, keepdims=True),
    )
    line = jnp.zeros((R, 128), jnp.float32)
    for place, value in enumerate(pieces):
        line = jnp.where(lane_r == place, value, line)
    rsum[...] = line
    pair_copy(rsum, rsum_in, 1).start()

    pair_copy(terms, terms_in, 0).wait_recv()
    for i in range(2):
        rows = slice(i * HALF_T, (i + 1) * HALF_T)
        both = terms[rows, :] + terms_in[rows, :]
        ing_ref[rows, :] = (
            st[rows, 1:2]
            * (
                scaled_buf[rows, :]
                - both[:, 0:1] / D
                - normed_buf[rows, :] * (both[:, 1:2] / D)
            )
            + yin[rows, :].astype(jnp.float32)
        ).astype(jnp.bfloat16)
    pair_copy(rsum, rsum_in, 1).wait_recv()
    rows_after = renew_stat(row_old[...], (rsum[...] + rsum_in[...])[:, :4])
    row_new[...] = jnp.concatenate(
        [rows_after, jnp.zeros((R, 128 - 4), jnp.float32)], axis=1
    )

    chain_waits(pay, z_in, 0)
    acc = z_in[0]
    for j in range(1, outer):
        acc = acc + z_in[j]
    z_sum[...] = acc
    plane_sends(z_sum, p_in, 0, start)
    p_in[q] = acc
    plane_waits(z_sum, p_in, 0)
    p_sum[...] = p_in[0] + p_in[1] + p_in[2] + p_in[3]
    pair_copy(p_sum, s_in, 2).start()

    inverse_rows = 1.0 / rows_after
    head_acc = [jnp.zeros((R, 3 * HD), jnp.float32), jnp.zeros((R, HD), jnp.float32)]
    cut_acc = [jnp.zeros((R, CUT), jnp.float32), jnp.zeros((R, CUT), jnp.float32)]
    for part in range(INNER):
        sums = p_in[part]
        for h in range(HEADS_DEV):
            gradient = gr[h, part].astype(jnp.float32)
            square = gradient * gradient
            found = sums[h // 2 : h // 2 + 1, h % 2 * WIDE : (h % 2 + 1) * WIDE]
            cols = pl.ds(part * HEADS_DEV * HD + h * HD, HD)
            parts = []
            for p in range(3):
                fresh = renew_stat(qc_old[p : p + 1, cols], found[:, p * HD : (p + 1) * HD])
                qc_new[p : p + 1, cols] = fresh
                parts.append(1.0 / fresh)
            head_acc[0] = head_acc[0] + square[:, : 3 * HD] * jnp.concatenate(parts, axis=1)
            fresh = renew_stat(or_old[:, cols], found[:, 3 * HD :])
            or_new[:, cols] = fresh
            head_acc[1] = head_acc[1] + square[:, 3 * HD :] * (1.0 / fresh)
        for f in range(CUTS):
            k = HEADS_DEV + f
            gradient = gr[k, part].astype(jnp.float32)
            square = gradient * gradient
            found = sums[k // 2 : k // 2 + 1, k % 2 * WIDE : (k % 2 + 1) * WIDE]
            cols = slice(f * CUT, (f + 1) * CUT)
            fresh = renew_stat(f1_old[part : part + 1, cols], found[:, :CUT])
            f1_new[part, :, cols] = fresh
            cut_acc[0] = cut_acc[0] + square[:, :CUT] * (1.0 / fresh)
            fresh = renew_stat(f2_old[part : part + 1, cols], found[:, CUT:])
            f2_new[part, :, cols] = fresh
            cut_acc[1] = cut_acc[1] + square[:, CUT:] * (1.0 / fresh)
    for part in range(INNER):
        for h in range(HEADS_DEV):
            for p in range(3):
                low = h * 3 * HD + p * HD
                bias_grad[p : p + 1, pl.ds(part * HEADS_DEV * HD + h * HD, HD)] = p_in[
                    part, 3:4, low : low + HD
                ]
        fcb_grad[part : part + 1, :] = p_in[part, 4:5, :]
    bias_grad[3:4, :] = p_sum[9:10, :]
    bias_grad[4:5, :] = p_sum[9:10, :]
    bias_after, bias_update = second_step(bias_grad[...], bias_second[...])
    pack[17:22, :] = bias_after
    fcb_after, fcb_update = second_step(fcb_grad[...], fcb_second[...])
    pack[31:35, :] = fcb_after
    usq = jnp.sum(bias_update * bias_update, axis=1, keepdims=True) * on_b
    scalars = (
        [
            total_of(rows_after[:, 0:1]) * on_c,
            total_of(head_acc[0] * inverse_rows[:, 0:1]),
            total_of(rows_after[:, 1:2]) * on_c,
            total_of(cut_acc[0] * inverse_rows[:, 1:2]),
            total_of(or_new[...]) * on_b,
            total_of(head_acc[1] * inverse_rows[:, 2:3]),
            sum(total_of(f2_new[part]) for part in range(INNER)) * on_b,
            total_of(cut_acc[1] * inverse_rows[:, 3:4]),
        ]
        + [usq[i : i + 1] for i in range(5)]
        + [total_of(fcb_update * fcb_update) * on_b]
    )
    lane_s = lax.broadcasted_iota(jnp.int32, (8, 128), 1)
    line = jnp.zeros((8, 128), jnp.float32)
    for place, value in enumerate(scalars):
        line = jnp.where(lane_s == place, value, line)
    pay2[...] = line
    chain_sends(pay2, z2_in, 1, start)
    z2_in[o] = line
    pack[0:3, :] = qc_new[...]
    pack[3:4, :] = or_new[...]
    for part in range(INNER):
        pack[4 + part : 5 + part, :] = f1_new[part]
        pack[8 + part : 9 + part, :] = f2_new[part]
    pack[12:17, :] = bias_grad[...]
    pack[27:31, :] = fcb_grad[...]

    pair_copy(p_sum, s_in, 2).wait_recv()
    norm_grad[:, own_half] = p_sum[5:9, :]
    norm_grad[:, other_half] = s_in[5:9, :]
    old = p_sum[10:11, :] + s_in[10:11, :]
    norm_after, norm_update = second_step(norm_grad[...], norm_second[...])
    norm_pack[0:4, :] = norm_grad[...]
    norm_pack[4:8, :] = norm_after

    def moved(vector, update, update_square, old_square, entries):
        clip_factor = jnp.maximum(1.0, jnp.sqrt(update_square / entries))
        step_rate = RATE * jnp.maximum(FLOOR_RATE, jnp.sqrt(old_square / entries))
        return vector - step_rate * update / clip_factor

    norm_values = norm_ref[...]
    norm_pack[8:12, :] = moved(
        norm_values,
        norm_update,
        jnp.sum(norm_update * norm_update, axis=1, keepdims=True),
        jnp.sum(norm_values * norm_values, axis=1, keepdims=True),
        D,
    )

    chain_waits(pay2, z2_in, 1)
    acc = z2_in[0]
    for j in range(1, outer):
        acc = acc + z2_in[j]
    z2_sum[...] = acc
    plane_sends(z2_sum, p2_in, 1, start)
    p2_in[q] = acc
    plane_waits(z2_sum, p2_in, 1)
    acc = p2_in[0] + p2_in[1] + p2_in[2] + p2_in[3]
    p2_sum[...] = acc
    pair_copy(p2_sum, s2_in, 3).start()
    pair_copy(p2_sum, s2_in, 3).wait_recv()
    sums = (acc + s2_in[...])[0:1, :]

    def scalar(place):
        return sums[:, place : place + 1]

    def factor(total, inverse, place, entries):
        clip_factor = jnp.maximum(1.0, jnp.sqrt(total * inverse / entries))
        rate = RATE * jnp.maximum(FLOOR_RATE, jnp.sqrt(old[:, place : place + 1] / entries))
        return rate * jnp.sqrt(total) / clip_factor

    factors = (
        factor(scalar(0), scalar(1), 0, 3 * D * D),
        factor(scalar(2), scalar(3), 2, D * FF),
        factor(scalar(4), scalar(5), 1, D * D),
        factor(scalar(6), scalar(7), 3, FF * D),
    )
    line = jnp.zeros((8, 128), jnp.float32)
    for place, value in enumerate(factors):
        line = jnp.where(lane_s == place, value, line)
    pack[39:40, :] = jnp.concatenate(
        [line[0:1, :], jnp.zeros((1, half - 128), jnp.float32)], axis=1
    )
    for i in range(5):
        pack[22 + i : 23 + i, :] = moved(
            pb[i : i + 1, :], bias_update[i : i + 1], scalar(8 + i), old[:, 4 + i : 5 + i], D
        )
    pack[35:39, :] = moved(fcb[...], fcb_update, scalar(13), old[:, 9:10], FF)

    finish = lambda copy: copy.wait_send()
    chain_sends(pay, z_in, 0, finish)
    chain_sends(pay2, z2_in, 1, finish)
    plane_sends(z_sum, p_in, 0, finish)
    plane_sends(z2_sum, p2_in, 1, finish)
    pair_copy(terms, terms_in, 0).wait_send()
    pair_copy(rsum, rsum_in, 1).wait_send()
    pair_copy(p_sum, s_in, 2).wait_send()
    pair_copy(p2_sum, s2_in, 3).wait_send()


def tail_call(count, *args):
    outer = count // INNER
    received, xin = args[0], args[7]
    tokens, half = xin.shape
    rows = received.shape[2]
    high = jnp.float32
    spec = pl.BlockSpec(memory_space=pltpu.VMEM)
    dma = pltpu.SemaphoreType.DMA

    def out(*shape, dtype=high):
        return jax.ShapeDtypeStruct(shape, dtype)

    outs = [
        out(tokens, half, dtype=jnp.bfloat16),
        out(tokens, half, dtype=jnp.bfloat16),
        out(rows, 128),
        out(PACK_ROWS, half),
        out(12, D),
    ]
    slot = (SLOT_ROWS, half)
    return pl.pallas_call(
        functools.partial(tail_kernel, count),
        out_shape=outs,
        in_specs=[spec] * len(args),
        out_specs=[spec] * len(outs),
        scratch_shapes=[
            pltpu.VMEM((3, half), high),
            pltpu.VMEM((1, half), high),
            pltpu.VMEM((INNER, 1, half), high),
            pltpu.VMEM((INNER, 1, half), high),
            pltpu.VMEM((4, D), high),
            pltpu.VMEM((5, half), high),
            pltpu.VMEM((INNER, half), high),
            pltpu.VMEM((tokens, half), high),
            pltpu.VMEM((tokens, half), high),
            pltpu.VMEM((tokens, 128), high),
            pltpu.VMEM((tokens, 128), high),
            pltpu.VMEM((rows, 128), high),
            pltpu.VMEM((rows, 128), high),
            pltpu.VMEM(slot, high),
            pltpu.VMEM((outer, *slot), high),
            pltpu.VMEM(slot, high),
            pltpu.VMEM((INNER, *slot), high),
            pltpu.VMEM(slot, high),
            pltpu.VMEM(slot, high),
            pltpu.VMEM((8, 128), high),
            pltpu.VMEM((outer, 8, 128), high),
            pltpu.VMEM((8, 128), high),
            pltpu.VMEM((INNER, 8, 128), high),
            pltpu.VMEM((8, 128), high),
            pltpu.VMEM((8, 128), high),
            dma((2, outer - 1)),
            dma((2, outer - 1)),
            dma((2, INNER - 1)),
            dma((2, INNER - 1)),
            dma((4,)),
            dma((4,)),
        ],
        compiler_params=pltpu.CompilerParams(
            collective_id=1, has_side_effects=True, vmem_limit_bytes=58 * 1024 * 1024
        ),
        cost_estimate=pl.CostEstimate(
            flops=50_000_000, bytes_accessed=40_000_000, transcendentals=100_000
        ),
    )(*args)


def update_kernel(*refs):
    gr, wq, wo, w1, w2, row_new, pack, norm_pack, output, input_grad = refs[:10]
    q_grad, q_next, q_copy, o_grad, o_next, o_copy = refs[10:16]
    f1_grad, f1_next, f1_copy, f2_grad, f2_next, f2_copy = refs[16:22]
    row_out, whole_out, pack_out, norm_out = refs[22:26], refs[26:28], refs[28:38], refs[38:]
    part = pl.program_id(0)
    side = lax.rsqrt(row_new[:, :4]) * pack[39:40, :4]
    width_q = HEADS_DEV * HD

    @pl.when(part == 0)
    def _():
        whole_out[0][...] = output[...]
        whole_out[1][...] = input_grad[...]
        for place, target in enumerate(pack_out):
            target[...] = pack[PACK_ENDS[place] : PACK_ENDS[place + 1], :]
        for place, target in enumerate(norm_out):
            target[...] = norm_pack[4 * place : 4 * place + 4, :]
        turned = row_new[...].T
        for place in range(4):
            row_out[place][...] = turned[place : place + 1, :]

    def put(grad_ref, next_ref, copy_ref, where, weight, gradient, update):
        fresh = weight[where] - update
        grad_ref[where] = gradient
        next_ref[where] = fresh
        copy_ref[where] = fresh.astype(jnp.bfloat16)

    for h in range(HEADS_DEV):
        gradient = gr[h, 0].astype(jnp.float32)
        cols = pl.ds(pl.multiple_of(part * width_q + h * HD, HD), HD)
        for p in range(3):
            mine = gradient[:, p * HD : (p + 1) * HD]
            update = mine * side[:, 0:1] * lax.rsqrt(pack[p : p + 1, cols])
            where = (p, slice(None), slice(h * HD, (h + 1) * HD))
            put(q_grad, q_next, q_copy, where, wq, mine, update)
        mine = gradient[:, 3 * HD :]
        update = mine * side[:, 2:3] * lax.rsqrt(pack[3:4, cols])
        where = (slice(h * HD, (h + 1) * HD), slice(None))
        put(o_grad, o_next, o_copy, where, wo, mine.T, update.T)
    for f in range(CUTS):
        gradient = gr[HEADS_DEV + f, 0].astype(jnp.float32)
        cols = slice(f * CUT, (f + 1) * CUT)
        mine = gradient[:, :CUT]
        update = mine * side[:, 1:2] * lax.rsqrt(pack[pl.ds(4 + part, 1), cols])
        put(f1_grad, f1_next, f1_copy, (slice(None), cols), w1, mine, update)
        mine = gradient[:, CUT:]
        update = mine * side[:, 3:4] * lax.rsqrt(pack[pl.ds(8 + part, 1), cols])
        put(f2_grad, f2_next, f2_copy, (cols, slice(None)), w2, mine.T, update.T)


def update_call(gr, wq, wo, w1, w2, row_new, pack, norm_pack, output, input_grad):
    rows = gr.shape[2]
    half = pack.shape[1]
    width_q = HEADS_DEV * HD
    hidden_q = CUTS * CUT
    spec = pl.BlockSpec
    q_spec = spec((3, rows, width_q), lambda i: (0, 0, i))
    o_spec = spec((width_q, rows), lambda i: (i, 0))
    f1_spec = spec((rows, hidden_q), lambda i: (0, i))
    f2_spec = spec((hidden_q, rows), lambda i: (i, 0))
    outs, out_specs = [], []
    for array, its in ((wq, q_spec), (wo, o_spec), (w1, f1_spec), (w2, f2_spec)):
        for dtype in (jnp.float32, jnp.float32, jnp.bfloat16):
            outs.append(jax.ShapeDtypeStruct(array.shape, dtype))
            out_specs.append(its)

    def fixed(shape):
        return spec(shape, lambda i: (0,) * len(shape))

    shapes = [((1, rows), jnp.float32)] * 4 + [(output.shape, output.dtype)] * 2
    for place in range(len(PACK_ENDS) - 1):
        shapes.append(((PACK_ENDS[place + 1] - PACK_ENDS[place], half), jnp.float32))
    shapes += [((4, D), jnp.float32)] * 3
    for shape, dtype in shapes:
        outs.append(jax.ShapeDtypeStruct(shape, dtype))
        out_specs.append(fixed(shape))
    small = (row_new, pack, norm_pack, output, input_grad)
    return pl.pallas_call(
        update_kernel,
        grid=(INNER,),
        out_shape=outs,
        in_specs=[
            spec((CHUNKS, 1, rows, WIDE), lambda i: (0, i, 0, 0)),
            q_spec,
            o_spec,
            f1_spec,
            f2_spec,
        ]
        + [fixed(array.shape) for array in small],
        out_specs=out_specs,
        compiler_params=pltpu.CompilerParams(vmem_limit_bytes=48 * 1024 * 1024),
        cost_estimate=pl.CostEstimate(
            flops=20_000_000, bytes_accessed=30_000_000, transcendentals=100_000
        ),
    )(gr, wq, wo, w1, w2, *small)


def swap_pairs(count, step):
    return [(i, i ^ step) for i in range(count)]


def block_of(array, index, size, axis=0):
    return lax.dynamic_slice_in_dim(array, index * size, size, axis)


def on_device(
    inputs,
    cotangent,
    segment_ids,
    w_qkv,
    w_out,
    w_fc1,
    w_fc2,
    norm_params,
    proj_bias,
    fc1_bias,
    qkv_rows,
    qkv_cols,
    out_rows,
    out_cols,
    fc1_rows,
    fc1_cols,
    fc2_rows,
    fc2_cols,
    norm_second,
    bias_second,
    fc1b_second,
):
    tokens = inputs.shape[0]
    local_width = inputs.shape[1]
    local_hidden = fc1_bias.shape[0]
    rows = w_qkv.shape[0]
    count = lax.axis_size("batch")
    c = lax.axis_index("branch")
    b = lax.axis_index("batch")
    q = lax.rem(b, INNER)
    group = INNER * tokens
    width_q = local_width // INNER
    hidden_q = local_hidden // INNER
    qkv_low = w_qkv.astype(jnp.bfloat16).reshape(rows, 3, INNER, HEADS_DEV, HD)
    out_low = w_out.astype(jnp.bfloat16).reshape(INNER, HEADS_DEV, HD, rows)
    fc1_low = w_fc1.astype(jnp.bfloat16).reshape(rows, INNER, CUTS, CUT)
    fc2_low = w_fc2.astype(jnp.bfloat16).reshape(INNER, CUTS, CUT, rows)
    heads_low = jnp.concatenate(
        [
            qkv_low.transpose(3, 2, 0, 1, 4).reshape(HEADS_DEV, INNER, rows, 3 * HD),
            out_low.transpose(1, 0, 3, 2),
        ],
        axis=3,
    )
    cuts_low = jnp.concatenate(
        [fc1_low.transpose(2, 1, 0, 3), fc2_low.transpose(1, 0, 3, 2)], axis=3
    )
    wst = jnp.concatenate([heads_low, cuts_low], axis=0)

    segment = jnp.concatenate(
        [segment_ids]
        + [lax.ppermute(segment_ids, "batch", swap_pairs(count, d)) for d in range(1, INNER)],
        axis=0,
    )
    positions_idx = jnp.arange(tokens)
    earlier = jnp.sum((segment[:, None, :] < segment[:, :, None]).astype(jnp.int32), axis=2)
    starts = earlier.astype(jnp.float32).reshape(1, group)
    places = (positions_idx[None] - earlier).astype(jnp.float32).reshape(1, group)
    frequency = 10000.0 ** (-2.0 * jnp.arange(ROT // 2, dtype=jnp.float32) / ROT)
    angles = frequency[:, None] * places
    cos_part = jnp.cos(angles)
    sin_part = jnp.sin(angles)
    turns = jnp.concatenate(
        [
            cos_part,
            cos_part,
            -sin_part,
            sin_part,
            jnp.broadcast_to(starts, (HD - 2 * ROT, group)),
        ],
        axis=0,
    )
    bias_h = (
        block_of(proj_bias[0:3], q, width_q, 1)
        .reshape(3, HEADS_DEV, HD)
        .transpose(1, 0, 2)
        .reshape(HEADS_DEV, 1, 3 * HD)
    )
    bias_f = block_of(fc1_bias, q, hidden_q).reshape(CUTS, 1, CUT)
    received, plane_parts, plane_own, head_bias, cut_bias, col_sums, row_moments = block_call(
        count, wst, inputs, cotangent, turns, norm_params, bias_h, bias_f
    )
    by_part = (INNER, hidden_q)
    qkv_parts = w_qkv.transpose(1, 0, 2)
    output, input_grad, row_stats, pack, norm_pack = tail_call(
        count,
        received,
        qkv_parts.reshape(3 * rows, local_width),
        w_out,
        w_fc1,
        w_fc2,
        plane_parts,
        plane_own,
        inputs,
        cotangent,
        row_moments,
        norm_params,
        proj_bias,
        fc1_bias.reshape(by_part),
        jnp.stack([qkv_rows, fc1_rows, out_cols, fc2_cols], axis=1),
        qkv_cols,
        out_rows.reshape(1, local_width),
        fc1_cols.reshape(by_part),
        fc2_rows.reshape(by_part),
        norm_second,
        bias_second,
        fc1b_second.reshape(by_part),
        col_sums,
        head_bias,
        cut_bias,
    )
    updated = update_call(
        received,
        qkv_parts,
        w_out,
        w_fc1,
        w_fc2,
        row_stats,
        pack,
        norm_pack,
        output,
        input_grad,
    )
    qkv_grad, qkv_next, qkv_copy = (array.transpose(1, 0, 2) for array in updated[0:3])
    out_grad, out_next, out_copy = updated[3:6]
    fc1_grad, fc1_next, fc1_copy = updated[6:9]
    fc2_grad, fc2_next, fc2_copy = updated[9:12]
    qkv_rows_new, fc1_rows_new, out_cols_new, fc2_cols_new = (
        array.reshape(rows) for array in updated[12:16]
    )
    (
        output,
        input_grad,
        qkv_cols_new,
        out_rows_new,
        fc1_cols_new,
        fc2_rows_new,
        bias_grad,
        bias_moment,
        bias_new,
        fc1b_grad,
        fc1b_moment,
        fc1b_new,
        norm_grad,
        norm_moment,
        norm_new,
    ) = updated[16:]
    return (
        output,
        input_grad,
        qkv_grad,
        qkv_next,
        qkv_rows_new,
        qkv_cols_new,
        qkv_copy,
        out_grad,
        out_next,
        out_rows_new.reshape(local_width),
        out_cols_new,
        out_copy,
        fc1_grad,
        fc1_next,
        fc1_rows_new,
        fc1_cols_new.reshape(local_hidden),
        fc1_copy,
        fc2_grad,
        fc2_next,
        fc2_rows_new.reshape(local_hidden),
        fc2_cols_new,
        fc2_copy,
        norm_grad,
        norm_moment,
        norm_new,
        bias_grad,
        bias_moment,
        bias_new,
        fc1b_grad.reshape(local_hidden),
        fc1b_moment.reshape(local_hidden),
        fc1b_new.reshape(local_hidden),
    )


def solution(mesh):
    in_specs = (
        P("batch", "branch"),
        P("batch", "branch"),
        P("batch", None),
        P("batch", None, "branch"),
        P("branch", "batch"),
        P("batch", "branch"),
        P("branch", "batch"),
        P(),
        P(None, "branch"),
        P("branch"),
        P("batch"),
        P(None, "branch"),
        P("branch"),
        P("batch"),
        P("batch"),
        P("branch"),
        P("branch"),
        P("batch"),
        P(),
        P(None, "branch"),
        P("branch"),
    )
    out_specs = (
        P("batch", "branch"),
        P("batch", "branch"),
        P("batch", None, "branch"),
        P("batch", None, "branch"),
        P("batch"),
        P(None, "branch"),
        P("batch", None, "branch"),
        P("branch", "batch"),
        P("branch", "batch"),
        P("branch"),
        P("batch"),
        P("branch", "batch"),
        P("batch", "branch"),
        P("batch", "branch"),
        P("batch"),
        P("branch"),
        P("batch", "branch"),
        P("branch", "batch"),
        P("branch", "batch"),
        P("branch"),
        P("batch"),
        P("branch", "batch"),
        P(),
        P(),
        P(),
        P(None, "branch"),
        P(None, "branch"),
        P(None, "branch"),
        P("branch"),
        P("branch"),
        P("branch"),
    )
    return jax.shard_map(
        on_device, mesh=mesh, in_specs=in_specs, out_specs=out_specs, check_vma=False
    )
```

```python
import functools

import jax
import jax.numpy as jnp
from jax import lax
from jax.experimental import pallas as pl
from jax.experimental.pallas import tpu as pltpu
from jax.sharding import PartitionSpec as P

D = 2048
HD = 128
ROT = 32
FF = 8192
STEP = 10


EPS_NORM = 1e-05
EPS_SQUARE = 1e-30
RATE = 0.3
FLOOR_RATE = 0.001


def decay_rate():
    return 1.0 - STEP ** (-0.8)


def squares(gradient):
    return gradient * gradient + EPS_SQUARE


def renew_stat(old_stat, new_sum):
    decay = decay_rate()
    return decay * old_stat + (1.0 - decay) * new_sum


def second_step(gradient, second):
    second_new = renew_stat(second, squares(gradient))
    return (second_new, gradient * lax.rsqrt(second_new))


INNER = 4
HEADS_DEV = 2
CUTS = 4
CHUNKS = HEADS_DEV + CUTS
CUT = 256
WIDE = 512
MESH = pl.DeviceIdType.MESH


def flip(index, step):
    return index + step * (1 - 2 * lax.rem(index // step, 2))


def nn(left, right):
    return jnp.dot(left, right, preferred_element_type=jnp.float32)


def nt(left, right):
    return lax.dot_general(
        left, right, (((1,), (1,)), ((), ())), preferred_element_type=jnp.float32
    )


def tn(left, right):
    return lax.dot_general(
        left, right, (((0,), (0,)), ((), ())), preferred_element_type=jnp.float32
    )


def block_kernel(
    count,
    wst,
    xin,
    yin,
    turn_ref,
    norm_ref,
    bias_h,
    bias_f,
    gr,
    xr,
    xo,
    qb,
    fb,
    cs,
    st,
    H1,
    H2,
    DY,
    W,
    TA,
    G,
    sbuf,
    fbuf,
    rsb,
    sib_send,
    sib_land,
    own,
    a2a_s,
    a2a_r,
    loc_s,
    ag_s,
    ag_r,
    x_s,
    x_r,
    sx_s,
    sx_r,
    rs_s,
    rs_r,
    gr_s,
    gr_r,
    sib_s,
    sib_r,
    p_s,
    p_r,
    tmp_s,
    free_s,
):
    outer = count // INNER
    S = outer - 1
    T, half = xin.shape
    R = wst.shape[2]
    block = INNER * R
    QT = T // 2
    b = lax.axis_index("batch")
    c = lax.axis_index("branch")
    q = lax.rem(b, INNER)
    o = b // INNER
    bx, by = flip(b, 1), flip(b, 2)
    bxy = flip(bx, 2)
    near = (bx, by, bxy)
    da = 1 + c
    db = 2 - c
    b_first = bx * (1 - c) + by * c
    b_second = by * (1 - c) + bx * c

    def remote(src, dst, ssem, rsem, to_b, to_c):
        return pltpu.make_async_remote_copy(
            src_ref=src,
            dst_ref=dst,
            send_sem=ssem,
            recv_sem=rsem,
            device_id=(to_b, to_c),
            device_id_type=MESH,
        )

    barrier = pltpu.get_barrier_semaphore()
    for who in near:
        pl.semaphore_signal(barrier, inc=1, device_id=(who, c), device_id_type=MESH)
    pl.semaphore_signal(barrier, inc=1, device_id=(b, 1 - c), device_id_type=MESH)

    @pl.when(o > 0)
    def _():
        pl.semaphore_signal(barrier, inc=1, device_id=(b - INNER, c), device_id_type=MESH)

    @pl.when(o < outer - 1)
    def _():
        pl.semaphore_signal(barrier, inc=1, device_id=(b + INNER, c), device_id_type=MESH)

    pl.semaphore_wait(barrier, 4 + jnp.minimum(o, 1) + jnp.minimum(outer - 1 - o, 1))

    def a2a_copy(k, d, received=False):
        to = near[d - 1]
        row = (to if received else b) * R
        return remote(
            wst.at[k, lax.rem(to, INNER)],
            W.at[k, pl.ds(pl.multiple_of(row, 16), R)],
            a2a_s.at[k, d - 1],
            a2a_r.at[k, d - 1],
            to,
            c,
        )

    def a2a_local(k):
        return pltpu.make_async_copy(
            wst.at[k, q], W.at[k, pl.ds(pl.multiple_of(b * R, 16), R)], loc_s.at[k]
        )

    def a2a_start(k):
        for d in range(1, INNER):
            a2a_copy(k, d).start()
        a2a_local(k).start()

    def a2a_wait(k):
        for d in range(1, INNER):
            a2a_copy(k, d, True).wait_recv()
        a2a_local(k).wait()

    def ag_copy(k, way, s, part):
        rows = pl.ds(pl.multiple_of(part * block, 16), block)
        to = b + INNER if way == 0 else b - INNER
        return remote(
            W.at[k, rows], W.at[k, rows], ag_s.at[k, way, s - 1], ag_r.at[k, way, s - 1], to, c
        )

    def ag_sends(k, s, what):
        @pl.when((o >= s - 1) & (o <= outer - 2))
        def _():
            what(ag_copy(k, 0, s, o - s + 1))

        @pl.when((o >= 1) & (o <= outer - s))
        def _():
            what(ag_copy(k, 1, s, o + s - 1))

    def ag_wait(k, s):
        @pl.when(o >= s)
        def _():
            ag_copy(k, 0, s, o - s).wait_recv()

        @pl.when(o <= outer - 1 - s)
        def _():
            ag_copy(k, 1, s, o + s).wait_recv()

    def ag_range(low, high):
        def step(n, carry):
            k = n // S
            s = lax.rem(n, S) + 1

            @pl.when(s == 1)
            def _():
                a2a_wait(k)

            @pl.when(s > 1)
            def _():
                ag_wait(k, s - 1)

            ag_sends(k, s, lambda copy: copy.start())
            return carry

        lax.fori_loop(low, high, step, 0)

    def ag(low, high):
        ag_range(low * S // 3, high * S // 3)

    def spot(buf, slot):
        return buf.at[
            pl.ds(pl.multiple_of(slot * T, 16), T), pl.ds(pl.multiple_of(c * half, 128), half)
        ]

    def other_spot(buf, slot):
        return buf.at[
            pl.ds(pl.multiple_of(slot * T, 16), T), pl.ds(pl.multiple_of((1 - c) * half, 128), half)
        ]

    def sx_copy(i, buf, slot, src=None):
        place = spot(buf, slot)
        return remote(place if src is None else src, place, sx_s.at[i, slot], sx_r.at[i, slot], b, 1 - c)

    def sx_wait(i, buf, slot):
        remote(
            other_spot(buf, slot), other_spot(buf, slot), sx_s.at[i, slot], sx_r.at[i, slot], b, 1 - c
        ).wait_recv()

    def x_first(i, src, buf):
        return remote(src, spot(buf, da), x_s.at[i, da - 1], x_r.at[i, da - 1], b_first, c)

    def x_second(i, src, buf):
        return remote(src, spot(buf, db), x_s.at[i, db - 1], x_r.at[i, db - 1], b_second, c)

    def x_forward(i, buf):
        return remote(spot(buf, da), spot(buf, 3), x_s.at[i, 2], x_r.at[i, 2], b_second, c)

    def x_diag(i, buf):
        return remote(spot(buf, 3), spot(buf, 3), x_s.at[i, 2], x_r.at[i, 2], b_second, c)

    def x_local(i, src, buf):
        return pltpu.make_async_copy(src, spot(buf, 0), tmp_s.at[i])

    def gather_one(i, src, buf):
        x_first(i, src, buf).start()
        x_local(i, src, buf).start()
        sx_copy(i, buf, 0, src).start()

    def gather_two(i, src, buf):
        x_first(i, src, buf).wait_recv()
        x_second(i, src, buf).start()
        x_forward(i, buf).start()
        sx_copy(i, buf, da).start()

    def gather_three(i, src, buf):
        x_second(i, src, buf).wait_recv()
        sx_copy(i, buf, db).start()
        x_diag(i, buf).wait_recv()
        sx_copy(i, buf, 3).start()

    def gather_sent(i, src, buf):
        x_first(i, src, buf).wait_send()
        x_second(i, src, buf).wait_send()
        x_forward(i, buf).wait_send()
        sx_copy(i, buf, 0, src).wait_send()
        for slot in range(1, INNER):
            sx_copy(i, buf, slot).wait_send()

    lane_n = lax.broadcasted_iota(jnp.int32, (64, 128), 1)

    def norm_rows(slot):
        def step(i, carry):
            rows = pl.ds(pl.multiple_of(slot * T + i * 64, 64), 64)
            values = H1[rows, :].astype(jnp.float32)
            mean = jnp.mean(values, axis=-1, keepdims=True)
            centered = values - mean
            inverse = lax.rsqrt(jnp.mean(centered * centered, axis=-1, keepdims=True) + EPS_NORM)
            normed = centered * inverse
            if slot == 0:
                st[pl.ds(pl.multiple_of(i * 64, 64), 64), :] = jnp.where(lane_n == 0, mean, inverse)
            H1[rows, :] = (normed * norm_ref[0:1, :] + norm_ref[1:2, :]).astype(jnp.bfloat16)
            H2[rows, :] = (normed * norm_ref[2:3, :] + norm_ref[3:4, :]).astype(jnp.bfloat16)
            return carry

        lax.fori_loop(0, T // 64, step, 0)

    lane = lax.broadcasted_iota(jnp.int32, (T, HD), 1)
    scale = HD ** (-0.5)

    def partner(tensor):
        return jnp.where(
            lane < ROT // 2,
            pltpu.roll(tensor, HD - ROT // 2, 1),
            jnp.where(lane < ROT, pltpu.roll(tensor, ROT // 2, 1), 0.0),
        )

    def turns_of(rows):
        table = turn_ref[:, rows].T
        cos_rows = jnp.where(lane < ROT, table, 1.0)
        sin_rows = pltpu.roll(table, HD - ROT, 1)
        return cos_rows, sin_rows, table[:, 2 * ROT : 2 * ROT + 1]

    def probs_at(h, slot, i):
        seen = QT * (i + 1)
        wide = min(block, seen)
        part = slice(QT * i, QT * (i + 1))
        base = slot * (outer // INNER)
        return [(h, base + j, part, slice(0, wide)) for j in range(seen // wide)]

    def forward_piece(h, slot):
        start = pl.multiple_of(slot * T, 128)
        rows = pl.ds(start, T)
        cos_rows, sin_rows, starts = turns_of(rows)
        projected = nn(H1[rows, :], W[h, :, : 3 * HD]) + bias_h[h]
        first = projected[:, :HD]
        queries = (first * cos_rows + partner(first) * sin_rows).astype(jnp.bfloat16)
        second = projected[:, HD : 2 * HD]
        keys = (second * cos_rows + partner(second) * sin_rows).astype(jnp.bfloat16)
        values = projected[:, 2 * HD :].astype(jnp.bfloat16)
        TA[h, :, pl.ds(start, HD)] = queries
        TA[h, :, pl.ds(start + HD, HD)] = keys
        TA[h, :, pl.ds(start + 2 * HD, HD)] = values
        for i in range(2):
            seen = QT * (i + 1)
            part = slice(QT * i, QT * (i + 1))
            raw = nt(queries[part], keys[:seen]) * scale
            query_at = lax.broadcasted_iota(jnp.int32, (QT, seen), 0) + QT * i
            key_at = lax.broadcasted_iota(jnp.int32, (QT, seen), 1)
            allowed = (key_at <= query_at) & (key_at.astype(jnp.float32) >= starts[part])
            scores = jnp.where(allowed, raw, -1e30)
            exponent = jnp.exp(scores - jnp.max(scores, axis=-1, keepdims=True))
            probs = exponent * (1.0 / jnp.sum(exponent, axis=-1, keepdims=True))
            for j, place in enumerate(probs_at(h, slot, i)):
                wide = min(block, seen)
                G[place] = probs[:, j * wide : (j + 1) * wide]
            TA[h, part, pl.ds(start + 3 * HD, HD)] = nn(
                probs.astype(jnp.bfloat16), values[:seen]
            ).astype(jnp.bfloat16)

    def head_piece(h, slot):
        start = pl.multiple_of(slot * T, 128)
        rows = pl.ds(start, T)
        cos_rows, sin_rows, _ = turns_of(rows)
        queries = TA[h, :, pl.ds(start, HD)]
        keys = TA[h, :, pl.ds(start + HD, HD)]
        values = TA[h, :, pl.ds(start + 2 * HD, HD)]
        context = TA[h, :, pl.ds(start + 3 * HD, HD)]
        back = nn(DY[rows, :], W[h, :, 3 * HD :]).astype(jnp.bfloat16)
        grad_q = []
        grad_k, grad_v = [None, None], [None, None]
        for i in range(2):
            seen = QT * (i + 1)
            part = slice(QT * i, QT * (i + 1))
            probs = [G[place] for place in probs_at(h, slot, i)]
            probs = probs[0] if len(probs) == 1 else jnp.concatenate(probs, axis=1)
            soft = probs.astype(jnp.bfloat16)
            grad_probs = nt(back[part], values[:seen])
            inner = jnp.sum(probs * grad_probs, axis=-1, keepdims=True)
            grad_scores = (probs * (grad_probs - inner)).astype(jnp.bfloat16)
            grad_q.append((nn(grad_scores, keys[:seen]) * scale).astype(jnp.bfloat16))
            for j in range(i + 1):
                cut = slice(QT * j, QT * (j + 1))
                term_v = tn(soft[:, cut], back[part])
                term_k = tn(grad_scores[:, cut], queries[part])
                grad_v[j] = term_v if grad_v[j] is None else grad_v[j] + term_v
                grad_k[j] = term_k if grad_k[j] is None else grad_k[j] + term_k
        dq = jnp.concatenate(grad_q, axis=0).astype(jnp.float32)
        dk = (jnp.concatenate(grad_k, axis=0) * scale).astype(jnp.bfloat16).astype(jnp.float32)
        dv = jnp.concatenate(grad_v, axis=0)
        turned = jnp.concatenate(
            [
                dq * cos_rows - partner(dq) * sin_rows,
                dk * cos_rows - partner(dk) * sin_rows,
                dv,
            ],
            axis=1,
        ).astype(jnp.bfloat16)
        TA[h, : 3 * HD, rows] = turned.T
        TA[h, 3 * HD :, rows] = context.T
        total = jnp.sum(turned.astype(jnp.float32), axis=0, keepdims=True)
        qb[h] = jnp.where(slot == 0, total, qb[h] + total)

    def cut_piece(f, slot):
        rows = pl.ds(pl.multiple_of(slot * T, 128), T)
        k = HEADS_DEV + f
        pre = nn(H2[rows, :], W[k, :, :CUT]) + bias_f[f]
        grad = nn(DY[rows, :], W[k, :, CUT:])
        normal = 0.5 * (1.0 + lax.erf(pre * (0.5**0.5)))
        slope = normal + pre * (jnp.exp(-0.5 * pre * pre) * (0.5 * 0.7978845608028654))
        active = (pre * normal).astype(jnp.bfloat16)
        pulled = (grad * slope).astype(jnp.bfloat16)
        low = pl.multiple_of(f * WIDE, WIDE)
        H1[pl.ds(low, CUT), rows] = pulled.T
        H1[pl.ds(low + CUT, CUT), rows] = active.T
        total = jnp.sum(pulled.astype(jnp.float32), axis=0, keepdims=True)
        fb[f] = jnp.where(slot == 0, total, fb[f] + total)

    def grads(k, turned, left, edge):
        def step(j, carry):
            cols = pl.ds(pl.multiple_of(j * block, 128), block)
            G[lax.rem(k, 2), j, :edge, :] = nn(turned(0, edge), left[:, cols])
            G[lax.rem(k, 2), j, edge:, :] = nn(turned(edge, WIDE - edge), DY[:, cols])
            return carry

        lax.fori_loop(0, outer, step, 0)

    def head_turned(h):
        return lambda low, size: TA[h, pl.ds(low, size), :]

    def cut_turned(f):
        return lambda low, size: H1[pl.ds(pl.multiple_of(f * WIDE + low, 128), size), :]

    def rs_copy(k, way, t):
        to = b + INNER if way == 0 else b - INNER
        return remote(
            sbuf.at[way],
            rsb.at[way, t - 1],
            rs_s.at[k, way, t - 1],
            rs_r.at[k, way, t - 1],
            to,
            c,
        )

    def rs_sends(way, t):
        if way == 0:
            return (o <= t - 1) & (o <= outer - 2)
        return (o >= outer - t) & (o >= 1)

    def rs_receives(way, t):
        if way == 0:
            return (o >= 1) & (o <= t)
        return (o <= outer - 2) & (o >= outer - 1 - t)

    def rs_fetch(k, way, t):
        rs_copy(k, way, t).wait_recv()
        return rsb[way, t - 1].astype(jnp.float32)

    def rs_step(k, t):
        n = k * S + t - 1

        @pl.when((t == 1) & (k >= 1) & (o < outer - 1))
        def _():
            pl.semaphore_wait(free_s.at[0], 1)

        @pl.when((t == 1) & (k >= 1) & (o > 0))
        def _():
            pl.semaphore_wait(free_s.at[1], 1)

        before = jnp.maximum(n - 1, 0)
        k_before = before // S
        t_before = lax.rem(before, S) + 1
        for way in range(2):
            owner = o + outer - t if way == 0 else o - outer + t

            @pl.when((n >= 1) & rs_sends(way, t_before))
            def _():
                rs_copy(k_before, way, t_before).wait_send()

            @pl.when(rs_sends(way, t))
            def _():
                @pl.when(rs_receives(way, t - 1) & (t > 1))
                def _():
                    sbuf[way] = (
                        G[lax.rem(k, 2), owner] + rs_fetch(k, way, t - 1)
                    ).astype(jnp.bfloat16)

                @pl.when(jnp.logical_not(rs_receives(way, t - 1) & (t > 1)))
                def _():
                    sbuf[way] = G[lax.rem(k, 2), owner].astype(jnp.bfloat16)

                rs_copy(k, way, t).start()

    def gr_copy(k, d, received=False):
        to = near[d - 1]
        slot = lax.rem(to, INNER)
        return remote(
            fbuf.at[pl.ds(pl.multiple_of(slot * R, 16), R)],
            gr.at[k, slot if received else q],
            gr_s.at[k, d - 1],
            gr_r.at[k, d - 1],
            to,
            c,
        )

    def gr_local(k):
        return pltpu.make_async_copy(
            fbuf.at[pl.ds(pl.multiple_of(q * R, 16), R)],
            gr.at[k, q],
            gr_s.at[k, 3],
        )

    def gr_sent(k):
        for d in range(1, INNER):
            gr_copy(k, d).wait_send()
        gr_local(k).wait()

    def rs_final(k):
        for way in range(2):

            @pl.when(rs_receives(way, S))
            def _():
                G[lax.rem(k, 2), o] = G[lax.rem(k, 2), o] + rs_fetch(k, way, S)

        @pl.when((k < CHUNKS - 1) & (o > 0))
        def _():
            pl.semaphore_signal(
                free_s.at[0], inc=1, device_id=(b - INNER, c), device_id_type=MESH
            )

        @pl.when((k < CHUNKS - 1) & (o < outer - 1))
        def _():
            pl.semaphore_signal(
                free_s.at[1], inc=1, device_id=(b + INNER, c), device_id_type=MESH
            )

        @pl.when(k >= 1)
        def _():
            gr_sent(k - 1)

        final = G[lax.rem(k, 2), o].T
        cs[k] = jnp.sum(squares(final), axis=0, keepdims=True)
        fbuf[...] = final.astype(jnp.bfloat16)
        for d in range(1, INNER):
            gr_copy(k, d).start()
        gr_local(k).start()

    def rs_range(low, high):
        def step(n, carry):
            k = n // (S + 1)
            t = lax.rem(n, S + 1) + 1

            @pl.when(t <= S)
            def _():
                rs_step(k, t)

            @pl.when(t == S + 1)
            def _():
                rs_final(k)

            return carry

        lax.fori_loop(low, high, step, 0)

    TILE = half // 2
    TILES = 2 * INNER
    PER_ROW = D // T

    def tile_slot(i):
        return INNER - 1 - i // 2

    def product(which, i, side):
        toks = pl.ds(pl.multiple_of(tile_slot(i) * T, 128), T)
        features = pl.ds(pl.multiple_of(side * half + lax.rem(i, 2) * TILE, 128), TILE)
        terms = []
        if which == 0:
            for h in range(HEADS_DEV):
                terms.append((h, slice(0, 3 * HD), lambda h=h: TA[h, : 3 * HD, toks]))
        elif which == 1:
            for f in range(CUTS):
                low = f * WIDE
                terms.append(
                    (HEADS_DEV + f, slice(0, CUT), lambda low=low: H1[low : low + CUT, toks])
                )
        else:
            for h in range(HEADS_DEV):
                terms.append((h, slice(3 * HD, WIDE), lambda h=h: TA[h, 3 * HD :, toks]))
            for f in range(CUTS):
                low = f * WIDE + CUT
                terms.append(
                    (HEADS_DEV + f, slice(CUT, WIDE), lambda low=low: H1[low : low + CUT, toks])
                )
        for place, (k, cols, right) in enumerate(terms):
            term = nn(W[k, features, cols], right())
            own[...] = term if place == 0 else own[...] + term

    def sib_copy(which, i):
        return remote(
            sib_send.at[lax.rem(i, 2)],
            sib_land.at[lax.rem(i, 4)],
            sib_s.at[which, i],
            sib_r.at[which, i],
            b,
            1 - c,
        )

    def stage(which, i):
        buf, t = (H1, PER_ROW * (half // TILE) + i) if which == 0 else (H2, (which - 1) * (TILES - 2) + i)
        return buf.at[
            pl.ds(pl.multiple_of(t // PER_ROW * TILE, 128), TILE),
            pl.ds(pl.multiple_of(lax.rem(t, PER_ROW) * T, 128), T),
        ]

    def plane_copy(which, i):
        slot = tile_slot(i)
        low, high = lax.rem(slot, 2), slot // 2
        to = b + low * (1 - 2 * lax.rem(b, 2)) + high * 2 * (1 - 2 * lax.rem(b // 2, 2))
        src = stage(which, i)
        return remote(
            src,
            xr.at[which, slot - 1, lax.rem(i, 2)],
            p_s.at[which, i],
            p_r.at[which, i],
            to,
            c,
        )

    def tile_a(which, i):
        @pl.when(i >= 2)
        def _():
            sib_copy(which, i - 2).wait_send()

        product(which, i, 1 - c)
        sib_send[lax.rem(i, 2)] = own[...].astype(jnp.bfloat16)
        sib_copy(which, i).start()

    def tile_b(which, i):
        product(which, i, c)
        sib_copy(which, i).wait_recv()

        @pl.when(i < TILES - 2)
        def _():
            total = (own[...] + sib_land[lax.rem(i, 4)].astype(jnp.float32)).astype(jnp.bfloat16)
            stage(which, i)[...] = total
            plane_copy(which, i).start()

        @pl.when(i >= TILES - 2)
        def _():
            own[...] = own[...] + sib_land[lax.rem(i, 4)].astype(jnp.float32)
            keep = pltpu.make_async_copy(own, xo.at[which, lax.rem(i, 2)], tmp_s.at[2])
            keep.start()
            keep.wait()

    def sum_tiles(which, beside):
        tile_a(which, 0)

        def step(i, carry):
            @pl.when(i < TILES - 1)
            def _():
                tile_a(which, i + 1)

            tile_b(which, i)
            beside(i)
            return carry

        lax.fori_loop(0, TILES, step, 0)

    def sib_sent(which):
        for i in range(TILES - 2, TILES):
            sib_copy(which, i).wait_send()

    def spread(first, last, i, pieces, run):
        steps = last - first
        run(
            first + (steps * i + pieces - 1) // pieces,
            first + (steps * (i + 1) + pieces - 1) // pieces,
        )

    def ag_share(low, high, i, pieces):
        spread(low * S // 3, high * S // 3, i, pieces, ag_range)

    def rs_share(low, high, i, pieces):
        spread(low * (S + 1) // 4, high * (S + 1) // 4, i, pieces, rs_range)

    a2a_start(0)
    gather_one(0, xin, H1)
    gather_one(1, yin, DY)
    ag(0, 1)
    a2a_start(1)
    gather_two(0, xin, H1)
    gather_two(1, yin, DY)
    ag(1, 2)
    a2a_start(2)
    x_local(0, xin, H1).wait()
    sx_wait(0, H1, 0)
    norm_rows(0)
    ag(2, 3)
    gather_three(0, xin, H1)
    gather_sent(0, xin, H1)
    for k in range(3, CHUNKS):
        a2a_start(k)
    for slot in range(1, INNER):
        sx_wait(0, H1, slot)
        norm_rows(slot)
        if slot < 3:
            ag(2 + slot, 3 + slot)

    def project_step(h):
        ag_wait(h, S)

        def slot_step(slot, inner_carry):
            forward_piece(h, slot)
            ag_share(5 + h, 6 + h, slot, INNER)
            return inner_carry

        lax.fori_loop(0, INNER, slot_step, 0)

    project_step(0)
    gather_three(1, yin, DY)
    project_step(1)
    x_local(1, yin, DY).wait()
    for slot in range(INNER):
        sx_wait(1, DY, slot)
    gather_sent(1, yin, DY)

    def head_step(h, carry):
        def slot_step(slot, inner_carry):
            head_piece(h, slot)
            ag_share(7 + 2 * h, 9 + 2 * h, slot, INNER)
            rs_share(0, 2 * h, slot, INNER)
            return inner_carry

        lax.fori_loop(0, INNER, slot_step, 0)
        grads(h, head_turned(h), H1, 3 * HD)
        return carry

    lax.fori_loop(0, HEADS_DEV, head_step, 0)

    def beside_one(i):
        ag_share(13, 15, i, TILES)
        rs_share(4, 7, i, TILES)

    def cut_step(f, carry):
        ag_wait(HEADS_DEV + f, S)

        @pl.when(f == CUTS // 2)
        def _():
            for i in range(TILES - 2):
                plane_copy(0, i).wait_send()

        def slot_step(slot, inner_carry):
            cut_piece(f, slot)
            ag_share(
                jnp.where(f == 0, 11, jnp.minimum(13 + 2 * f, 18)),
                jnp.where(f == 0, 13, jnp.minimum(15 + 2 * f, 18)),
                slot,
                INNER,
            )
            rs_share(
                jnp.where(f == 0, 2, jnp.where(f == 1, 7, 2 + 4 * f)),
                jnp.where(f == 0, 4, 6 + 4 * f),
                slot,
                INNER,
            )
            return inner_carry

        lax.fori_loop(0, INNER, slot_step, 0)
        grads(HEADS_DEV + f, cut_turned(f), H2, CUT)

        @pl.when(f == 0)
        def _():
            sum_tiles(0, beside_one)

        return carry

    lax.fori_loop(0, CUTS, cut_step, 0)
    sib_sent(0)
    sum_tiles(1, lambda i: rs_share(18, 22, i, TILES))
    sib_sent(1)
    sum_tiles(2, lambda i: rs_share(22, 24, i, TILES))
    sib_sent(2)

    gr_sent(CHUNKS - 1)

    def drain_chunk(k, carry):
        for d in range(1, INNER):
            a2a_copy(k, d).wait_send()
            gr_copy(k, d, True).wait_recv()

        def drain_step(s, inner_carry):
            ag_sends(k, s, lambda copy: copy.wait_send())
            return inner_carry

        lax.fori_loop(1, S + 1, drain_step, 0)
        return carry

    lax.fori_loop(0, CHUNKS, drain_chunk, 0)
    for way in range(2):

        @pl.when(rs_sends(way, S))
        def _():
            rs_copy(CHUNKS - 1, way, S).wait_send()

    for which in range(3):

        def drain_tile(i, carry):
            if which:
                plane_copy(which, i).wait_send()
            plane_copy(which, i).wait_recv()
            return carry

        lax.fori_loop(0, TILES - 2, drain_tile, 0)


def block_call(count, wst, xin, yin, turns, norm_params, bias_h, bias_f):
    outer = count // INNER
    S = outer - 1
    tokens, half = xin.shape
    group = INNER * tokens
    rows = wst.shape[2]
    tile = half // 2
    low, high = jnp.bfloat16, jnp.float32
    any_spec = pl.BlockSpec(memory_space=pl.ANY)
    vmem_spec = pl.BlockSpec(memory_space=pltpu.VMEM)
    dma = pltpu.SemaphoreType.DMA
    return pl.pallas_call(
        functools.partial(block_kernel, count),
        out_shape=[
            jax.ShapeDtypeStruct((CHUNKS, INNER, rows, WIDE), low),
            jax.ShapeDtypeStruct((3, INNER - 1, 2, tile, tokens), low),
            jax.ShapeDtypeStruct((3, 2, tile, tokens), high),
            jax.ShapeDtypeStruct((HEADS_DEV, 1, 3 * HD), high),
            jax.ShapeDtypeStruct((CUTS, 1, CUT), high),
            jax.ShapeDtypeStruct((CHUNKS, 1, WIDE), high),
            jax.ShapeDtypeStruct((tokens, 128), high),
        ],
        in_specs=[any_spec] * 3 + [vmem_spec] * 4,
        out_specs=[any_spec] * 3 + [vmem_spec] * 4,
        scratch_shapes=[
            pltpu.VMEM((group, D), low),
            pltpu.VMEM((group, D), low),
            pltpu.VMEM((group, D), low),
            pltpu.VMEM((CHUNKS, D, WIDE), low),
            pltpu.VMEM((HEADS_DEV, WIDE, group), low),
            pltpu.VMEM((2, outer, WIDE, INNER * rows), high),
            pltpu.VMEM((2, WIDE, INNER * rows), low),
            pltpu.VMEM((INNER * rows, WIDE), low),
            pltpu.VMEM((2, S, WIDE, INNER * rows), low),
            pltpu.VMEM((2, tile, tokens), low),
            pltpu.VMEM((4, tile, tokens), low),
            pltpu.VMEM((tile, tokens), high),
            dma((CHUNKS, INNER - 1)),
            dma((CHUNKS, INNER - 1)),
            dma((CHUNKS,)),
            dma((CHUNKS, 2, S)),
            dma((CHUNKS, 2, S)),
            dma((2, INNER - 1)),
            dma((2, INNER - 1)),
            dma((2, INNER)),
            dma((2, INNER)),
            dma((CHUNKS, 2, S)),
            dma((CHUNKS, 2, S)),
            dma((CHUNKS, INNER)),
            dma((CHUNKS, INNER - 1)),
            dma((3, 2 * INNER)),
            dma((3, 2 * INNER)),
            dma((3, 2 * INNER)),
            dma((3, 2 * INNER)),
            dma((3,)),
            pltpu.SemaphoreType.REGULAR((2,)),
        ],
        compiler_params=pltpu.CompilerParams(
            collective_id=0, has_side_effects=True, vmem_limit_bytes=64 * 1024 * 1024
        ),
        cost_estimate=pl.CostEstimate(
            flops=80_000_000_000, bytes_accessed=60_000_000, transcendentals=10_000_000
        ),
    )(wst, xin, yin, turns, norm_params, bias_h, bias_f)


SLOT_ROWS = 16
PACK_ROWS = 40
PACK_ENDS = (0, 3, 4, 8, 12, 17, 22, 27, 31, 35, 39)


def total_of(values):
    return jnp.sum(jnp.sum(values, axis=0, keepdims=True), axis=1, keepdims=True)


def tail_kernel(
    count,
    gr,
    wq,
    wo,
    w1,
    w2,
    xr,
    xo,
    xin,
    yin,
    st,
    norm_ref,
    pb,
    fcb,
    row_old,
    qc_old,
    or_old,
    f1_old,
    f2_old,
    norm_second,
    bias_second,
    fcb_second,
    cs,
    qb,
    fb,
    out_ref,
    ing_ref,
    row_new,
    pack,
    norm_pack,
    qc_new,
    or_new,
    f1_new,
    f2_new,
    norm_grad,
    bias_grad,
    fcb_grad,
    scaled_buf,
    normed_buf,
    terms,
    terms_in,
    rsum,
    rsum_in,
    pay,
    z_in,
    z_sum,
    p_in,
    p_sum,
    s_in,
    pay2,
    z2_in,
    z2_sum,
    p2_in,
    p2_sum,
    s2_in,
    z_s,
    z_r,
    p_s,
    p_r,
    s_s,
    s_r,
):
    outer = count // INNER
    T, half = xin.shape
    R = gr.shape[2]
    b = lax.axis_index("batch")
    c = lax.axis_index("branch")
    q = lax.rem(b, INNER)
    o = b // INNER
    bx, by = flip(b, 1), flip(b, 2)
    near = (bx, by, flip(bx, 2))
    on_b = (b == 0).astype(jnp.float32)
    on_c = (c == 0).astype(jnp.float32)

    def remote(src, dst, ssem, rsem, to_b, to_c):
        return pltpu.make_async_remote_copy(
            src_ref=src,
            dst_ref=dst,
            send_sem=ssem,
            recv_sem=rsem,
            device_id=(to_b, to_c),
            device_id_type=MESH,
        )

    def chain(d):
        return lax.rem(o + d, outer)

    barrier = pltpu.get_barrier_semaphore()
    for who in near:
        pl.semaphore_signal(barrier, inc=1, device_id=(who, c), device_id_type=MESH)
    pl.semaphore_signal(barrier, inc=1, device_id=(b, 1 - c), device_id_type=MESH)
    for d in range(1, outer):
        pl.semaphore_signal(
            barrier, inc=1, device_id=(chain(d) * INNER + q, c), device_id_type=MESH
        )

    HALF_T = T // 2
    HALF_F = half // 2
    lane_t = lax.broadcasted_iota(jnp.int32, (T, 128), 1)
    own_half = pl.ds(pl.multiple_of(c * half, 128), half)
    other_half = pl.ds(pl.multiple_of((1 - c) * half, 128), half)
    pay[...] = jnp.zeros_like(pay)
    first_sum, second_sum = 0.0, 0.0
    for i in range(2):
        cols = slice(i * HALF_F, (i + 1) * HALF_F)
        gains = pl.ds(pl.multiple_of(c * half + i * HALF_F, 128), HALF_F)

        def whole(which):
            return (
                xo[which, i]
                + xr[which, 0, i].astype(jnp.float32)
                + xr[which, 1, i].astype(jnp.float32)
                + xr[which, 2, i].astype(jnp.float32)
            ).T

        values = xin[:, cols].astype(jnp.float32)
        out_ref[:, cols] = (values + whole(2) + pb[3:4, cols] + pb[4:5, cols]).astype(jnp.bfloat16)
        normed = (values - st[:, 0:1]) * st[:, 1:2]
        one = whole(0)
        two = whole(1)
        scaled = one * norm_ref[0:1, gains] + two * norm_ref[2:3, gains]
        scaled_buf[:, cols] = scaled
        normed_buf[:, cols] = normed
        first_sum = first_sum + jnp.sum(scaled, axis=1, keepdims=True)
        second_sum = second_sum + jnp.sum(scaled * normed, axis=1, keepdims=True)
        pay[5:6, cols] = jnp.sum(one * normed, axis=0, keepdims=True)
        pay[6:7, cols] = jnp.sum(one, axis=0, keepdims=True)
        pay[7:8, cols] = jnp.sum(two * normed, axis=0, keepdims=True)
        pay[8:9, cols] = jnp.sum(two, axis=0, keepdims=True)
        pay[9:10, cols] = jnp.sum(yin[:, cols].astype(jnp.float32), axis=0, keepdims=True)
    terms[...] = jnp.where(lane_t == 0, first_sum, jnp.where(lane_t == 1, second_sum, 0.0))
    for k in range(CHUNKS):
        pay[k // 2 : k // 2 + 1, k % 2 * WIDE : (k % 2 + 1) * WIDE] = cs[k]
    for h in range(HEADS_DEV):
        pay[3:4, h * 3 * HD : (h + 1) * 3 * HD] = qb[h]
    for f in range(CUTS):
        pay[4:5, f * CUT : (f + 1) * CUT] = fb[f]
    lane_p = lax.broadcasted_iota(jnp.int32, (1, half), 1)
    biases = jnp.sum(pb[...] * pb[...], axis=1, keepdims=True) * on_b
    scalars = (
        [total_of(w[...] * w[...]) for w in (wq, wo, w1, w2)]
        + [biases[i : i + 1] for i in range(5)]
        + [total_of(fcb[...] * fcb[...]) * on_b]
    )
    line = jnp.zeros((1, half), jnp.float32)
    for place, value in enumerate(scalars):
        line = jnp.where(lane_p == place, value, line)
    pay[10:11, :] = line

    pl.semaphore_wait(barrier, INNER + outer - 1)

    def chain_sends(src, buf, base, what):
        for d in range(1, outer):
            what(
                remote(
                    src,
                    buf.at[o],
                    z_s.at[base, d - 1],
                    z_r.at[base, d - 1],
                    chain(d) * INNER + q,
                    c,
                )
            )

    def chain_waits(src, buf, base):
        for d in range(1, outer):
            source = chain(outer - d)
            remote(
                src,
                buf.at[source],
                z_s.at[base, d - 1],
                z_r.at[base, d - 1],
                source * INNER + q,
                c,
            ).wait_recv()

    def plane_sends(src, buf, base, what):
        for d in range(1, INNER):
            what(remote(src, buf.at[q], p_s.at[base, d - 1], p_r.at[base, d - 1], near[d - 1], c))

    def plane_waits(src, buf, base):
        for d in range(1, INNER):
            remote(
                src,
                buf.at[lax.rem(near[d - 1], INNER)],
                p_s.at[base, d - 1],
                p_r.at[base, d - 1],
                near[d - 1],
                c,
            ).wait_recv()

    def pair_copy(src, dst, place):
        return remote(src, dst, s_s.at[place], s_r.at[place], b, 1 - c)

    start = lambda copy: copy.start()
    chain_sends(pay, z_in, 0, start)
    z_in[o] = pay[...]
    pair_copy(terms, terms_in, 0).start()

    lane_r = lax.broadcasted_iota(jnp.int32, (R, 128), 1)
    head_square = jnp.zeros((R, WIDE), jnp.float32)
    cut_square = jnp.zeros((R, WIDE), jnp.float32)
    for part in range(INNER):
        for k in range(CHUNKS):
            gradient = gr[k, part].astype(jnp.float32)
            if k < HEADS_DEV:
                head_square = head_square + squares(gradient)
            else:
                cut_square = cut_square + squares(gradient)
    pieces = (
        jnp.sum(head_square[:, : 3 * HD], axis=1, keepdims=True),
        jnp.sum(cut_square[:, :CUT], axis=1, keepdims=True),
        jnp.sum(head_square[:, 3 * HD :], axis=1, keepdims=True),
        jnp.sum(cut_square[:, CUT:], axis=1, keepdims=True),
    )
    line = jnp.zeros((R, 128), jnp.float32)
    for place, value in enumerate(pieces):
        line = jnp.where(lane_r == place, value, line)
    rsum[...] = line
    pair_copy(rsum, rsum_in, 1).start()

    pair_copy(terms, terms_in, 0).wait_recv()
    for i in range(2):
        rows = slice(i * HALF_T, (i + 1) * HALF_T)
        both = terms[rows, :] + terms_in[rows, :]
        ing_ref[rows, :] = (
            st[rows, 1:2]
            * (
                scaled_buf[rows, :]
                - both[:, 0:1] / D
                - normed_buf[rows, :] * (both[:, 1:2] / D)
            )
            + yin[rows, :].astype(jnp.float32)
        ).astype(jnp.bfloat16)
    pair_copy(rsum, rsum_in, 1).wait_recv()
    rows_after = renew_stat(row_old[...], (rsum[...] + rsum_in[...])[:, :4])
    row_new[...] = jnp.concatenate(
        [rows_after, jnp.zeros((R, 128 - 4), jnp.float32)], axis=1
    )

    chain_waits(pay, z_in, 0)
    acc = z_in[0]
    for j in range(1, outer):
        acc = acc + z_in[j]
    z_sum[...] = acc
    plane_sends(z_sum, p_in, 0, start)
    p_in[q] = acc
    plane_waits(z_sum, p_in, 0)
    p_sum[...] = p_in[0] + p_in[1] + p_in[2] + p_in[3]
    pair_copy(p_sum, s_in, 2).start()

    inverse_rows = 1.0 / rows_after
    head_acc = [jnp.zeros((R, 3 * HD), jnp.float32), jnp.zeros((R, HD), jnp.float32)]
    cut_acc = [jnp.zeros((R, CUT), jnp.float32), jnp.zeros((R, CUT), jnp.float32)]
    for part in range(INNER):
        sums = p_in[part]
        for h in range(HEADS_DEV):
            gradient = gr[h, part].astype(jnp.float32)
            square = gradient * gradient
            found = sums[h // 2 : h // 2 + 1, h % 2 * WIDE : (h % 2 + 1) * WIDE]
            cols = pl.ds(part * HEADS_DEV * HD + h * HD, HD)
            parts = []
            for p in range(3):
                fresh = renew_stat(qc_old[p : p + 1, cols], found[:, p * HD : (p + 1) * HD])
                qc_new[p : p + 1, cols] = fresh
                parts.append(1.0 / fresh)
            head_acc[0] = head_acc[0] + square[:, : 3 * HD] * jnp.concatenate(parts, axis=1)
            fresh = renew_stat(or_old[:, cols], found[:, 3 * HD :])
            or_new[:, cols] = fresh
            head_acc[1] = head_acc[1] + square[:, 3 * HD :] * (1.0 / fresh)
        for f in range(CUTS):
            k = HEADS_DEV + f
            gradient = gr[k, part].astype(jnp.float32)
            square = gradient * gradient
            found = sums[k // 2 : k // 2 + 1, k % 2 * WIDE : (k % 2 + 1) * WIDE]
            cols = slice(f * CUT, (f + 1) * CUT)
            fresh = renew_stat(f1_old[part : part + 1, cols], found[:, :CUT])
            f1_new[part, :, cols] = fresh
            cut_acc[0] = cut_acc[0] + square[:, :CUT] * (1.0 / fresh)
            fresh = renew_stat(f2_old[part : part + 1, cols], found[:, CUT:])
            f2_new[part, :, cols] = fresh
            cut_acc[1] = cut_acc[1] + square[:, CUT:] * (1.0 / fresh)
    for part in range(INNER):
        for h in range(HEADS_DEV):
            for p in range(3):
                low = h * 3 * HD + p * HD
                bias_grad[p : p + 1, pl.ds(part * HEADS_DEV * HD + h * HD, HD)] = p_in[
                    part, 3:4, low : low + HD
                ]
        fcb_grad[part : part + 1, :] = p_in[part, 4:5, :]
    bias_grad[3:4, :] = p_sum[9:10, :]
    bias_grad[4:5, :] = p_sum[9:10, :]
    bias_after, bias_update = second_step(bias_grad[...], bias_second[...])
    pack[17:22, :] = bias_after
    fcb_after, fcb_update = second_step(fcb_grad[...], fcb_second[...])
    pack[31:35, :] = fcb_after
    usq = jnp.sum(bias_update * bias_update, axis=1, keepdims=True) * on_b
    scalars = (
        [
            total_of(rows_after[:, 0:1]) * on_c,
            total_of(head_acc[0] * inverse_rows[:, 0:1]),
            total_of(rows_after[:, 1:2]) * on_c,
            total_of(cut_acc[0] * inverse_rows[:, 1:2]),
            total_of(or_new[...]) * on_b,
            total_of(head_acc[1] * inverse_rows[:, 2:3]),
            sum(total_of(f2_new[part]) for part in range(INNER)) * on_b,
            total_of(cut_acc[1] * inverse_rows[:, 3:4]),
        ]
        + [usq[i : i + 1] for i in range(5)]
        + [total_of(fcb_update * fcb_update) * on_b]
    )
    lane_s = lax.broadcasted_iota(jnp.int32, (8, 128), 1)
    line = jnp.zeros((8, 128), jnp.float32)
    for place, value in enumerate(scalars):
        line = jnp.where(lane_s == place, value, line)
    pay2[...] = line
    chain_sends(pay2, z2_in, 1, start)
    z2_in[o] = line
    pack[0:3, :] = qc_new[...]
    pack[3:4, :] = or_new[...]
    for part in range(INNER):
        pack[4 + part : 5 + part, :] = f1_new[part]
        pack[8 + part : 9 + part, :] = f2_new[part]
    pack[12:17, :] = bias_grad[...]
    pack[27:31, :] = fcb_grad[...]

    pair_copy(p_sum, s_in, 2).wait_recv()
    norm_grad[:, own_half] = p_sum[5:9, :]
    norm_grad[:, other_half] = s_in[5:9, :]
    old = p_sum[10:11, :] + s_in[10:11, :]
    norm_after, norm_update = second_step(norm_grad[...], norm_second[...])
    norm_pack[0:4, :] = norm_grad[...]
    norm_pack[4:8, :] = norm_after

    def moved(vector, update, update_square, old_square, entries):
        clip_factor = jnp.maximum(1.0, jnp.sqrt(update_square / entries))
        step_rate = RATE * jnp.maximum(FLOOR_RATE, jnp.sqrt(old_square / entries))
        return vector - step_rate * update / clip_factor

    norm_values = norm_ref[...]
    norm_pack[8:12, :] = moved(
        norm_values,
        norm_update,
        jnp.sum(norm_update * norm_update, axis=1, keepdims=True),
        jnp.sum(norm_values * norm_values, axis=1, keepdims=True),
        D,
    )

    chain_waits(pay2, z2_in, 1)
    acc = z2_in[0]
    for j in range(1, outer):
        acc = acc + z2_in[j]
    z2_sum[...] = acc
    plane_sends(z2_sum, p2_in, 1, start)
    p2_in[q] = acc
    plane_waits(z2_sum, p2_in, 1)
    acc = p2_in[0] + p2_in[1] + p2_in[2] + p2_in[3]
    p2_sum[...] = acc
    pair_copy(p2_sum, s2_in, 3).start()
    pair_copy(p2_sum, s2_in, 3).wait_recv()
    sums = (acc + s2_in[...])[0:1, :]

    def scalar(place):
        return sums[:, place : place + 1]

    def factor(total, inverse, place, entries):
        clip_factor = jnp.maximum(1.0, jnp.sqrt(total * inverse / entries))
        rate = RATE * jnp.maximum(FLOOR_RATE, jnp.sqrt(old[:, place : place + 1] / entries))
        return rate * jnp.sqrt(total) / clip_factor

    factors = (
        factor(scalar(0), scalar(1), 0, 3 * D * D),
        factor(scalar(2), scalar(3), 2, D * FF),
        factor(scalar(4), scalar(5), 1, D * D),
        factor(scalar(6), scalar(7), 3, FF * D),
    )
    line = jnp.zeros((8, 128), jnp.float32)
    for place, value in enumerate(factors):
        line = jnp.where(lane_s == place, value, line)
    pack[39:40, :] = jnp.concatenate(
        [line[0:1, :], jnp.zeros((1, half - 128), jnp.float32)], axis=1
    )
    for i in range(5):
        pack[22 + i : 23 + i, :] = moved(
            pb[i : i + 1, :], bias_update[i : i + 1], scalar(8 + i), old[:, 4 + i : 5 + i], D
        )
    pack[35:39, :] = moved(fcb[...], fcb_update, scalar(13), old[:, 9:10], FF)

    finish = lambda copy: copy.wait_send()
    chain_sends(pay, z_in, 0, finish)
    chain_sends(pay2, z2_in, 1, finish)
    plane_sends(z_sum, p_in, 0, finish)
    plane_sends(z2_sum, p2_in, 1, finish)
    pair_copy(terms, terms_in, 0).wait_send()
    pair_copy(rsum, rsum_in, 1).wait_send()
    pair_copy(p_sum, s_in, 2).wait_send()
    pair_copy(p2_sum, s2_in, 3).wait_send()


def tail_call(count, *args):
    outer = count // INNER
    received, xin = args[0], args[7]
    tokens, half = xin.shape
    rows = received.shape[2]
    high = jnp.float32
    spec = pl.BlockSpec(memory_space=pltpu.VMEM)
    dma = pltpu.SemaphoreType.DMA

    def out(*shape, dtype=high):
        return jax.ShapeDtypeStruct(shape, dtype)

    outs = [
        out(tokens, half, dtype=jnp.bfloat16),
        out(tokens, half, dtype=jnp.bfloat16),
        out(rows, 128),
        out(PACK_ROWS, half),
        out(12, D),
    ]
    slot = (SLOT_ROWS, half)
    return pl.pallas_call(
        functools.partial(tail_kernel, count),
        out_shape=outs,
        in_specs=[spec] * len(args),
        out_specs=[spec] * len(outs),
        scratch_shapes=[
            pltpu.VMEM((3, half), high),
            pltpu.VMEM((1, half), high),
            pltpu.VMEM((INNER, 1, half), high),
            pltpu.VMEM((INNER, 1, half), high),
            pltpu.VMEM((4, D), high),
            pltpu.VMEM((5, half), high),
            pltpu.VMEM((INNER, half), high),
            pltpu.VMEM((tokens, half), high),
            pltpu.VMEM((tokens, half), high),
            pltpu.VMEM((tokens, 128), high),
            pltpu.VMEM((tokens, 128), high),
            pltpu.VMEM((rows, 128), high),
            pltpu.VMEM((rows, 128), high),
            pltpu.VMEM(slot, high),
            pltpu.VMEM((outer, *slot), high),
            pltpu.VMEM(slot, high),
            pltpu.VMEM((INNER, *slot), high),
            pltpu.VMEM(slot, high),
            pltpu.VMEM(slot, high),
            pltpu.VMEM((8, 128), high),
            pltpu.VMEM((outer, 8, 128), high),
            pltpu.VMEM((8, 128), high),
            pltpu.VMEM((INNER, 8, 128), high),
            pltpu.VMEM((8, 128), high),
            pltpu.VMEM((8, 128), high),
            dma((2, outer - 1)),
            dma((2, outer - 1)),
            dma((2, INNER - 1)),
            dma((2, INNER - 1)),
            dma((4,)),
            dma((4,)),
        ],
        compiler_params=pltpu.CompilerParams(
            collective_id=1, has_side_effects=True, vmem_limit_bytes=58 * 1024 * 1024
        ),
        cost_estimate=pl.CostEstimate(
            flops=50_000_000, bytes_accessed=40_000_000, transcendentals=100_000
        ),
    )(*args)


def update_kernel(*refs):
    gr, wq, wo, w1, w2, row_new, pack, norm_pack, output, input_grad = refs[:10]
    q_grad, q_next, q_copy, o_grad, o_next, o_copy = refs[10:16]
    f1_grad, f1_next, f1_copy, f2_grad, f2_next, f2_copy = refs[16:22]
    row_out, whole_out, pack_out, norm_out = refs[22:26], refs[26:28], refs[28:38], refs[38:]
    part = pl.program_id(0)
    side = lax.rsqrt(row_new[:, :4]) * pack[39:40, :4]
    width_q = HEADS_DEV * HD

    @pl.when(part == 0)
    def _():
        whole_out[0][...] = output[...]
        whole_out[1][...] = input_grad[...]
        for place, target in enumerate(pack_out):
            target[...] = pack[PACK_ENDS[place] : PACK_ENDS[place + 1], :]
        for place, target in enumerate(norm_out):
            target[...] = norm_pack[4 * place : 4 * place + 4, :]
        turned = row_new[...].T
        for place in range(4):
            row_out[place][...] = turned[place : place + 1, :]

    def put(grad_ref, next_ref, copy_ref, where, weight, gradient, update):
        fresh = weight[where] - update
        grad_ref[where] = gradient
        next_ref[where] = fresh
        copy_ref[where] = fresh.astype(jnp.bfloat16)

    for h in range(HEADS_DEV):
        gradient = gr[h, 0].astype(jnp.float32)
        cols = pl.ds(pl.multiple_of(part * width_q + h * HD, HD), HD)
        for p in range(3):
            mine = gradient[:, p * HD : (p + 1) * HD]
            update = mine * side[:, 0:1] * lax.rsqrt(pack[p : p + 1, cols])
            where = (p, slice(None), slice(h * HD, (h + 1) * HD))
            put(q_grad, q_next, q_copy, where, wq, mine, update)
        mine = gradient[:, 3 * HD :]
        update = mine * side[:, 2:3] * lax.rsqrt(pack[3:4, cols])
        where = (slice(h * HD, (h + 1) * HD), slice(None))
        put(o_grad, o_next, o_copy, where, wo, mine.T, update.T)
    for f in range(CUTS):
        gradient = gr[HEADS_DEV + f, 0].astype(jnp.float32)
        cols = slice(f * CUT, (f + 1) * CUT)
        mine = gradient[:, :CUT]
        update = mine * side[:, 1:2] * lax.rsqrt(pack[pl.ds(4 + part, 1), cols])
        put(f1_grad, f1_next, f1_copy, (slice(None), cols), w1, mine, update)
        mine = gradient[:, CUT:]
        update = mine * side[:, 3:4] * lax.rsqrt(pack[pl.ds(8 + part, 1), cols])
        put(f2_grad, f2_next, f2_copy, (cols, slice(None)), w2, mine.T, update.T)


def update_call(gr, wq, wo, w1, w2, row_new, pack, norm_pack, output, input_grad):
    rows = gr.shape[2]
    half = pack.shape[1]
    width_q = HEADS_DEV * HD
    hidden_q = CUTS * CUT
    spec = pl.BlockSpec
    q_spec = spec((3, rows, width_q), lambda i: (0, 0, i))
    o_spec = spec((width_q, rows), lambda i: (i, 0))
    f1_spec = spec((rows, hidden_q), lambda i: (0, i))
    f2_spec = spec((hidden_q, rows), lambda i: (i, 0))
    outs, out_specs = [], []
    for array, its in ((wq, q_spec), (wo, o_spec), (w1, f1_spec), (w2, f2_spec)):
        for dtype in (jnp.float32, jnp.float32, jnp.bfloat16):
            outs.append(jax.ShapeDtypeStruct(array.shape, dtype))
            out_specs.append(its)

    def fixed(shape):
        return spec(shape, lambda i: (0,) * len(shape))

    shapes = [((1, rows), jnp.float32)] * 4 + [(output.shape, output.dtype)] * 2
    for place in range(len(PACK_ENDS) - 1):
        shapes.append(((PACK_ENDS[place + 1] - PACK_ENDS[place], half), jnp.float32))
    shapes += [((4, D), jnp.float32)] * 3
    for shape, dtype in shapes:
        outs.append(jax.ShapeDtypeStruct(shape, dtype))
        out_specs.append(fixed(shape))
    small = (row_new, pack, norm_pack, output, input_grad)
    return pl.pallas_call(
        update_kernel,
        grid=(INNER,),
        out_shape=outs,
        in_specs=[
            spec((CHUNKS, 1, rows, WIDE), lambda i: (0, i, 0, 0)),
            q_spec,
            o_spec,
            f1_spec,
            f2_spec,
        ]
        + [fixed(array.shape) for array in small],
        out_specs=out_specs,
        compiler_params=pltpu.CompilerParams(vmem_limit_bytes=48 * 1024 * 1024),
        cost_estimate=pl.CostEstimate(
            flops=20_000_000, bytes_accessed=30_000_000, transcendentals=100_000
        ),
    )(gr, wq, wo, w1, w2, *small)


def swap_pairs(count, step):
    return [(i, i ^ step) for i in range(count)]


def block_of(array, index, size, axis=0):
    return lax.dynamic_slice_in_dim(array, index * size, size, axis)


def on_device(
    inputs,
    cotangent,
    segment_ids,
    w_qkv,
    w_out,
    w_fc1,
    w_fc2,
    norm_params,
    proj_bias,
    fc1_bias,
    qkv_rows,
    qkv_cols,
    out_rows,
    out_cols,
    fc1_rows,
    fc1_cols,
    fc2_rows,
    fc2_cols,
    norm_second,
    bias_second,
    fc1b_second,
):
    tokens = inputs.shape[0]
    local_width = inputs.shape[1]
    local_hidden = fc1_bias.shape[0]
    rows = w_qkv.shape[0]
    count = lax.axis_size("batch")
    c = lax.axis_index("branch")
    b = lax.axis_index("batch")
    q = lax.rem(b, INNER)
    group = INNER * tokens
    width_q = local_width // INNER
    hidden_q = local_hidden // INNER
    qkv_low = w_qkv.astype(jnp.bfloat16).reshape(rows, 3, INNER, HEADS_DEV, HD)
    out_low = w_out.astype(jnp.bfloat16).reshape(INNER, HEADS_DEV, HD, rows)
    fc1_low = w_fc1.astype(jnp.bfloat16).reshape(rows, INNER, CUTS, CUT)
    fc2_low = w_fc2.astype(jnp.bfloat16).reshape(INNER, CUTS, CUT, rows)
    heads_low = jnp.concatenate(
        [
            qkv_low.transpose(3, 2, 0, 1, 4).reshape(HEADS_DEV, INNER, rows, 3 * HD),
            out_low.transpose(1, 0, 3, 2),
        ],
        axis=3,
    )
    cuts_low = jnp.concatenate(
        [fc1_low.transpose(2, 1, 0, 3), fc2_low.transpose(1, 0, 3, 2)], axis=3
    )
    wst = jnp.concatenate([heads_low, cuts_low], axis=0)

    segment = jnp.concatenate(
        [segment_ids]
        + [lax.ppermute(segment_ids, "batch", swap_pairs(count, d)) for d in range(1, INNER)],
        axis=0,
    )
    positions_idx = jnp.arange(tokens)
    earlier = jnp.sum((segment[:, None, :] < segment[:, :, None]).astype(jnp.int32), axis=2)
    starts = earlier.astype(jnp.float32).reshape(1, group)
    places = (positions_idx[None] - earlier).astype(jnp.float32).reshape(1, group)
    frequency = 10000.0 ** (-2.0 * jnp.arange(ROT // 2, dtype=jnp.float32) / ROT)
    angles = frequency[:, None] * places
    cos_part = jnp.cos(angles)
    sin_part = jnp.sin(angles)
    turns = jnp.concatenate(
        [
            cos_part,
            cos_part,
            -sin_part,
            sin_part,
            jnp.broadcast_to(starts, (HD - 2 * ROT, group)),
        ],
        axis=0,
    )
    bias_h = (
        block_of(proj_bias[0:3], q, width_q, 1)
        .reshape(3, HEADS_DEV, HD)
        .transpose(1, 0, 2)
        .reshape(HEADS_DEV, 1, 3 * HD)
    )
    bias_f = block_of(fc1_bias, q, hidden_q).reshape(CUTS, 1, CUT)
    received, plane_parts, plane_own, head_bias, cut_bias, col_sums, row_moments = block_call(
        count, wst, inputs, cotangent, turns, norm_params, bias_h, bias_f
    )
    by_part = (INNER, hidden_q)
    qkv_parts = w_qkv.transpose(1, 0, 2)
    output, input_grad, row_stats, pack, norm_pack = tail_call(
        count,
        received,
        qkv_parts.reshape(3 * rows, local_width),
        w_out,
        w_fc1,
        w_fc2,
        plane_parts,
        plane_own,
        inputs,
        cotangent,
        row_moments,
        norm_params,
        proj_bias,
        fc1_bias.reshape(by_part),
        jnp.stack([qkv_rows, fc1_rows, out_cols, fc2_cols], axis=1),
        qkv_cols,
        out_rows.reshape(1, local_width),
        fc1_cols.reshape(by_part),
        fc2_rows.reshape(by_part),
        norm_second,
        bias_second,
        fc1b_second.reshape(by_part),
        col_sums,
        head_bias,
        cut_bias,
    )
    updated = update_call(
        received,
        qkv_parts,
        w_out,
        w_fc1,
        w_fc2,
        row_stats,
        pack,
        norm_pack,
        output,
        input_grad,
    )
    qkv_grad, qkv_next, qkv_copy = (array.transpose(1, 0, 2) for array in updated[0:3])
    out_grad, out_next, out_copy = updated[3:6]
    fc1_grad, fc1_next, fc1_copy = updated[6:9]
    fc2_grad, fc2_next, fc2_copy = updated[9:12]
    qkv_rows_new, fc1_rows_new, out_cols_new, fc2_cols_new = (
        array.reshape(rows) for array in updated[12:16]
    )
    (
        output,
        input_grad,
        qkv_cols_new,
        out_rows_new,
        fc1_cols_new,
        fc2_rows_new,
        bias_grad,
        bias_moment,
        bias_new,
        fc1b_grad,
        fc1b_moment,
        fc1b_new,
        norm_grad,
        norm_moment,
        norm_new,
    ) = updated[16:]
    return (
        output,
        input_grad,
        qkv_grad,
        qkv_next,
        qkv_rows_new,
        qkv_cols_new,
        qkv_copy,
        out_grad,
        out_next,
        out_rows_new.reshape(local_width),
        out_cols_new,
        out_copy,
        fc1_grad,
        fc1_next,
        fc1_rows_new,
        fc1_cols_new.reshape(local_hidden),
        fc1_copy,
        fc2_grad,
        fc2_next,
        fc2_rows_new.reshape(local_hidden),
        fc2_cols_new,
        fc2_copy,
        norm_grad,
        norm_moment,
        norm_new,
        bias_grad,
        bias_moment,
        bias_new,
        fc1b_grad.reshape(local_hidden),
        fc1b_moment.reshape(local_hidden),
        fc1b_new.reshape(local_hidden),
    )


def solution(mesh):
    in_specs = (
        P("batch", "branch"),
        P("batch", "branch"),
        P("batch", None),
        P("batch", None, "branch"),
        P("branch", "batch"),
        P("batch", "branch"),
        P("branch", "batch"),
        P(),
        P(None, "branch"),
        P("branch"),
        P("batch"),
        P(None, "branch"),
        P("branch"),
        P("batch"),
        P("batch"),
        P("branch"),
        P("branch"),
        P("batch"),
        P(),
        P(None, "branch"),
        P("branch"),
    )
    out_specs = (
        P("batch", "branch"),
        P("batch", "branch"),
        P("batch", None, "branch"),
        P("batch", None, "branch"),
        P("batch"),
        P(None, "branch"),
        P("batch", None, "branch"),
        P("branch", "batch"),
        P("branch", "batch"),
        P("branch"),
        P("batch"),
        P("branch", "batch"),
        P("batch", "branch"),
        P("batch", "branch"),
        P("batch"),
        P("branch"),
        P("batch", "branch"),
        P("branch", "batch"),
        P("branch", "batch"),
        P("branch"),
        P("batch"),
        P("branch", "batch"),
        P(),
        P(),
        P(),
        P(None, "branch"),
        P(None, "branch"),
        P(None, "branch"),
        P("branch"),
        P("branch"),
        P("branch"),
    )
    return jax.shard_map(
        on_device, mesh=mesh, in_specs=in_specs, out_specs=out_specs, check_vma=False
    )
```

```python
import functools

import jax
import jax.numpy as jnp
from jax import lax
from jax.experimental import pallas as pl
from jax.experimental.pallas import tpu as pltpu
from jax.sharding import PartitionSpec as P

D = 2048
HD = 128
ROT = 32
FF = 8192
STEP = 10


EPS_NORM = 1e-05
EPS_SQUARE = 1e-30
RATE = 0.3
FLOOR_RATE = 0.001


def decay_rate():
    return 1.0 - STEP ** (-0.8)


def squares(gradient):
    return gradient * gradient + EPS_SQUARE


def renew_stat(old_stat, new_sum):
    decay = decay_rate()
    return decay * old_stat + (1.0 - decay) * new_sum


def second_step(gradient, second):
    second_new = renew_stat(second, squares(gradient))
    return (second_new, gradient * lax.rsqrt(second_new))


INNER = 4
HEADS_DEV = 2
CUTS = 4
CHUNKS = HEADS_DEV + CUTS
CUT = 256
WIDE = 512
MESH = pl.DeviceIdType.MESH


def flip(index, step):
    return index + step * (1 - 2 * lax.rem(index // step, 2))


def nn(left, right):
    return jnp.dot(left, right, preferred_element_type=jnp.float32)


def nt(left, right):
    return lax.dot_general(
        left, right, (((1,), (1,)), ((), ())), preferred_element_type=jnp.float32
    )


def tn(left, right):
    return lax.dot_general(
        left, right, (((0,), (0,)), ((), ())), preferred_element_type=jnp.float32
    )


def block_kernel(
    count,
    wst,
    xin,
    yin,
    turn_ref,
    norm_ref,
    bias_h,
    bias_f,
    gr,
    xr,
    xo,
    qb,
    fb,
    cs,
    st,
    H1,
    H2,
    DY,
    W,
    TA,
    G,
    sbuf,
    fbuf,
    rsb,
    sib_send,
    sib_land,
    own,
    a2a_s,
    a2a_r,
    loc_s,
    ag_s,
    ag_r,
    x_s,
    x_r,
    sx_s,
    sx_r,
    rs_s,
    rs_r,
    gr_s,
    gr_r,
    sib_s,
    sib_r,
    p_s,
    p_r,
    tmp_s,
    free_s,
):
    outer = count // INNER
    S = outer - 1
    T, half = xin.shape
    R = wst.shape[2]
    block = INNER * R
    QT = T // 2
    b = lax.axis_index("batch")
    c = lax.axis_index("branch")
    q = lax.rem(b, INNER)
    o = b // INNER
    bx, by = flip(b, 1), flip(b, 2)
    bxy = flip(bx, 2)
    near = (bx, by, bxy)
    da = 1 + c
    db = 2 - c
    b_first = bx * (1 - c) + by * c
    b_second = by * (1 - c) + bx * c

    def remote(src, dst, ssem, rsem, to_b, to_c):
        return pltpu.make_async_remote_copy(
            src_ref=src,
            dst_ref=dst,
            send_sem=ssem,
            recv_sem=rsem,
            device_id=(to_b, to_c),
            device_id_type=MESH,
        )

    barrier = pltpu.get_barrier_semaphore()
    for who in near:
        pl.semaphore_signal(barrier, inc=1, device_id=(who, c), device_id_type=MESH)
    pl.semaphore_signal(barrier, inc=1, device_id=(b, 1 - c), device_id_type=MESH)

    @pl.when(o > 0)
    def _():
        pl.semaphore_signal(barrier, inc=1, device_id=(b - INNER, c), device_id_type=MESH)

    @pl.when(o < outer - 1)
    def _():
        pl.semaphore_signal(barrier, inc=1, device_id=(b + INNER, c), device_id_type=MESH)

    pl.semaphore_wait(barrier, 4 + jnp.minimum(o, 1) + jnp.minimum(outer - 1 - o, 1))

    def a2a_copy(k, d, received=False):
        to = near[d - 1]
        row = (to if received else b) * R
        return remote(
            wst.at[k, lax.rem(to, INNER)],
            W.at[k, pl.ds(pl.multiple_of(row, 16), R)],
            a2a_s.at[k, d - 1],
            a2a_r.at[k, d - 1],
            to,
            c,
        )

    def a2a_local(k):
        return pltpu.make_async_copy(
            wst.at[k, q], W.at[k, pl.ds(pl.multiple_of(b * R, 16), R)], loc_s.at[k]
        )

    def a2a_start(k):
        for d in range(1, INNER):
            a2a_copy(k, d).start()
        a2a_local(k).start()

    def a2a_wait(k):
        for d in range(1, INNER):
            a2a_copy(k, d, True).wait_recv()
        a2a_local(k).wait()

    def ag_copy(k, way, s, part):
        rows = pl.ds(pl.multiple_of(part * block, 16), block)
        to = b + INNER if way == 0 else b - INNER
        return remote(
            W.at[k, rows], W.at[k, rows], ag_s.at[k, way, s - 1], ag_r.at[k, way, s - 1], to, c
        )

    def ag_sends(k, s, what):
        @pl.when((o >= s - 1) & (o <= outer - 2))
        def _():
            what(ag_copy(k, 0, s, o - s + 1))

        @pl.when((o >= 1) & (o <= outer - s))
        def _():
            what(ag_copy(k, 1, s, o + s - 1))

    def ag_wait(k, s):
        @pl.when(o >= s)
        def _():
            ag_copy(k, 0, s, o - s).wait_recv()

        @pl.when(o <= outer - 1 - s)
        def _():
            ag_copy(k, 1, s, o + s).wait_recv()

    def ag_range(low, high):
        def step(n, carry):
            k = n // S
            s = lax.rem(n, S) + 1

            @pl.when(s == 1)
            def _():
                a2a_wait(k)

            @pl.when(s > 1)
            def _():
                ag_wait(k, s - 1)

            ag_sends(k, s, lambda copy: copy.start())
            return carry

        lax.fori_loop(low, high, step, 0)

    def ag(low, high):
        ag_range(low * S // 3, high * S // 3)

    def spot(buf, slot):
        return buf.at[
            pl.ds(pl.multiple_of(slot * T, 16), T), pl.ds(pl.multiple_of(c * half, 128), half)
        ]

    def other_spot(buf, slot):
        return buf.at[
            pl.ds(pl.multiple_of(slot * T, 16), T), pl.ds(pl.multiple_of((1 - c) * half, 128), half)
        ]

    def sx_copy(i, buf, slot, src=None):
        place = spot(buf, slot)
        return remote(place if src is None else src, place, sx_s.at[i, slot], sx_r.at[i, slot], b, 1 - c)

    def sx_wait(i, buf, slot):
        remote(
            other_spot(buf, slot), other_spot(buf, slot), sx_s.at[i, slot], sx_r.at[i, slot], b, 1 - c
        ).wait_recv()

    def x_first(i, src, buf):
        return remote(src, spot(buf, da), x_s.at[i, da - 1], x_r.at[i, da - 1], b_first, c)

    def x_second(i, src, buf):
        return remote(src, spot(buf, db), x_s.at[i, db - 1], x_r.at[i, db - 1], b_second, c)

    def x_forward(i, buf):
        return remote(spot(buf, da), spot(buf, 3), x_s.at[i, 2], x_r.at[i, 2], b_second, c)

    def x_diag(i, buf):
        return remote(spot(buf, 3), spot(buf, 3), x_s.at[i, 2], x_r.at[i, 2], b_second, c)

    def x_local(i, src, buf):
        return pltpu.make_async_copy(src, spot(buf, 0), tmp_s.at[i])

    def gather_one(i, src, buf):
        x_first(i, src, buf).start()
        x_local(i, src, buf).start()
        sx_copy(i, buf, 0, src).start()

    def gather_two(i, src, buf):
        x_first(i, src, buf).wait_recv()
        x_second(i, src, buf).start()
        x_forward(i, buf).start()
        sx_copy(i, buf, da).start()

    def gather_three(i, src, buf):
        x_second(i, src, buf).wait_recv()
        sx_copy(i, buf, db).start()
        x_diag(i, buf).wait_recv()
        sx_copy(i, buf, 3).start()

    def gather_sent(i, src, buf):
        x_first(i, src, buf).wait_send()
        x_second(i, src, buf).wait_send()
        x_forward(i, buf).wait_send()
        sx_copy(i, buf, 0, src).wait_send()
        for slot in range(1, INNER):
            sx_copy(i, buf, slot).wait_send()

    lane_n = lax.broadcasted_iota(jnp.int32, (64, 128), 1)

    def norm_rows(slot):
        def step(i, carry):
            rows = pl.ds(pl.multiple_of(slot * T + i * 64, 64), 64)
            values = H1[rows, :].astype(jnp.float32)
            mean = jnp.mean(values, axis=-1, keepdims=True)
            centered = values - mean
            inverse = lax.rsqrt(jnp.mean(centered * centered, axis=-1, keepdims=True) + EPS_NORM)
            normed = centered * inverse
            if slot == 0:
                st[pl.ds(pl.multiple_of(i * 64, 64), 64), :] = jnp.where(lane_n == 0, mean, inverse)
            H1[rows, :] = (normed * norm_ref[0:1, :] + norm_ref[1:2, :]).astype(jnp.bfloat16)
            H2[rows, :] = (normed * norm_ref[2:3, :] + norm_ref[3:4, :]).astype(jnp.bfloat16)
            return carry

        lax.fori_loop(0, T // 64, step, 0)

    lane = lax.broadcasted_iota(jnp.int32, (T, HD), 1)
    scale = HD ** (-0.5)

    def partner(tensor):
        return jnp.where(
            lane < ROT // 2,
            pltpu.roll(tensor, HD - ROT // 2, 1),
            jnp.where(lane < ROT, pltpu.roll(tensor, ROT // 2, 1), 0.0),
        )

    def turns_of(rows):
        table = turn_ref[:, rows].T
        cos_rows = jnp.where(lane < ROT, table, 1.0)
        sin_rows = pltpu.roll(table, HD - ROT, 1)
        return cos_rows, sin_rows, table[:, 2 * ROT : 2 * ROT + 1]

    def probs_at(h, slot, i):
        seen = QT * (i + 1)
        wide = min(block, seen)
        part = slice(QT * i, QT * (i + 1))
        base = slot * (outer // INNER)
        return [(h, base + j, part, slice(0, wide)) for j in range(seen // wide)]

    def forward_piece(h, slot):
        start = pl.multiple_of(slot * T, 128)
        rows = pl.ds(start, T)
        cos_rows, sin_rows, starts = turns_of(rows)
        projected = nn(H1[rows, :], W[h, :, : 3 * HD]) + bias_h[h]
        first = projected[:, :HD]
        queries = (first * cos_rows + partner(first) * sin_rows).astype(jnp.bfloat16)
        second = projected[:, HD : 2 * HD]
        keys = (second * cos_rows + partner(second) * sin_rows).astype(jnp.bfloat16)
        values = projected[:, 2 * HD :].astype(jnp.bfloat16)
        TA[h, :, pl.ds(start, HD)] = queries
        TA[h, :, pl.ds(start + HD, HD)] = keys
        TA[h, :, pl.ds(start + 2 * HD, HD)] = values
        for i in range(2):
            seen = QT * (i + 1)
            part = slice(QT * i, QT * (i + 1))
            raw = nt(queries[part], keys[:seen]) * scale
            query_at = lax.broadcasted_iota(jnp.int32, (QT, seen), 0) + QT * i
            key_at = lax.broadcasted_iota(jnp.int32, (QT, seen), 1)
            allowed = (key_at <= query_at) & (key_at.astype(jnp.float32) >= starts[part])
            scores = jnp.where(allowed, raw, -1e30)
            exponent = jnp.exp(scores - jnp.max(scores, axis=-1, keepdims=True))
            probs = exponent * (1.0 / jnp.sum(exponent, axis=-1, keepdims=True))
            for j, place in enumerate(probs_at(h, slot, i)):
                wide = min(block, seen)
                G[place] = probs[:, j * wide : (j + 1) * wide]
            TA[h, part, pl.ds(start + 3 * HD, HD)] = nn(
                probs.astype(jnp.bfloat16), values[:seen]
            ).astype(jnp.bfloat16)

    def head_piece(h, slot):
        start = pl.multiple_of(slot * T, 128)
        rows = pl.ds(start, T)
        cos_rows, sin_rows, _ = turns_of(rows)
        queries = TA[h, :, pl.ds(start, HD)]
        keys = TA[h, :, pl.ds(start + HD, HD)]
        values = TA[h, :, pl.ds(start + 2 * HD, HD)]
        context = TA[h, :, pl.ds(start + 3 * HD, HD)]
        back = nn(DY[rows, :], W[h, :, 3 * HD :]).astype(jnp.bfloat16)
        grad_q = []
        grad_k, grad_v = [None, None], [None, None]
        for i in range(2):
            seen = QT * (i + 1)
            part = slice(QT * i, QT * (i + 1))
            probs = [G[place] for place in probs_at(h, slot, i)]
            probs = probs[0] if len(probs) == 1 else jnp.concatenate(probs, axis=1)
            soft = probs.astype(jnp.bfloat16)
            grad_probs = nt(back[part], values[:seen])
            inner = jnp.sum(probs * grad_probs, axis=-1, keepdims=True)
            grad_scores = (probs * (grad_probs - inner)).astype(jnp.bfloat16)
            grad_q.append((nn(grad_scores, keys[:seen]) * scale).astype(jnp.bfloat16))
            for j in range(i + 1):
                cut = slice(QT * j, QT * (j + 1))
                term_v = tn(soft[:, cut], back[part])
                term_k = tn(grad_scores[:, cut], queries[part])
                grad_v[j] = term_v if grad_v[j] is None else grad_v[j] + term_v
                grad_k[j] = term_k if grad_k[j] is None else grad_k[j] + term_k
        dq = jnp.concatenate(grad_q, axis=0).astype(jnp.float32)
        dk = (jnp.concatenate(grad_k, axis=0) * scale).astype(jnp.bfloat16).astype(jnp.float32)
        dv = jnp.concatenate(grad_v, axis=0)
        turned = jnp.concatenate(
            [
                dq * cos_rows - partner(dq) * sin_rows,
                dk * cos_rows - partner(dk) * sin_rows,
                dv,
            ],
            axis=1,
        ).astype(jnp.bfloat16)
        TA[h, : 3 * HD, rows] = turned.T
        TA[h, 3 * HD :, rows] = context.T
        total = jnp.sum(turned.astype(jnp.float32), axis=0, keepdims=True)
        qb[h] = jnp.where(slot == 0, total, qb[h] + total)

    def cut_piece(f, slot):
        rows = pl.ds(pl.multiple_of(slot * T, 128), T)
        k = HEADS_DEV + f
        pre = nn(H2[rows, :], W[k, :, :CUT]) + bias_f[f]
        grad = nn(DY[rows, :], W[k, :, CUT:])
        normal = 0.5 * (1.0 + lax.erf(pre * (0.5**0.5)))
        slope = normal + pre * (jnp.exp(-0.5 * pre * pre) * (0.5 * 0.7978845608028654))
        active = (pre * normal).astype(jnp.bfloat16)
        pulled = (grad * slope).astype(jnp.bfloat16)
        low = pl.multiple_of(f * WIDE, WIDE)
        H1[pl.ds(low, CUT), rows] = pulled.T
        H1[pl.ds(low + CUT, CUT), rows] = active.T
        total = jnp.sum(pulled.astype(jnp.float32), axis=0, keepdims=True)
        fb[f] = jnp.where(slot == 0, total, fb[f] + total)

    def grads(k, turned, left, edge):
        def step(j, carry):
            cols = pl.ds(pl.multiple_of(j * block, 128), block)
            G[lax.rem(k, 2), j, :edge, :] = nn(turned(0, edge), left[:, cols])
            G[lax.rem(k, 2), j, edge:, :] = nn(turned(edge, WIDE - edge), DY[:, cols])
            return carry

        lax.fori_loop(0, outer, step, 0)

    def head_turned(h):
        return lambda low, size: TA[h, pl.ds(low, size), :]

    def cut_turned(f):
        return lambda low, size: H1[pl.ds(pl.multiple_of(f * WIDE + low, 128), size), :]

    def rs_copy(k, way, t):
        to = b + INNER if way == 0 else b - INNER
        return remote(
            sbuf.at[way],
            rsb.at[way, t - 1],
            rs_s.at[k, way, t - 1],
            rs_r.at[k, way, t - 1],
            to,
            c,
        )

    def rs_sends(way, t):
        if way == 0:
            return (o <= t - 1) & (o <= outer - 2)
        return (o >= outer - t) & (o >= 1)

    def rs_receives(way, t):
        if way == 0:
            return (o >= 1) & (o <= t)
        return (o <= outer - 2) & (o >= outer - 1 - t)

    def rs_fetch(k, way, t):
        rs_copy(k, way, t).wait_recv()
        return rsb[way, t - 1].astype(jnp.float32)

    def rs_step(k, t):
        n = k * S + t - 1

        @pl.when((t == 1) & (k >= 1) & (o < outer - 1))
        def _():
            pl.semaphore_wait(free_s.at[0], 1)

        @pl.when((t == 1) & (k >= 1) & (o > 0))
        def _():
            pl.semaphore_wait(free_s.at[1], 1)

        before = jnp.maximum(n - 1, 0)
        k_before = before // S
        t_before = lax.rem(before, S) + 1
        for way in range(2):
            owner = o + outer - t if way == 0 else o - outer + t

            @pl.when((n >= 1) & rs_sends(way, t_before))
            def _():
                rs_copy(k_before, way, t_before).wait_send()

            @pl.when(rs_sends(way, t))
            def _():
                @pl.when(rs_receives(way, t - 1) & (t > 1))
                def _():
                    sbuf[way] = (
                        G[lax.rem(k, 2), owner] + rs_fetch(k, way, t - 1)
                    ).astype(jnp.bfloat16)

                @pl.when(jnp.logical_not(rs_receives(way, t - 1) & (t > 1)))
                def _():
                    sbuf[way] = G[lax.rem(k, 2), owner].astype(jnp.bfloat16)

                rs_copy(k, way, t).start()

    def gr_copy(k, d, received=False):
        to = near[d - 1]
        slot = lax.rem(to, INNER)
        return remote(
            fbuf.at[pl.ds(pl.multiple_of(slot * R, 16), R)],
            gr.at[k, slot if received else q],
            gr_s.at[k, d - 1],
            gr_r.at[k, d - 1],
            to,
            c,
        )

    def gr_local(k):
        return pltpu.make_async_copy(
            fbuf.at[pl.ds(pl.multiple_of(q * R, 16), R)],
            gr.at[k, q],
            gr_s.at[k, 3],
        )

    def gr_sent(k):
        for d in range(1, INNER):
            gr_copy(k, d).wait_send()
        gr_local(k).wait()

    def rs_final(k):
        for way in range(2):

            @pl.when(rs_receives(way, S))
            def _():
                G[lax.rem(k, 2), o] = G[lax.rem(k, 2), o] + rs_fetch(k, way, S)

        @pl.when((k < CHUNKS - 1) & (o > 0))
        def _():
            pl.semaphore_signal(
                free_s.at[0], inc=1, device_id=(b - INNER, c), device_id_type=MESH
            )

        @pl.when((k < CHUNKS - 1) & (o < outer - 1))
        def _():
            pl.semaphore_signal(
                free_s.at[1], inc=1, device_id=(b + INNER, c), device_id_type=MESH
            )

        @pl.when(k >= 1)
        def _():
            gr_sent(k - 1)

        final = G[lax.rem(k, 2), o].T
        cs[k] = jnp.sum(squares(final), axis=0, keepdims=True)
        fbuf[...] = final.astype(jnp.bfloat16)
        for d in range(1, INNER):
            gr_copy(k, d).start()
        gr_local(k).start()

    def rs_range(low, high):
        def step(n, carry):
            k = n // (S + 1)
            t = lax.rem(n, S + 1) + 1

            @pl.when(t <= S)
            def _():
                rs_step(k, t)

            @pl.when(t == S + 1)
            def _():
                rs_final(k)

            return carry

        lax.fori_loop(low, high, step, 0)

    TILE = half // 2
    TILES = 2 * INNER
    PER_ROW = D // T

    def tile_slot(i):
        return INNER - 1 - i // 2

    def product(which, i, side):
        toks = pl.ds(pl.multiple_of(tile_slot(i) * T, 128), T)
        features = pl.ds(pl.multiple_of(side * half + lax.rem(i, 2) * TILE, 128), TILE)
        terms = []
        if which == 0:
            for h in range(HEADS_DEV):
                terms.append((h, slice(0, 3 * HD), lambda h=h: TA[h, : 3 * HD, toks]))
        elif which == 1:
            for f in range(CUTS):
                low = f * WIDE
                terms.append(
                    (HEADS_DEV + f, slice(0, CUT), lambda low=low: H1[low : low + CUT, toks])
                )
        else:
            for h in range(HEADS_DEV):
                terms.append((h, slice(3 * HD, WIDE), lambda h=h: TA[h, 3 * HD :, toks]))
            for f in range(CUTS):
                low = f * WIDE + CUT
                terms.append(
                    (HEADS_DEV + f, slice(CUT, WIDE), lambda low=low: H1[low : low + CUT, toks])
                )
        for place, (k, cols, right) in enumerate(terms):
            term = nn(W[k, features, cols], right())
            own[...] = term if place == 0 else own[...] + term

    def sib_copy(which, i):
        return remote(
            sib_send.at[lax.rem(i, 2)],
            sib_land.at[lax.rem(i, 4)],
            sib_s.at[which, i],
            sib_r.at[which, i],
            b,
            1 - c,
        )

    def stage(which, i):
        buf, t = (H1, PER_ROW * (half // TILE) + i) if which == 0 else (H2, (which - 1) * (TILES - 2) + i)
        return buf.at[
            pl.ds(pl.multiple_of(t // PER_ROW * TILE, 128), TILE),
            pl.ds(pl.multiple_of(lax.rem(t, PER_ROW) * T, 128), T),
        ]

    def plane_copy(which, i):
        slot = tile_slot(i)
        low, high = lax.rem(slot, 2), slot // 2
        to = b + low * (1 - 2 * lax.rem(b, 2)) + high * 2 * (1 - 2 * lax.rem(b // 2, 2))
        src = stage(which, i)
        return remote(
            src,
            xr.at[which, slot - 1, lax.rem(i, 2)],
            p_s.at[which, i],
            p_r.at[which, i],
            to,
            c,
        )

    def tile_a(which, i):
        @pl.when(i >= 2)
        def _():
            sib_copy(which, i - 2).wait_send()

        product(which, i, 1 - c)
        sib_send[lax.rem(i, 2)] = own[...].astype(jnp.bfloat16)
        sib_copy(which, i).start()

    def tile_b(which, i):
        product(which, i, c)
        sib_copy(which, i).wait_recv()

        @pl.when(i < TILES - 2)
        def _():
            total = (own[...] + sib_land[lax.rem(i, 4)].astype(jnp.float32)).astype(jnp.bfloat16)
            stage(which, i)[...] = total
            plane_copy(which, i).start()

        @pl.when(i >= TILES - 2)
        def _():
            own[...] = own[...] + sib_land[lax.rem(i, 4)].astype(jnp.float32)
            keep = pltpu.make_async_copy(own, xo.at[which, lax.rem(i, 2)], tmp_s.at[2])
            keep.start()
            keep.wait()

    def sum_tiles(which, beside):
        tile_a(which, 0)

        def step(i, carry):
            @pl.when(i < TILES - 1)
            def _():
                tile_a(which, i + 1)

            tile_b(which, i)
            beside(i)
            return carry

        lax.fori_loop(0, TILES, step, 0)

    def sib_sent(which):
        for i in range(TILES - 2, TILES):
            sib_copy(which, i).wait_send()

    def spread(first, last, i, pieces, run):
        steps = last - first
        run(
            first + (steps * i + pieces - 1) // pieces,
            first + (steps * (i + 1) + pieces - 1) // pieces,
        )

    def ag_share(low, high, i, pieces):
        spread(low * S // 3, high * S // 3, i, pieces, ag_range)

    def rs_share(low, high, i, pieces):
        spread(low * (S + 1) // 4, high * (S + 1) // 4, i, pieces, rs_range)

    a2a_start(0)
    gather_one(0, xin, H1)
    gather_one(1, yin, DY)
    ag(0, 1)
    a2a_start(1)
    gather_two(0, xin, H1)
    gather_two(1, yin, DY)
    ag(1, 2)
    a2a_start(2)
    x_local(0, xin, H1).wait()
    sx_wait(0, H1, 0)
    norm_rows(0)
    ag(2, 3)
    gather_three(0, xin, H1)
    gather_sent(0, xin, H1)
    for k in range(3, CHUNKS):
        a2a_start(k)
    for slot in range(1, INNER):
        sx_wait(0, H1, slot)
        norm_rows(slot)
        if slot < 3:
            ag(2 + slot, 3 + slot)

    def project_step(h):
        ag_wait(h, S)

        def slot_step(slot, inner_carry):
            forward_piece(h, slot)
            ag_share(5 + h, 6 + h, slot, INNER)
            return inner_carry

        lax.fori_loop(0, INNER, slot_step, 0)

    project_step(0)
    gather_three(1, yin, DY)
    project_step(1)
    x_local(1, yin, DY).wait()
    for slot in range(INNER):
        sx_wait(1, DY, slot)
    gather_sent(1, yin, DY)

    def head_step(h, carry):
        def slot_step(slot, inner_carry):
            head_piece(h, slot)
            ag_share(7 + 2 * h, 9 + 2 * h, slot, INNER)
            rs_share(0, 2 * h, slot, INNER)
            return inner_carry

        lax.fori_loop(0, INNER, slot_step, 0)
        grads(h, head_turned(h), H1, 3 * HD)
        return carry

    lax.fori_loop(0, HEADS_DEV, head_step, 0)

    def beside_one(i):
        ag_share(13, 15, i, TILES)
        rs_share(4, 7, i, TILES)

    def cut_step(f, carry):
        ag_wait(HEADS_DEV + f, S)

        @pl.when(f == CUTS // 2)
        def _():
            for i in range(TILES - 2):
                plane_copy(0, i).wait_send()

        def slot_step(slot, inner_carry):
            cut_piece(f, slot)
            ag_share(
                jnp.where(f == 0, 11, jnp.minimum(13 + 2 * f, 18)),
                jnp.where(f == 0, 13, jnp.minimum(15 + 2 * f, 18)),
                slot,
                INNER,
            )
            rs_share(
                jnp.where(f == 0, 2, jnp.where(f == 1, 7, 3 + 3 * f)),
                jnp.where(f == 0, 4, jnp.where(f == 3, 16, 6 + 3 * f)),
                slot,
                INNER,
            )
            return inner_carry

        lax.fori_loop(0, INNER, slot_step, 0)
        grads(HEADS_DEV + f, cut_turned(f), H2, CUT)

        @pl.when(f == 0)
        def _():
            sum_tiles(0, beside_one)

        return carry

    lax.fori_loop(0, CUTS, cut_step, 0)
    sib_sent(0)
    sum_tiles(1, lambda i: rs_share(16, 20, i, TILES))
    sib_sent(1)
    sum_tiles(2, lambda i: rs_share(20, 24, i, TILES))
    sib_sent(2)

    gr_sent(CHUNKS - 1)

    def drain_chunk(k, carry):
        for d in range(1, INNER):
            a2a_copy(k, d).wait_send()
            gr_copy(k, d, True).wait_recv()

        def drain_step(s, inner_carry):
            ag_sends(k, s, lambda copy: copy.wait_send())
            return inner_carry

        lax.fori_loop(1, S + 1, drain_step, 0)
        return carry

    lax.fori_loop(0, CHUNKS, drain_chunk, 0)
    for way in range(2):

        @pl.when(rs_sends(way, S))
        def _():
            rs_copy(CHUNKS - 1, way, S).wait_send()

    for which in range(3):

        def drain_tile(i, carry):
            if which:
                plane_copy(which, i).wait_send()
            plane_copy(which, i).wait_recv()
            return carry

        lax.fori_loop(0, TILES - 2, drain_tile, 0)


def block_call(count, wst, xin, yin, turns, norm_params, bias_h, bias_f):
    outer = count // INNER
    S = outer - 1
    tokens, half = xin.shape
    group = INNER * tokens
    rows = wst.shape[2]
    tile = half // 2
    low, high = jnp.bfloat16, jnp.float32
    any_spec = pl.BlockSpec(memory_space=pl.ANY)
    vmem_spec = pl.BlockSpec(memory_space=pltpu.VMEM)
    dma = pltpu.SemaphoreType.DMA
    return pl.pallas_call(
        functools.partial(block_kernel, count),
        out_shape=[
            jax.ShapeDtypeStruct((CHUNKS, INNER, rows, WIDE), low),
            jax.ShapeDtypeStruct((3, INNER - 1, 2, tile, tokens), low),
            jax.ShapeDtypeStruct((3, 2, tile, tokens), high),
            jax.ShapeDtypeStruct((HEADS_DEV, 1, 3 * HD), high),
            jax.ShapeDtypeStruct((CUTS, 1, CUT), high),
            jax.ShapeDtypeStruct((CHUNKS, 1, WIDE), high),
            jax.ShapeDtypeStruct((tokens, 128), high),
        ],
        in_specs=[any_spec] * 3 + [vmem_spec] * 4,
        out_specs=[any_spec] * 3 + [vmem_spec] * 4,
        scratch_shapes=[
            pltpu.VMEM((group, D), low),
            pltpu.VMEM((group, D), low),
            pltpu.VMEM((group, D), low),
            pltpu.VMEM((CHUNKS, D, WIDE), low),
            pltpu.VMEM((HEADS_DEV, WIDE, group), low),
            pltpu.VMEM((2, outer, WIDE, INNER * rows), high),
            pltpu.VMEM((2, WIDE, INNER * rows), low),
            pltpu.VMEM((INNER * rows, WIDE), low),
            pltpu.VMEM((2, S, WIDE, INNER * rows), low),
            pltpu.VMEM((2, tile, tokens), low),
            pltpu.VMEM((4, tile, tokens), low),
            pltpu.VMEM((tile, tokens), high),
            dma((CHUNKS, INNER - 1)),
            dma((CHUNKS, INNER - 1)),
            dma((CHUNKS,)),
            dma((CHUNKS, 2, S)),
            dma((CHUNKS, 2, S)),
            dma((2, INNER - 1)),
            dma((2, INNER - 1)),
            dma((2, INNER)),
            dma((2, INNER)),
            dma((CHUNKS, 2, S)),
            dma((CHUNKS, 2, S)),
            dma((CHUNKS, INNER)),
            dma((CHUNKS, INNER - 1)),
            dma((3, 2 * INNER)),
            dma((3, 2 * INNER)),
            dma((3, 2 * INNER)),
            dma((3, 2 * INNER)),
            dma((3,)),
            pltpu.SemaphoreType.REGULAR((2,)),
        ],
        compiler_params=pltpu.CompilerParams(
            collective_id=0, has_side_effects=True, vmem_limit_bytes=64 * 1024 * 1024
        ),
        cost_estimate=pl.CostEstimate(
            flops=80_000_000_000, bytes_accessed=60_000_000, transcendentals=10_000_000
        ),
    )(wst, xin, yin, turns, norm_params, bias_h, bias_f)


SLOT_ROWS = 16
PACK_ROWS = 40
PACK_ENDS = (0, 3, 4, 8, 12, 17, 22, 27, 31, 35, 39)


def total_of(values):
    return jnp.sum(jnp.sum(values, axis=0, keepdims=True), axis=1, keepdims=True)


def tail_kernel(
    count,
    gr,
    wq,
    wo,
    w1,
    w2,
    xr,
    xo,
    xin,
    yin,
    st,
    norm_ref,
    pb,
    fcb,
    row_old,
    qc_old,
    or_old,
    f1_old,
    f2_old,
    norm_second,
    bias_second,
    fcb_second,
    cs,
    qb,
    fb,
    out_ref,
    ing_ref,
    row_new,
    pack,
    norm_pack,
    qc_new,
    or_new,
    f1_new,
    f2_new,
    norm_grad,
    bias_grad,
    fcb_grad,
    scaled_buf,
    normed_buf,
    terms,
    terms_in,
    rsum,
    rsum_in,
    pay,
    z_in,
    z_sum,
    p_in,
    p_sum,
    s_in,
    pay2,
    z2_in,
    z2_sum,
    p2_in,
    p2_sum,
    s2_in,
    z_s,
    z_r,
    p_s,
    p_r,
    s_s,
    s_r,
):
    outer = count // INNER
    T, half = xin.shape
    R = gr.shape[2]
    b = lax.axis_index("batch")
    c = lax.axis_index("branch")
    q = lax.rem(b, INNER)
    o = b // INNER
    bx, by = flip(b, 1), flip(b, 2)
    near = (bx, by, flip(bx, 2))
    on_b = (b == 0).astype(jnp.float32)
    on_c = (c == 0).astype(jnp.float32)

    def remote(src, dst, ssem, rsem, to_b, to_c):
        return pltpu.make_async_remote_copy(
            src_ref=src,
            dst_ref=dst,
            send_sem=ssem,
            recv_sem=rsem,
            device_id=(to_b, to_c),
            device_id_type=MESH,
        )

    def chain(d):
        return lax.rem(o + d, outer)

    barrier = pltpu.get_barrier_semaphore()
    for who in near:
        pl.semaphore_signal(barrier, inc=1, device_id=(who, c), device_id_type=MESH)
    pl.semaphore_signal(barrier, inc=1, device_id=(b, 1 - c), device_id_type=MESH)
    for d in range(1, outer):
        pl.semaphore_signal(
            barrier, inc=1, device_id=(chain(d) * INNER + q, c), device_id_type=MESH
        )

    HALF_T = T // 2
    HALF_F = half // 2
    lane_t = lax.broadcasted_iota(jnp.int32, (T, 128), 1)
    own_half = pl.ds(pl.multiple_of(c * half, 128), half)
    other_half = pl.ds(pl.multiple_of((1 - c) * half, 128), half)
    pay[...] = jnp.zeros_like(pay)
    first_sum, second_sum = 0.0, 0.0
    for i in range(2):
        cols = slice(i * HALF_F, (i + 1) * HALF_F)
        gains = pl.ds(pl.multiple_of(c * half + i * HALF_F, 128), HALF_F)

        def whole(which):
            return (
                xo[which, i]
                + xr[which, 0, i].astype(jnp.float32)
                + xr[which, 1, i].astype(jnp.float32)
                + xr[which, 2, i].astype(jnp.float32)
            ).T

        values = xin[:, cols].astype(jnp.float32)
        out_ref[:, cols] = (values + whole(2) + pb[3:4, cols] + pb[4:5, cols]).astype(jnp.bfloat16)
        normed = (values - st[:, 0:1]) * st[:, 1:2]
        one = whole(0)
        two = whole(1)
        scaled = one * norm_ref[0:1, gains] + two * norm_ref[2:3, gains]
        scaled_buf[:, cols] = scaled
        normed_buf[:, cols] = normed
        first_sum = first_sum + jnp.sum(scaled, axis=1, keepdims=True)
        second_sum = second_sum + jnp.sum(scaled * normed, axis=1, keepdims=True)
        pay[5:6, cols] = jnp.sum(one * normed, axis=0, keepdims=True)
        pay[6:7, cols] = jnp.sum(one, axis=0, keepdims=True)
        pay[7:8, cols] = jnp.sum(two * normed, axis=0, keepdims=True)
        pay[8:9, cols] = jnp.sum(two, axis=0, keepdims=True)
        pay[9:10, cols] = jnp.sum(yin[:, cols].astype(jnp.float32), axis=0, keepdims=True)
    terms[...] = jnp.where(lane_t == 0, first_sum, jnp.where(lane_t == 1, second_sum, 0.0))
    for k in range(CHUNKS):
        pay[k // 2 : k // 2 + 1, k % 2 * WIDE : (k % 2 + 1) * WIDE] = cs[k]
    for h in range(HEADS_DEV):
        pay[3:4, h * 3 * HD : (h + 1) * 3 * HD] = qb[h]
    for f in range(CUTS):
        pay[4:5, f * CUT : (f + 1) * CUT] = fb[f]
    lane_p = lax.broadcasted_iota(jnp.int32, (1, half), 1)
    biases = jnp.sum(pb[...] * pb[...], axis=1, keepdims=True) * on_b
    scalars = (
        [total_of(w[...] * w[...]) for w in (wq, wo, w1, w2)]
        + [biases[i : i + 1] for i in range(5)]
        + [total_of(fcb[...] * fcb[...]) * on_b]
    )
    line = jnp.zeros((1, half), jnp.float32)
    for place, value in enumerate(scalars):
        line = jnp.where(lane_p == place, value, line)
    pay[10:11, :] = line

    pl.semaphore_wait(barrier, INNER + outer - 1)

    def chain_sends(src, buf, base, what):
        for d in range(1, outer):
            what(
                remote(
                    src,
                    buf.at[o],
                    z_s.at[base, d - 1],
                    z_r.at[base, d - 1],
                    chain(d) * INNER + q,
                    c,
                )
            )

    def chain_waits(src, buf, base):
        for d in range(1, outer):
            source = chain(outer - d)
            remote(
                src,
                buf.at[source],
                z_s.at[base, d - 1],
                z_r.at[base, d - 1],
                source * INNER + q,
                c,
            ).wait_recv()

    def plane_sends(src, buf, base, what):
        for d in range(1, INNER):
            what(remote(src, buf.at[q], p_s.at[base, d - 1], p_r.at[base, d - 1], near[d - 1], c))

    def plane_waits(src, buf, base):
        for d in range(1, INNER):
            remote(
                src,
                buf.at[lax.rem(near[d - 1], INNER)],
                p_s.at[base, d - 1],
                p_r.at[base, d - 1],
                near[d - 1],
                c,
            ).wait_recv()

    def pair_copy(src, dst, place):
        return remote(src, dst, s_s.at[place], s_r.at[place], b, 1 - c)

    start = lambda copy: copy.start()
    chain_sends(pay, z_in, 0, start)
    z_in[o] = pay[...]
    pair_copy(terms, terms_in, 0).start()

    lane_r = lax.broadcasted_iota(jnp.int32, (R, 128), 1)
    head_square = jnp.zeros((R, WIDE), jnp.float32)
    cut_square = jnp.zeros((R, WIDE), jnp.float32)
    for part in range(INNER):
        for k in range(CHUNKS):
            gradient = gr[k, part].astype(jnp.float32)
            if k < HEADS_DEV:
                head_square = head_square + squares(gradient)
            else:
                cut_square = cut_square + squares(gradient)
    pieces = (
        jnp.sum(head_square[:, : 3 * HD], axis=1, keepdims=True),
        jnp.sum(cut_square[:, :CUT], axis=1, keepdims=True),
        jnp.sum(head_square[:, 3 * HD :], axis=1, keepdims=True),
        jnp.sum(cut_square[:, CUT:], axis=1, keepdims=True),
    )
    line = jnp.zeros((R, 128), jnp.float32)
    for place, value in enumerate(pieces):
        line = jnp.where(lane_r == place, value, line)
    rsum[...] = line
    pair_copy(rsum, rsum_in, 1).start()

    pair_copy(terms, terms_in, 0).wait_recv()
    for i in range(2):
        rows = slice(i * HALF_T, (i + 1) * HALF_T)
        both = terms[rows, :] + terms_in[rows, :]
        ing_ref[rows, :] = (
            st[rows, 1:2]
            * (
                scaled_buf[rows, :]
                - both[:, 0:1] / D
                - normed_buf[rows, :] * (both[:, 1:2] / D)
            )
            + yin[rows, :].astype(jnp.float32)
        ).astype(jnp.bfloat16)
    pair_copy(rsum, rsum_in, 1).wait_recv()
    rows_after = renew_stat(row_old[...], (rsum[...] + rsum_in[...])[:, :4])
    row_new[...] = jnp.concatenate(
        [rows_after, jnp.zeros((R, 128 - 4), jnp.float32)], axis=1
    )

    chain_waits(pay, z_in, 0)
    acc = z_in[0]
    for j in range(1, outer):
        acc = acc + z_in[j]
    z_sum[...] = acc
    plane_sends(z_sum, p_in, 0, start)
    p_in[q] = acc
    plane_waits(z_sum, p_in, 0)
    p_sum[...] = p_in[0] + p_in[1] + p_in[2] + p_in[3]
    pair_copy(p_sum, s_in, 2).start()

    inverse_rows = 1.0 / rows_after
    head_acc = [jnp.zeros((R, 3 * HD), jnp.float32), jnp.zeros((R, HD), jnp.float32)]
    cut_acc = [jnp.zeros((R, CUT), jnp.float32), jnp.zeros((R, CUT), jnp.float32)]
    for part in range(INNER):
        sums = p_in[part]
        for h in range(HEADS_DEV):
            gradient = gr[h, part].astype(jnp.float32)
            square = gradient * gradient
            found = sums[h // 2 : h // 2 + 1, h % 2 * WIDE : (h % 2 + 1) * WIDE]
            cols = pl.ds(part * HEADS_DEV * HD + h * HD, HD)
            parts = []
            for p in range(3):
                fresh = renew_stat(qc_old[p : p + 1, cols], found[:, p * HD : (p + 1) * HD])
                qc_new[p : p + 1, cols] = fresh
                parts.append(1.0 / fresh)
            head_acc[0] = head_acc[0] + square[:, : 3 * HD] * jnp.concatenate(parts, axis=1)
            fresh = renew_stat(or_old[:, cols], found[:, 3 * HD :])
            or_new[:, cols] = fresh
            head_acc[1] = head_acc[1] + square[:, 3 * HD :] * (1.0 / fresh)
        for f in range(CUTS):
            k = HEADS_DEV + f
            gradient = gr[k, part].astype(jnp.float32)
            square = gradient * gradient
            found = sums[k // 2 : k // 2 + 1, k % 2 * WIDE : (k % 2 + 1) * WIDE]
            cols = slice(f * CUT, (f + 1) * CUT)
            fresh = renew_stat(f1_old[part : part + 1, cols], found[:, :CUT])
            f1_new[part, :, cols] = fresh
            cut_acc[0] = cut_acc[0] + square[:, :CUT] * (1.0 / fresh)
            fresh = renew_stat(f2_old[part : part + 1, cols], found[:, CUT:])
            f2_new[part, :, cols] = fresh
            cut_acc[1] = cut_acc[1] + square[:, CUT:] * (1.0 / fresh)
    for part in range(INNER):
        for h in range(HEADS_DEV):
            for p in range(3):
                low = h * 3 * HD + p * HD
                bias_grad[p : p + 1, pl.ds(part * HEADS_DEV * HD + h * HD, HD)] = p_in[
                    part, 3:4, low : low + HD
                ]
        fcb_grad[part : part + 1, :] = p_in[part, 4:5, :]
    bias_grad[3:4, :] = p_sum[9:10, :]
    bias_grad[4:5, :] = p_sum[9:10, :]
    bias_after, bias_update = second_step(bias_grad[...], bias_second[...])
    pack[17:22, :] = bias_after
    fcb_after, fcb_update = second_step(fcb_grad[...], fcb_second[...])
    pack[31:35, :] = fcb_after
    usq = jnp.sum(bias_update * bias_update, axis=1, keepdims=True) * on_b
    scalars = (
        [
            total_of(rows_after[:, 0:1]) * on_c,
            total_of(head_acc[0] * inverse_rows[:, 0:1]),
            total_of(rows_after[:, 1:2]) * on_c,
            total_of(cut_acc[0] * inverse_rows[:, 1:2]),
            total_of(or_new[...]) * on_b,
            total_of(head_acc[1] * inverse_rows[:, 2:3]),
            sum(total_of(f2_new[part]) for part in range(INNER)) * on_b,
            total_of(cut_acc[1] * inverse_rows[:, 3:4]),
        ]
        + [usq[i : i + 1] for i in range(5)]
        + [total_of(fcb_update * fcb_update) * on_b]
    )
    lane_s = lax.broadcasted_iota(jnp.int32, (8, 128), 1)
    line = jnp.zeros((8, 128), jnp.float32)
    for place, value in enumerate(scalars):
        line = jnp.where(lane_s == place, value, line)
    pay2[...] = line
    chain_sends(pay2, z2_in, 1, start)
    z2_in[o] = line
    pack[0:3, :] = qc_new[...]
    pack[3:4, :] = or_new[...]
    for part in range(INNER):
        pack[4 + part : 5 + part, :] = f1_new[part]
        pack[8 + part : 9 + part, :] = f2_new[part]
    pack[12:17, :] = bias_grad[...]
    pack[27:31, :] = fcb_grad[...]

    pair_copy(p_sum, s_in, 2).wait_recv()
    norm_grad[:, own_half] = p_sum[5:9, :]
    norm_grad[:, other_half] = s_in[5:9, :]
    old = p_sum[10:11, :] + s_in[10:11, :]
    norm_after, norm_update = second_step(norm_grad[...], norm_second[...])
    norm_pack[0:4, :] = norm_grad[...]
    norm_pack[4:8, :] = norm_after

    def moved(vector, update, update_square, old_square, entries):
        clip_factor = jnp.maximum(1.0, jnp.sqrt(update_square / entries))
        step_rate = RATE * jnp.maximum(FLOOR_RATE, jnp.sqrt(old_square / entries))
        return vector - step_rate * update / clip_factor

    norm_values = norm_ref[...]
    norm_pack[8:12, :] = moved(
        norm_values,
        norm_update,
        jnp.sum(norm_update * norm_update, axis=1, keepdims=True),
        jnp.sum(norm_values * norm_values, axis=1, keepdims=True),
        D,
    )

    chain_waits(pay2, z2_in, 1)
    acc = z2_in[0]
    for j in range(1, outer):
        acc = acc + z2_in[j]
    z2_sum[...] = acc
    plane_sends(z2_sum, p2_in, 1, start)
    p2_in[q] = acc
    plane_waits(z2_sum, p2_in, 1)
    acc = p2_in[0] + p2_in[1] + p2_in[2] + p2_in[3]
    p2_sum[...] = acc
    pair_copy(p2_sum, s2_in, 3).start()
    pair_copy(p2_sum, s2_in, 3).wait_recv()
    sums = (acc + s2_in[...])[0:1, :]

    def scalar(place):
        return sums[:, place : place + 1]

    def factor(total, inverse, place, entries):
        clip_factor = jnp.maximum(1.0, jnp.sqrt(total * inverse / entries))
        rate = RATE * jnp.maximum(FLOOR_RATE, jnp.sqrt(old[:, place : place + 1] / entries))
        return rate * jnp.sqrt(total) / clip_factor

    factors = (
        factor(scalar(0), scalar(1), 0, 3 * D * D),
        factor(scalar(2), scalar(3), 2, D * FF),
        factor(scalar(4), scalar(5), 1, D * D),
        factor(scalar(6), scalar(7), 3, FF * D),
    )
    line = jnp.zeros((8, 128), jnp.float32)
    for place, value in enumerate(factors):
        line = jnp.where(lane_s == place, value, line)
    pack[39:40, :] = jnp.concatenate(
        [line[0:1, :], jnp.zeros((1, half - 128), jnp.float32)], axis=1
    )
    for i in range(5):
        pack[22 + i : 23 + i, :] = moved(
            pb[i : i + 1, :], bias_update[i : i + 1], scalar(8 + i), old[:, 4 + i : 5 + i], D
        )
    pack[35:39, :] = moved(fcb[...], fcb_update, scalar(13), old[:, 9:10], FF)

    finish = lambda copy: copy.wait_send()
    chain_sends(pay, z_in, 0, finish)
    chain_sends(pay2, z2_in, 1, finish)
    plane_sends(z_sum, p_in, 0, finish)
    plane_sends(z2_sum, p2_in, 1, finish)
    pair_copy(terms, terms_in, 0).wait_send()
    pair_copy(rsum, rsum_in, 1).wait_send()
    pair_copy(p_sum, s_in, 2).wait_send()
    pair_copy(p2_sum, s2_in, 3).wait_send()


def tail_call(count, *args):
    outer = count // INNER
    received, xin = args[0], args[7]
    tokens, half = xin.shape
    rows = received.shape[2]
    high = jnp.float32
    spec = pl.BlockSpec(memory_space=pltpu.VMEM)
    dma = pltpu.SemaphoreType.DMA

    def out(*shape, dtype=high):
        return jax.ShapeDtypeStruct(shape, dtype)

    outs = [
        out(tokens, half, dtype=jnp.bfloat16),
        out(tokens, half, dtype=jnp.bfloat16),
        out(rows, 128),
        out(PACK_ROWS, half),
        out(12, D),
    ]
    slot = (SLOT_ROWS, half)
    return pl.pallas_call(
        functools.partial(tail_kernel, count),
        out_shape=outs,
        in_specs=[spec] * len(args),
        out_specs=[spec] * len(outs),
        scratch_shapes=[
            pltpu.VMEM((3, half), high),
            pltpu.VMEM((1, half), high),
            pltpu.VMEM((INNER, 1, half), high),
            pltpu.VMEM((INNER, 1, half), high),
            pltpu.VMEM((4, D), high),
            pltpu.VMEM((5, half), high),
            pltpu.VMEM((INNER, half), high),
            pltpu.VMEM((tokens, half), high),
            pltpu.VMEM((tokens, half), high),
            pltpu.VMEM((tokens, 128), high),
            pltpu.VMEM((tokens, 128), high),
            pltpu.VMEM((rows, 128), high),
            pltpu.VMEM((rows, 128), high),
            pltpu.VMEM(slot, high),
            pltpu.VMEM((outer, *slot), high),
            pltpu.VMEM(slot, high),
            pltpu.VMEM((INNER, *slot), high),
            pltpu.VMEM(slot, high),
            pltpu.VMEM(slot, high),
            pltpu.VMEM((8, 128), high),
            pltpu.VMEM((outer, 8, 128), high),
            pltpu.VMEM((8, 128), high),
            pltpu.VMEM((INNER, 8, 128), high),
            pltpu.VMEM((8, 128), high),
            pltpu.VMEM((8, 128), high),
            dma((2, outer - 1)),
            dma((2, outer - 1)),
            dma((2, INNER - 1)),
            dma((2, INNER - 1)),
            dma((4,)),
            dma((4,)),
        ],
        compiler_params=pltpu.CompilerParams(
            collective_id=1, has_side_effects=True, vmem_limit_bytes=58 * 1024 * 1024
        ),
        cost_estimate=pl.CostEstimate(
            flops=50_000_000, bytes_accessed=40_000_000, transcendentals=100_000
        ),
    )(*args)


def update_kernel(*refs):
    gr, wq, wo, w1, w2, row_new, pack, norm_pack, output, input_grad = refs[:10]
    q_grad, q_next, q_copy, o_grad, o_next, o_copy = refs[10:16]
    f1_grad, f1_next, f1_copy, f2_grad, f2_next, f2_copy = refs[16:22]
    row_out, whole_out, pack_out, norm_out = refs[22:26], refs[26:28], refs[28:38], refs[38:]
    part = pl.program_id(0)
    side = lax.rsqrt(row_new[:, :4]) * pack[39:40, :4]
    width_q = HEADS_DEV * HD

    @pl.when(part == 0)
    def _():
        whole_out[0][...] = output[...]
        whole_out[1][...] = input_grad[...]
        for place, target in enumerate(pack_out):
            target[...] = pack[PACK_ENDS[place] : PACK_ENDS[place + 1], :]
        for place, target in enumerate(norm_out):
            target[...] = norm_pack[4 * place : 4 * place + 4, :]
        turned = row_new[...].T
        for place in range(4):
            row_out[place][...] = turned[place : place + 1, :]

    def put(grad_ref, next_ref, copy_ref, where, weight, gradient, update):
        fresh = weight[where] - update
        grad_ref[where] = gradient
        next_ref[where] = fresh
        copy_ref[where] = fresh.astype(jnp.bfloat16)

    for h in range(HEADS_DEV):
        gradient = gr[h, 0].astype(jnp.float32)
        cols = pl.ds(pl.multiple_of(part * width_q + h * HD, HD), HD)
        for p in range(3):
            mine = gradient[:, p * HD : (p + 1) * HD]
            update = mine * side[:, 0:1] * lax.rsqrt(pack[p : p + 1, cols])
            where = (p, slice(None), slice(h * HD, (h + 1) * HD))
            put(q_grad, q_next, q_copy, where, wq, mine, update)
        mine = gradient[:, 3 * HD :]
        update = mine * side[:, 2:3] * lax.rsqrt(pack[3:4, cols])
        where = (slice(h * HD, (h + 1) * HD), slice(None))
        put(o_grad, o_next, o_copy, where, wo, mine.T, update.T)
    for f in range(CUTS):
        gradient = gr[HEADS_DEV + f, 0].astype(jnp.float32)
        cols = slice(f * CUT, (f + 1) * CUT)
        mine = gradient[:, :CUT]
        update = mine * side[:, 1:2] * lax.rsqrt(pack[pl.ds(4 + part, 1), cols])
        put(f1_grad, f1_next, f1_copy, (slice(None), cols), w1, mine, update)
        mine = gradient[:, CUT:]
        update = mine * side[:, 3:4] * lax.rsqrt(pack[pl.ds(8 + part, 1), cols])
        put(f2_grad, f2_next, f2_copy, (cols, slice(None)), w2, mine.T, update.T)


def update_call(gr, wq, wo, w1, w2, row_new, pack, norm_pack, output, input_grad):
    rows = gr.shape[2]
    half = pack.shape[1]
    width_q = HEADS_DEV * HD
    hidden_q = CUTS * CUT
    spec = pl.BlockSpec
    q_spec = spec((3, rows, width_q), lambda i: (0, 0, i))
    o_spec = spec((width_q, rows), lambda i: (i, 0))
    f1_spec = spec((rows, hidden_q), lambda i: (0, i))
    f2_spec = spec((hidden_q, rows), lambda i: (i, 0))
    outs, out_specs = [], []
    for array, its in ((wq, q_spec), (wo, o_spec), (w1, f1_spec), (w2, f2_spec)):
        for dtype in (jnp.float32, jnp.float32, jnp.bfloat16):
            outs.append(jax.ShapeDtypeStruct(array.shape, dtype))
            out_specs.append(its)

    def fixed(shape):
        return spec(shape, lambda i: (0,) * len(shape))

    shapes = [((1, rows), jnp.float32)] * 4 + [(output.shape, output.dtype)] * 2
    for place in range(len(PACK_ENDS) - 1):
        shapes.append(((PACK_ENDS[place + 1] - PACK_ENDS[place], half), jnp.float32))
    shapes += [((4, D), jnp.float32)] * 3
    for shape, dtype in shapes:
        outs.append(jax.ShapeDtypeStruct(shape, dtype))
        out_specs.append(fixed(shape))
    small = (row_new, pack, norm_pack, output, input_grad)
    return pl.pallas_call(
        update_kernel,
        grid=(INNER,),
        out_shape=outs,
        in_specs=[
            spec((CHUNKS, 1, rows, WIDE), lambda i: (0, i, 0, 0)),
            q_spec,
            o_spec,
            f1_spec,
            f2_spec,
        ]
        + [fixed(array.shape) for array in small],
        out_specs=out_specs,
        compiler_params=pltpu.CompilerParams(vmem_limit_bytes=48 * 1024 * 1024),
        cost_estimate=pl.CostEstimate(
            flops=20_000_000, bytes_accessed=30_000_000, transcendentals=100_000
        ),
    )(gr, wq, wo, w1, w2, *small)


def swap_pairs(count, step):
    return [(i, i ^ step) for i in range(count)]


def block_of(array, index, size, axis=0):
    return lax.dynamic_slice_in_dim(array, index * size, size, axis)


def on_device(
    inputs,
    cotangent,
    segment_ids,
    w_qkv,
    w_out,
    w_fc1,
    w_fc2,
    norm_params,
    proj_bias,
    fc1_bias,
    qkv_rows,
    qkv_cols,
    out_rows,
    out_cols,
    fc1_rows,
    fc1_cols,
    fc2_rows,
    fc2_cols,
    norm_second,
    bias_second,
    fc1b_second,
):
    tokens = inputs.shape[0]
    local_width = inputs.shape[1]
    local_hidden = fc1_bias.shape[0]
    rows = w_qkv.shape[0]
    count = lax.axis_size("batch")
    c = lax.axis_index("branch")
    b = lax.axis_index("batch")
    q = lax.rem(b, INNER)
    group = INNER * tokens
    width_q = local_width // INNER
    hidden_q = local_hidden // INNER
    qkv_low = w_qkv.astype(jnp.bfloat16).reshape(rows, 3, INNER, HEADS_DEV, HD)
    out_low = w_out.astype(jnp.bfloat16).reshape(INNER, HEADS_DEV, HD, rows)
    fc1_low = w_fc1.astype(jnp.bfloat16).reshape(rows, INNER, CUTS, CUT)
    fc2_low = w_fc2.astype(jnp.bfloat16).reshape(INNER, CUTS, CUT, rows)
    heads_low = jnp.concatenate(
        [
            qkv_low.transpose(3, 2, 0, 1, 4).reshape(HEADS_DEV, INNER, rows, 3 * HD),
            out_low.transpose(1, 0, 3, 2),
        ],
        axis=3,
    )
    cuts_low = jnp.concatenate(
        [fc1_low.transpose(2, 1, 0, 3), fc2_low.transpose(1, 0, 3, 2)], axis=3
    )
    wst = jnp.concatenate([heads_low, cuts_low], axis=0)

    segment = jnp.concatenate(
        [segment_ids]
        + [lax.ppermute(segment_ids, "batch", swap_pairs(count, d)) for d in range(1, INNER)],
        axis=0,
    )
    positions_idx = jnp.arange(tokens)
    earlier = jnp.sum((segment[:, None, :] < segment[:, :, None]).astype(jnp.int32), axis=2)
    starts = earlier.astype(jnp.float32).reshape(1, group)
    places = (positions_idx[None] - earlier).astype(jnp.float32).reshape(1, group)
    frequency = 10000.0 ** (-2.0 * jnp.arange(ROT // 2, dtype=jnp.float32) / ROT)
    angles = frequency[:, None] * places
    cos_part = jnp.cos(angles)
    sin_part = jnp.sin(angles)
    turns = jnp.concatenate(
        [
            cos_part,
            cos_part,
            -sin_part,
            sin_part,
            jnp.broadcast_to(starts, (HD - 2 * ROT, group)),
        ],
        axis=0,
    )
    bias_h = (
        block_of(proj_bias[0:3], q, width_q, 1)
        .reshape(3, HEADS_DEV, HD)
        .transpose(1, 0, 2)
        .reshape(HEADS_DEV, 1, 3 * HD)
    )
    bias_f = block_of(fc1_bias, q, hidden_q).reshape(CUTS, 1, CUT)
    received, plane_parts, plane_own, head_bias, cut_bias, col_sums, row_moments = block_call(
        count, wst, inputs, cotangent, turns, norm_params, bias_h, bias_f
    )
    by_part = (INNER, hidden_q)
    qkv_parts = w_qkv.transpose(1, 0, 2)
    output, input_grad, row_stats, pack, norm_pack = tail_call(
        count,
        received,
        qkv_parts.reshape(3 * rows, local_width),
        w_out,
        w_fc1,
        w_fc2,
        plane_parts,
        plane_own,
        inputs,
        cotangent,
        row_moments,
        norm_params,
        proj_bias,
        fc1_bias.reshape(by_part),
        jnp.stack([qkv_rows, fc1_rows, out_cols, fc2_cols], axis=1),
        qkv_cols,
        out_rows.reshape(1, local_width),
        fc1_cols.reshape(by_part),
        fc2_rows.reshape(by_part),
        norm_second,
        bias_second,
        fc1b_second.reshape(by_part),
        col_sums,
        head_bias,
        cut_bias,
    )
    updated = update_call(
        received,
        qkv_parts,
        w_out,
        w_fc1,
        w_fc2,
        row_stats,
        pack,
        norm_pack,
        output,
        input_grad,
    )
    qkv_grad, qkv_next, qkv_copy = (array.transpose(1, 0, 2) for array in updated[0:3])
    out_grad, out_next, out_copy = updated[3:6]
    fc1_grad, fc1_next, fc1_copy = updated[6:9]
    fc2_grad, fc2_next, fc2_copy = updated[9:12]
    qkv_rows_new, fc1_rows_new, out_cols_new, fc2_cols_new = (
        array.reshape(rows) for array in updated[12:16]
    )
    (
        output,
        input_grad,
        qkv_cols_new,
        out_rows_new,
        fc1_cols_new,
        fc2_rows_new,
        bias_grad,
        bias_moment,
        bias_new,
        fc1b_grad,
        fc1b_moment,
        fc1b_new,
        norm_grad,
        norm_moment,
        norm_new,
    ) = updated[16:]
    return (
        output,
        input_grad,
        qkv_grad,
        qkv_next,
        qkv_rows_new,
        qkv_cols_new,
        qkv_copy,
        out_grad,
        out_next,
        out_rows_new.reshape(local_width),
        out_cols_new,
        out_copy,
        fc1_grad,
        fc1_next,
        fc1_rows_new,
        fc1_cols_new.reshape(local_hidden),
        fc1_copy,
        fc2_grad,
        fc2_next,
        fc2_rows_new.reshape(local_hidden),
        fc2_cols_new,
        fc2_copy,
        norm_grad,
        norm_moment,
        norm_new,
        bias_grad,
        bias_moment,
        bias_new,
        fc1b_grad.reshape(local_hidden),
        fc1b_moment.reshape(local_hidden),
        fc1b_new.reshape(local_hidden),
    )


def solution(mesh):
    in_specs = (
        P("batch", "branch"),
        P("batch", "branch"),
        P("batch", None),
        P("batch", None, "branch"),
        P("branch", "batch"),
        P("batch", "branch"),
        P("branch", "batch"),
        P(),
        P(None, "branch"),
        P("branch"),
        P("batch"),
        P(None, "branch"),
        P("branch"),
        P("batch"),
        P("batch"),
        P("branch"),
        P("branch"),
        P("batch"),
        P(),
        P(None, "branch"),
        P("branch"),
    )
    out_specs = (
        P("batch", "branch"),
        P("batch", "branch"),
        P("batch", None, "branch"),
        P("batch", None, "branch"),
        P("batch"),
        P(None, "branch"),
        P("batch", None, "branch"),
        P("branch", "batch"),
        P("branch", "batch"),
        P("branch"),
        P("batch"),
        P("branch", "batch"),
        P("batch", "branch"),
        P("batch", "branch"),
        P("batch"),
        P("branch"),
        P("batch", "branch"),
        P("branch", "batch"),
        P("branch", "batch"),
        P("branch"),
        P("batch"),
        P("branch", "batch"),
        P(),
        P(),
        P(),
        P(None, "branch"),
        P(None, "branch"),
        P(None, "branch"),
        P("branch"),
        P("branch"),
        P("branch"),
    )
    return jax.shard_map(
        on_device, mesh=mesh, in_specs=in_specs, out_specs=out_specs, check_vma=False
    )
```
